32 devices in a mesh: dp: 8 (over z, y), mp: 4 (over x, core).
Axes of the slice: x: 2, y: 2, z: 4, core: 2. Of those that a mesh axis runs over, the one named last changes fastest.
Arguments:
- inputs: bfloat16 [1024, 4, 5632], P('mp', None, 'dp'), may hold values from -13 to 13
- pixel_mask: int32 [4, 5632], P(None, 'dp'), may hold values from 0 to 1, as said below
- widths: int32 [2], replicated, may hold values from 288 to 512, as said below
- output_grad: bfloat16 [2048, 5632], P('mp', 'dp'), may hold values from -6 to 6
- first_weight: float32 [1024, 512], P('dp', 'mp'), may hold values from -1.5 to 1.5
- shortcut_weight: float32 [1024, 2048], P('dp', 'mp'), may hold values from -1.5 to 1.5
- middle_weight: float32 [2, 9, 512, 512], P(None, None, 'dp', 'mp'), may hold values from -1.5 to 1.5
- last_weight: float32 [2, 512, 2048], P(None, 'mp', 'dp'), may hold values from -1.5 to 1.5
- second_weight: float32 [2048, 512], P('dp', 'mp'), may hold values from -1.5 to 1.5
- narrow_norms: float32 [4, 2, 512], P(None, None, 'mp'), may hold values from -2 to 5, as said below
- wide_norms: float32 [3, 2, 2048], P(None, None, 'mp'), may hold values from -2 to 5, as said below
- first_mean: float32 [1024, 512], P('dp', 'mp'), may hold values from -38 to 38
- first_square: float32 [1024, 512], P('dp', 'mp'), may hold values from 0 to 19
- shortcut_mean: float32 [1024, 2048], P('dp', 'mp'), may hold values from -38 to 38
- shortcut_square: float32 [1024, 2048], P('dp', 'mp'), may hold values from 0 to 19
- middle_mean: float32 [2, 9, 512, 512], P(None, None, 'dp', 'mp'), may hold values from -38 to 38
- middle_square: float32 [2, 9, 512, 512], P(None, None, 'dp', 'mp'), may hold values from 0 to 19
- last_mean: float32 [2, 512, 2048], P(None, 'mp', 'dp'), may hold values from -38 to 38
- last_square: float32 [2, 512, 2048], P(None, 'mp', 'dp'), may hold values from 0 to 19
- second_mean: float32 [2048, 512], P('dp', 'mp'), may hold values from -38 to 38
- second_square: float32 [2048, 512], P('dp', 'mp'), may hold values from 0 to 19
- narrow_mean: float32 [4, 2, 512], P(None, None, 'mp'), may hold values from -38 to 38
- narrow_square: float32 [4, 2, 512], P(None, None, 'mp'), may hold values from 0 to 19
- wide_mean: float32 [3, 2, 2048], P(None, None, 'mp'), may hold values from -38 to 38
- wide_square: float32 [3, 2, 2048], P(None, None, 'mp'), may hold values from 0 to 19
Outputs:
- block_output: bfloat16 [2048, 5632], P('mp', 'dp')
- input_grad: bfloat16 [1024, 4, 5632], P('mp', None, 'dp')
- first_mean_next: float32 [1024, 512], P('dp', 'mp')
- first_square_next: float32 [1024, 512], P('dp', 'mp')
- first_weight_next: float32 [1024, 512], P('dp', 'mp')
- shortcut_mean_next: float32 [1024, 2048], P('dp', 'mp')
- shortcut_square_next: float32 [1024, 2048], P('dp', 'mp')
- shortcut_weight_next: float32 [1024, 2048], P('dp', 'mp')
- middle_mean_next: float32 [2, 9, 512, 512], P(None, None, 'dp', 'mp')
- middle_square_next: float32 [2, 9, 512, 512], P(None, None, 'dp', 'mp')
- middle_weight_next: float32 [2, 9, 512, 512], P(None, None, 'dp', 'mp')
- last_mean_next: float32 [2, 512, 2048], P(None, 'mp', 'dp')
- last_square_next: float32 [2, 512, 2048], P(None, 'mp', 'dp')
- last_weight_next: float32 [2, 512, 2048], P(None, 'mp', 'dp')
- second_mean_next: float32 [2048, 512], P('dp', 'mp')
- second_square_next: float32 [2048, 512], P('dp', 'mp')
- second_weight_next: float32 [2048, 512], P('dp', 'mp')
- narrow_mean_next: float32 [4, 2, 512], P(None, None, 'mp')
- narrow_square_next: float32 [4, 2, 512], P(None, None, 'mp')
- narrow_norms_next: float32 [4, 2, 512], P(None, None, 'mp')
- wide_mean_next: float32 [3, 2, 2048], P(None, None, 'mp')
- wide_square_next: float32 [3, 2, 2048], P(None, None, 'mp')
- wide_norms_next: float32 [3, 2, 2048], P(None, None, 'mp')
- matrix_norms: float32 [7, 2], replicated
- first_weight_copy: bfloat16 [1024, 512], P('dp', 'mp')
- shortcut_weight_copy: bfloat16 [1024, 2048], P('dp', 'mp')
- middle_weight_copy: bfloat16 [2, 9, 512, 512], P(None, None, 'dp', 'mp')
- last_weight_copy: bfloat16 [2, 512, 2048], P(None, 'mp', 'dp')
- second_weight_copy: bfloat16 [2048, 512], P('dp', 'mp')
The draws below stay inside these ranges and needn't reach their ends.
Inputs may be any that keep to these rules, and one draw needn't show every extreme that they name: `pixel_mask`: each image's ones form the top-left rectangle of its 32 x 2 * 11 pixels, seen through the four phases; every image of the last index of dp is all ones. `widths`: both are multiples of 32, at least 288; one of the two is 512. `narrow_norms`: index 0 of the second dimension holds gains, index 1 biases. `wide_norms`: index 0 of the second dimension holds gains, index 1 biases.
All inputs are finite; a program needn't handle non-finite values.
Results may differ from the reference program's by a relative error of at most 0.02.
Values may be sent and summed in bfloat16 or wider, within the bound.
No kernel may reach another device: no remote copies, remote signals or barrier semaphores. Data moves between devices by JAX's collectives and lax.ppermute only.
A program may use at most 192 MiB of HBM per device.

```python
import jax
import jax.numpy as jnp
from jax import lax

CIN = 1024
C = 512
COUT = 2048
IMG_DEV = 4
HO = 16
WO = 11
STEP = 10
IMGS = 32
PIX = 5632


def ramp(count, top):
    steps = jnp.arange(count, dtype=jnp.float32) / max(count - 1, 1)
    return 1.0 + (top - 1.0) * steps


def grid(shape, dims, top):
    total = jnp.ones(shape, jnp.float32)
    for dim in dims:
        sizes = [1] * len(shape)
        sizes[dim] = shape[dim]
        total = total * ramp(shape[dim], top).reshape(sizes)
    return total


def entries(key, shape, flat):
    normal = jnp.clip(jax.random.normal(key, shape, jnp.float32), -5.0, 5.0)
    even = jax.random.uniform(jax.random.fold_in(key, 1), shape, jnp.float32, -1.7320508, 1.7320508)
    return (1.0 - flat) * normal + flat * even


def matrix(key, shape, dims, fan_in, top, flat):
    level = ((1.0 + top) / 2.0) ** len(dims)
    return entries(key, shape, flat) * jnp.sqrt(grid(shape, dims, top) / level) / fan_in ** 0.5


def first_state(key, shape, size):
    return entries(key, shape, 0.0) * (size / 9.0)


def second_state(key, shape, dims, size):
    spread = jnp.exp(jax.random.uniform(key, shape, jnp.float32, -0.6931472, 0.6931472))
    return spread * grid(shape, dims, 2.0) * (size * size / 999.0)


def grad_size(factor):
    return factor * float(IMGS * HO * WO) ** 0.5


def norm_table(key, rows, width, top, flat):
    scale = jnp.exp(jax.random.uniform(key, (rows, 1, width), jnp.float32, -0.35, 0.35))
    gains = 0.6 * ramp(width, top).reshape(1, 1, width) * scale
    biases = 0.3 * entries(jax.random.fold_in(key, 2), (rows, 1, width), flat)
    return jnp.concatenate([gains, biases], 1)


def draw_inputs(key, part):
    key = jax.random.fold_in(key, 1)
    top = 3.0
    flat = 0.0
    scale = 0.6 * ramp(CIN, top) * jnp.exp(jax.random.uniform(jax.random.fold_in(key, 5), (CIN,), jnp.float32, -0.35, 0.35))
    return (entries(key, (CIN, 4, IMGS * HO * WO), flat) * scale[:, None, None]).astype(jnp.bfloat16)


def draw_pixel_mask(key, part):
    key = jax.random.fold_in(key, 11)
    owners = jnp.arange(IMGS, dtype=jnp.int32) // IMG_DEV
    span = max(IMGS // IMG_DEV - 1, 1)
    tall = 2 * HO
    broad = 2 * WO
    low_rows = tall // 4 + (tall - tall // 4) * owners // span
    low_cols = broad // 4 + (broad - broad // 4) * owners // span
    heights = jax.random.randint(key, (IMGS,), low_rows, tall + 1)
    lengths = jax.random.randint(jax.random.fold_in(key, 1), (IMGS,), low_cols, broad + 1)
    phase = jnp.arange(4, dtype=jnp.int32)
    rows_at = 2 * jnp.arange(HO, dtype=jnp.int32)[None, None, :, None] + (phase // 2)[:, None, None, None]
    cols_at = 2 * jnp.arange(WO, dtype=jnp.int32)[None, None, None, :] + (phase % 2)[:, None, None, None]
    inside = (rows_at < heights[None, :, None, None]) & (cols_at < lengths[None, :, None, None])
    return inside.astype(jnp.int32).reshape(4, IMGS * HO * WO)


def draw_widths(key, part):
    key = jax.random.fold_in(key, 12)
    picks = jax.random.randint(key, (2,), 9, 17) * (C // 16)
    full_one = jax.random.randint(jax.random.fold_in(key, 1), (), 0, 2)
    return jnp.where(jnp.arange(2) == full_one, C, picks).astype(jnp.int32)


def draw_first_weight(key, part):
    key = jax.random.fold_in(key, 21)
    return matrix(key, (CIN, C), (0, 1), CIN, 3.0, 0.0)


def draw_shortcut_weight(key, part):
    key = jax.random.fold_in(key, 22)
    return matrix(key, (CIN, COUT), (0, 1), CIN, 3.0, 0.0)


def draw_middle_weight(key, part):
    key = jax.random.fold_in(key, 23)
    return matrix(key, (2, 9, C, C), (2, 3), 9 * C, 3.0, 0.0)


def draw_last_weight(key, part):
    key = jax.random.fold_in(key, 24)
    return matrix(key, (2, C, COUT), (1, 2), C, 3.0, 0.0)


def draw_second_weight(key, part):
    key = jax.random.fold_in(key, 25)
    return matrix(key, (COUT, C), (0, 1), COUT, 3.0, 0.0)


def draw_narrow_norms(key, part):
    key = jax.random.fold_in(key, 26)
    return norm_table(key, 4, C, 3.0, 0.0)


def draw_wide_norms(key, part):
    key = jax.random.fold_in(key, 27)
    return norm_table(key, 3, COUT, 3.0, 0.0)


def draw_first_mean(key, part):
    key = jax.random.fold_in(key, 31)
    return first_state(key, (CIN, C), grad_size(0.6))


def draw_first_square(key, part):
    key = jax.random.fold_in(key, 32)
    return second_state(key, (CIN, C), (0, 1), grad_size(0.6))


def draw_shortcut_mean(key, part):
    key = jax.random.fold_in(key, 33)
    return first_state(key, (CIN, COUT), grad_size(0.3))


def draw_shortcut_square(key, part):
    key = jax.random.fold_in(key, 34)
    return second_state(key, (CIN, COUT), (0, 1), grad_size(0.3))


def draw_middle_mean(key, part):
    key = jax.random.fold_in(key, 35)
    return first_state(key, (2, 9, C, C), grad_size(0.3))


def draw_middle_square(key, part):
    key = jax.random.fold_in(key, 36)
    return second_state(key, (2, 9, C, C), (2, 3), grad_size(0.3))


def draw_last_mean(key, part):
    key = jax.random.fold_in(key, 37)
    return first_state(key, (2, C, COUT), grad_size(0.3))


def draw_last_square(key, part):
    key = jax.random.fold_in(key, 38)
    return second_state(key, (2, C, COUT), (1, 2), grad_size(0.3))


def draw_second_mean(key, part):
    key = jax.random.fold_in(key, 39)
    return first_state(key, (COUT, C), grad_size(0.3))


def draw_second_square(key, part):
    key = jax.random.fold_in(key, 40)
    return second_state(key, (COUT, C), (0, 1), grad_size(0.3))


def draw_narrow_mean(key, part):
    key = jax.random.fold_in(key, 41)
    return first_state(key, (4, 2, C), grad_size(0.4))


def draw_narrow_square(key, part):
    key = jax.random.fold_in(key, 42)
    return second_state(key, (4, 2, C), (2,), grad_size(0.4))


def draw_wide_mean(key, part):
    key = jax.random.fold_in(key, 43)
    return first_state(key, (3, 2, COUT), grad_size(0.3))


def draw_wide_square(key, part):
    key = jax.random.fold_in(key, 44)
    return second_state(key, (3, 2, COUT), (2,), grad_size(0.3))


def block_levels(key, extent, cuts, least, top_value):
    def one(axis_at, shards_of):
        steps = jax.random.uniform(jax.random.fold_in(jax.random.fold_in(key, 6), axis_at), (shards_of,), jnp.float32, least / len(cuts), top_value / len(cuts))
        return jnp.repeat(jnp.exp(steps), extent[axis_at] // shards_of).reshape((-1,) + (1,) * (len(extent) - axis_at - 1))

    level = one(*cuts[0])
    for cut in cuts[1:]:
        level = level * one(*cut)
    return level


def bell_draw(rng, extent, scale, reach, split=(), kind=jnp.bfloat16):
    values = scale * jax.random.normal(rng, extent, jnp.float32)
    if split:
        values = values * block_levels(rng, extent, split, -0.22, 0.18)
    return jnp.clip(values, -reach, reach).astype(kind)


def setup_inputs(seed: int = 0) -> dict:
    streams_of = jax.random.split(jax.random.key(seed), 26)
    return {
        "inputs": draw_inputs(jax.random.fold_in(streams_of[25], 71), 0),
        "pixel_mask": draw_pixel_mask(jax.random.fold_in(streams_of[25], 71), 0),
        "widths": draw_widths(jax.random.fold_in(streams_of[25], 71), 0),
        "output_grad": bell_draw(streams_of[3], (COUT, PIX), 1.0, 6.0, ((0, 4), (1, 8))),
        "first_weight": draw_first_weight(jax.random.fold_in(streams_of[25], 71), 0),
        "shortcut_weight": draw_shortcut_weight(jax.random.fold_in(streams_of[25], 71), 0),
        "middle_weight": draw_middle_weight(jax.random.fold_in(streams_of[25], 71), 0),
        "last_weight": draw_last_weight(jax.random.fold_in(streams_of[25], 71), 0),
        "second_weight": draw_second_weight(jax.random.fold_in(streams_of[25], 71), 0),
        "narrow_norms": draw_narrow_norms(jax.random.fold_in(streams_of[25], 71), 0),
        "wide_norms": draw_wide_norms(jax.random.fold_in(streams_of[25], 71), 0),
        "first_mean": draw_first_mean(jax.random.fold_in(streams_of[25], 71), 0),
        "first_square": draw_first_square(jax.random.fold_in(streams_of[25], 71), 0),
        "shortcut_mean": draw_shortcut_mean(jax.random.fold_in(streams_of[25], 71), 0),
        "shortcut_square": draw_shortcut_square(jax.random.fold_in(streams_of[25], 71), 0),
        "middle_mean": draw_middle_mean(jax.random.fold_in(streams_of[25], 71), 0),
        "middle_square": draw_middle_square(jax.random.fold_in(streams_of[25], 71), 0),
        "last_mean": draw_last_mean(jax.random.fold_in(streams_of[25], 71), 0),
        "last_square": draw_last_square(jax.random.fold_in(streams_of[25], 71), 0),
        "second_mean": draw_second_mean(jax.random.fold_in(streams_of[25], 71), 0),
        "second_square": draw_second_square(jax.random.fold_in(streams_of[25], 71), 0),
        "narrow_mean": draw_narrow_mean(jax.random.fold_in(streams_of[25], 71), 0),
        "narrow_square": draw_narrow_square(jax.random.fold_in(streams_of[25], 71), 0),
        "wide_mean": draw_wide_mean(jax.random.fold_in(streams_of[25], 71), 0),
        "wide_square": draw_wide_square(jax.random.fold_in(streams_of[25], 71), 0),
    }


EPS_NORM = 1e-05
BETA_ONE = 0.9
BETA_TWO = 0.999
EPS_ADAM = 1e-06
DECAY = 0.01
RATE = 0.3
RATE_NORM = 0.3
EPS_TRUST = 1e-06
HIGH = lax.Precision.HIGHEST
PHASES = ((1, -1), (0, 0), (1, 0))

@jax.custom_vjp
def low(v):
    return lax.optimization_barrier(v.astype(jnp.bfloat16)).astype(jnp.float32)

@jax.custom_vjp
def low_back(v):
    return v

def low_keep(v):
    return (low(v), None)

def low_pass(kept, grad):
    return (grad,)

def back_keep(v):
    return (v, None)

def back_low(kept, grad):
    return (low(grad),)
low.defvjp(low_keep, low_pass)
low_back.defvjp(back_keep, back_low)

def move(values, drow, dcol):
    chans = values.shape[0]
    grid = values.reshape(chans, -1, HO, WO)
    grid = jnp.pad(grid, ((0, 0), (0, 0), (1, 1), (1, 1)))
    grid = grid[:, :, 1 + drow:1 + drow + HO, 1 + dcol:1 + dcol + WO]
    return grid.reshape(chans, -1)

def mix(weight, values):
    return jnp.einsum('kc,kp->cp', weight, values, precision=HIGH)

def normalize(values, mask, gain, bias):
    count = jnp.sum(mask)
    mean = lax.optimization_barrier(jnp.sum(values * mask[None, :], 1)) / count
    square = lax.optimization_barrier(jnp.sum(values * values * mask[None, :], 1)) / count
    scale = lax.rsqrt(square - mean * mean + EPS_NORM)
    return (values - mean[:, None]) * (scale * gain)[:, None] + bias[:, None]

def conv(hidden, kernel, strided, pixels):
    total = 0.0
    for above in range(3):
        for beside in range(3):
            if strided:
                row_phase, drow = PHASES[above]
                col_phase, dcol = PHASES[beside]
                phase = 2 * row_phase + col_phase
                source = hidden[:, phase * pixels:(phase + 1) * pixels]
            else:
                drow, dcol = (above - 1, beside - 1)
                source = hidden
            total = total + mix(kernel[3 * above + beside], move(source, drow, dcol))
    return total

def forward(inputs, first, shortcut, middle, last, second, narrow, wide, masks, keep_one, keep_two):
    pixels = masks.shape[1]
    mask_in = masks.reshape(-1)
    mask_out = masks[0]
    field = (inputs * masks[None]).reshape(inputs.shape[0], -1)
    first_b = low(first)
    shortcut_b = low(shortcut)
    middle_b = low(middle)
    last_b = low(last)
    second_b = low(second)
    pre_one = low_back(mix(first_b, field))
    hid_one = low(jax.nn.silu(normalize(pre_one, mask_in, narrow[0, 0], narrow[0, 1])) * mask_in[None, :] * keep_one[:, None])
    pre_two = low_back(conv(hid_one, middle_b[0], True, pixels))
    hid_two = low(jax.nn.silu(normalize(pre_two, mask_out, narrow[1, 0], narrow[1, 1])) * mask_out[None, :] * keep_one[:, None])
    pre_three = low_back(mix(last_b[0], hid_two))
    pre_side = low_back(mix(shortcut_b, field[:, :pixels]))
    total_one = normalize(pre_three, mask_out, wide[0, 0], wide[0, 1]) + normalize(pre_side, mask_out, wide[1, 0], wide[1, 1])
    out_one = low(jax.nn.silu(total_one) * mask_out[None, :])
    pre_four = low_back(mix(second_b, out_one))
    hid_four = low(jax.nn.silu(normalize(pre_four, mask_out, narrow[2, 0], narrow[2, 1])) * mask_out[None, :] * keep_two[:, None])
    pre_five = low_back(conv(hid_four, middle_b[1], False, pixels))
    hid_five = low(jax.nn.silu(normalize(pre_five, mask_out, narrow[3, 0], narrow[3, 1])) * mask_out[None, :] * keep_two[:, None])
    pre_six = low_back(mix(last_b[1], hid_five))
    total_two = normalize(pre_six, mask_out, wide[2, 0], wide[2, 1]) + out_one
    return jax.nn.silu(total_two) * mask_out[None, :]

def adapt(grad_in, mean, square):
    mean_next = BETA_ONE * mean + (1.0 - BETA_ONE) * grad_in
    square_next = BETA_TWO * square + (1.0 - BETA_TWO) * grad_in * grad_in
    step = mean_next / (1.0 - BETA_ONE ** STEP) / (jnp.sqrt(square_next / (1.0 - BETA_TWO ** STEP)) + EPS_ADAM)
    return (mean_next, square_next, step)

def trusted(weight, update):
    weight_norm = jnp.sqrt(jnp.sum(weight * weight))
    update_norm = jnp.sqrt(jnp.sum(update * update))
    return (weight - RATE * (weight_norm / (update_norm + EPS_TRUST)) * update, weight_norm, update_norm)

def reference(inputs, pixel_mask, widths, output_grad, first_weight, shortcut_weight, middle_weight, last_weight, second_weight, narrow_norms, wide_norms, first_mean, first_square, shortcut_mean, shortcut_square, middle_mean, middle_square, last_mean, last_square, second_mean, second_square, narrow_mean, narrow_square, wide_mean, wide_square):
    masks = pixel_mask.astype(jnp.float32)
    channel = jnp.arange(C, dtype=jnp.int32)
    keep_one = (channel < widths[0]).astype(jnp.float32)
    keep_two = (channel < widths[1]).astype(jnp.float32)

    def run(inputs_f, first, shortcut, middle, last, second, narrow, wide):
        return forward(inputs_f, first, shortcut, middle, last, second, narrow, wide, masks, keep_one, keep_two)
    result, pull = jax.vjp(run, inputs.astype(jnp.float32), first_weight, shortcut_weight, middle_weight, last_weight, second_weight, narrow_norms, wide_norms)
    grads = pull(output_grad.astype(jnp.float32))
    block_output = result.astype(jnp.bfloat16)
    input_grad = grads[0].astype(jnp.bfloat16)
    weights = (first_weight, shortcut_weight, middle_weight, last_weight, second_weight)
    means = (first_mean, shortcut_mean, middle_mean, last_mean, second_mean)
    squares = (first_square, shortcut_square, middle_square, last_square, second_square)
    outputs = []
    norm_rows = []
    copies = []
    for index in range(5):
        mean_next, square_next, step = adapt(grads[index + 1], means[index], squares[index])
        update = step + DECAY * weights[index]
        if index in (2, 3):
            parts = []
            for block in range(2):
                fresh, weight_norm, update_norm = trusted(weights[index][block], update[block])
                parts.append(fresh)
                norm_rows.append(jnp.stack([weight_norm, update_norm]))
            fresh = jnp.stack(parts)
        else:
            fresh, weight_norm, update_norm = trusted(weights[index], update)
            norm_rows.append(jnp.stack([weight_norm, update_norm]))
        outputs.extend([mean_next, square_next, fresh])
        copies.append(fresh.astype(jnp.bfloat16))
    for table, grad_in, mean, square in ((narrow_norms, grads[6], narrow_mean, narrow_square), (wide_norms, grads[7], wide_mean, wide_square)):
        mean_next, square_next, step = adapt(grad_in, mean, square)
        outputs.extend([mean_next, square_next, table - RATE_NORM * step])
    matrix_norms = jnp.stack(norm_rows)
    return (block_output, input_grad, outputs[0], outputs[1], outputs[2], outputs[3], outputs[4], outputs[5], outputs[6], outputs[7], outputs[8], outputs[9], outputs[10], outputs[11], outputs[12], outputs[13], outputs[14], outputs[15], outputs[16], outputs[17], outputs[18], outputs[19], outputs[20], matrix_norms, copies[0], copies[1], copies[2], copies[3], copies[4])
```

```python
import jax
import jax.numpy as jnp
from jax import lax
from jax.sharding import PartitionSpec as P

HO = 16
WO = 11
STEP = 10


EPS_NORM = 1e-05
BETA_ONE = 0.9
BETA_TWO = 0.999
EPS_ADAM = 1e-06
DECAY = 0.01
RATE = 0.3
RATE_NORM = 0.3
EPS_TRUST = 1e-06
PHASES = ((1, -1), (0, 0), (1, 0))
STRIDED_TAPS = tuple(
    (
        (
            3 * above + beside,
            2 * PHASES[above][0] + PHASES[beside][0],
            PHASES[above][1],
            PHASES[beside][1],
        )
        for above in range(3)
        for beside in range(3)
    )
)
PLAIN_TAPS = tuple(
    ((3 * above + beside, 0, above - 1, beside - 1) for above in range(3) for beside in range(3))
)


def slope(values):
    gate = jax.nn.sigmoid(values)
    return gate * (1.0 + values * (1.0 - gate))


def shifted(values, drow, dcol):
    length = values.shape[1]
    offset = drow * WO + dcol
    place = lax.iota(jnp.int32, length)
    row_at = place // WO % HO + drow
    col_at = place % WO + dcol
    inside = (row_at >= 0) & (row_at < HO) & (col_at >= 0) & (col_at < WO)
    moved = jnp.roll(values, -offset, axis=1)
    return jnp.where(inside[None, :], moved, jnp.zeros_like(moved))


def over_images(first, second):
    return lax.psum((first, second), "dp")


def moments(values, mask):
    weighted = values * mask[None, :]
    return over_images(jnp.sum(weighted, 1), jnp.sum(weighted * values, 1))


def normalize(values, totals, squares, count, gain, bias):
    mean = totals / count
    scale = lax.rsqrt(squares / count - mean * mean + EPS_NORM)
    centred = (values - mean[:, None]) * scale[:, None]
    return (centred, scale, centred * gain[:, None] + bias[:, None])


def back_sums(grad_in, centred):
    return over_images(jnp.sum(grad_in * centred, 1), jnp.sum(grad_in, 1))


def norm_back(grad_in, centred, scale, gain, mask, gain_sum, bias_sum, count):
    return (gain * scale)[:, None] * (
        grad_in - mask[None, :] * (bias_sum[:, None] + centred * gain_sum[:, None]) / count
    )


def input_mix(values, weight, side_weight, pixels):
    start_sum = (jnp.zeros((weight.shape[1], values.shape[1]), jnp.float32),)
    if side_weight is not None:
        start_sum = start_sum + (jnp.zeros((side_weight.shape[1], pixels), jnp.float32),)
    piece = lax.all_gather(values, "mp", axis=0, tiled=True)
    result = (jnp.einsum("kc,kp->cp", weight, piece, preferred_element_type=jnp.float32),)
    if side_weight is not None:
        result = result + (
            jnp.einsum(
                "kc,kp->cp", side_weight, piece[:, :pixels], preferred_element_type=jnp.float32
            ),
        )
    return result


def mid_gathered(hidden):
    return lax.all_gather(hidden, "mp", axis=0, tiled=True)


def conv_forward(gathered, kernel, taps, pixels):
    result = jnp.zeros((kernel.shape[2], pixels), jnp.float32)
    for tap, phase, drow, dcol in taps:
        source = gathered[:, phase * pixels : (phase + 1) * pixels]
        part = jnp.einsum("kc,kp->cp", kernel[tap], source, preferred_element_type=jnp.float32)
        result = result + shifted(part, drow, dcol)
    return result


def conv_backward(grad_b, gathered, kernel, taps, pixels, phases):
    moved = [shifted(grad_b, -drow, -dcol) for tap, phase, drow, dcol in taps]
    count = gathered.shape[0] // lax.axis_size("mp") * lax.axis_size("mp")
    blocks = []
    for target in range(phases):
        result = jnp.zeros((count, pixels), jnp.float32)
        for conv_index, (conv_tap, conv_phase, conv_drow, conv_dcol) in enumerate(taps):
            if conv_phase == target:
                part = kernel[conv_tap]
                result = result + jnp.dot(
                    part, moved[conv_index], preferred_element_type=jnp.float32
                )
        blocks.append(result)
    hidden_grad = lax.psum_scatter(
        jnp.concatenate(blocks, 1), "mp", scatter_dimension=0, tiled=True
    )
    kernel_grad = jnp.stack(
        [
            jnp.einsum(
                "kp,cp->kc",
                gathered[:, phase * pixels : (phase + 1) * pixels],
                moved[index],
                preferred_element_type=jnp.float32,
            )
            for index, (tap, phase, drow, dcol) in enumerate(taps)
        ]
    )
    return (hidden_grad, kernel_grad)


def output_mix(hidden, kernel):
    return lax.psum_scatter(
        jnp.einsum("kc,kp->cp", kernel, hidden, preferred_element_type=jnp.float32),
        "mp",
        scatter_dimension=0,
        tiled=True,
    )


def output_back(grad_b, kernel, hidden):
    piece = lax.all_gather(grad_b, "mp", axis=0, tiled=True)
    hidden_grad = jnp.dot(kernel, piece, preferred_element_type=jnp.float32)
    columns = jnp.einsum("cp,kp->ck", hidden, piece, preferred_element_type=jnp.float32)
    return (hidden_grad, columns)


def input_back(values, grad_b, side_b, weight, side_weight, pixels):
    width = weight.shape[1]
    result = jnp.dot(weight, grad_b, preferred_element_type=jnp.float32)
    if side_weight is not None:
        result = jnp.concatenate(
            [
                result[:, :pixels]
                + jnp.dot(side_weight, side_b, preferred_element_type=jnp.float32),
                result[:, pixels:],
            ],
            1,
        )
    values_grad = lax.psum_scatter(result, "mp", scatter_dimension=0, tiled=True)
    piece = lax.all_gather(values, "mp", axis=0, tiled=True)
    blocks = [jnp.einsum("kp,cp->kc", piece, grad_b, preferred_element_type=jnp.float32)]
    if side_weight is not None:
        blocks.append(
            jnp.einsum("kp,cp->kc", piece[:, :pixels], side_b, preferred_element_type=jnp.float32)
        )
    joined = jnp.concatenate(blocks, 1)
    return (values_grad, joined[:, :width], joined[:, width:])


def adapt(grad_in, mean, square, first_fix, second_fix):
    mean_next = BETA_ONE * mean + (1.0 - BETA_ONE) * grad_in
    square_next = BETA_TWO * square + (1.0 - BETA_TWO) * grad_in * grad_in
    step = mean_next / first_fix / (jnp.sqrt(square_next / second_fix) + EPS_ADAM)
    return (mean_next, square_next, step)


def shards(
    inputs,
    pixel_mask,
    widths,
    output_grad,
    first_weight,
    shortcut_weight,
    middle_weight,
    last_weight,
    second_weight,
    narrow_norms,
    wide_norms,
    first_mean,
    first_square,
    shortcut_mean,
    shortcut_square,
    middle_mean,
    middle_square,
    last_mean,
    last_square,
    second_mean,
    second_square,
    narrow_mean,
    narrow_square,
    wide_mean,
    wide_square,
):
    pixels = pixel_mask.shape[1]
    width = first_weight.shape[1]
    rank = lax.axis_index("mp")
    channel = rank * width + lax.iota(jnp.int32, width)
    keep_one = (channel < widths[0]).astype(jnp.float32)[:, None]
    keep_two = (channel < widths[1]).astype(jnp.float32)[:, None]
    masks = pixel_mask.astype(jnp.float32)
    mask_in = masks.reshape(-1)
    mask_out = masks[0]
    field = (inputs * pixel_mask.astype(jnp.bfloat16)[None]).reshape(inputs.shape[0], -1)
    first_w, short_w, middle_w, last_w, second_w = (
        lax.all_gather(first_weight.astype(jnp.bfloat16), "dp", axis=0, tiled=True),
        lax.all_gather(shortcut_weight.astype(jnp.bfloat16), "dp", axis=0, tiled=True),
        lax.all_gather(middle_weight.astype(jnp.bfloat16), "dp", axis=2, tiled=True),
        lax.all_gather(last_weight.astype(jnp.bfloat16), "dp", axis=2, tiled=True),
        lax.all_gather(second_weight.astype(jnp.bfloat16), "dp", axis=0, tiled=True),
    )
    count_in, count_out = over_images(jnp.sum(mask_in), jnp.sum(mask_out))
    pre_one, pre_side = input_mix(field, first_w, short_w, pixels)
    totals, squares = moments(pre_one, mask_in)
    cen_one, scale_one, act_one = normalize(
        pre_one, totals, squares, count_in, narrow_norms[0, 0], narrow_norms[0, 1]
    )
    hid_one = (jax.nn.silu(act_one) * mask_in[None, :] * keep_one).astype(jnp.bfloat16)
    gat_one = mid_gathered(hid_one)
    pre_two = conv_forward(gat_one, middle_w[0], STRIDED_TAPS, pixels)
    totals, squares = moments(pre_two, mask_out)
    cen_two, scale_two, act_two = normalize(
        pre_two, totals, squares, count_out, narrow_norms[1, 0], narrow_norms[1, 1]
    )
    hid_two = (jax.nn.silu(act_two) * mask_out[None, :] * keep_one).astype(jnp.bfloat16)
    pre_three = output_mix(hid_two, last_w[0])
    weighted_three = pre_three * mask_out[None, :]
    weighted_side = pre_side * mask_out[None, :]
    totals, squares = over_images(
        jnp.stack([jnp.sum(weighted_three, 1), jnp.sum(weighted_side, 1)]),
        jnp.stack([jnp.sum(weighted_three * pre_three, 1), jnp.sum(weighted_side * pre_side, 1)]),
    )
    cen_three, scale_three, act_three = normalize(
        pre_three, totals[0], squares[0], count_out, wide_norms[0, 0], wide_norms[0, 1]
    )
    cen_side, scale_side, act_side = normalize(
        pre_side, totals[1], squares[1], count_out, wide_norms[1, 0], wide_norms[1, 1]
    )
    total_one = act_three + act_side
    out_one = (jax.nn.silu(total_one) * mask_out[None, :]).astype(jnp.bfloat16)
    (pre_four,) = input_mix(out_one, second_w, None, pixels)
    totals, squares = moments(pre_four, mask_out)
    cen_four, scale_four, act_four = normalize(
        pre_four, totals, squares, count_out, narrow_norms[2, 0], narrow_norms[2, 1]
    )
    hid_four = (jax.nn.silu(act_four) * mask_out[None, :] * keep_two).astype(jnp.bfloat16)
    gat_four = mid_gathered(hid_four)
    pre_five = conv_forward(gat_four, middle_w[1], PLAIN_TAPS, pixels)
    totals, squares = moments(pre_five, mask_out)
    cen_five, scale_five, act_five = normalize(
        pre_five, totals, squares, count_out, narrow_norms[3, 0], narrow_norms[3, 1]
    )
    hid_five = (jax.nn.silu(act_five) * mask_out[None, :] * keep_two).astype(jnp.bfloat16)
    pre_six = output_mix(hid_five, last_w[1])
    totals, squares = moments(pre_six, mask_out)
    cen_six, scale_six, act_six = normalize(
        pre_six, totals, squares, count_out, wide_norms[2, 0], wide_norms[2, 1]
    )
    total_two = act_six + out_one.astype(jnp.float32)
    block_output = (jax.nn.silu(total_two) * mask_out[None, :]).astype(jnp.bfloat16)
    grad_two = output_grad.astype(jnp.float32) * mask_out[None, :] * slope(total_two)
    gain_six, bias_six = back_sums(grad_two, cen_six)
    grad_six = norm_back(
        grad_two, cen_six, scale_six, wide_norms[2, 0], mask_out, gain_six, bias_six, count_out
    ).astype(jnp.bfloat16)
    hid_five_grad, last_one_grad = output_back(grad_six, last_w[1], hid_five)
    act_five_grad = hid_five_grad * keep_two * mask_out[None, :] * slope(act_five)
    gain_five, bias_five = back_sums(act_five_grad, cen_five)
    grad_five = norm_back(
        act_five_grad,
        cen_five,
        scale_five,
        narrow_norms[3, 0],
        mask_out,
        gain_five,
        bias_five,
        count_out,
    ).astype(jnp.bfloat16)
    hid_four_grad, middle_one_grad = conv_backward(
        grad_five, gat_four, middle_w[1], PLAIN_TAPS, pixels, 1
    )
    act_four_grad = hid_four_grad * keep_two * mask_out[None, :] * slope(act_four)
    gain_four, bias_four = back_sums(act_four_grad, cen_four)
    grad_four = norm_back(
        act_four_grad,
        cen_four,
        scale_four,
        narrow_norms[2, 0],
        mask_out,
        gain_four,
        bias_four,
        count_out,
    ).astype(jnp.bfloat16)
    out_one_grad, second_grad, unused_side = input_back(
        out_one, grad_four, None, second_w, None, pixels
    )
    grad_one = (grad_two + out_one_grad) * mask_out[None, :] * slope(total_one)
    gains_pair, bias_pair = over_images(
        jnp.stack([jnp.sum(grad_one * cen_three, 1), jnp.sum(grad_one * cen_side, 1)]),
        jnp.sum(grad_one, 1),
    )
    grad_three = norm_back(
        grad_one,
        cen_three,
        scale_three,
        wide_norms[0, 0],
        mask_out,
        gains_pair[0],
        bias_pair,
        count_out,
    ).astype(jnp.bfloat16)
    grad_side = norm_back(
        grad_one,
        cen_side,
        scale_side,
        wide_norms[1, 0],
        mask_out,
        gains_pair[1],
        bias_pair,
        count_out,
    ).astype(jnp.bfloat16)
    hid_two_grad, last_zero_grad = output_back(grad_three, last_w[0], hid_two)
    act_two_grad = hid_two_grad * keep_one * mask_out[None, :] * slope(act_two)
    gain_two, bias_two = back_sums(act_two_grad, cen_two)
    grad_mid = norm_back(
        act_two_grad,
        cen_two,
        scale_two,
        narrow_norms[1, 0],
        mask_out,
        gain_two,
        bias_two,
        count_out,
    ).astype(jnp.bfloat16)
    hid_one_grad, middle_zero_grad = conv_backward(
        grad_mid, gat_one, middle_w[0], STRIDED_TAPS, pixels, 4
    )
    act_one_grad = hid_one_grad * keep_one * mask_in[None, :] * slope(act_one)
    gain_one, bias_one = back_sums(act_one_grad, cen_one)
    grad_first = norm_back(
        act_one_grad, cen_one, scale_one, narrow_norms[0, 0], mask_in, gain_one, bias_one, count_in
    ).astype(jnp.bfloat16)
    field_grad, first_grad, short_grad = input_back(
        field, grad_first, grad_side, first_w, short_w, pixels
    )
    input_grad = (field_grad * mask_in[None, :]).astype(jnp.bfloat16).reshape(inputs.shape)
    grads = (
        lax.psum_scatter(first_grad, "dp", scatter_dimension=0, tiled=True),
        lax.psum_scatter(short_grad, "dp", scatter_dimension=0, tiled=True),
        lax.psum_scatter(
            jnp.stack([middle_zero_grad, middle_one_grad]), "dp", scatter_dimension=2, tiled=True
        ),
        lax.psum_scatter(
            jnp.stack([last_zero_grad, last_one_grad]), "dp", scatter_dimension=2, tiled=True
        ),
        lax.psum_scatter(second_grad, "dp", scatter_dimension=0, tiled=True),
    )
    first_fix = 1.0 - BETA_ONE**STEP
    second_fix = 1.0 - BETA_TWO**STEP
    weights = (first_weight, shortcut_weight, middle_weight, last_weight, second_weight)
    means = (first_mean, shortcut_mean, middle_mean, last_mean, second_mean)
    squares_old = (first_square, shortcut_square, middle_square, last_square, second_square)
    states = []
    updates = []
    for index in range(5):
        mean_next, square_next, step = adapt(
            grads[index], means[index], squares_old[index], first_fix, second_fix
        )
        states.append((mean_next, square_next))
        updates.append(step + DECAY * weights[index])
    pairs = [
        (weights[0], updates[0]),
        (weights[1], updates[1]),
        (weights[2][0], updates[2][0]),
        (weights[2][1], updates[2][1]),
        (weights[3][0], updates[3][0]),
        (weights[3][1], updates[3][1]),
        (weights[4], updates[4]),
    ]
    partial_value = jnp.stack(
        [
            jnp.stack([jnp.sum(weight * weight), jnp.sum(update * update)])
            for weight, update in pairs
        ]
    )
    matrix_norms = jnp.sqrt(lax.psum(partial_value, ("dp", "mp")))
    ratio = matrix_norms[:, 0] / (matrix_norms[:, 1] + EPS_TRUST)
    first_next = first_weight - RATE * ratio[0] * updates[0]
    short_next = shortcut_weight - RATE * ratio[1] * updates[1]
    middle_next = middle_weight - RATE * ratio[2:4].reshape(2, 1, 1, 1) * updates[2]
    last_next = last_weight - RATE * ratio[4:6].reshape(2, 1, 1) * updates[3]
    second_next = second_weight - RATE * ratio[6] * updates[4]
    narrow_grad = jnp.stack(
        [
            jnp.stack([gain_one, bias_one]),
            jnp.stack([gain_two, bias_two]),
            jnp.stack([gain_four, bias_four]),
            jnp.stack([gain_five, bias_five]),
        ]
    )
    wide_grad = jnp.stack(
        [
            jnp.stack([gains_pair[0], bias_pair]),
            jnp.stack([gains_pair[1], bias_pair]),
            jnp.stack([gain_six, bias_six]),
        ]
    )
    narrow_mean_next, narrow_square_next, narrow_step = adapt(
        narrow_grad, narrow_mean, narrow_square, first_fix, second_fix
    )
    wide_mean_next, wide_square_next, wide_step = adapt(
        wide_grad, wide_mean, wide_square, first_fix, second_fix
    )
    return (
        block_output,
        input_grad,
        states[0][0],
        states[0][1],
        first_next,
        states[1][0],
        states[1][1],
        short_next,
        states[2][0],
        states[2][1],
        middle_next,
        states[3][0],
        states[3][1],
        last_next,
        states[4][0],
        states[4][1],
        second_next,
        narrow_mean_next,
        narrow_square_next,
        narrow_norms - RATE_NORM * narrow_step,
        wide_mean_next,
        wide_square_next,
        wide_norms - RATE_NORM * wide_step,
        matrix_norms,
        first_next.astype(jnp.bfloat16),
        short_next.astype(jnp.bfloat16),
        middle_next.astype(jnp.bfloat16),
        last_next.astype(jnp.bfloat16),
        second_next.astype(jnp.bfloat16),
    )


def fits(mesh, pixel_mask):
    sizes = (mesh.shape["dp"], mesh.shape["mp"])
    powers = all(size >= 2 and size & (size - 1) == 0 for size in sizes)
    return powers and pixel_mask.shape[1] % (HO * WO * sizes[1]) == 0


def swap(values, axis, mask):
    size = lax.axis_size(axis)
    return lax.ppermute(values, axis, [(place, place ^ mask) for place in range(size)])


def bit_of(axis, mask):
    return (lax.axis_index(axis) & mask) // mask


def high_bits(axis):
    masks = []
    mask = lax.axis_size(axis) // 2
    while mask:
        masks.append(mask)
        mask //= 2
    return masks


def tree_sum(terms):
    while len(terms) > 1:
        terms = [terms[place] + terms[place + 1] for place in range(0, len(terms), 2)]
    return terms[0]


def everywhere(values):
    for axis in ("mp", "dp"):
        values = tree_sum(
            [values] + [swap(values, axis, mask) for mask in range(1, lax.axis_size(axis))]
        )
    return values


def sum_all(parts):
    flat = [part.reshape(-1, 128) for part in parts]
    total = everywhere(jnp.concatenate(flat, 0))
    result = []
    start = 0
    for part, rows in zip(parts, flat):
        result.append(total[start : start + rows.shape[0]].reshape(part.shape))
        start += rows.shape[0]
    return result


def routes(late_rows):
    rows = high_bits("dp")
    columns = high_bits("mp")[:-1]
    order = [("dp", mask) for mask in rows[:-1]]
    last_row = [("dp", rows[-1])]
    sides = [("mp", mask) for mask in reversed(columns)]
    return order + (sides + last_row if late_rows else last_row + sides)


def gather(block, late_rows):
    lead, _, _ = block.shape
    outer = 1
    for axis, mask in routes(late_rows):
        other = swap(block, axis, mask)
        high = bit_of(axis, mask) > 0
        first = jnp.where(high, other, block)
        second = jnp.where(high, block, other)
        if axis == "dp":
            rows, cols = block.shape[1:]
            pair = [part.reshape(lead, outer, rows // outer, cols) for part in (first, second)]
            block = jnp.stack(pair, 2).reshape(lead, 2 * rows, cols)
            outer *= 2
        else:
            block = jnp.concatenate([first, second], 2)
    return (block, swap(block, "mp", 1))


def scatter(keep, send, late_rows):
    masks = high_bits("dp")
    lead, rows, cols = keep.shape
    unit = rows >> len(masks)
    shape = (lead,) + (2,) * len(masks) + (unit, cols)
    terms = [keep.reshape(shape), swap(send, "mp", 1).reshape(shape)]
    for axis, mask in reversed(routes(late_rows)):
        place = bit_of(axis, mask)
        if axis == "dp":
            dim = 1 + masks.index(mask)
            size = 1
        else:
            dim = len(shape) - 1
            size = terms[0].shape[dim] // 2

        def pick(term, which):
            return lax.dynamic_slice_in_dim(term, which * size, size, dim)

        out = sum(pick(term, 1 - place).astype(jnp.float32) for term in terms)
        arrived = swap(out.astype(jnp.bfloat16), axis, mask)
        terms = [pick(term, place) for term in terms] + [arrived]
    total = sum(term.astype(jnp.float32) for term in terms)
    return total.reshape(lead, unit, -1)


def halves(values):
    count = lax.axis_size("mp")
    width = values.shape[-1] // count
    blocks = [values[..., place * width : (place + 1) * width] for place in range(count)]
    even = jnp.concatenate(blocks[0::2], -1)
    odd = jnp.concatenate(blocks[1::2], -1)
    high = bit_of("mp", 1) > 0
    return (jnp.where(high, odd, even), jnp.where(high, even, odd))


def joined(mine, other):
    count = lax.axis_size("mp")
    width = 2 * mine.shape[-1] // count
    high = bit_of("mp", 1) > 0
    even = jnp.where(high, other, mine)
    odd = jnp.where(high, mine, other)
    blocks = []
    for place in range(count // 2):
        blocks.append(even[..., place * width : (place + 1) * width])
        blocks.append(odd[..., place * width : (place + 1) * width])
    return jnp.concatenate(blocks, -1)


def dot(first, second, dims):
    return lax.dot_general(first, second, (dims, ((), ())), preferred_element_type=jnp.float32)


def times(values, weight):
    return joined(*[dot(values, part, ((1,), (0,))) for part in weight])


def times_turned(values, weight):
    parts = [
        dot(value, part, ((1,), (1,))) for value, part in zip(halves(values), weight)
    ]
    return parts[0] + parts[1]


def outer_parts(rows_of, cols_of):
    return [
        dot(rows_of, part, ((0,), (0,))).astype(jnp.bfloat16) for part in halves(cols_of)
    ]


def reach(values, drow, dcol):
    offset = drow * WO + dcol
    count = values.shape[0]
    place = lax.iota(jnp.int32, count)
    row_at = place // WO % HO + drow
    col_at = place % WO + dcol
    inside = (row_at >= 0) & (row_at < HO) & (col_at >= 0) & (col_at < WO)
    moved = jnp.roll(values, -offset, axis=0)
    return jnp.where(inside[:, None], moved, jnp.zeros_like(moved))


def tap_columns(values, taps, pixels):
    return jnp.concatenate(
        [
            reach(values[phase * pixels : (phase + 1) * pixels], drow, dcol)
            for tap, phase, drow, dcol in taps
        ],
        1,
    )


def tap_back(columns, taps, width, phases):
    blocks = []
    for target in range(phases):
        total = 0.0
        for tap, phase, drow, dcol in taps:
            if phase == target:
                total = total + reach(columns[:, tap * width : (tap + 1) * width], -drow, -dcol)
        blocks.append(total)
    return jnp.concatenate(blocks, 0)


def flat_pair(pair):
    return [part.reshape(-1, part.shape[-1]) for part in pair]


def sums_of(values, mask):
    weighted = values * mask
    return [jnp.sum(weighted, 0), jnp.sum(weighted * values, 0)]


def normed(values, totals, count, table):
    mean = totals[0] / count
    scale = lax.rsqrt(totals[1] / count - mean * mean + EPS_NORM)
    centred = (values - mean[None]) * scale[None]
    return (centred, scale, centred * table[0][None] + table[1][None])


def grad_sums(grad_in, centred):
    return [jnp.sum(grad_in * centred, 0), jnp.sum(grad_in, 0)]


def normed_back(grad_in, centred, scale, gain, mask, totals, count):
    return (
        (gain * scale)[None]
        * (grad_in - mask * (totals[1][None] + centred * totals[0][None]) / count)
    ).astype(jnp.bfloat16)


def by_image(
    inputs,
    pixel_mask,
    widths,
    output_grad,
    first_weight,
    shortcut_weight,
    middle_weight,
    last_weight,
    second_weight,
    narrow_norms,
    wide_norms,
    first_mean,
    first_square,
    shortcut_mean,
    shortcut_square,
    middle_mean,
    middle_square,
    last_mean,
    last_square,
    second_mean,
    second_square,
    narrow_mean,
    narrow_square,
    wide_mean,
    wide_square,
):
    ranks = lax.axis_size("mp")
    rank = lax.axis_index("mp")
    pixels = pixel_mask.shape[1] // ranks
    narrow = first_weight.shape[1] * ranks
    wide = shortcut_weight.shape[1] * ranks
    low = jnp.bfloat16
    first_w = gather(first_weight.astype(low)[None], False)
    mid_zero_w = gather(middle_weight[0].astype(low), True)
    last_zero_w = gather(last_weight[0].astype(low).T[None], False)
    short_w = gather(shortcut_weight.astype(low)[None], True)
    second_w = gather(second_weight.astype(low)[None], False)
    mid_one_w = gather(middle_weight[1].astype(low), False)
    last_one_w = gather(last_weight[1].astype(low).T[None], True)
    first_w, short_w, second_w, mid_zero_w, mid_one_w, last_zero_w, last_one_w = [
        flat_pair(pair)
        for pair in (first_w, short_w, second_w, mid_zero_w, mid_one_w, last_zero_w, last_one_w)
    ]
    tables = lax.all_gather(
        jnp.concatenate([narrow_norms.reshape(-1, 128), wide_norms.reshape(-1, 128)], 0), "mp"
    )
    split = narrow_norms.size // 128
    narrow_all = (
        tables[:, :split].reshape(ranks, 4, 2, -1).transpose(1, 2, 0, 3).reshape(4, 2, narrow)
    )
    wide_all = tables[:, split:].reshape(ranks, 3, 2, -1).transpose(1, 2, 0, 3).reshape(3, 2, wide)

    own_mask = lax.dynamic_slice_in_dim(pixel_mask, rank * pixels, pixels, 1).astype(jnp.float32)
    mask_in = own_mask.reshape(-1, 1)
    mask_out = own_mask[0][:, None]
    channel = lax.iota(jnp.int32, narrow)
    keep_one = (channel < widths[0]).astype(jnp.float32)[None]
    keep_two = (channel < widths[1]).astype(jnp.float32)[None]

    field = lax.all_to_all(inputs, "mp", split_axis=2, concat_axis=0, tiled=True)
    field = field.transpose(1, 2, 0).reshape(4 * pixels, -1) * mask_in.astype(low)
    above = lax.all_to_all(output_grad, "mp", split_axis=1, concat_axis=0, tiled=True).T

    pre_one = times(field, first_w)
    counts = jnp.stack([jnp.sum(mask_in), jnp.sum(mask_out)])
    counts = jnp.concatenate([counts, jnp.zeros(126, jnp.float32)])
    *totals, counts = sum_all(sums_of(pre_one, mask_in) + [counts])
    count_in, count_out = counts[0], counts[1]
    cen_one, scale_one, act_one = normed(pre_one, totals, count_in, narrow_all[0])
    hid_one = (jax.nn.silu(act_one) * mask_in * keep_one).astype(low)
    cols_one = tap_columns(hid_one, STRIDED_TAPS, pixels)
    pre_two = times(cols_one, mid_zero_w)
    totals = sum_all(sums_of(pre_two, mask_out))
    cen_two, scale_two, act_two = normed(pre_two, totals, count_out, narrow_all[1])
    hid_two = (jax.nn.silu(act_two) * mask_out * keep_one).astype(low)
    pre_three = times_turned(hid_two, last_zero_w)
    pre_side = times(field[:pixels], short_w)
    totals = sum_all(sums_of(pre_three, mask_out) + sums_of(pre_side, mask_out))
    cen_three, scale_three, act_three = normed(pre_three, totals[:2], count_out, wide_all[0])
    cen_side, scale_side, act_side = normed(pre_side, totals[2:], count_out, wide_all[1])
    total_one = act_three + act_side
    out_one = (jax.nn.silu(total_one) * mask_out).astype(low)
    pre_four = times(out_one, second_w)
    totals = sum_all(sums_of(pre_four, mask_out))
    cen_four, scale_four, act_four = normed(pre_four, totals, count_out, narrow_all[2])
    hid_four = (jax.nn.silu(act_four) * mask_out * keep_two).astype(low)
    cols_four = tap_columns(hid_four, PLAIN_TAPS, pixels)
    pre_five = times(cols_four, mid_one_w)
    totals = sum_all(sums_of(pre_five, mask_out))
    cen_five, scale_five, act_five = normed(pre_five, totals, count_out, narrow_all[3])
    hid_five = (jax.nn.silu(act_five) * mask_out * keep_two).astype(low)
    pre_six = times_turned(hid_five, last_one_w)
    totals = sum_all(sums_of(pre_six, mask_out))
    cen_six, scale_six, act_six = normed(pre_six, totals, count_out, wide_all[2])
    total_two = act_six + out_one.astype(jnp.float32)
    block_output = (jax.nn.silu(total_two) * mask_out).astype(low)
    block_output = lax.all_to_all(block_output.T, "mp", split_axis=0, concat_axis=1, tiled=True)

    grad_two = above.astype(jnp.float32) * mask_out * slope(total_two)
    sums_six = sum_all(grad_sums(grad_two, cen_six))
    grad_six = normed_back(
        grad_two, cen_six, scale_six, wide_all[2, 0], mask_out, sums_six, count_out
    )
    hid_five_grad = times(grad_six, last_one_w)
    keep, send = outer_parts(grad_six, hid_five)
    last_one_grad = scatter(keep[None], send[None], True)
    act_five_grad = hid_five_grad * keep_two * mask_out * slope(act_five)
    sums_five = sum_all(grad_sums(act_five_grad, cen_five))
    grad_five = normed_back(
        act_five_grad, cen_five, scale_five, narrow_all[3, 0], mask_out, sums_five, count_out
    )
    keep, send = outer_parts(cols_four, grad_five)
    mid_one_grad = scatter(keep.reshape(9, narrow, -1), send.reshape(9, narrow, -1), False)
    hid_four_grad = tap_back(times_turned(grad_five, mid_one_w), PLAIN_TAPS, narrow, 1)
    act_four_grad = hid_four_grad * keep_two * mask_out * slope(act_four)
    sums_four = sum_all(grad_sums(act_four_grad, cen_four))
    grad_four = normed_back(
        act_four_grad, cen_four, scale_four, narrow_all[2, 0], mask_out, sums_four, count_out
    )
    keep, send = outer_parts(out_one, grad_four)
    second_grad = scatter(keep[None], send[None], False)
    grad_one = (
        (grad_two + times_turned(grad_four, second_w)) * mask_out * slope(total_one)
    )
    gain_three, gain_side, bias_pair = sum_all(
        [
            jnp.sum(grad_one * cen_three, 0),
            jnp.sum(grad_one * cen_side, 0),
            jnp.sum(grad_one, 0),
        ]
    )
    grad_three = normed_back(
        grad_one, cen_three, scale_three, wide_all[0, 0], mask_out, (gain_three, bias_pair), count_out
    )
    grad_side = normed_back(
        grad_one, cen_side, scale_side, wide_all[1, 0], mask_out, (gain_side, bias_pair), count_out
    )
    hid_two_grad = times(grad_three, last_zero_w)
    keep, send = outer_parts(grad_three, hid_two)
    last_zero_grad = scatter(keep[None], send[None], False)
    keep, send = outer_parts(field[:pixels], grad_side)
    short_grad = scatter(keep[None], send[None], True)
    act_two_grad = hid_two_grad * keep_one * mask_out * slope(act_two)
    sums_two = sum_all(grad_sums(act_two_grad, cen_two))
    grad_mid = normed_back(
        act_two_grad, cen_two, scale_two, narrow_all[1, 0], mask_out, sums_two, count_out
    )
    keep, send = outer_parts(cols_one, grad_mid)
    mid_zero_grad = scatter(keep.reshape(9, narrow, -1), send.reshape(9, narrow, -1), True)
    hid_one_grad = tap_back(times_turned(grad_mid, mid_zero_w), STRIDED_TAPS, narrow, 4)
    act_one_grad = hid_one_grad * keep_one * mask_in * slope(act_one)
    sums_one = sum_all(grad_sums(act_one_grad, cen_one))
    grad_first = normed_back(
        act_one_grad, cen_one, scale_one, narrow_all[0, 0], mask_in, sums_one, count_in
    )
    keep, send = outer_parts(field, grad_first)
    first_grad = scatter(keep[None], send[None], False)
    field_grad = times_turned(grad_first, first_w)
    side_grad = times_turned(grad_side, short_w)
    field_grad = jnp.concatenate([field_grad[:pixels] + side_grad, field_grad[pixels:]], 0)
    field_grad = (field_grad * mask_in).astype(low).reshape(4, pixels, -1).transpose(2, 0, 1)
    input_grad = lax.all_to_all(field_grad, "mp", split_axis=0, concat_axis=2, tiled=True)

    grads = (
        first_grad[0],
        short_grad[0],
        jnp.stack([mid_zero_grad, mid_one_grad]),
        jnp.stack([last_zero_grad[0].T, last_one_grad[0].T]),
        second_grad[0],
    )
    first_fix = 1.0 - BETA_ONE**STEP
    second_fix = 1.0 - BETA_TWO**STEP
    weights = (first_weight, shortcut_weight, middle_weight, last_weight, second_weight)
    means = (first_mean, shortcut_mean, middle_mean, last_mean, second_mean)
    squares_old = (first_square, shortcut_square, middle_square, last_square, second_square)
    states = []
    updates = []
    for index in range(5):
        mean_next, square_next, step = adapt(
            grads[index], means[index], squares_old[index], first_fix, second_fix
        )
        states.append((mean_next, square_next))
        updates.append(step + DECAY * weights[index])
    pairs = [
        (weights[0], updates[0]),
        (weights[1], updates[1]),
        (weights[2][0], updates[2][0]),
        (weights[2][1], updates[2][1]),
        (weights[3][0], updates[3][0]),
        (weights[3][1], updates[3][1]),
        (weights[4], updates[4]),
    ]
    own = [jnp.sum(value * value) for pair in pairs for value in pair]
    own = jnp.concatenate([jnp.stack(own), jnp.zeros(128 - len(own), jnp.float32)])
    (powers,) = sum_all([own])
    matrix_norms = jnp.sqrt(powers[: 2 * len(pairs)].reshape(-1, 2))
    ratio = matrix_norms[:, 0] / (matrix_norms[:, 1] + EPS_TRUST)
    first_next = first_weight - RATE * ratio[0] * updates[0]
    short_next = shortcut_weight - RATE * ratio[1] * updates[1]
    middle_next = middle_weight - RATE * ratio[2:4].reshape(2, 1, 1, 1) * updates[2]
    last_next = last_weight - RATE * ratio[4:6].reshape(2, 1, 1) * updates[3]
    second_next = second_weight - RATE * ratio[6] * updates[4]

    def own_channels(values):
        width = values.shape[-1] // ranks
        return lax.dynamic_slice_in_dim(values, rank * width, width, values.ndim - 1)

    narrow_grad = own_channels(
        jnp.stack([jnp.stack(pair) for pair in (sums_one, sums_two, sums_four, sums_five)])
    )
    wide_grad = own_channels(
        jnp.stack(
            [
                jnp.stack([gain_three, bias_pair]),
                jnp.stack([gain_side, bias_pair]),
                jnp.stack(sums_six),
            ]
        )
    )
    narrow_mean_next, narrow_square_next, narrow_step = adapt(
        narrow_grad, narrow_mean, narrow_square, first_fix, second_fix
    )
    wide_mean_next, wide_square_next, wide_step = adapt(
        wide_grad, wide_mean, wide_square, first_fix, second_fix
    )
    return (
        block_output,
        input_grad,
        states[0][0],
        states[0][1],
        first_next,
        states[1][0],
        states[1][1],
        short_next,
        states[2][0],
        states[2][1],
        middle_next,
        states[3][0],
        states[3][1],
        last_next,
        states[4][0],
        states[4][1],
        second_next,
        narrow_mean_next,
        narrow_square_next,
        narrow_norms - RATE_NORM * narrow_step,
        wide_mean_next,
        wide_square_next,
        wide_norms - RATE_NORM * wide_step,
        matrix_norms,
        first_next.astype(jnp.bfloat16),
        short_next.astype(jnp.bfloat16),
        middle_next.astype(jnp.bfloat16),
        last_next.astype(jnp.bfloat16),
        second_next.astype(jnp.bfloat16),
    )


def solution(mesh):
    in_specs = (
        P("mp", None, "dp"),
        P(None, "dp"),
        P(),
        P("mp", "dp"),
        P("dp", "mp"),
        P("dp", "mp"),
        P(None, None, "dp", "mp"),
        P(None, "mp", "dp"),
        P("dp", "mp"),
        P(None, None, "mp"),
        P(None, None, "mp"),
        P("dp", "mp"),
        P("dp", "mp"),
        P("dp", "mp"),
        P("dp", "mp"),
        P(None, None, "dp", "mp"),
        P(None, None, "dp", "mp"),
        P(None, "mp", "dp"),
        P(None, "mp", "dp"),
        P("dp", "mp"),
        P("dp", "mp"),
        P(None, None, "mp"),
        P(None, None, "mp"),
        P(None, None, "mp"),
        P(None, None, "mp"),
    )
    out_specs = (
        P("mp", "dp"),
        P("mp", None, "dp"),
        P("dp", "mp"),
        P("dp", "mp"),
        P("dp", "mp"),
        P("dp", "mp"),
        P("dp", "mp"),
        P("dp", "mp"),
        P(None, None, "dp", "mp"),
        P(None, None, "dp", "mp"),
        P(None, None, "dp", "mp"),
        P(None, "mp", "dp"),
        P(None, "mp", "dp"),
        P(None, "mp", "dp"),
        P("dp", "mp"),
        P("dp", "mp"),
        P("dp", "mp"),
        P(None, None, "mp"),
        P(None, None, "mp"),
        P(None, None, "mp"),
        P(None, None, "mp"),
        P(None, None, "mp"),
        P(None, None, "mp"),
        P(),
        P("dp", "mp"),
        P("dp", "mp"),
        P(None, None, "dp", "mp"),
        P(None, "mp", "dp"),
        P("dp", "mp"),
    )
    return jax.shard_map(
        lambda *values: (by_image if fits(mesh, values[1]) else shards)(*values),
        mesh=mesh,
        in_specs=in_specs,
        out_specs=out_specs,
        check_vma=False,
    )
```

```python
import functools

import jax
import jax.numpy as jnp
from jax import lax
from jax.experimental import pallas as pl
from jax.experimental.pallas import tpu as pltpu
from jax.sharding import PartitionSpec as P

HO = 16
WO = 11
STEP = 10


EPS_NORM = 1e-05
BETA_ONE = 0.9
BETA_TWO = 0.999
EPS_ADAM = 1e-06
DECAY = 0.01
RATE = 0.3
RATE_NORM = 0.3
EPS_TRUST = 1e-06
PHASES = ((1, -1), (0, 0), (1, 0))
STRIDED_TAPS = tuple(
    (
        (
            3 * above + beside,
            2 * PHASES[above][0] + PHASES[beside][0],
            PHASES[above][1],
            PHASES[beside][1],
        )
        for above in range(3)
        for beside in range(3)
    )
)
PLAIN_TAPS = tuple(
    ((3 * above + beside, 0, above - 1, beside - 1) for above in range(3) for beside in range(3))
)


def slope(values):
    gate = jax.nn.sigmoid(values)
    return gate * (1.0 + values * (1.0 - gate))


def shifted(values, drow, dcol):
    length = values.shape[1]
    offset = drow * WO + dcol
    place = lax.iota(jnp.int32, length)
    row_at = place // WO % HO + drow
    col_at = place % WO + dcol
    inside = (row_at >= 0) & (row_at < HO) & (col_at >= 0) & (col_at < WO)
    moved = jnp.roll(values, -offset, axis=1)
    return jnp.where(inside[None, :], moved, jnp.zeros_like(moved))


def over_images(first, second):
    return lax.psum((first, second), "dp")


def moments(values, mask):
    weighted = values * mask[None, :]
    return over_images(jnp.sum(weighted, 1), jnp.sum(weighted * values, 1))


def normalize(values, totals, squares, count, gain, bias):
    mean = totals / count
    scale = lax.rsqrt(squares / count - mean * mean + EPS_NORM)
    centred = (values - mean[:, None]) * scale[:, None]
    return (centred, scale, centred * gain[:, None] + bias[:, None])


def back_sums(grad_in, centred):
    return over_images(jnp.sum(grad_in * centred, 1), jnp.sum(grad_in, 1))


def norm_back(grad_in, centred, scale, gain, mask, gain_sum, bias_sum, count):
    return (gain * scale)[:, None] * (
        grad_in - mask[None, :] * (bias_sum[:, None] + centred * gain_sum[:, None]) / count
    )


def input_mix(values, weight, side_weight, pixels):
    start_sum = (jnp.zeros((weight.shape[1], values.shape[1]), jnp.float32),)
    if side_weight is not None:
        start_sum = start_sum + (jnp.zeros((side_weight.shape[1], pixels), jnp.float32),)
    piece = lax.all_gather(values, "mp", axis=0, tiled=True)
    result = (jnp.einsum("kc,kp->cp", weight, piece, preferred_element_type=jnp.float32),)
    if side_weight is not None:
        result = result + (
            jnp.einsum(
                "kc,kp->cp", side_weight, piece[:, :pixels], preferred_element_type=jnp.float32
            ),
        )
    return result


def mid_gathered(hidden):
    return lax.all_gather(hidden, "mp", axis=0, tiled=True)


def conv_forward(gathered, kernel, taps, pixels):
    result = jnp.zeros((kernel.shape[2], pixels), jnp.float32)
    for tap, phase, drow, dcol in taps:
        source = gathered[:, phase * pixels : (phase + 1) * pixels]
        part = jnp.einsum("kc,kp->cp", kernel[tap], source, preferred_element_type=jnp.float32)
        result = result + shifted(part, drow, dcol)
    return result


def conv_backward(grad_b, gathered, kernel, taps, pixels, phases):
    moved = [shifted(grad_b, -drow, -dcol) for tap, phase, drow, dcol in taps]
    count = gathered.shape[0] // lax.axis_size("mp") * lax.axis_size("mp")
    blocks = []
    for target in range(phases):
        result = jnp.zeros((count, pixels), jnp.float32)
        for conv_index, (conv_tap, conv_phase, conv_drow, conv_dcol) in enumerate(taps):
            if conv_phase == target:
                part = kernel[conv_tap]
                result = result + jnp.dot(
                    part, moved[conv_index], preferred_element_type=jnp.float32
                )
        blocks.append(result)
    hidden_grad = lax.psum_scatter(
        jnp.concatenate(blocks, 1), "mp", scatter_dimension=0, tiled=True
    )
    kernel_grad = jnp.stack(
        [
            jnp.einsum(
                "kp,cp->kc",
                gathered[:, phase * pixels : (phase + 1) * pixels],
                moved[index],
                preferred_element_type=jnp.float32,
            )
            for index, (tap, phase, drow, dcol) in enumerate(taps)
        ]
    )
    return (hidden_grad, kernel_grad)


def output_mix(hidden, kernel):
    return lax.psum_scatter(
        jnp.einsum("kc,kp->cp", kernel, hidden, preferred_element_type=jnp.float32),
        "mp",
        scatter_dimension=0,
        tiled=True,
    )


def output_back(grad_b, kernel, hidden):
    piece = lax.all_gather(grad_b, "mp", axis=0, tiled=True)
    hidden_grad = jnp.dot(kernel, piece, preferred_element_type=jnp.float32)
    columns = jnp.einsum("cp,kp->ck", hidden, piece, preferred_element_type=jnp.float32)
    return (hidden_grad, columns)


def input_back(values, grad_b, side_b, weight, side_weight, pixels):
    width = weight.shape[1]
    result = jnp.dot(weight, grad_b, preferred_element_type=jnp.float32)
    if side_weight is not None:
        result = jnp.concatenate(
            [
                result[:, :pixels]
                + jnp.dot(side_weight, side_b, preferred_element_type=jnp.float32),
                result[:, pixels:],
            ],
            1,
        )
    values_grad = lax.psum_scatter(result, "mp", scatter_dimension=0, tiled=True)
    piece = lax.all_gather(values, "mp", axis=0, tiled=True)
    blocks = [jnp.einsum("kp,cp->kc", piece, grad_b, preferred_element_type=jnp.float32)]
    if side_weight is not None:
        blocks.append(
            jnp.einsum("kp,cp->kc", piece[:, :pixels], side_b, preferred_element_type=jnp.float32)
        )
    joined = jnp.concatenate(blocks, 1)
    return (values_grad, joined[:, :width], joined[:, width:])


def adapt(grad_in, mean, square, first_fix, second_fix):
    mean_next = BETA_ONE * mean + (1.0 - BETA_ONE) * grad_in
    square_next = BETA_TWO * square + (1.0 - BETA_TWO) * grad_in * grad_in
    step = mean_next / first_fix / (jnp.sqrt(square_next / second_fix) + EPS_ADAM)
    return (mean_next, square_next, step)


def shards(
    inputs,
    pixel_mask,
    widths,
    output_grad,
    first_weight,
    shortcut_weight,
    middle_weight,
    last_weight,
    second_weight,
    narrow_norms,
    wide_norms,
    first_mean,
    first_square,
    shortcut_mean,
    shortcut_square,
    middle_mean,
    middle_square,
    last_mean,
    last_square,
    second_mean,
    second_square,
    narrow_mean,
    narrow_square,
    wide_mean,
    wide_square,
):
    pixels = pixel_mask.shape[1]
    width = first_weight.shape[1]
    rank = lax.axis_index("mp")
    channel = rank * width + lax.iota(jnp.int32, width)
    keep_one = (channel < widths[0]).astype(jnp.float32)[:, None]
    keep_two = (channel < widths[1]).astype(jnp.float32)[:, None]
    masks = pixel_mask.astype(jnp.float32)
    mask_in = masks.reshape(-1)
    mask_out = masks[0]
    field = (inputs * pixel_mask.astype(jnp.bfloat16)[None]).reshape(inputs.shape[0], -1)
    first_w, short_w, middle_w, last_w, second_w = (
        lax.all_gather(first_weight.astype(jnp.bfloat16), "dp", axis=0, tiled=True),
        lax.all_gather(shortcut_weight.astype(jnp.bfloat16), "dp", axis=0, tiled=True),
        lax.all_gather(middle_weight.astype(jnp.bfloat16), "dp", axis=2, tiled=True),
        lax.all_gather(last_weight.astype(jnp.bfloat16), "dp", axis=2, tiled=True),
        lax.all_gather(second_weight.astype(jnp.bfloat16), "dp", axis=0, tiled=True),
    )
    count_in, count_out = over_images(jnp.sum(mask_in), jnp.sum(mask_out))
    pre_one, pre_side = input_mix(field, first_w, short_w, pixels)
    totals, squares = moments(pre_one, mask_in)
    cen_one, scale_one, act_one = normalize(
        pre_one, totals, squares, count_in, narrow_norms[0, 0], narrow_norms[0, 1]
    )
    hid_one = (jax.nn.silu(act_one) * mask_in[None, :] * keep_one).astype(jnp.bfloat16)
    gat_one = mid_gathered(hid_one)
    pre_two = conv_forward(gat_one, middle_w[0], STRIDED_TAPS, pixels)
    totals, squares = moments(pre_two, mask_out)
    cen_two, scale_two, act_two = normalize(
        pre_two, totals, squares, count_out, narrow_norms[1, 0], narrow_norms[1, 1]
    )
    hid_two = (jax.nn.silu(act_two) * mask_out[None, :] * keep_one).astype(jnp.bfloat16)
    pre_three = output_mix(hid_two, last_w[0])
    weighted_three = pre_three * mask_out[None, :]
    weighted_side = pre_side * mask_out[None, :]
    totals, squares = over_images(
        jnp.stack([jnp.sum(weighted_three, 1), jnp.sum(weighted_side, 1)]),
        jnp.stack([jnp.sum(weighted_three * pre_three, 1), jnp.sum(weighted_side * pre_side, 1)]),
    )
    cen_three, scale_three, act_three = normalize(
        pre_three, totals[0], squares[0], count_out, wide_norms[0, 0], wide_norms[0, 1]
    )
    cen_side, scale_side, act_side = normalize(
        pre_side, totals[1], squares[1], count_out, wide_norms[1, 0], wide_norms[1, 1]
    )
    total_one = act_three + act_side
    out_one = (jax.nn.silu(total_one) * mask_out[None, :]).astype(jnp.bfloat16)
    (pre_four,) = input_mix(out_one, second_w, None, pixels)
    totals, squares = moments(pre_four, mask_out)
    cen_four, scale_four, act_four = normalize(
        pre_four, totals, squares, count_out, narrow_norms[2, 0], narrow_norms[2, 1]
    )
    hid_four = (jax.nn.silu(act_four) * mask_out[None, :] * keep_two).astype(jnp.bfloat16)
    gat_four = mid_gathered(hid_four)
    pre_five = conv_forward(gat_four, middle_w[1], PLAIN_TAPS, pixels)
    totals, squares = moments(pre_five, mask_out)
    cen_five, scale_five, act_five = normalize(
        pre_five, totals, squares, count_out, narrow_norms[3, 0], narrow_norms[3, 1]
    )
    hid_five = (jax.nn.silu(act_five) * mask_out[None, :] * keep_two).astype(jnp.bfloat16)
    pre_six = output_mix(hid_five, last_w[1])
    totals, squares = moments(pre_six, mask_out)
    cen_six, scale_six, act_six = normalize(
        pre_six, totals, squares, count_out, wide_norms[2, 0], wide_norms[2, 1]
    )
    total_two = act_six + out_one.astype(jnp.float32)
    block_output = (jax.nn.silu(total_two) * mask_out[None, :]).astype(jnp.bfloat16)
    grad_two = output_grad.astype(jnp.float32) * mask_out[None, :] * slope(total_two)
    gain_six, bias_six = back_sums(grad_two, cen_six)
    grad_six = norm_back(
        grad_two, cen_six, scale_six, wide_norms[2, 0], mask_out, gain_six, bias_six, count_out
    ).astype(jnp.bfloat16)
    hid_five_grad, last_one_grad = output_back(grad_six, last_w[1], hid_five)
    act_five_grad = hid_five_grad * keep_two * mask_out[None, :] * slope(act_five)
    gain_five, bias_five = back_sums(act_five_grad, cen_five)
    grad_five = norm_back(
        act_five_grad,
        cen_five,
        scale_five,
        narrow_norms[3, 0],
        mask_out,
        gain_five,
        bias_five,
        count_out,
    ).astype(jnp.bfloat16)
    hid_four_grad, middle_one_grad = conv_backward(
        grad_five, gat_four, middle_w[1], PLAIN_TAPS, pixels, 1
    )
    act_four_grad = hid_four_grad * keep_two * mask_out[None, :] * slope(act_four)
    gain_four, bias_four = back_sums(act_four_grad, cen_four)
    grad_four = norm_back(
        act_four_grad,
        cen_four,
        scale_four,
        narrow_norms[2, 0],
        mask_out,
        gain_four,
        bias_four,
        count_out,
    ).astype(jnp.bfloat16)
    out_one_grad, second_grad, unused_side = input_back(
        out_one, grad_four, None, second_w, None, pixels
    )
    grad_one = (grad_two + out_one_grad) * mask_out[None, :] * slope(total_one)
    gains_pair, bias_pair = over_images(
        jnp.stack([jnp.sum(grad_one * cen_three, 1), jnp.sum(grad_one * cen_side, 1)]),
        jnp.sum(grad_one, 1),
    )
    grad_three = norm_back(
        grad_one,
        cen_three,
        scale_three,
        wide_norms[0, 0],
        mask_out,
        gains_pair[0],
        bias_pair,
        count_out,
    ).astype(jnp.bfloat16)
    grad_side = norm_back(
        grad_one,
        cen_side,
        scale_side,
        wide_norms[1, 0],
        mask_out,
        gains_pair[1],
        bias_pair,
        count_out,
    ).astype(jnp.bfloat16)
    hid_two_grad, last_zero_grad = output_back(grad_three, last_w[0], hid_two)
    act_two_grad = hid_two_grad * keep_one * mask_out[None, :] * slope(act_two)
    gain_two, bias_two = back_sums(act_two_grad, cen_two)
    grad_mid = norm_back(
        act_two_grad,
        cen_two,
        scale_two,
        narrow_norms[1, 0],
        mask_out,
        gain_two,
        bias_two,
        count_out,
    ).astype(jnp.bfloat16)
    hid_one_grad, middle_zero_grad = conv_backward(
        grad_mid, gat_one, middle_w[0], STRIDED_TAPS, pixels, 4
    )
    act_one_grad = hid_one_grad * keep_one * mask_in[None, :] * slope(act_one)
    gain_one, bias_one = back_sums(act_one_grad, cen_one)
    grad_first = norm_back(
        act_one_grad, cen_one, scale_one, narrow_norms[0, 0], mask_in, gain_one, bias_one, count_in
    ).astype(jnp.bfloat16)
    field_grad, first_grad, short_grad = input_back(
        field, grad_first, grad_side, first_w, short_w, pixels
    )
    input_grad = (field_grad * mask_in[None, :]).astype(jnp.bfloat16).reshape(inputs.shape)
    grads = (
        lax.psum_scatter(first_grad, "dp", scatter_dimension=0, tiled=True),
        lax.psum_scatter(short_grad, "dp", scatter_dimension=0, tiled=True),
        lax.psum_scatter(
            jnp.stack([middle_zero_grad, middle_one_grad]), "dp", scatter_dimension=2, tiled=True
        ),
        lax.psum_scatter(
            jnp.stack([last_zero_grad, last_one_grad]), "dp", scatter_dimension=2, tiled=True
        ),
        lax.psum_scatter(second_grad, "dp", scatter_dimension=0, tiled=True),
    )
    first_fix = 1.0 - BETA_ONE**STEP
    second_fix = 1.0 - BETA_TWO**STEP
    weights = (first_weight, shortcut_weight, middle_weight, last_weight, second_weight)
    means = (first_mean, shortcut_mean, middle_mean, last_mean, second_mean)
    squares_old = (first_square, shortcut_square, middle_square, last_square, second_square)
    states = []
    updates = []
    for index in range(5):
        mean_next, square_next, step = adapt(
            grads[index], means[index], squares_old[index], first_fix, second_fix
        )
        states.append((mean_next, square_next))
        updates.append(step + DECAY * weights[index])
    pairs = [
        (weights[0], updates[0]),
        (weights[1], updates[1]),
        (weights[2][0], updates[2][0]),
        (weights[2][1], updates[2][1]),
        (weights[3][0], updates[3][0]),
        (weights[3][1], updates[3][1]),
        (weights[4], updates[4]),
    ]
    partial_value = jnp.stack(
        [
            jnp.stack([jnp.sum(weight * weight), jnp.sum(update * update)])
            for weight, update in pairs
        ]
    )
    matrix_norms = jnp.sqrt(lax.psum(partial_value, ("dp", "mp")))
    ratio = matrix_norms[:, 0] / (matrix_norms[:, 1] + EPS_TRUST)
    first_next = first_weight - RATE * ratio[0] * updates[0]
    short_next = shortcut_weight - RATE * ratio[1] * updates[1]
    middle_next = middle_weight - RATE * ratio[2:4].reshape(2, 1, 1, 1) * updates[2]
    last_next = last_weight - RATE * ratio[4:6].reshape(2, 1, 1) * updates[3]
    second_next = second_weight - RATE * ratio[6] * updates[4]
    narrow_grad = jnp.stack(
        [
            jnp.stack([gain_one, bias_one]),
            jnp.stack([gain_two, bias_two]),
            jnp.stack([gain_four, bias_four]),
            jnp.stack([gain_five, bias_five]),
        ]
    )
    wide_grad = jnp.stack(
        [
            jnp.stack([gains_pair[0], bias_pair]),
            jnp.stack([gains_pair[1], bias_pair]),
            jnp.stack([gain_six, bias_six]),
        ]
    )
    narrow_mean_next, narrow_square_next, narrow_step = adapt(
        narrow_grad, narrow_mean, narrow_square, first_fix, second_fix
    )
    wide_mean_next, wide_square_next, wide_step = adapt(
        wide_grad, wide_mean, wide_square, first_fix, second_fix
    )
    return (
        block_output,
        input_grad,
        states[0][0],
        states[0][1],
        first_next,
        states[1][0],
        states[1][1],
        short_next,
        states[2][0],
        states[2][1],
        middle_next,
        states[3][0],
        states[3][1],
        last_next,
        states[4][0],
        states[4][1],
        second_next,
        narrow_mean_next,
        narrow_square_next,
        narrow_norms - RATE_NORM * narrow_step,
        wide_mean_next,
        wide_square_next,
        wide_norms - RATE_NORM * wide_step,
        matrix_norms,
        first_next.astype(jnp.bfloat16),
        short_next.astype(jnp.bfloat16),
        middle_next.astype(jnp.bfloat16),
        last_next.astype(jnp.bfloat16),
        second_next.astype(jnp.bfloat16),
    )


def fits(mesh, pixel_mask):
    sizes = (mesh.shape["dp"], mesh.shape["mp"])
    powers = all(size >= 2 and size & (size - 1) == 0 for size in sizes)
    return powers and pixel_mask.shape[1] % (HO * WO * sizes[1]) == 0


def swap(values, axis, mask):
    size = lax.axis_size(axis)
    return lax.ppermute(values, axis, [(place, place ^ mask) for place in range(size)])


def bit_of(axis, mask):
    return (lax.axis_index(axis) & mask) // mask


def high_bits(axis):
    masks = []
    mask = lax.axis_size(axis) // 2
    while mask:
        masks.append(mask)
        mask //= 2
    return masks


def tree_sum(terms):
    while len(terms) > 1:
        terms = [terms[place] + terms[place + 1] for place in range(0, len(terms), 2)]
    return terms[0]


def everywhere(values):
    if values.shape[0] <= 16:
        count = lax.axis_size("dp") * lax.axis_size("mp")
        copies = jnp.broadcast_to(values[None], (count,) + values.shape)
        return jnp.sum(lax.all_to_all(copies, ("dp", "mp"), 0, 0, tiled=True), 0)
    for axis in ("mp", "dp"):
        mask = 1
        while mask < lax.axis_size(axis):
            values = values + swap(values, axis, mask)
            mask *= 2
    return values


def sum_all(parts):
    flat = [part.reshape(-1, 128) for part in parts]
    total = everywhere(jnp.concatenate(flat, 0))
    result = []
    start = 0
    for part, rows in zip(parts, flat):
        result.append(total[start : start + rows.shape[0]].reshape(part.shape))
        start += rows.shape[0]
    return result


def pack(block):
    lead, rows, cols = block.shape
    parts = block.reshape(lead, rows, cols // 128, 128).transpose(0, 2, 1, 3)
    return parts.reshape(-1, 128)


def column_bits():
    return [("mp", mask) for mask in high_bits("mp")[:-1]]


def row_bits():
    return [("dp", mask) for mask in high_bits("dp")]


def lanes_of(rows):
    first = rows // 32 * 16
    return ((0, first), (first, rows))


def merge(mine, other, bit, dim):
    high = bit_of(*bit) > 0
    pair = [jnp.where(high, other, mine), jnp.where(high, mine, other)]
    return jnp.concatenate(pair, dim)


class Gather:
    def __init__(self, rows, lanes=True):
        self.bits = column_bits() + row_bits()
        self.common = row_bits()[:-1]
        near = row_bits()[-1:]
        self.orders = [near + column_bits(), column_bits() + near]
        if not lanes:
            self.orders = self.orders[:1]
        self.value = rows.reshape((1,) * len(self.bits) + rows.shape)
        self.parts = None
        self.step = 0

    def operands(self):
        if self.step < len(self.common):
            return [self.value]
        if self.step < len(self.common) + len(self.orders[0]):
            if self.parts is None:
                spans = lanes_of(self.value.shape[-2])
                if len(self.orders) == 1:
                    spans = ((0, self.value.shape[-2]),)
                self.parts = [self.value[..., low:high, :] for low, high in spans]
            return self.parts
        if self.parts is not None:
            self.value = jnp.concatenate(self.parts, -2)
            self.parts = None
        return [self.value]

    def launch(self, operands):
        if self.step < len(self.common):
            bit = self.common[self.step]
            self.value = merge(operands[0], swap(operands[0], *bit), bit, self.bits.index(bit))
        elif self.step < len(self.common) + len(self.orders[0]):
            bits = [order[self.step - len(self.common)] for order in self.orders]
            self.parts = [
                merge(part, swap(part, *bit), bit, self.bits.index(bit))
                for part, bit in zip(operands, bits)
            ]
        else:
            self.value = operands[0]
            self.other = swap(operands[0], "mp", 1)
        self.step += 1

    def matrix(self, start, lead, units, columns):
        columns = columns // 128
        result = []
        for value in (self.value, self.other):
            value = value[..., start : start + lead * columns * units, :]
            value = value.reshape(
                1 << len(column_bits()), lax.axis_size("dp"), lead, columns, units, 128
            )
            value = value.transpose(2, 1, 4, 0, 3, 5)
            result.append(value.reshape(lead * value.shape[1] * units, -1))
        return result


class Scatter:
    def __init__(self, keep, send, lanes=True):
        self.bits = column_bits() + row_bits()
        shape = (2,) * len(self.bits) + keep.shape[2:]
        self.keep = keep.reshape(shape)
        self.send = send.reshape(shape)
        self.orders = [column_bits() + row_bits()[-1:], row_bits()[-1:] + column_bits()]
        if not lanes:
            self.orders = self.orders[:1]
        self.common = row_bits()[:-1][::-1]
        rows = keep.shape[-2]
        self.spans = lanes_of(rows) if lanes else ((0, rows),)
        self.step = 0

    def pick(self, term, bit, turn):
        place = bit_of(*bit)
        place = 1 - place if turn else place
        return lax.dynamic_slice_in_dim(term, place, 1, self.bits.index(bit))

    def total(self, terms):
        result = terms[0].astype(jnp.float32)
        for term in terms[1:]:
            result = result + term.astype(jnp.float32)
        return result

    def operands(self):
        step = self.step - 1
        if step < 0:
            return [self.send]
        if step < len(self.orders[0]):
            return [
                self.total([self.pick(term, order[step], True) for term in lane]).astype(
                    jnp.bfloat16
                )
                for lane, order in zip(self.lanes, self.orders)
            ]
        if step == len(self.orders[0]):
            counts = [[lane[place] for lane in self.lanes] for place in range(len(self.lanes[0]))]
            self.terms = [
                jnp.concatenate(parts, -2) if len(parts) > 1 else parts[0] for parts in counts
            ]
        bit = self.common[step - len(self.orders[0])]
        return [self.total([self.pick(term, bit, True) for term in self.terms]).astype(jnp.bfloat16)]

    def launch(self, operands):
        step = self.step - 1
        if step < 0:
            other = swap(operands[0], "mp", 1).reshape(self.keep.shape)
            self.lanes = [
                [term[..., low:high, :] for term in (self.keep, other)] for low, high in self.spans
            ]
        elif step < len(self.orders[0]):
            for place, order in enumerate(self.orders):
                arrived = swap(operands[place], *order[step])
                self.lanes[place] = [
                    self.pick(term, order[step], False) for term in self.lanes[place]
                ] + [arrived]
        else:
            bit = self.common[step - len(self.orders[0])]
            arrived = swap(operands[0], *bit)
            self.terms = [self.pick(term, bit, False) for term in self.terms] + [arrived]
        self.step += 1

    def rows(self):
        total = self.total(self.terms)
        return total.reshape(total.shape[-2:])


def wave(flows, anchor=()):
    operands = [flow.operands() for flow in flows]
    anchor, operands = lax.optimization_barrier((anchor, operands))
    for flow, values in zip(flows, operands):
        flow.launch(values)
    return anchor


def unpack(rows, start, lead, units, columns):
    count = lead * units * columns // 128
    value = rows[start : start + count].reshape(lead, columns // 128, units, 128)
    return value.transpose(0, 2, 1, 3).reshape(lead, units, columns)


def chunk_kernel(units, columns, rows_ref, cols_ref, *refs):
    outs = refs[-2:]
    product = lax.dot_general(
        rows_ref[...], cols_ref[...], (((0,), (0,)), ((), ())), preferred_element_type=jnp.float32
    ).astype(jnp.bfloat16)
    groups = outs[0].shape[0]
    chunks = outs[0].shape[1]
    for half, out in enumerate(outs):
        for group in range(groups):
            for part in range(columns):
                place = ((half * groups + group) * columns + part) * 128
                block = product[:, place : place + 128].reshape(chunks, units, 128)
                out[group, :, part * units : (part + 1) * units, :] = block


def chunks_into(bundle, total, start, rows_of, cols_of, lead, units, columns):
    count = lax.axis_size("dp")
    groups = 1 << len(column_bits())
    columns = columns // 128
    pixels = rows_of.shape[0]
    height = units * columns
    if lead > 1:
        steps, wide, chunks = lead, count * units, count
        place = lambda step: (0, 0, start // height + step, 0)
    else:
        steps, wide, chunks = count, units, 1
        place = lambda step: (0, step, start // height, 0)
    turned = jnp.concatenate(halves(cols_of), 1)
    shape = jax.ShapeDtypeStruct((groups, count, total, 128), jnp.bfloat16)
    block = pl.BlockSpec((groups, chunks, height, 128), place)
    earlier = () if bundle is None else tuple(bundle)
    return pl.pallas_call(
        functools.partial(chunk_kernel, units, columns),
        grid=(steps,),
        in_specs=[
            pl.BlockSpec((pixels, wide), lambda step: (0, step)),
            pl.BlockSpec(turned.shape, lambda step: (0, 0)),
        ]
        + [pl.BlockSpec(memory_space=pl.ANY)] * len(earlier),
        out_specs=[block, block],
        out_shape=[shape, shape],
        input_output_aliases={2 + place: place for place in range(len(earlier))},
        compiler_params=pltpu.CompilerParams(vmem_limit_bytes=40 * 2**20),
        cost_estimate=pl.CostEstimate(
            flops=2 * rows_of.size * cols_of.shape[1],
            bytes_accessed=2 * (rows_of.size + cols_of.size)
            + 2 * rows_of.shape[1] * cols_of.shape[1],
            transcendentals=0,
        ),
    )(rows_of, turned, *earlier)


def halves(values):
    count = lax.axis_size("mp")
    width = values.shape[-1] // count
    blocks = [values[..., place * width : (place + 1) * width] for place in range(count)]
    even = jnp.concatenate(blocks[0::2], -1)
    odd = jnp.concatenate(blocks[1::2], -1)
    high = bit_of("mp", 1) > 0
    return (jnp.where(high, odd, even), jnp.where(high, even, odd))


def joined(mine, other):
    count = lax.axis_size("mp")
    width = 2 * mine.shape[-1] // count
    high = bit_of("mp", 1) > 0
    even = jnp.where(high, other, mine)
    odd = jnp.where(high, mine, other)
    blocks = []
    for place in range(count // 2):
        blocks.append(even[..., place * width : (place + 1) * width])
        blocks.append(odd[..., place * width : (place + 1) * width])
    return jnp.concatenate(blocks, -1)


def dot(first, second, dims):
    return lax.dot_general(first, second, (dims, ((), ())), preferred_element_type=jnp.float32)


def times(values, weight):
    return joined(*[dot(values, part, ((1,), (0,))) for part in weight])


def times_turned(values, weight):
    parts = [
        dot(value, part, ((1,), (1,))) for value, part in zip(halves(values), weight)
    ]
    return parts[0] + parts[1]


def reach(values, drow, dcol):
    offset = drow * WO + dcol
    count = values.shape[0]
    place = lax.iota(jnp.int32, count)
    row_at = place // WO % HO + drow
    col_at = place % WO + dcol
    inside = (row_at >= 0) & (row_at < HO) & (col_at >= 0) & (col_at < WO)
    moved = jnp.roll(values, -offset, axis=0)
    return jnp.where(inside[:, None], moved, jnp.zeros_like(moved))


def tap_columns(values, taps, pixels):
    return jnp.concatenate(
        [
            reach(values[phase * pixels : (phase + 1) * pixels], drow, dcol)
            for tap, phase, drow, dcol in taps
        ],
        1,
    )


def tap_back(columns, taps, width, phases):
    blocks = []
    for target in range(phases):
        total = 0.0
        for tap, phase, drow, dcol in taps:
            if phase == target:
                total = total + reach(columns[:, tap * width : (tap + 1) * width], -drow, -dcol)
        blocks.append(total)
    return jnp.concatenate(blocks, 0)


def sums_of(values, mask):
    weighted = values * mask
    return [jnp.sum(weighted, 0), jnp.sum(weighted * values, 0)]


def normed(values, totals, count, table):
    mean = totals[0] / count
    scale = lax.rsqrt(totals[1] / count - mean * mean + EPS_NORM)
    centred = (values - mean[None]) * scale[None]
    return (centred, scale, centred * table[0][None] + table[1][None])


def grad_sums(grad_in, centred):
    return [jnp.sum(grad_in * centred, 0), jnp.sum(grad_in, 0)]


def normed_back(grad_in, centred, scale, gain, mask, totals, count):
    return (
        (gain * scale)[None]
        * (grad_in - mask * (totals[1][None] + centred * totals[0][None]) / count)
    ).astype(jnp.bfloat16)


def by_image(
    inputs,
    pixel_mask,
    widths,
    output_grad,
    first_weight,
    shortcut_weight,
    middle_weight,
    last_weight,
    second_weight,
    narrow_norms,
    wide_norms,
    first_mean,
    first_square,
    shortcut_mean,
    shortcut_square,
    middle_mean,
    middle_square,
    last_mean,
    last_square,
    second_mean,
    second_square,
    narrow_mean,
    narrow_square,
    wide_mean,
    wide_square,
):
    ranks = lax.axis_size("mp")
    rank = lax.axis_index("mp")
    pixels = pixel_mask.shape[1] // ranks
    narrow = first_weight.shape[1] * ranks
    wide = shortcut_weight.shape[1] * ranks
    low = jnp.bfloat16
    flow_a = Gather(pack(first_weight.astype(low)[None]), False)
    flow_b = Gather(pack(middle_weight[0].astype(low)))
    flow_c = Gather(
        jnp.concatenate(
            [
                pack(shortcut_weight.astype(low)[None]),
                pack(last_weight[0].astype(low).T[None]),
                pack(second_weight.astype(low)[None]),
            ]
        )
    )
    flow_d = Gather(
        jnp.concatenate(
            [pack(last_weight[1].astype(low).T[None]), pack(middle_weight[1].astype(low))]
        )
    )
    wave([flow_a])
    wave([flow_a, flow_b])
    wave([flow_a, flow_b])
    wave([flow_a, flow_b, flow_c])
    wave([flow_a, flow_b, flow_c])
    wave([flow_b, flow_c, flow_d])
    wave([flow_c, flow_d])
    wave([flow_c, flow_d])
    wave([flow_d])
    wave([flow_d])
    unit_in, column = first_weight.shape
    column_wide = shortcut_weight.shape[1]
    unit_mid = middle_weight.shape[2]
    unit_out = second_weight.shape[0]
    size_short = unit_in * column_wide // 128
    size_out = unit_out * column // 128
    size_mid = 9 * unit_mid * column // 128
    first_w = flow_a.matrix(0, 1, unit_in, column)
    mid_zero_w = flow_b.matrix(0, 9, unit_mid, column)
    short_w = flow_c.matrix(0, 1, unit_in, column_wide)
    last_zero_w = flow_c.matrix(size_short, 1, unit_out, column)
    second_w = flow_c.matrix(size_short + size_out, 1, unit_out, column)
    last_one_w = flow_d.matrix(0, 1, unit_out, column)
    mid_one_w = flow_d.matrix(size_out, 9, unit_mid, column)
    tables = jnp.concatenate([narrow_norms.reshape(-1, 128), wide_norms.reshape(-1, 128)], 0)
    tables = jnp.broadcast_to(tables[None], (ranks,) + tables.shape)
    tables = lax.all_to_all(tables, "mp", 0, 0, tiled=True)
    split = narrow_norms.size // 128
    narrow_all = (
        tables[:, :split].reshape(ranks, 4, 2, -1).transpose(1, 2, 0, 3).reshape(4, 2, narrow)
    )
    wide_all = tables[:, split:].reshape(ranks, 3, 2, -1).transpose(1, 2, 0, 3).reshape(3, 2, wide)

    own_mask = lax.dynamic_slice_in_dim(pixel_mask, rank * pixels, pixels, 1).astype(jnp.float32)
    mask_in = own_mask.reshape(-1, 1)
    mask_out = own_mask[0][:, None]
    channel = lax.iota(jnp.int32, narrow)
    keep_one = (channel < widths[0]).astype(jnp.float32)[None]
    keep_two = (channel < widths[1]).astype(jnp.float32)[None]

    field = lax.all_to_all(inputs, "mp", split_axis=2, concat_axis=0, tiled=True)
    field = field.transpose(1, 2, 0).reshape(4 * pixels, -1) * mask_in.astype(low)
    above = lax.all_to_all(output_grad, "mp", split_axis=1, concat_axis=0, tiled=True).T

    pre_one = times(field, first_w)
    counts = jnp.stack([jnp.sum(mask_in), jnp.sum(mask_out)])
    counts = jnp.concatenate([counts, jnp.zeros(126, jnp.float32)])
    *totals, counts = sum_all(sums_of(pre_one, mask_in) + [counts])
    count_in, count_out = counts[0], counts[1]
    cen_one, scale_one, act_one = normed(pre_one, totals, count_in, narrow_all[0])
    hid_one = (jax.nn.silu(act_one) * mask_in * keep_one).astype(low)
    cols_one = tap_columns(hid_one, STRIDED_TAPS, pixels)
    pre_two = times(cols_one, mid_zero_w)
    totals = sum_all(sums_of(pre_two, mask_out))
    cen_two, scale_two, act_two = normed(pre_two, totals, count_out, narrow_all[1])
    hid_two = (jax.nn.silu(act_two) * mask_out * keep_one).astype(low)
    pre_three = times_turned(hid_two, last_zero_w)
    pre_side = times(field[:pixels], short_w)
    totals = sum_all(sums_of(pre_three, mask_out) + sums_of(pre_side, mask_out))
    cen_three, scale_three, act_three = normed(pre_three, totals[:2], count_out, wide_all[0])
    cen_side, scale_side, act_side = normed(pre_side, totals[2:], count_out, wide_all[1])
    total_one = act_three + act_side
    out_one = (jax.nn.silu(total_one) * mask_out).astype(low)
    pre_four = times(out_one, second_w)
    totals = sum_all(sums_of(pre_four, mask_out))
    cen_four, scale_four, act_four = normed(pre_four, totals, count_out, narrow_all[2])
    hid_four = (jax.nn.silu(act_four) * mask_out * keep_two).astype(low)
    cols_four = tap_columns(hid_four, PLAIN_TAPS, pixels)
    pre_five = times(cols_four, mid_one_w)
    totals = sum_all(sums_of(pre_five, mask_out))
    cen_five, scale_five, act_five = normed(pre_five, totals, count_out, narrow_all[3])
    hid_five = (jax.nn.silu(act_five) * mask_out * keep_two).astype(low)
    pre_six = times_turned(hid_five, last_one_w)
    totals = sum_all(sums_of(pre_six, mask_out))
    cen_six, scale_six, act_six = normed(pre_six, totals, count_out, wide_all[2])
    total_two = act_six + out_one.astype(jnp.float32)
    block_output = (jax.nn.silu(total_two) * mask_out).astype(low)
    block_output = lax.all_to_all(block_output.T, "mp", split_axis=0, concat_axis=1, tiled=True)

    grad_two = above.astype(jnp.float32) * mask_out * slope(total_two)
    sums_six = sum_all(grad_sums(grad_two, cen_six))
    grad_six = normed_back(
        grad_two, cen_six, scale_six, wide_all[2, 0], mask_out, sums_six, count_out
    )
    hid_five_grad = times(grad_six, last_one_w)
    act_five_grad = hid_five_grad * keep_two * mask_out * slope(act_five)
    total = size_out + size_mid
    bundle = chunks_into(None, total, 0, grad_six, hid_five, 1, unit_out, column)
    sums_five = sum_all(grad_sums(act_five_grad, cen_five))
    grad_five = normed_back(
        act_five_grad, cen_five, scale_five, narrow_all[3, 0], mask_out, sums_five, count_out
    )
    bundle = chunks_into(bundle, total, size_out, cols_four, grad_five, 9, unit_mid, column)
    back_a = Scatter(*bundle)
    grad_five = wave([back_a], grad_five)
    hid_four_grad = tap_back(times_turned(grad_five, mid_one_w), PLAIN_TAPS, narrow, 1)
    act_four_grad = hid_four_grad * keep_two * mask_out * slope(act_four)
    sums_four = sum_all(wave([back_a], grad_sums(act_four_grad, cen_four)))
    grad_four = normed_back(
        act_four_grad, cen_four, scale_four, narrow_all[2, 0], mask_out, sums_four, count_out
    )
    grad_one = (
        (grad_two + times_turned(grad_four, second_w)) * mask_out * slope(total_one)
    )
    gain_three, gain_side, bias_pair = sum_all(
        wave(
            [back_a],
            [
                jnp.sum(grad_one * cen_three, 0),
                jnp.sum(grad_one * cen_side, 0),
                jnp.sum(grad_one, 0),
            ],
        )
    )
    total = size_short + 2 * size_out
    bundle = chunks_into(
        None, total, size_short + size_out, out_one, grad_four, 1, unit_out, column
    )
    grad_three = normed_back(
        grad_one, cen_three, scale_three, wide_all[0, 0], mask_out, (gain_three, bias_pair), count_out
    )
    grad_side = normed_back(
        grad_one, cen_side, scale_side, wide_all[1, 0], mask_out, (gain_side, bias_pair), count_out
    )
    bundle = chunks_into(bundle, total, size_short, grad_three, hid_two, 1, unit_out, column)
    bundle = chunks_into(bundle, total, 0, field[:pixels], grad_side, 1, unit_in, column_wide)
    back_b = Scatter(*bundle)
    grad_three = wave([back_a, back_b], grad_three)
    hid_two_grad = times(grad_three, last_zero_w)
    act_two_grad = hid_two_grad * keep_one * mask_out * slope(act_two)
    sums_two = sum_all(wave([back_a, back_b], grad_sums(act_two_grad, cen_two)))
    grad_mid = normed_back(
        act_two_grad, cen_two, scale_two, narrow_all[1, 0], mask_out, sums_two, count_out
    )
    bundle = chunks_into(None, size_mid, 0, cols_one, grad_mid, 9, unit_mid, column)
    back_c = Scatter(*bundle)
    grad_mid = wave([back_c], grad_mid)
    hid_one_grad = tap_back(times_turned(grad_mid, mid_zero_w), STRIDED_TAPS, narrow, 4)
    act_one_grad = hid_one_grad * keep_one * mask_in * slope(act_one)
    sums_one = sum_all(wave([back_b, back_c], grad_sums(act_one_grad, cen_one)))
    grad_first = normed_back(
        act_one_grad, cen_one, scale_one, narrow_all[0, 0], mask_in, sums_one, count_in
    )
    bundle = chunks_into(None, unit_in * column // 128, 0, field, grad_first, 1, unit_in, column)
    back_d = Scatter(*bundle, False)
    grad_first, grad_side = wave([back_b, back_c, back_d], (grad_first, grad_side))
    field_grad = times_turned(grad_first, first_w)
    side_grad = times_turned(grad_side, short_w)
    field_grad = jnp.concatenate([field_grad[:pixels] + side_grad, field_grad[pixels:]], 0)
    field_grad = (field_grad * mask_in).astype(low).reshape(4, pixels, -1).transpose(2, 0, 1)
    input_grad = lax.all_to_all(field_grad, "mp", split_axis=0, concat_axis=2, tiled=True)
    wave([back_b, back_c, back_d])
    wave([back_c, back_d])
    wave([back_d])
    wave([back_d])
    rows_a, rows_b, rows_c, rows_d = [flow.rows() for flow in (back_a, back_b, back_c, back_d)]
    grads = (
        unpack(rows_d, 0, 1, unit_in, column)[0],
        unpack(rows_b, 0, 1, unit_in, column_wide)[0],
        jnp.stack(
            [
                unpack(rows_c, 0, 9, unit_mid, column),
                unpack(rows_a, size_out, 9, unit_mid, column),
            ]
        ),
        jnp.stack(
            [
                unpack(rows_b, size_short, 1, unit_out, column)[0].T,
                unpack(rows_a, 0, 1, unit_out, column)[0].T,
            ]
        ),
        unpack(rows_b, size_short + size_out, 1, unit_out, column)[0],
    )
    first_fix = 1.0 - BETA_ONE**STEP
    second_fix = 1.0 - BETA_TWO**STEP
    weights = (first_weight, shortcut_weight, middle_weight, last_weight, second_weight)
    means = (first_mean, shortcut_mean, middle_mean, last_mean, second_mean)
    squares_old = (first_square, shortcut_square, middle_square, last_square, second_square)
    states = []
    updates = []
    for index in range(5):
        mean_next, square_next, step = adapt(
            grads[index], means[index], squares_old[index], first_fix, second_fix
        )
        states.append((mean_next, square_next))
        updates.append(step + DECAY * weights[index])
    pairs = [
        (weights[0], updates[0]),
        (weights[1], updates[1]),
        (weights[2][0], updates[2][0]),
        (weights[2][1], updates[2][1]),
        (weights[3][0], updates[3][0]),
        (weights[3][1], updates[3][1]),
        (weights[4], updates[4]),
    ]
    own = [jnp.sum((value * value).reshape(-1, 128), 0) for pair in pairs for value in pair]
    powers = jnp.sum(everywhere(jnp.stack(own)), 1)
    matrix_norms = jnp.sqrt(powers.reshape(-1, 2))
    ratio = matrix_norms[:, 0] / (matrix_norms[:, 1] + EPS_TRUST)
    first_next = first_weight - RATE * ratio[0] * updates[0]
    short_next = shortcut_weight - RATE * ratio[1] * updates[1]
    middle_next = middle_weight - RATE * ratio[2:4].reshape(2, 1, 1, 1) * updates[2]
    last_next = last_weight - RATE * ratio[4:6].reshape(2, 1, 1) * updates[3]
    second_next = second_weight - RATE * ratio[6] * updates[4]

    def own_channels(values):
        width = values.shape[-1] // ranks
        return lax.dynamic_slice_in_dim(values, rank * width, width, values.ndim - 1)

    narrow_grad = own_channels(
        jnp.stack([jnp.stack(pair) for pair in (sums_one, sums_two, sums_four, sums_five)])
    )
    wide_grad = own_channels(
        jnp.stack(
            [
                jnp.stack([gain_three, bias_pair]),
                jnp.stack([gain_side, bias_pair]),
                jnp.stack(sums_six),
            ]
        )
    )
    narrow_mean_next, narrow_square_next, narrow_step = adapt(
        narrow_grad, narrow_mean, narrow_square, first_fix, second_fix
    )
    wide_mean_next, wide_square_next, wide_step = adapt(
        wide_grad, wide_mean, wide_square, first_fix, second_fix
    )
    return (
        block_output,
        input_grad,
        states[0][0],
        states[0][1],
        first_next,
        states[1][0],
        states[1][1],
        short_next,
        states[2][0],
        states[2][1],
        middle_next,
        states[3][0],
        states[3][1],
        last_next,
        states[4][0],
        states[4][1],
        second_next,
        narrow_mean_next,
        narrow_square_next,
        narrow_norms - RATE_NORM * narrow_step,
        wide_mean_next,
        wide_square_next,
        wide_norms - RATE_NORM * wide_step,
        matrix_norms,
        first_next.astype(jnp.bfloat16),
        short_next.astype(jnp.bfloat16),
        middle_next.astype(jnp.bfloat16),
        last_next.astype(jnp.bfloat16),
        second_next.astype(jnp.bfloat16),
    )


def solution(mesh):
    in_specs = (
        P("mp", None, "dp"),
        P(None, "dp"),
        P(),
        P("mp", "dp"),
        P("dp", "mp"),
        P("dp", "mp"),
        P(None, None, "dp", "mp"),
        P(None, "mp", "dp"),
        P("dp", "mp"),
        P(None, None, "mp"),
        P(None, None, "mp"),
        P("dp", "mp"),
        P("dp", "mp"),
        P("dp", "mp"),
        P("dp", "mp"),
        P(None, None, "dp", "mp"),
        P(None, None, "dp", "mp"),
        P(None, "mp", "dp"),
        P(None, "mp", "dp"),
        P("dp", "mp"),
        P("dp", "mp"),
        P(None, None, "mp"),
        P(None, None, "mp"),
        P(None, None, "mp"),
        P(None, None, "mp"),
    )
    out_specs = (
        P("mp", "dp"),
        P("mp", None, "dp"),
        P("dp", "mp"),
        P("dp", "mp"),
        P("dp", "mp"),
        P("dp", "mp"),
        P("dp", "mp"),
        P("dp", "mp"),
        P(None, None, "dp", "mp"),
        P(None, None, "dp", "mp"),
        P(None, None, "dp", "mp"),
        P(None, "mp", "dp"),
        P(None, "mp", "dp"),
        P(None, "mp", "dp"),
        P("dp", "mp"),
        P("dp", "mp"),
        P("dp", "mp"),
        P(None, None, "mp"),
        P(None, None, "mp"),
        P(None, None, "mp"),
        P(None, None, "mp"),
        P(None, None, "mp"),
        P(None, None, "mp"),
        P(),
        P("dp", "mp"),
        P("dp", "mp"),
        P(None, None, "dp", "mp"),
        P(None, "mp", "dp"),
        P("dp", "mp"),
    )
    return jax.shard_map(
        lambda *values: (by_image if fits(mesh, values[1]) else shards)(*values),
        mesh=mesh,
        in_specs=in_specs,
        out_specs=out_specs,
        check_vma=False,
    )
```

```python
import functools

import jax
import jax.numpy as jnp
from jax import lax
from jax.experimental import pallas as pl
from jax.experimental.pallas import tpu as pltpu
from jax.sharding import PartitionSpec as P

HO = 16
WO = 11
STEP = 10


EPS_NORM = 1e-05
BETA_ONE = 0.9
BETA_TWO = 0.999
EPS_ADAM = 1e-06
DECAY = 0.01
RATE = 0.3
RATE_NORM = 0.3
EPS_TRUST = 1e-06
PHASES = ((1, -1), (0, 0), (1, 0))
STRIDED_TAPS = tuple(
    (
        (
            3 * above + beside,
            2 * PHASES[above][0] + PHASES[beside][0],
            PHASES[above][1],
            PHASES[beside][1],
        )
        for above in range(3)
        for beside in range(3)
    )
)
PLAIN_TAPS = tuple(
    ((3 * above + beside, 0, above - 1, beside - 1) for above in range(3) for beside in range(3))
)


def slope(values):
    gate = jax.nn.sigmoid(values)
    return gate * (1.0 + values * (1.0 - gate))


def shifted(values, drow, dcol):
    length = values.shape[1]
    offset = drow * WO + dcol
    place = lax.iota(jnp.int32, length)
    row_at = place // WO % HO + drow
    col_at = place % WO + dcol
    inside = (row_at >= 0) & (row_at < HO) & (col_at >= 0) & (col_at < WO)
    moved = jnp.roll(values, -offset, axis=1)
    return jnp.where(inside[None, :], moved, jnp.zeros_like(moved))


def over_images(first, second):
    return lax.psum((first, second), "dp")


def moments(values, mask):
    weighted = values * mask[None, :]
    return over_images(jnp.sum(weighted, 1), jnp.sum(weighted * values, 1))


def normalize(values, totals, squares, count, gain, bias):
    mean = totals / count
    scale = lax.rsqrt(squares / count - mean * mean + EPS_NORM)
    centred = (values - mean[:, None]) * scale[:, None]
    return (centred, scale, centred * gain[:, None] + bias[:, None])


def back_sums(grad_in, centred):
    return over_images(jnp.sum(grad_in * centred, 1), jnp.sum(grad_in, 1))


def norm_back(grad_in, centred, scale, gain, mask, gain_sum, bias_sum, count):
    return (gain * scale)[:, None] * (
        grad_in - mask[None, :] * (bias_sum[:, None] + centred * gain_sum[:, None]) / count
    )


def input_mix(values, weight, side_weight, pixels):
    start_sum = (jnp.zeros((weight.shape[1], values.shape[1]), jnp.float32),)
    if side_weight is not None:
        start_sum = start_sum + (jnp.zeros((side_weight.shape[1], pixels), jnp.float32),)
    piece = lax.all_gather(values, "mp", axis=0, tiled=True)
    result = (jnp.einsum("kc,kp->cp", weight, piece, preferred_element_type=jnp.float32),)
    if side_weight is not None:
        result = result + (
            jnp.einsum(
                "kc,kp->cp", side_weight, piece[:, :pixels], preferred_element_type=jnp.float32
            ),
        )
    return result


def mid_gathered(hidden):
    return lax.all_gather(hidden, "mp", axis=0, tiled=True)


def conv_forward(gathered, kernel, taps, pixels):
    result = jnp.zeros((kernel.shape[2], pixels), jnp.float32)
    for tap, phase, drow, dcol in taps:
        source = gathered[:, phase * pixels : (phase + 1) * pixels]
        part = jnp.einsum("kc,kp->cp", kernel[tap], source, preferred_element_type=jnp.float32)
        result = result + shifted(part, drow, dcol)
    return result


def conv_backward(grad_b, gathered, kernel, taps, pixels, phases):
    moved = [shifted(grad_b, -drow, -dcol) for tap, phase, drow, dcol in taps]
    count = gathered.shape[0] // lax.axis_size("mp") * lax.axis_size("mp")
    blocks = []
    for target in range(phases):
        result = jnp.zeros((count, pixels), jnp.float32)
        for conv_index, (conv_tap, conv_phase, conv_drow, conv_dcol) in enumerate(taps):
            if conv_phase == target:
                part = kernel[conv_tap]
                result = result + jnp.dot(
                    part, moved[conv_index], preferred_element_type=jnp.float32
                )
        blocks.append(result)
    hidden_grad = lax.psum_scatter(
        jnp.concatenate(blocks, 1), "mp", scatter_dimension=0, tiled=True
    )
    kernel_grad = jnp.stack(
        [
            jnp.einsum(
                "kp,cp->kc",
                gathered[:, phase * pixels : (phase + 1) * pixels],
                moved[index],
                preferred_element_type=jnp.float32,
            )
            for index, (tap, phase, drow, dcol) in enumerate(taps)
        ]
    )
    return (hidden_grad, kernel_grad)


def output_mix(hidden, kernel):
    return lax.psum_scatter(
        jnp.einsum("kc,kp->cp", kernel, hidden, preferred_element_type=jnp.float32),
        "mp",
        scatter_dimension=0,
        tiled=True,
    )


def output_back(grad_b, kernel, hidden):
    piece = lax.all_gather(grad_b, "mp", axis=0, tiled=True)
    hidden_grad = jnp.dot(kernel, piece, preferred_element_type=jnp.float32)
    columns = jnp.einsum("cp,kp->ck", hidden, piece, preferred_element_type=jnp.float32)
    return (hidden_grad, columns)


def input_back(values, grad_b, side_b, weight, side_weight, pixels):
    width = weight.shape[1]
    result = jnp.dot(weight, grad_b, preferred_element_type=jnp.float32)
    if side_weight is not None:
        result = jnp.concatenate(
            [
                result[:, :pixels]
                + jnp.dot(side_weight, side_b, preferred_element_type=jnp.float32),
                result[:, pixels:],
            ],
            1,
        )
    values_grad = lax.psum_scatter(result, "mp", scatter_dimension=0, tiled=True)
    piece = lax.all_gather(values, "mp", axis=0, tiled=True)
    blocks = [jnp.einsum("kp,cp->kc", piece, grad_b, preferred_element_type=jnp.float32)]
    if side_weight is not None:
        blocks.append(
            jnp.einsum("kp,cp->kc", piece[:, :pixels], side_b, preferred_element_type=jnp.float32)
        )
    joined = jnp.concatenate(blocks, 1)
    return (values_grad, joined[:, :width], joined[:, width:])


def adapt(grad_in, mean, square, first_fix, second_fix):
    mean_next = BETA_ONE * mean + (1.0 - BETA_ONE) * grad_in
    square_next = BETA_TWO * square + (1.0 - BETA_TWO) * grad_in * grad_in
    step = mean_next / first_fix / (jnp.sqrt(square_next / second_fix) + EPS_ADAM)
    return (mean_next, square_next, step)


def shards(
    inputs,
    pixel_mask,
    widths,
    output_grad,
    first_weight,
    shortcut_weight,
    middle_weight,
    last_weight,
    second_weight,
    narrow_norms,
    wide_norms,
    first_mean,
    first_square,
    shortcut_mean,
    shortcut_square,
    middle_mean,
    middle_square,
    last_mean,
    last_square,
    second_mean,
    second_square,
    narrow_mean,
    narrow_square,
    wide_mean,
    wide_square,
):
    pixels = pixel_mask.shape[1]
    width = first_weight.shape[1]
    rank = lax.axis_index("mp")
    channel = rank * width + lax.iota(jnp.int32, width)
    keep_one = (channel < widths[0]).astype(jnp.float32)[:, None]
    keep_two = (channel < widths[1]).astype(jnp.float32)[:, None]
    masks = pixel_mask.astype(jnp.float32)
    mask_in = masks.reshape(-1)
    mask_out = masks[0]
    field = (inputs * pixel_mask.astype(jnp.bfloat16)[None]).reshape(inputs.shape[0], -1)
    first_w, short_w, middle_w, last_w, second_w = (
        lax.all_gather(first_weight.astype(jnp.bfloat16), "dp", axis=0, tiled=True),
        lax.all_gather(shortcut_weight.astype(jnp.bfloat16), "dp", axis=0, tiled=True),
        lax.all_gather(middle_weight.astype(jnp.bfloat16), "dp", axis=2, tiled=True),
        lax.all_gather(last_weight.astype(jnp.bfloat16), "dp", axis=2, tiled=True),
        lax.all_gather(second_weight.astype(jnp.bfloat16), "dp", axis=0, tiled=True),
    )
    count_in, count_out = over_images(jnp.sum(mask_in), jnp.sum(mask_out))
    pre_one, pre_side = input_mix(field, first_w, short_w, pixels)
    totals, squares = moments(pre_one, mask_in)
    cen_one, scale_one, act_one = normalize(
        pre_one, totals, squares, count_in, narrow_norms[0, 0], narrow_norms[0, 1]
    )
    hid_one = (jax.nn.silu(act_one) * mask_in[None, :] * keep_one).astype(jnp.bfloat16)
    gat_one = mid_gathered(hid_one)
    pre_two = conv_forward(gat_one, middle_w[0], STRIDED_TAPS, pixels)
    totals, squares = moments(pre_two, mask_out)
    cen_two, scale_two, act_two = normalize(
        pre_two, totals, squares, count_out, narrow_norms[1, 0], narrow_norms[1, 1]
    )
    hid_two = (jax.nn.silu(act_two) * mask_out[None, :] * keep_one).astype(jnp.bfloat16)
    pre_three = output_mix(hid_two, last_w[0])
    weighted_three = pre_three * mask_out[None, :]
    weighted_side = pre_side * mask_out[None, :]
    totals, squares = over_images(
        jnp.stack([jnp.sum(weighted_three, 1), jnp.sum(weighted_side, 1)]),
        jnp.stack([jnp.sum(weighted_three * pre_three, 1), jnp.sum(weighted_side * pre_side, 1)]),
    )
    cen_three, scale_three, act_three = normalize(
        pre_three, totals[0], squares[0], count_out, wide_norms[0, 0], wide_norms[0, 1]
    )
    cen_side, scale_side, act_side = normalize(
        pre_side, totals[1], squares[1], count_out, wide_norms[1, 0], wide_norms[1, 1]
    )
    total_one = act_three + act_side
    out_one = (jax.nn.silu(total_one) * mask_out[None, :]).astype(jnp.bfloat16)
    (pre_four,) = input_mix(out_one, second_w, None, pixels)
    totals, squares = moments(pre_four, mask_out)
    cen_four, scale_four, act_four = normalize(
        pre_four, totals, squares, count_out, narrow_norms[2, 0], narrow_norms[2, 1]
    )
    hid_four = (jax.nn.silu(act_four) * mask_out[None, :] * keep_two).astype(jnp.bfloat16)
    gat_four = mid_gathered(hid_four)
    pre_five = conv_forward(gat_four, middle_w[1], PLAIN_TAPS, pixels)
    totals, squares = moments(pre_five, mask_out)
    cen_five, scale_five, act_five = normalize(
        pre_five, totals, squares, count_out, narrow_norms[3, 0], narrow_norms[3, 1]
    )
    hid_five = (jax.nn.silu(act_five) * mask_out[None, :] * keep_two).astype(jnp.bfloat16)
    pre_six = output_mix(hid_five, last_w[1])
    totals, squares = moments(pre_six, mask_out)
    cen_six, scale_six, act_six = normalize(
        pre_six, totals, squares, count_out, wide_norms[2, 0], wide_norms[2, 1]
    )
    total_two = act_six + out_one.astype(jnp.float32)
    block_output = (jax.nn.silu(total_two) * mask_out[None, :]).astype(jnp.bfloat16)
    grad_two = output_grad.astype(jnp.float32) * mask_out[None, :] * slope(total_two)
    gain_six, bias_six = back_sums(grad_two, cen_six)
    grad_six = norm_back(
        grad_two, cen_six, scale_six, wide_norms[2, 0], mask_out, gain_six, bias_six, count_out
    ).astype(jnp.bfloat16)
    hid_five_grad, last_one_grad = output_back(grad_six, last_w[1], hid_five)
    act_five_grad = hid_five_grad * keep_two * mask_out[None, :] * slope(act_five)
    gain_five, bias_five = back_sums(act_five_grad, cen_five)
    grad_five = norm_back(
        act_five_grad,
        cen_five,
        scale_five,
        narrow_norms[3, 0],
        mask_out,
        gain_five,
        bias_five,
        count_out,
    ).astype(jnp.bfloat16)
    hid_four_grad, middle_one_grad = conv_backward(
        grad_five, gat_four, middle_w[1], PLAIN_TAPS, pixels, 1
    )
    act_four_grad = hid_four_grad * keep_two * mask_out[None, :] * slope(act_four)
    gain_four, bias_four = back_sums(act_four_grad, cen_four)
    grad_four = norm_back(
        act_four_grad,
        cen_four,
        scale_four,
        narrow_norms[2, 0],
        mask_out,
        gain_four,
        bias_four,
        count_out,
    ).astype(jnp.bfloat16)
    out_one_grad, second_grad, unused_side = input_back(
        out_one, grad_four, None, second_w, None, pixels
    )
    grad_one = (grad_two + out_one_grad) * mask_out[None, :] * slope(total_one)
    gains_pair, bias_pair = over_images(
        jnp.stack([jnp.sum(grad_one * cen_three, 1), jnp.sum(grad_one * cen_side, 1)]),
        jnp.sum(grad_one, 1),
    )
    grad_three = norm_back(
        grad_one,
        cen_three,
        scale_three,
        wide_norms[0, 0],
        mask_out,
        gains_pair[0],
        bias_pair,
        count_out,
    ).astype(jnp.bfloat16)
    grad_side = norm_back(
        grad_one,
        cen_side,
        scale_side,
        wide_norms[1, 0],
        mask_out,
        gains_pair[1],
        bias_pair,
        count_out,
    ).astype(jnp.bfloat16)
    hid_two_grad, last_zero_grad = output_back(grad_three, last_w[0], hid_two)
    act_two_grad = hid_two_grad * keep_one * mask_out[None, :] * slope(act_two)
    gain_two, bias_two = back_sums(act_two_grad, cen_two)
    grad_mid = norm_back(
        act_two_grad,
        cen_two,
        scale_two,
        narrow_norms[1, 0],
        mask_out,
        gain_two,
        bias_two,
        count_out,
    ).astype(jnp.bfloat16)
    hid_one_grad, middle_zero_grad = conv_backward(
        grad_mid, gat_one, middle_w[0], STRIDED_TAPS, pixels, 4
    )
    act_one_grad = hid_one_grad * keep_one * mask_in[None, :] * slope(act_one)
    gain_one, bias_one = back_sums(act_one_grad, cen_one)
    grad_first = norm_back(
        act_one_grad, cen_one, scale_one, narrow_norms[0, 0], mask_in, gain_one, bias_one, count_in
    ).astype(jnp.bfloat16)
    field_grad, first_grad, short_grad = input_back(
        field, grad_first, grad_side, first_w, short_w, pixels
    )
    input_grad = (field_grad * mask_in[None, :]).astype(jnp.bfloat16).reshape(inputs.shape)
    grads = (
        lax.psum_scatter(first_grad, "dp", scatter_dimension=0, tiled=True),
        lax.psum_scatter(short_grad, "dp", scatter_dimension=0, tiled=True),
        lax.psum_scatter(
            jnp.stack([middle_zero_grad, middle_one_grad]), "dp", scatter_dimension=2, tiled=True
        ),
        lax.psum_scatter(
            jnp.stack([last_zero_grad, last_one_grad]), "dp", scatter_dimension=2, tiled=True
        ),
        lax.psum_scatter(second_grad, "dp", scatter_dimension=0, tiled=True),
    )
    first_fix = 1.0 - BETA_ONE**STEP
    second_fix = 1.0 - BETA_TWO**STEP
    weights = (first_weight, shortcut_weight, middle_weight, last_weight, second_weight)
    means = (first_mean, shortcut_mean, middle_mean, last_mean, second_mean)
    squares_old = (first_square, shortcut_square, middle_square, last_square, second_square)
    states = []
    updates = []
    for index in range(5):
        mean_next, square_next, step = adapt(
            grads[index], means[index], squares_old[index], first_fix, second_fix
        )
        states.append((mean_next, square_next))
        updates.append(step + DECAY * weights[index])
    pairs = [
        (weights[0], updates[0]),
        (weights[1], updates[1]),
        (weights[2][0], updates[2][0]),
        (weights[2][1], updates[2][1]),
        (weights[3][0], updates[3][0]),
        (weights[3][1], updates[3][1]),
        (weights[4], updates[4]),
    ]
    partial_value = jnp.stack(
        [
            jnp.stack([jnp.sum(weight * weight), jnp.sum(update * update)])
            for weight, update in pairs
        ]
    )
    matrix_norms = jnp.sqrt(lax.psum(partial_value, ("dp", "mp")))
    ratio = matrix_norms[:, 0] / (matrix_norms[:, 1] + EPS_TRUST)
    first_next = first_weight - RATE * ratio[0] * updates[0]
    short_next = shortcut_weight - RATE * ratio[1] * updates[1]
    middle_next = middle_weight - RATE * ratio[2:4].reshape(2, 1, 1, 1) * updates[2]
    last_next = last_weight - RATE * ratio[4:6].reshape(2, 1, 1) * updates[3]
    second_next = second_weight - RATE * ratio[6] * updates[4]
    narrow_grad = jnp.stack(
        [
            jnp.stack([gain_one, bias_one]),
            jnp.stack([gain_two, bias_two]),
            jnp.stack([gain_four, bias_four]),
            jnp.stack([gain_five, bias_five]),
        ]
    )
    wide_grad = jnp.stack(
        [
            jnp.stack([gains_pair[0], bias_pair]),
            jnp.stack([gains_pair[1], bias_pair]),
            jnp.stack([gain_six, bias_six]),
        ]
    )
    narrow_mean_next, narrow_square_next, narrow_step = adapt(
        narrow_grad, narrow_mean, narrow_square, first_fix, second_fix
    )
    wide_mean_next, wide_square_next, wide_step = adapt(
        wide_grad, wide_mean, wide_square, first_fix, second_fix
    )
    return (
        block_output,
        input_grad,
        states[0][0],
        states[0][1],
        first_next,
        states[1][0],
        states[1][1],
        short_next,
        states[2][0],
        states[2][1],
        middle_next,
        states[3][0],
        states[3][1],
        last_next,
        states[4][0],
        states[4][1],
        second_next,
        narrow_mean_next,
        narrow_square_next,
        narrow_norms - RATE_NORM * narrow_step,
        wide_mean_next,
        wide_square_next,
        wide_norms - RATE_NORM * wide_step,
        matrix_norms,
        first_next.astype(jnp.bfloat16),
        short_next.astype(jnp.bfloat16),
        middle_next.astype(jnp.bfloat16),
        last_next.astype(jnp.bfloat16),
        second_next.astype(jnp.bfloat16),
    )


def fits(mesh, pixel_mask):
    sizes = (mesh.shape["dp"], mesh.shape["mp"])
    powers = all(size >= 2 and size & (size - 1) == 0 for size in sizes)
    return powers and pixel_mask.shape[1] % (HO * WO * sizes[1]) == 0


def swap(values, *bits):
    sizes = {axis: lax.axis_size(axis) for axis in ("dp", "mp")}
    masks = {axis: sum(mask for at, mask in bits if at == axis) for axis in sizes}
    if not masks["dp"]:
        return lax.ppermute(values, "mp", [(at, at ^ masks["mp"]) for at in range(sizes["mp"])])
    if not masks["mp"]:
        return lax.ppermute(values, "dp", [(at, at ^ masks["dp"]) for at in range(sizes["dp"])])
    mask = masks["dp"] * sizes["mp"] + masks["mp"]
    return lax.ppermute(
        values, ("dp", "mp"), [(at, at ^ mask) for at in range(sizes["dp"] * sizes["mp"])]
    )


def subsets(bits):
    return [
        [bit for place, bit in enumerate(bits) if index >> place & 1]
        for index in range(1 << len(bits))
    ]


def bit_of(axis, mask):
    return (lax.axis_index(axis) & mask) // mask


def high_bits(axis):
    masks = []
    mask = lax.axis_size(axis) // 2
    while mask:
        masks.append(mask)
        mask //= 2
    return masks


def everywhere(values):
    if values.shape[0] <= 16:
        count = lax.axis_size("dp") * lax.axis_size("mp")
        copies = jnp.broadcast_to(values[None], (count,) + values.shape)
        return jnp.sum(lax.all_to_all(copies, ("dp", "mp"), 0, 0, tiled=True), 0)
    for axis in ("mp", "dp"):
        mask = 1
        while mask < lax.axis_size(axis):
            values = values + swap(values, (axis, mask))
            mask *= 2
    return values


def pack(block):
    lead, rows, cols = block.shape
    parts = block.reshape(lead, rows, cols // 128, 128).transpose(0, 2, 1, 3)
    return parts.reshape(-1, 128)


def column_bits():
    return [("mp", mask) for mask in high_bits("mp")[:-1]]


def row_bits():
    return [("dp", mask) for mask in high_bits("dp")]


def lanes_of(rows):
    first = rows // 32 * 16
    return ((0, first), (first, rows))


def merged(parts, bits, dims):
    if not bits:
        return parts[0]
    high = bit_of(*bits[-1]) > 0
    half = len(parts) // 2
    first = [jnp.where(high, parts[half + at], parts[at]) for at in range(half)]
    second = [jnp.where(high, parts[at], parts[half + at]) for at in range(half)]
    pair = [merged(first, bits[:-1], dims), merged(second, bits[:-1], dims)]
    return jnp.concatenate(pair, dims.index(bits[-1]))


class Gather:
    def __init__(self, rows, lanes=True):
        self.dims = column_bits() + row_bits()
        near = row_bits()[-1:]
        if lanes:
            self.steps = [[row_bits()[:-1]], [near, column_bits()], [column_bits(), near]]
            self.spans = lanes_of(rows.shape[0])
        else:
            self.steps = [[row_bits()[:-1]], [near + column_bits()]]
            self.spans = ((0, rows.shape[0]),)
        self.parts = [([rows.reshape((1,) * len(self.dims) + rows.shape)], [])]
        self.step = 0

    def pending(self):
        return [values for values, bits in self.parts]

    def resume(self, values):
        self.parts = [(value, bits) for value, (_, bits) in zip(values, self.parts)]

    def launch(self):
        values = [merged(parts, bits, self.dims) for parts, bits in self.parts]
        if self.step < len(self.steps):
            groups = self.steps[self.step]
            if len(groups) > len(values):
                values = [values[0][..., low:high, :] for low, high in self.spans]
            self.parts = [
                ([value] + [swap(value, *bits) for bits in subsets(group)[1:]], group)
                for value, group in zip(values, groups)
            ]
        else:
            value = jnp.concatenate(values, -2) if len(values) > 1 else values[0]
            self.parts = [([value, swap(value, ("mp", 1))], [])]
        self.step += 1

    def bundles(self):
        shape = (1 << len(column_bits()), lax.axis_size("dp")) + self.parts[0][0][0].shape[-2:]
        return [value.reshape(shape) for value in self.parts[0][0]]


class Scatter:
    def __init__(self, keep, send, lanes=True):
        self.dims = column_bits() + row_bits()
        shape = (2,) * len(self.dims) + keep.shape[2:]
        near = row_bits()[-1:]
        far = row_bits()[:-1]
        if lanes:
            self.steps = [None, [column_bits(), near], [near, column_bits()], [far, far]]
            self.spans = lanes_of(keep.shape[2])
        else:
            self.steps = [None, [column_bits() + near], [far]]
            self.spans = (None,)
        self.lanes = [[] for _ in self.spans]
        self.raw = [keep.reshape(shape), send.reshape(shape)]
        self.step = 0

    def pending(self):
        return self.raw

    def resume(self, values):
        self.raw = list(values)

    def fold(self, lane, group=(), turned=()):
        total = 0.0
        for index, settled, span in self.lanes[lane]:
            value = self.raw[index]
            for bit in settled + list(group):
                place = bit_of(*bit)
                place = 1 - place if bit in turned else place
                value = lax.dynamic_slice_in_dim(value, place, 1, self.dims.index(bit))
            if span is not None:
                value = value[..., span[0] : span[1], :]
            total = total + value.astype(jnp.float32)
        return total

    def settle(self, lane, group, arrived, span):
        old = [(index, settled + group, part) for index, settled, part in self.lanes[lane]]
        self.lanes[lane] = old + [(index, [], span) for index in arrived]

    def launch(self):
        groups = self.steps[self.step]
        whole = self.step == len(self.steps) - 1
        if groups is None:
            self.raw[1] = swap(self.raw[1], ("mp", 1))
            for lane, span in zip(self.lanes, self.spans):
                lane += [(0, [], span), (1, [], span)]
        elif whole:
            arrived = []
            for bits in subsets(groups[0])[1:]:
                out = [
                    self.fold(lane, groups[0], bits).astype(jnp.bfloat16)
                    for lane in range(len(self.lanes))
                ]
                out = jnp.concatenate(out, -2) if len(out) > 1 else out[0]
                arrived.append(len(self.raw))
                self.raw.append(swap(out, *bits))
            for lane, span in enumerate(self.spans):
                self.settle(lane, groups[lane], arrived, span)
        else:
            for lane, group in enumerate(groups):
                arrived = []
                for bits in subsets(group)[1:]:
                    out = self.fold(lane, group, bits).astype(jnp.bfloat16)
                    arrived.append(len(self.raw))
                    self.raw.append(swap(out, *bits))
                self.settle(lane, group, arrived, None)
        self.step += 1

    def rows(self):
        total = [self.fold(lane) for lane in range(len(self.lanes))]
        total = jnp.concatenate(total, -2) if len(total) > 1 else total[0]
        return total.reshape(total.shape[-2:])


def wave(flows, anchor=()):
    anchor, values = lax.optimization_barrier((anchor, [flow.pending() for flow in flows]))
    for flow, value in zip(flows, values):
        flow.resume(value)
        flow.launch()
    return anchor


def chunk_kernel(units, columns, rows_ref, cols_ref, *refs):
    outs = refs[-2:]
    product = lax.dot_general(
        rows_ref[...], cols_ref[...], (((0,), (0,)), ((), ())), preferred_element_type=jnp.float32
    ).astype(jnp.bfloat16)
    groups = outs[0].shape[0]
    chunks = outs[0].shape[1]
    for half, out in enumerate(outs):
        for group in range(groups):
            for part in range(columns):
                place = ((half * groups + group) * columns + part) * 128
                block = product[:, place : place + 128].reshape(chunks, units, 128)
                out[group, :, part * units : (part + 1) * units, :] = block


def chunks_into(bundle, total, start, rows_of, cols_of, lead, units, columns):
    count = lax.axis_size("dp")
    groups = 1 << len(column_bits())
    columns = columns // 128
    pixels = cols_of.shape[0]
    height = units * columns
    if lead > 1:
        steps, wide, chunks = lead, count * units, count
        place = lambda step: (0, 0, start // height + step, 0)
    else:
        steps, wide, chunks = count, units, 1
        place = lambda step: (0, step, start // height, 0)
    shape = jax.ShapeDtypeStruct((groups, count, total, 128), jnp.bfloat16)
    block = pl.BlockSpec((groups, chunks, height, 128), place)
    earlier = () if bundle is None else tuple(bundle)
    return pl.pallas_call(
        functools.partial(chunk_kernel, units, columns),
        grid=(steps,),
        in_specs=[
            pl.BlockSpec((pixels, wide), lambda step: (0, step)),
            pl.BlockSpec(cols_of.shape, lambda step: (0, 0)),
        ]
        + [pl.BlockSpec(memory_space=pltpu.HBM)] * len(earlier),
        out_specs=[block, block],
        out_shape=[shape, shape],
        input_output_aliases={2 + place: place for place in range(len(earlier))},
        compiler_params=pltpu.CompilerParams(vmem_limit_bytes=24 * 2**20),
        cost_estimate=pl.CostEstimate(
            flops=2 * rows_of.size * cols_of.shape[1],
            bytes_accessed=2 * (rows_of.size + cols_of.size)
            + 2 * rows_of.shape[1] * cols_of.shape[1],
            transcendentals=0,
        ),
    )(rows_of, cols_of, *earlier)


def total_of(ref):
    return jnp.sum(ref[...], 0) if len(ref.shape) == 3 else ref[...]


def as_row(block):
    return jnp.concatenate([block[place : place + 1] for place in range(block.shape[0])], 1)


def as_rows(row):
    return jnp.concatenate(
        [row[:, place : place + 128] for place in range(0, row.shape[1], 128)], 0
    )


def hand_out(out, rows):
    missing = out.shape[-2] - sum(row.shape[0] for row in rows)
    if missing:
        rows = rows + [jnp.zeros((missing, 128), jnp.float32)]
    block = jnp.concatenate(rows, 0)
    out[...] = jnp.broadcast_to(block[None], out.shape) if len(out.shape) == 3 else block


def levels(total, first, width, count):
    rows = width // 128
    mean = total[first : first + rows] / count
    scale = lax.rsqrt(total[first + rows : first + 2 * rows] / count - mean * mean + EPS_NORM)
    return (as_row(mean), as_row(scale))


def standard(values, level):
    return (values - level[0]) * level[1]


def back_through(grad, centred, level, gain, mask, total, first, bias_first, count):
    rows = grad.shape[1] // 128
    gain_sum = as_row(total[first : first + rows] / count)
    bias_sum = as_row(total[bias_first : bias_first + rows] / count)
    return (gain * level[1]) * (grad - mask * (bias_sum + centred * gain_sum))


def column_sums(values, mask):
    weighted = values * mask
    return [
        as_rows(jnp.sum(weighted, 0, keepdims=True)),
        as_rows(jnp.sum(weighted * values, 0, keepdims=True)),
    ]


def product_sums(grad, centred):
    return as_rows(jnp.sum(grad * centred, 0, keepdims=True))


def plain_sums(grad):
    return as_rows(jnp.sum(grad, 0, keepdims=True))


def fetch(bundles, held, sems, start):
    rows = held.shape[3]
    copies = [
        pltpu.make_async_copy(ref.at[:, :, pl.ds(start, rows), :], held.at[half], sems.at[half])
        for half, ref in enumerate(bundles)
    ]
    for copy in copies:
        copy.start()
    return copies


def arrive(copies):
    for copy in copies:
        copy.wait()


def weight_part(held, chunk, chunks, start, units, columns):
    return jnp.concatenate(
        [
            held[half, group, chunk : chunk + chunks, start + part * units : start + (part + 1) * units, :]
            .reshape(chunks * units, 128)
            for half in range(2)
            for group in range(held.shape[1])
            for part in range(columns)
        ],
        1,
    )


def spots(core, groups, width):
    return [
        pl.multiple_of((2 * group + (core if half == 0 else 1 - core)) * width, 128)
        for half in range(2)
        for group in range(groups)
    ]


def in_turn(ref, core, groups):
    width = ref.shape[1] // (2 * groups)
    return jnp.concatenate([ref[:, pl.ds(at, width)] for at in spots(core, groups, width)], 1)


def in_order(ref, values, core, groups):
    width = ref.shape[1] // (2 * groups)
    for place, at in enumerate(spots(core, groups, width)):
        ref[:, pl.ds(at, width)] = values[:, place * width : (place + 1) * width]


def product(first, second):
    return lax.dot_general(
        first, second, (((1,), (0,)), ((), ())), preferred_element_type=jnp.float32
    )


def product_turned(first, second):
    return lax.dot_general(
        first, second, (((1,), (1,)), ((), ())), preferred_element_type=jnp.float32
    )


def many_in(values, held, units, columns):
    chunks = max(1, 256 // units)
    total = 0.0
    for chunk in range(0, held.shape[2], chunks):
        part = weight_part(held, chunk, chunks, 0, units, columns)
        total = total + product(
            values[:, chunk * units : (chunk + chunks) * units], part
        )
    return total


def many_out(values, held, units, columns):
    chunks = max(1, 256 // units)
    return [
        product_turned(values, weight_part(held, chunk, chunks, 0, units, columns))
        for chunk in range(0, held.shape[2], chunks)
    ]


def slid(values, offset):
    count = values.shape[0]
    return pltpu.roll(values, (-offset) % count, 0) if offset % count else values


def within(inside, drow, dcol):
    place = 3 * (drow + 1) + dcol + 1
    return inside[:, place : place + 1]


def first_layer(core, raw, mask, first, second, field, out, sums, held, sems):
    copies = fetch((first, second), held, sems, 0)
    core = core[0]
    weights = mask[...]
    width = raw.shape[2]
    for place in range(raw.shape[0]):
        part = raw[place].astype(jnp.float32) * weights
        field[:, place * width : (place + 1) * width] = part.astype(jnp.bfloat16)
    arrive(copies)
    result = many_in(field, held, held.shape[3], 1)
    in_order(out, result, core, held.shape[1])
    rows = column_sums(out[...], weights)
    pixels = weights.shape[0] // 4
    for part in (weights, weights[:pixels]):
        rows.append(jnp.broadcast_to(jnp.sum(part, 0, keepdims=True), (1, 128)))
    hand_out(sums, rows)


def side_layer(start, core, field, mask, first, second, out, sums, held, sems):
    copies = fetch((first, second), held, sems, start)
    core = core[0]
    pixels = mask.shape[0]
    arrive(copies)
    columns = out.shape[1] // (2 * held.shape[1] * 128)
    result = many_in(field[:pixels, :], held, held.shape[3] // columns, columns)
    in_order(out, result, core, held.shape[1])
    hand_out(sums, column_sums(out[...], mask[...]))


def spread_layer(start, norm, taps, core, before, sums_in, counts, tables, keep, mask_in, mask, inside,
                 first, second, cols, out, sums, held, sems):
    copies = fetch((first, second), held, sems, start)
    core = core[0]
    pixels = mask.shape[0]
    width = before.shape[1]
    counted = 0 if before.shape[0] > pixels else 1
    level = levels(total_of(sums_in), 0, width, counts[counted : counted + 1, :])
    act = standard(before[...], level) * tables[2 * norm : 2 * norm + 1, :] + tables[2 * norm + 1 : 2 * norm + 2, :]
    row = norm // 2
    hidden = jax.nn.silu(act) * mask_in[...] * keep[row : row + 1, :]
    for tap, phase, drow, dcol in taps:
        source = hidden[phase * pixels : (phase + 1) * pixels]
        moved = slid(source, drow * WO + dcol) * within(inside, drow, dcol)
        cols[:, tap * width : (tap + 1) * width] = moved.astype(jnp.bfloat16)
    arrive(copies)
    units = held.shape[3] // 9
    total = 0.0
    for tap in range(9):
        part = weight_part(held, 0, held.shape[2], tap * units, units, 1)
        total = total + product(cols[:, tap * width : (tap + 1) * width], part)
    in_order(out, total, core, held.shape[1])
    hand_out(sums, column_sums(out[...], mask[...]))


def widen_layer(start, norm, core, before, sums_in, counts, tables, keep, mask, first, second,
                hidden, out, sums, held, scratch, sems):
    copies = fetch((first, second), held, sems, start)
    core = core[0]
    level = levels(total_of(sums_in), 0, before.shape[1], counts[1:2, :])
    act = standard(before[...], level) * tables[2 * norm : 2 * norm + 1, :] + tables[2 * norm + 1 : 2 * norm + 2, :]
    row = norm // 2
    scratch[...] = jax.nn.silu(act) * mask[...] * keep[row : row + 1, :]
    hidden[...] = in_turn(scratch, core, held.shape[1]).astype(jnp.bfloat16)
    arrive(copies)
    parts = many_out(hidden[...], held, held.shape[3], 1)
    size = out.shape[1] // len(parts)
    for place, part in enumerate(parts):
        out[:, place * size : (place + 1) * size] = part
    hand_out(sums, column_sums(out[...], mask[...]))


def joined_acts(total, third, side, wide, count):
    width = third.shape[1]
    rows = width // 128
    centred_third = standard(third[...], levels(total, 0, width, count))
    centred_side = standard(side[...], levels(total, 2 * rows, width, count))
    act = (
        centred_third * wide[0:1, :]
        + wide[1:2, :]
        + (centred_side * wide[2:3, :] + wide[3:4, :])
    )
    return (centred_third, centred_side, act)


def narrow_layer(start, core, third, side, sums_in, counts, wide, mask, first, second,
                 above, out, sums, held, sems):
    copies = fetch((first, second), held, sems, start)
    core = core[0]
    centred_third, centred_side, act = joined_acts(
        sums_in[...], third, side, wide, counts[1:2, :]
    )
    above[...] = (jax.nn.silu(act) * mask[...]).astype(jnp.bfloat16)
    arrive(copies)
    result = many_in(above, held, held.shape[3], 1)
    in_order(out, result, core, held.shape[1])
    hand_out(sums, column_sums(out[...], mask[...]))


def last_layer(sixth, sums_in, counts, wide, above, cotangent, mask, out, grad, sums):
    level = levels(sums_in[...], 0, sixth.shape[1], counts[1:2, :])
    centred = standard(sixth[...], level)
    act = centred * wide[4:5, :] + wide[5:6, :] + above[...].astype(jnp.float32)
    weights = mask[...]
    result = (jax.nn.silu(act) * weights).astype(jnp.bfloat16)
    inner = weights * slope(act)
    width = out.shape[2]
    for place in range(out.shape[0]):
        span = slice(place * width, (place + 1) * width)
        out[place] = result[:, span]
        grad[:, span] = cotangent[place].astype(jnp.float32) * inner[:, span]
    result = grad[...]
    hand_out(sums, [product_sums(result, centred), plain_sums(result)])


def narrow_grad(grad, before, sums_in, counts, tables, norm, keep, mask):
    counted = 0 if norm == 0 else 1
    level = levels(total_of(sums_in), 0, before.shape[1], counts[counted : counted + 1, :])
    centred = standard(before[...], level)
    act = centred * tables[2 * norm : 2 * norm + 1, :] + tables[2 * norm + 1 : 2 * norm + 2, :]
    row = norm // 2
    result = grad * keep[row : row + 1, :] * mask * slope(act)
    return (result, [product_sums(result, centred), plain_sums(result)])


def narrow_back(norm, grad, before, sums_in, sums_back, counts, tables, mask):
    counted = 0 if norm == 0 else 1
    count = counts[counted : counted + 1, :]
    width = before.shape[1]
    level = levels(total_of(sums_in), 0, width, count)
    return back_through(
        grad[...],
        standard(before[...], level),
        level,
        tables[2 * norm : 2 * norm + 1, :],
        mask,
        total_of(sums_back),
        0,
        width // 128,
        count,
    )


def last_back(start, norm, core, grad, sixth, sums_six, back_six, counts, wide, before, sums_in, tables,
              keep, mask, first, second, grad_out, grad_in, sums, held, scratch, sems):
    copies = fetch((first, second), held, sems, start)
    core = core[0]
    width = sixth.shape[1]
    count = counts[1:2, :]
    level = levels(sums_six[...], 0, width, count)
    grad_out[...] = back_through(
        grad[...], standard(sixth[...], level), level, wide[4:5, :], mask[...], back_six[...], 0,
        width // 128, count,
    ).astype(jnp.bfloat16)
    arrive(copies)
    in_order(scratch, many_in(grad_out, held, held.shape[3], 1), core, held.shape[1])
    result, rows = narrow_grad(scratch[...], before, sums_in, counts, tables, norm, keep, mask[...])
    grad_in[...] = result
    hand_out(sums, rows)


def pair_back(start, norm, core, grad, third, side, sums_pair, back_pair, counts, wide, before, sums_in,
              tables, keep, mask, first, second, grad_third, grad_side, grad_in, sums, held, scratch,
              big, sems):
    copies = fetch((first, second), held, sems, start)
    core = core[0]
    width = third.shape[1]
    rows = width // 128
    count = counts[1:2, :]
    total = sums_pair[...]
    back = back_pair[...]
    groups = held.shape[1]
    level = levels(total, 0, width, count)
    grad_third[...] = back_through(
        grad[...], standard(third[...], level), level, wide[0:1, :], mask[...], back, 0, 2 * rows, count
    ).astype(jnp.bfloat16)
    arrive(copies)
    in_order(scratch, many_in(grad_third, held, held.shape[3], 1), core, groups)
    result, parts = narrow_grad(scratch[...], before, sums_in, counts, tables, norm, keep, mask[...])
    grad_in[...] = result
    hand_out(sums, parts)
    level = levels(total, 2 * rows, width, count)
    big[...] = back_through(
        grad[...], standard(side[...], level), level, wide[2:3, :], mask[...], back, rows, 2 * rows, count
    )
    grad_side[...] = in_turn(big, core, groups).astype(jnp.bfloat16)


def spread_back(start, norm, taps, core, grad, after, sums_after, back_after, counts, tables, before,
                sums_in, keep, mask_in, mask, inside, first, second, grad_out, grad_in, sums, held,
                scratch, sems):
    copies = fetch((first, second), held, sems, start)
    core = core[0]
    pixels = mask.shape[0]
    phases = before.shape[0] // pixels
    scratch[...] = narrow_back(norm + 1, grad, after, sums_after, back_after, counts, tables, mask[...])
    grad_out[...] = in_turn(scratch, core, held.shape[1]).astype(jnp.bfloat16)
    arrive(copies)
    units = held.shape[3] // 9
    totals = [0.0] * phases
    for tap, phase, drow, dcol in taps:
        part = weight_part(held, 0, held.shape[2], tap * units, units, 1)
        moved = product_turned(grad_out[...], part)
        totals[phase] = totals[phase] + slid(moved, -drow * WO - dcol) * within(inside, -drow, -dcol)
    hidden = jnp.concatenate(totals, 0) if phases > 1 else totals[0]
    result, rows = narrow_grad(hidden, before, sums_in, counts, tables, norm, keep, mask_in[...])
    grad_in[...] = result
    hand_out(sums, rows)


def narrow_layer_back(start, core, grad, fourth, sums_four, back_four, counts, tables, mask, grad_two,
                      third, side, sums_pair, wide, first, second, grad_out, grad_in, sums, held,
                      scratch, big, sems):
    copies = fetch((first, second), held, sems, start)
    core = core[0]
    scratch[...] = narrow_back(2, grad, fourth, sums_four, back_four, counts, tables, mask[...])
    grad_out[...] = in_turn(scratch, core, held.shape[1]).astype(jnp.bfloat16)
    arrive(copies)
    parts = many_out(grad_out[...], held, held.shape[3], 1)
    size = big.shape[1] // len(parts)
    for place, part in enumerate(parts):
        big[:, place * size : (place + 1) * size] = part
    centred_third, centred_side, act = joined_acts(
        sums_pair[...], third, side, wide, counts[1:2, :]
    )
    result = (grad_two[...] + big[...]) * mask[...] * slope(act)
    grad_in[...] = result
    hand_out(
        sums,
        [
            product_sums(result, centred_third),
            product_sums(result, centred_side),
            plain_sums(result),
        ],
    )


def side_back(start, grad, first, second, out, held, sems):
    copies = fetch((first, second), held, sems, start)
    arrive(copies)
    columns = grad.shape[1] // (2 * held.shape[1] * 128)
    parts = many_out(grad[...], held, held.shape[3] // columns, columns)
    size = out.shape[1] // len(parts)
    for place, part in enumerate(parts):
        out[:, place * size : (place + 1) * size] = part


def first_back(core, grad, before, sums_in, sums_back, counts, tables, mask, side, first, second,
               grad_out, out, held, scratch, sems):
    copies = fetch((first, second), held, sems, 0)
    core = core[0]
    scratch[...] = narrow_back(0, grad, before, sums_in, sums_back, counts, tables, mask[...])
    grad_out[...] = in_turn(scratch, core, held.shape[1]).astype(jnp.bfloat16)
    arrive(copies)
    parts = many_out(grad_out[...], held, held.shape[3], 1)
    size = side.shape[1] // len(parts)
    pixels = side.shape[0]
    weights = mask[...]
    width = out.shape[2]
    for place, part in enumerate(parts):
        owner = place * size // width
        span = slice(place * size % width, place * size % width + size)
        beside = side[:, place * size : (place + 1) * size]
        out[owner, :pixels, span] = ((part[:pixels] + beside) * weights[:pixels]).astype(jnp.bfloat16)
        out[owner, pixels:, span] = (part[pixels:] * weights[pixels:]).astype(jnp.bfloat16)


class Far:
    def __init__(self, value):
        self.value = value


class Coming:
    def __init__(self, ref, copy):
        self.ref = ref
        self.copy = copy
        self.shape = ref.shape

    def settle(self):
        if self.copy is not None:
            self.copy.wait()
            self.copy = None

    def __getitem__(self, place):
        self.settle()
        return self.ref[place]


def framed(kernel, places, count, *refs):
    refs = list(refs)
    rest, held, sems = refs[: len(refs) - len(places) - 1], refs[-len(places) - 1 : -1], refs[-1]
    coming = []
    for at, place in enumerate(places):
        copy = pltpu.make_async_copy(rest[place], held[at], sems.at[at])
        copy.start()
        rest[place] = Coming(held[at], copy)
        coming.append(rest[place])
    kernel(*rest)
    for value in coming:
        value.settle()


def launch(kernel, shapes, values, bundles=(), rows=0, scratch=(), work=0):
    held = []
    sems = []
    if bundles:
        held = [pltpu.VMEM((2,) + bundles[0].shape[:2] + (rows, 128), jnp.bfloat16)]
        sems = [pltpu.SemaphoreType.DMA((2,))]
    places = [place for place, value in enumerate(values) if isinstance(value, Far)]
    values = [value.value if isinstance(value, Far) else value for value in values]
    moved = sum(value.size * value.dtype.itemsize for value in list(values) + list(shapes))
    specs = []
    for place, value in enumerate(values):
        space = pltpu.SMEM if value.dtype == jnp.int32 else pltpu.VMEM
        specs.append(pl.BlockSpec(memory_space=pltpu.HBM if place in places else space))
    late = []
    if places:
        kernel = functools.partial(framed, kernel, places, len(values))
        late = [pltpu.VMEM(values[place].shape, values[place].dtype) for place in places]
        late.append(pltpu.SemaphoreType.DMA((len(places),)))
    return pl.pallas_call(
        kernel,
        in_specs=specs + [pl.BlockSpec(memory_space=pltpu.HBM)] * len(bundles),
        out_specs=[pl.BlockSpec(memory_space=pltpu.VMEM)] * len(shapes),
        out_shape=list(shapes),
        scratch_shapes=held + [pltpu.VMEM(shape, jnp.float32) for shape in scratch] + sems + late,
        compiler_params=pltpu.CompilerParams(vmem_limit_bytes=40 * 2**20),
        cost_estimate=pl.CostEstimate(
            flops=2 * work, bytes_accessed=moved + rows * 16 * 512, transcendentals=0
        ),
    )(*values, *bundles)


def moved_by(grad, mean, square, weight, mean_out, square_out, update_out, at):
    first_fix = 1.0 - BETA_ONE**STEP
    second_fix = 1.0 - BETA_TWO**STEP
    old = weight[at]
    mean_next, square_next, step = adapt(grad, mean[at], square[at], first_fix, second_fix)
    update = step + DECAY * old
    mean_out[at] = mean_next
    square_out[at] = square_next
    update_out[at] = update
    result = []
    for value in (old, update):
        power = value * value
        while len(power.shape) > 2:
            power = jnp.sum(power, 0)
        row = jnp.sum(power, 0, keepdims=True)
        result.append(
            sum(row[:, place : place + 128] for place in range(0, row.shape[1], 128))
        )
    return result


def early_moves(columns, rows_a, rows_c, short_m, short_v, short_w, last_m, last_v, last_w, second_m, second_v,
                second_w, short_mo, short_vo, short_uo, last_mo, last_vo, last_uo, second_mo, second_vo,
                second_uo, powers):
    unit_in = short_w.shape[0]
    unit_out = second_w.shape[0]
    parts = short_w.shape[1] // 128
    every = (slice(None), slice(None))
    grad = jnp.concatenate(
        [rows_c[part * unit_in : (part + 1) * unit_in, :] for part in range(parts)], 1
    )
    found = moved_by(grad, short_m, short_v, short_w, short_mo, short_vo, short_uo, every)
    start = parts * unit_in
    for block, rows in enumerate((rows_c[start : start + unit_out, :], rows_a[...])):
        found += moved_by(
            jnp.transpose(rows), last_m, last_v, last_w, last_mo, last_vo, last_uo, block
        )
    start += unit_out
    found += moved_by(
        rows_c[start : start + unit_out, :], second_m, second_v, second_w, second_mo, second_vo,
        second_uo, every,
    )
    powers[...] = jnp.concatenate(found, 0)


def late_moves(rows_b, rows_d, rows_e, powers_in, first_m, first_v, first_w, mid_m, mid_v, mid_w, first_mo,
               first_vo, first_uo, mid_mo, mid_vo, mid_uo, powers):
    every = (slice(None), slice(None))
    found = moved_by(
        rows_e[...], first_m, first_v, first_w, first_mo, first_vo, first_uo, every
    )
    shape = mid_w.shape[1:]
    middle = []
    for block, rows in enumerate((rows_d, rows_b)):
        middle += moved_by(
            rows[...].reshape(shape), mid_m, mid_v, mid_w, mid_mo, mid_vo, mid_uo, block
        )
    early = powers_in[...]
    order = [found[0], found[1], early[0:2]] + middle + [early[2:8]]
    hand_out(powers, order)


def final_moves(powers, first_w, first_u, short_w, short_u, mid_w, mid_u, last_w, last_u, second_w, second_u,
                norms, first_o, short_o, mid_o, last_o, second_o, first_c, short_c, mid_c, last_c, second_c):
    total = jnp.sqrt(jnp.sum(jnp.sum(powers[...], 0), 1, keepdims=True))
    norms[...] = jnp.broadcast_to(total, norms.shape)

    def step(row, weight, update, out, copy, at):
        ratio = total[2 * row : 2 * row + 1] / (total[2 * row + 1 : 2 * row + 2] + EPS_TRUST)
        fresh = weight[at] - (RATE * ratio) * update[at]
        out[at] = fresh
        copy[at] = fresh.astype(jnp.bfloat16)

    every = (slice(None), slice(None))
    step(0, first_w, first_u, first_o, first_c, every)
    step(1, short_w, short_u, short_o, short_c, every)
    for block in range(2):
        for tap in range(mid_w.shape[1]):
            step(2 + block, mid_w, mid_u, mid_o, mid_c, (block, tap))
        step(4 + block, last_w, last_u, last_o, last_c, block)
    step(6, second_w, second_u, second_o, second_c, every)


def exchange(copies):
    return lax.all_to_all(copies, ("dp", "mp"), 0, 0, tiled=True)


def by_image(
    inputs,
    pixel_mask,
    widths,
    output_grad,
    first_weight,
    shortcut_weight,
    middle_weight,
    last_weight,
    second_weight,
    narrow_norms,
    wide_norms,
    first_mean,
    first_square,
    shortcut_mean,
    shortcut_square,
    middle_mean,
    middle_square,
    last_mean,
    last_square,
    second_mean,
    second_square,
    narrow_mean,
    narrow_square,
    wide_mean,
    wide_square,
):
    ranks = lax.axis_size("mp")
    rank = lax.axis_index("mp")
    pixels = pixel_mask.shape[1] // ranks
    narrow = first_weight.shape[1] * ranks
    wide = shortcut_weight.shape[1] * ranks
    low = jnp.bfloat16
    channels = inputs.shape[0]
    field = inputs.reshape(channels, 4, ranks, pixels).transpose(2, 1, 3, 0)
    field = field.reshape(ranks, 4 * pixels, channels)
    flow_a = Gather(pack(first_weight.astype(low)[None]), False)
    flow_b = Gather(pack(middle_weight[0].astype(low)))
    flow_c = Gather(
        jnp.concatenate(
            [
                pack(shortcut_weight.astype(low)[None]),
                pack(last_weight[0].astype(low).T[None]),
                pack(second_weight.astype(low)[None]),
            ]
        )
    )
    flow_d = Gather(
        jnp.concatenate(
            [pack(last_weight[1].astype(low).T[None]), pack(middle_weight[1].astype(low))]
        )
    )
    field = wave([flow_a, flow_b], field)
    field = lax.all_to_all(field, "mp", 0, 0, tiled=True)
    wave([flow_a, flow_b])
    field = wave([flow_a, flow_b, flow_c], field)
    unit_in, column = first_weight.shape
    column_wide = shortcut_weight.shape[1]
    unit_mid = middle_weight.shape[2]
    unit_out = second_weight.shape[0]
    size_short = unit_in * column_wide // 128
    size_out = unit_out * column // 128
    size_mid = 9 * unit_mid * column // 128
    tables = jnp.concatenate([narrow_norms.reshape(-1, 128), wide_norms.reshape(-1, 128)], 0)
    tables = jnp.broadcast_to(tables[None], (ranks,) + tables.shape)
    tables = lax.all_to_all(tables, "mp", 0, 0, tiled=True)
    split = narrow_norms.size // 128
    narrow_all = (
        tables[:, :split].reshape(ranks, 4, 2, -1).transpose(1, 2, 0, 3).reshape(4, 2, narrow)
    )
    wide_all = tables[:, split:].reshape(ranks, 3, 2, -1).transpose(1, 2, 0, 3).reshape(3, 2, wide)

    narrow_all = narrow_all.reshape(8, narrow)
    wide_all = jnp.concatenate([wide_all.reshape(6, wide), jnp.zeros((2, wide), jnp.float32)], 0)

    own_mask = lax.dynamic_slice_in_dim(pixel_mask, rank * pixels, pixels, 1).astype(jnp.float32)
    mask_in = own_mask.reshape(-1, 1)
    mask = own_mask[0][:, None]
    channel = lax.iota(jnp.int32, narrow)[None]
    keep = (channel < widths[:, None]).astype(jnp.float32)
    keep = jnp.concatenate([keep, jnp.zeros((6, narrow), jnp.float32)], 0)
    place = lax.iota(jnp.int32, pixels)[:, None]
    step = lax.iota(jnp.int32, 9)[None]
    row_at = place // WO % HO + step // 3 - 1
    col_at = place % WO + step % 3 - 1
    inside = (row_at >= 0) & (row_at < HO) & (col_at >= 0) & (col_at < WO)
    inside = inside.astype(jnp.float32)
    core = bit_of("mp", 1)[None]

    above = output_grad.reshape(-1, ranks, pixels).transpose(1, 2, 0)
    above = lax.all_to_all(above, "mp", 0, 0, tiled=True)

    devices = ranks * lax.axis_size("dp")
    full = 4 * pixels

    def real(*shape):
        return jax.ShapeDtypeStruct(shape, jnp.float32)

    def short(*shape):
        return jax.ShapeDtypeStruct(shape, low)

    size = narrow // 128
    wide_rows = wide // 128
    copies = real(devices, 2 * size, 128)
    bundle_a = flow_a.bundles()
    field, pre_one, sums = launch(
        first_layer,
        [short(full, ranks * channels), real(full, narrow), real(devices, 2 * size + 8, 128)],
        [core, field, Far(mask_in)],
        bundle_a,
        unit_in,
        work=field.size * narrow,
    )
    sums = wave([flow_b, flow_c], sums)
    sums_one = exchange(sums)
    sums_one = wave([flow_c, flow_d], sums_one)
    counts = jnp.sum(sums_one[:, 2 * size :], 0)
    bundle_b = flow_b.bundles()
    cols_one, pre_two, sums = launch(
        functools.partial(spread_layer, 0, 0, STRIDED_TAPS),
        [short(pixels, 9 * narrow), real(pixels, narrow), copies],
        [core, pre_one, sums_one, Far(counts), Far(narrow_all), Far(keep), Far(mask_in), Far(mask), Far(inside)],
        bundle_b,
        size_mid,
        work=9 * pixels * narrow * narrow,
    )
    sums_two = exchange(sums)
    sums_two = wave([flow_c, flow_d], sums_two)
    bundle_c = flow_c.bundles()
    pre_side, side_sums = launch(
        functools.partial(side_layer, 0),
        [real(pixels, wide), real(2 * wide_rows, 128)],
        [core, Far(field), Far(mask)],
        bundle_c,
        size_short,
        work=pixels * field.shape[1] * wide,
    )
    hid_two, pre_three, sums = launch(
        functools.partial(widen_layer, size_short, 1),
        [short(pixels, narrow), real(pixels, wide), real(2 * wide_rows, 128)],
        [core, pre_two, sums_two, Far(counts), Far(narrow_all), Far(keep), Far(mask)],
        bundle_c,
        size_out,
        [(pixels, narrow)],
        work=pixels * narrow * wide,
    )
    sums = wave([flow_d], jnp.concatenate([sums, side_sums], 0))
    sums_pair = everywhere(sums)
    out_one, pre_four, sums = launch(
        functools.partial(narrow_layer, size_short + size_out),
        [short(pixels, wide), real(pixels, narrow), copies],
        [core, pre_three, Far(pre_side), sums_pair, Far(counts), Far(wide_all), Far(mask)],
        bundle_c,
        size_out,
        work=pixels * narrow * wide,
    )
    sums_four = exchange(sums)
    sums_four = wave([flow_d], sums_four)
    bundle_d = flow_d.bundles()
    cols_four, pre_five, sums = launch(
        functools.partial(spread_layer, size_out, 2, PLAIN_TAPS),
        [short(pixels, 9 * narrow), real(pixels, narrow), copies],
        [core, pre_four, sums_four, Far(counts), Far(narrow_all), Far(keep), Far(mask), Far(mask), Far(inside)],
        bundle_d,
        size_mid,
        work=9 * pixels * narrow * narrow,
    )
    sums_five = exchange(sums)
    hid_five, pre_six, sums = launch(
        functools.partial(widen_layer, 0, 3),
        [short(pixels, narrow), real(pixels, wide), real(2 * wide_rows, 128)],
        [core, pre_five, sums_five, Far(counts), Far(narrow_all), Far(keep), Far(mask)],
        bundle_d,
        size_out,
        [(pixels, narrow)],
        work=pixels * narrow * wide,
    )
    sums_six = everywhere(sums)
    block_output, grad_two, sums = launch(
        last_layer,
        [short(*above.shape), real(pixels, wide), real(2 * wide_rows, 128)],
        [pre_six, sums_six, Far(counts), Far(wide_all), Far(out_one), Far(above), Far(mask)],
    )
    back_six = everywhere(sums)
    block_output = lax.all_to_all(block_output, "mp", 0, 0, tiled=True)
    block_output = block_output.transpose(2, 0, 1).reshape(-1, ranks * pixels)

    grad_six, act_five_grad, sums = launch(
        functools.partial(last_back, 0, 3),
        [short(pixels, wide), real(pixels, narrow), copies],
        [core, grad_two, Far(pre_six), Far(sums_six), back_six, Far(counts), Far(wide_all), Far(pre_five),
         Far(sums_five), Far(narrow_all), Far(keep), Far(mask)],
        bundle_d,
        size_out,
        [(pixels, narrow)],
        work=pixels * narrow * wide,
    )
    bundle = chunks_into(None, size_out, 0, grad_six, hid_five, 1, unit_out, column)
    back_a = Scatter(*bundle)
    back_five = exchange(sums)
    back_five = wave([back_a], back_five)
    grad_five, act_four_grad, sums = launch(
        functools.partial(spread_back, size_out, 2, PLAIN_TAPS),
        [short(pixels, narrow), real(pixels, narrow), copies],
        [core, act_five_grad, Far(pre_five), Far(sums_five), back_five, Far(counts), Far(narrow_all),
         Far(pre_four), Far(sums_four), Far(keep), Far(mask), Far(mask), Far(inside)],
        bundle_d,
        size_mid,
        [(pixels, narrow)],
        work=9 * pixels * narrow * narrow,
    )
    sums = wave([back_a], sums)
    back_four = exchange(sums)
    bundle = chunks_into(None, size_mid, 0, cols_four, grad_five, 9, unit_mid, column)
    back_b = Scatter(*bundle)
    back_four = wave([back_b], back_four)
    grad_four, grad_one, sums = launch(
        functools.partial(narrow_layer_back, size_short + size_out),
        [short(pixels, narrow), real(pixels, wide), real(3 * wide_rows, 128)],
        [core, act_four_grad, Far(pre_four), Far(sums_four), back_four, Far(counts), Far(narrow_all), Far(mask),
         Far(grad_two), Far(pre_three), Far(pre_side), Far(sums_pair), Far(wide_all)],
        bundle_c,
        size_out,
        [(pixels, narrow), (pixels, wide)],
        work=pixels * narrow * wide,
    )
    sums = wave([back_a, back_b], sums)
    back_pair = everywhere(sums)
    total = size_short + 2 * size_out
    bundle = chunks_into(
        None, total, size_short + size_out, out_one, grad_four, 1, unit_out, column
    )
    back_pair, bundle = lax.optimization_barrier((back_pair, bundle))
    grad_three, grad_side, act_two_grad, sums = launch(
        functools.partial(pair_back, size_short, 1),
        [short(pixels, wide), short(pixels, wide), real(pixels, narrow), copies],
        [core, grad_one, Far(pre_three), Far(pre_side), Far(sums_pair), back_pair, Far(counts), Far(wide_all),
         Far(pre_two), Far(sums_two), Far(narrow_all), Far(keep), Far(mask)],
        bundle_c,
        size_out,
        [(pixels, narrow), (pixels, wide)],
        work=pixels * narrow * wide,
    )
    sums = wave([back_a, back_b], sums)
    back_two = exchange(sums)
    bundle = chunks_into(bundle, total, size_short, grad_three, hid_two, 1, unit_out, column)
    bundle = chunks_into(bundle, total, 0, field, grad_side, 1, unit_in, column_wide)
    back_c = Scatter(*bundle)
    back_two = wave([back_c], back_two)
    grad_mid, act_one_grad, sums = launch(
        functools.partial(spread_back, 0, 0, STRIDED_TAPS),
        [short(pixels, narrow), real(full, narrow), copies],
        [core, act_two_grad, Far(pre_two), Far(sums_two), back_two, Far(counts), Far(narrow_all), Far(pre_one),
         Far(sums_one), Far(keep), Far(mask_in), Far(mask), Far(inside)],
        bundle_b,
        size_mid,
        [(pixels, narrow)],
        work=9 * pixels * narrow * narrow,
    )
    sums = wave([back_b, back_c], sums)
    back_one = exchange(sums)
    bundle = chunks_into(None, size_mid, 0, cols_one, grad_mid, 9, unit_mid, column)
    back_d = Scatter(*bundle)
    (side_grad,) = launch(
        functools.partial(side_back, 0),
        [real(pixels, field.shape[1])],
        [grad_side],
        bundle_c,
        size_short,
        work=pixels * field.shape[1] * wide,
    )
    back_one, side_grad = wave([back_d], (back_one, side_grad))
    grad_first, field_grad = launch(
        first_back,
        [short(full, narrow), short(ranks, full, channels)],
        [core, act_one_grad, Far(pre_one), Far(sums_one), back_one, Far(counts), Far(narrow_all), Far(mask_in),
         Far(side_grad)],
        bundle_a,
        unit_in,
        [(full, narrow)],
        work=field.size * narrow,
    )
    bundle = chunks_into(None, unit_in * column // 128, 0, field, grad_first, 1, unit_in, column)
    back_e = Scatter(*bundle, False)
    field_grad = wave([back_c, back_d, back_e], field_grad)
    input_grad = lax.all_to_all(field_grad, "mp", 0, 0, tiled=True)
    input_grad = input_grad.reshape(ranks, 4, pixels, channels).transpose(3, 1, 0, 2)
    input_grad = input_grad.reshape(inputs.shape)
    wave([back_c, back_d, back_e])
    wave([back_d, back_e])
    rows_a, rows_b, rows_c, rows_d, rows_e = [
        flow.rows() for flow in (back_a, back_b, back_c, back_d, back_e)
    ]
    first_fix = 1.0 - BETA_ONE**STEP
    second_fix = 1.0 - BETA_TWO**STEP

    def like(*values):
        return [real(*value.shape) for value in values for _ in range(3)]

    early = launch(
        functools.partial(early_moves, column),
        like(shortcut_weight, last_weight, second_weight) + [real(8, 128)],
        [rows_a, rows_c]
        + [
            Far(value)
            for value in (
                shortcut_mean, shortcut_square, shortcut_weight, last_mean, last_square, last_weight,
                second_mean, second_square, second_weight,
            )
        ],
    )
    late = launch(
        late_moves,
        like(first_weight, middle_weight) + [real(devices, 16, 128)],
        [rows_b, rows_d, rows_e, early[-1]]
        + [
            Far(value)
            for value in (
                first_mean, first_square, first_weight, middle_mean, middle_square, middle_weight,
            )
        ],
    )
    powers = exchange(late[-1])
    weights = (first_weight, shortcut_weight, middle_weight, last_weight, second_weight)
    updates = (late[2], early[2], late[5], early[5], early[8])
    norms, *fresh = launch(
        final_moves,
        [real(16, 128)]
        + [real(*value.shape) for value in weights]
        + [short(*value.shape) for value in weights],
        [powers]
        + [Far(value) for pair in zip(weights, updates) for value in pair],
    )
    matrix_norms = norms[:14, 0].reshape(7, 2)
    first_next, short_next, middle_next, last_next, second_next = fresh[:5]
    states = [late[0:2], early[0:2], late[3:5], early[3:5], early[6:8]]

    def own_channels(values):
        width = values.shape[-1] // ranks
        return lax.dynamic_slice_in_dim(values, rank * width, width, values.ndim - 1)

    narrow_grads = jnp.stack([jnp.sum(rows, 0) for rows in (back_one, back_two, back_four, back_five)])
    narrow_grad = own_channels(narrow_grads.reshape(4, 2, narrow))
    gain_three, gain_side, bias_pair = back_pair.reshape(3, wide)
    wide_grad = own_channels(
        jnp.stack(
            [
                jnp.stack([gain_three, bias_pair]),
                jnp.stack([gain_side, bias_pair]),
                back_six.reshape(2, wide),
            ]
        )
    )
    narrow_mean_next, narrow_square_next, narrow_step = adapt(
        narrow_grad, narrow_mean, narrow_square, first_fix, second_fix
    )
    wide_mean_next, wide_square_next, wide_step = adapt(
        wide_grad, wide_mean, wide_square, first_fix, second_fix
    )
    return (
        block_output,
        input_grad,
        states[0][0],
        states[0][1],
        first_next,
        states[1][0],
        states[1][1],
        short_next,
        states[2][0],
        states[2][1],
        middle_next,
        states[3][0],
        states[3][1],
        last_next,
        states[4][0],
        states[4][1],
        second_next,
        narrow_mean_next,
        narrow_square_next,
        narrow_norms - RATE_NORM * narrow_step,
        wide_mean_next,
        wide_square_next,
        wide_norms - RATE_NORM * wide_step,
        matrix_norms,
        *fresh[5:],
    )


def solution(mesh):
    in_specs = (
        P("mp", None, "dp"),
        P(None, "dp"),
        P(),
        P("mp", "dp"),
        P("dp", "mp"),
        P("dp", "mp"),
        P(None, None, "dp", "mp"),
        P(None, "mp", "dp"),
        P("dp", "mp"),
        P(None, None, "mp"),
        P(None, None, "mp"),
        P("dp", "mp"),
        P("dp", "mp"),
        P("dp", "mp"),
        P("dp", "mp"),
        P(None, None, "dp", "mp"),
        P(None, None, "dp", "mp"),
        P(None, "mp", "dp"),
        P(None, "mp", "dp"),
        P("dp", "mp"),
        P("dp", "mp"),
        P(None, None, "mp"),
        P(None, None, "mp"),
        P(None, None, "mp"),
        P(None, None, "mp"),
    )
    out_specs = (
        P("mp", "dp"),
        P("mp", None, "dp"),
        P("dp", "mp"),
        P("dp", "mp"),
        P("dp", "mp"),
        P("dp", "mp"),
        P("dp", "mp"),
        P("dp", "mp"),
        P(None, None, "dp", "mp"),
        P(None, None, "dp", "mp"),
        P(None, None, "dp", "mp"),
        P(None, "mp", "dp"),
        P(None, "mp", "dp"),
        P(None, "mp", "dp"),
        P("dp", "mp"),
        P("dp", "mp"),
        P("dp", "mp"),
        P(None, None, "mp"),
        P(None, None, "mp"),
        P(None, None, "mp"),
        P(None, None, "mp"),
        P(None, None, "mp"),
        P(None, None, "mp"),
        P(),
        P("dp", "mp"),
        P("dp", "mp"),
        P(None, None, "dp", "mp"),
        P(None, "mp", "dp"),
        P("dp", "mp"),
    )
    return jax.shard_map(
        lambda *values: (by_image if fits(mesh, values[1]) else shards)(*values),
        mesh=mesh,
        in_specs=in_specs,
        out_specs=out_specs,
        check_vma=False,
    )
```

```python
import functools

import jax
import jax.numpy as jnp
from jax import lax
from jax.experimental import pallas as pl
from jax.experimental.pallas import tpu as pltpu
from jax.sharding import PartitionSpec as P

HO = 16
WO = 11
STEP = 10


EPS_NORM = 1e-05
BETA_ONE = 0.9
BETA_TWO = 0.999
EPS_ADAM = 1e-06
DECAY = 0.01
RATE = 0.3
RATE_NORM = 0.3
EPS_TRUST = 1e-06
PHASES = ((1, -1), (0, 0), (1, 0))
STRIDED_TAPS = tuple(
    (
        (
            3 * above + beside,
            2 * PHASES[above][0] + PHASES[beside][0],
            PHASES[above][1],
            PHASES[beside][1],
        )
        for above in range(3)
        for beside in range(3)
    )
)
PLAIN_TAPS = tuple(
    ((3 * above + beside, 0, above - 1, beside - 1) for above in range(3) for beside in range(3))
)


def slope(values):
    gate = jax.nn.sigmoid(values)
    return gate * (1.0 + values * (1.0 - gate))


def shifted(values, drow, dcol):
    length = values.shape[1]
    offset = drow * WO + dcol
    place = lax.iota(jnp.int32, length)
    row_at = place // WO % HO + drow
    col_at = place % WO + dcol
    inside = (row_at >= 0) & (row_at < HO) & (col_at >= 0) & (col_at < WO)
    moved = jnp.roll(values, -offset, axis=1)
    return jnp.where(inside[None, :], moved, jnp.zeros_like(moved))


def over_images(first, second):
    return lax.psum((first, second), "dp")


def moments(values, mask):
    weighted = values * mask[None, :]
    return over_images(jnp.sum(weighted, 1), jnp.sum(weighted * values, 1))


def normalize(values, totals, squares, count, gain, bias):
    mean = totals / count
    scale = lax.rsqrt(squares / count - mean * mean + EPS_NORM)
    centred = (values - mean[:, None]) * scale[:, None]
    return (centred, scale, centred * gain[:, None] + bias[:, None])


def back_sums(grad_in, centred):
    return over_images(jnp.sum(grad_in * centred, 1), jnp.sum(grad_in, 1))


def norm_back(grad_in, centred, scale, gain, mask, gain_sum, bias_sum, count):
    return (gain * scale)[:, None] * (
        grad_in - mask[None, :] * (bias_sum[:, None] + centred * gain_sum[:, None]) / count
    )


def input_mix(values, weight, side_weight, pixels):
    start_sum = (jnp.zeros((weight.shape[1], values.shape[1]), jnp.float32),)
    if side_weight is not None:
        start_sum = start_sum + (jnp.zeros((side_weight.shape[1], pixels), jnp.float32),)
    piece = lax.all_gather(values, "mp", axis=0, tiled=True)
    result = (jnp.einsum("kc,kp->cp", weight, piece, preferred_element_type=jnp.float32),)
    if side_weight is not None:
        result = result + (
            jnp.einsum(
                "kc,kp->cp", side_weight, piece[:, :pixels], preferred_element_type=jnp.float32
            ),
        )
    return result


def mid_gathered(hidden):
    return lax.all_gather(hidden, "mp", axis=0, tiled=True)


def conv_forward(gathered, kernel, taps, pixels):
    result = jnp.zeros((kernel.shape[2], pixels), jnp.float32)
    for tap, phase, drow, dcol in taps:
        source = gathered[:, phase * pixels : (phase + 1) * pixels]
        part = jnp.einsum("kc,kp->cp", kernel[tap], source, preferred_element_type=jnp.float32)
        result = result + shifted(part, drow, dcol)
    return result


def conv_backward(grad_b, gathered, kernel, taps, pixels, phases):
    moved = [shifted(grad_b, -drow, -dcol) for tap, phase, drow, dcol in taps]
    count = gathered.shape[0] // lax.axis_size("mp") * lax.axis_size("mp")
    blocks = []
    for target in range(phases):
        result = jnp.zeros((count, pixels), jnp.float32)
        for conv_index, (conv_tap, conv_phase, conv_drow, conv_dcol) in enumerate(taps):
            if conv_phase == target:
                part = kernel[conv_tap]
                result = result + jnp.dot(
                    part, moved[conv_index], preferred_element_type=jnp.float32
                )
        blocks.append(result)
    hidden_grad = lax.psum_scatter(
        jnp.concatenate(blocks, 1), "mp", scatter_dimension=0, tiled=True
    )
    kernel_grad = jnp.stack(
        [
            jnp.einsum(
                "kp,cp->kc",
                gathered[:, phase * pixels : (phase + 1) * pixels],
                moved[index],
                preferred_element_type=jnp.float32,
            )
            for index, (tap, phase, drow, dcol) in enumerate(taps)
        ]
    )
    return (hidden_grad, kernel_grad)


def output_mix(hidden, kernel):
    return lax.psum_scatter(
        jnp.einsum("kc,kp->cp", kernel, hidden, preferred_element_type=jnp.float32),
        "mp",
        scatter_dimension=0,
        tiled=True,
    )


def output_back(grad_b, kernel, hidden):
    piece = lax.all_gather(grad_b, "mp", axis=0, tiled=True)
    hidden_grad = jnp.dot(kernel, piece, preferred_element_type=jnp.float32)
    columns = jnp.einsum("cp,kp->ck", hidden, piece, preferred_element_type=jnp.float32)
    return (hidden_grad, columns)


def input_back(values, grad_b, side_b, weight, side_weight, pixels):
    width = weight.shape[1]
    result = jnp.dot(weight, grad_b, preferred_element_type=jnp.float32)
    if side_weight is not None:
        result = jnp.concatenate(
            [
                result[:, :pixels]
                + jnp.dot(side_weight, side_b, preferred_element_type=jnp.float32),
                result[:, pixels:],
            ],
            1,
        )
    values_grad = lax.psum_scatter(result, "mp", scatter_dimension=0, tiled=True)
    piece = lax.all_gather(values, "mp", axis=0, tiled=True)
    blocks = [jnp.einsum("kp,cp->kc", piece, grad_b, preferred_element_type=jnp.float32)]
    if side_weight is not None:
        blocks.append(
            jnp.einsum("kp,cp->kc", piece[:, :pixels], side_b, preferred_element_type=jnp.float32)
        )
    joined = jnp.concatenate(blocks, 1)
    return (values_grad, joined[:, :width], joined[:, width:])


def adapt(grad_in, mean, square, first_fix, second_fix):
    mean_next = BETA_ONE * mean + (1.0 - BETA_ONE) * grad_in
    square_next = BETA_TWO * square + (1.0 - BETA_TWO) * grad_in * grad_in
    step = mean_next / first_fix / (jnp.sqrt(square_next / second_fix) + EPS_ADAM)
    return (mean_next, square_next, step)


def shards(
    inputs,
    pixel_mask,
    widths,
    output_grad,
    first_weight,
    shortcut_weight,
    middle_weight,
    last_weight,
    second_weight,
    narrow_norms,
    wide_norms,
    first_mean,
    first_square,
    shortcut_mean,
    shortcut_square,
    middle_mean,
    middle_square,
    last_mean,
    last_square,
    second_mean,
    second_square,
    narrow_mean,
    narrow_square,
    wide_mean,
    wide_square,
):
    pixels = pixel_mask.shape[1]
    width = first_weight.shape[1]
    rank = lax.axis_index("mp")
    channel = rank * width + lax.iota(jnp.int32, width)
    keep_one = (channel < widths[0]).astype(jnp.float32)[:, None]
    keep_two = (channel < widths[1]).astype(jnp.float32)[:, None]
    masks = pixel_mask.astype(jnp.float32)
    mask_in = masks.reshape(-1)
    mask_out = masks[0]
    field = (inputs * pixel_mask.astype(jnp.bfloat16)[None]).reshape(inputs.shape[0], -1)
    first_w, short_w, middle_w, last_w, second_w = (
        lax.all_gather(first_weight.astype(jnp.bfloat16), "dp", axis=0, tiled=True),
        lax.all_gather(shortcut_weight.astype(jnp.bfloat16), "dp", axis=0, tiled=True),
        lax.all_gather(middle_weight.astype(jnp.bfloat16), "dp", axis=2, tiled=True),
        lax.all_gather(last_weight.astype(jnp.bfloat16), "dp", axis=2, tiled=True),
        lax.all_gather(second_weight.astype(jnp.bfloat16), "dp", axis=0, tiled=True),
    )
    count_in, count_out = over_images(jnp.sum(mask_in), jnp.sum(mask_out))
    pre_one, pre_side = input_mix(field, first_w, short_w, pixels)
    totals, squares = moments(pre_one, mask_in)
    cen_one, scale_one, act_one = normalize(
        pre_one, totals, squares, count_in, narrow_norms[0, 0], narrow_norms[0, 1]
    )
    hid_one = (jax.nn.silu(act_one) * mask_in[None, :] * keep_one).astype(jnp.bfloat16)
    gat_one = mid_gathered(hid_one)
    pre_two = conv_forward(gat_one, middle_w[0], STRIDED_TAPS, pixels)
    totals, squares = moments(pre_two, mask_out)
    cen_two, scale_two, act_two = normalize(
        pre_two, totals, squares, count_out, narrow_norms[1, 0], narrow_norms[1, 1]
    )
    hid_two = (jax.nn.silu(act_two) * mask_out[None, :] * keep_one).astype(jnp.bfloat16)
    pre_three = output_mix(hid_two, last_w[0])
    weighted_three = pre_three * mask_out[None, :]
    weighted_side = pre_side * mask_out[None, :]
    totals, squares = over_images(
        jnp.stack([jnp.sum(weighted_three, 1), jnp.sum(weighted_side, 1)]),
        jnp.stack([jnp.sum(weighted_three * pre_three, 1), jnp.sum(weighted_side * pre_side, 1)]),
    )
    cen_three, scale_three, act_three = normalize(
        pre_three, totals[0], squares[0], count_out, wide_norms[0, 0], wide_norms[0, 1]
    )
    cen_side, scale_side, act_side = normalize(
        pre_side, totals[1], squares[1], count_out, wide_norms[1, 0], wide_norms[1, 1]
    )
    total_one = act_three + act_side
    out_one = (jax.nn.silu(total_one) * mask_out[None, :]).astype(jnp.bfloat16)
    (pre_four,) = input_mix(out_one, second_w, None, pixels)
    totals, squares = moments(pre_four, mask_out)
    cen_four, scale_four, act_four = normalize(
        pre_four, totals, squares, count_out, narrow_norms[2, 0], narrow_norms[2, 1]
    )
    hid_four = (jax.nn.silu(act_four) * mask_out[None, :] * keep_two).astype(jnp.bfloat16)
    gat_four = mid_gathered(hid_four)
    pre_five = conv_forward(gat_four, middle_w[1], PLAIN_TAPS, pixels)
    totals, squares = moments(pre_five, mask_out)
    cen_five, scale_five, act_five = normalize(
        pre_five, totals, squares, count_out, narrow_norms[3, 0], narrow_norms[3, 1]
    )
    hid_five = (jax.nn.silu(act_five) * mask_out[None, :] * keep_two).astype(jnp.bfloat16)
    pre_six = output_mix(hid_five, last_w[1])
    totals, squares = moments(pre_six, mask_out)
    cen_six, scale_six, act_six = normalize(
        pre_six, totals, squares, count_out, wide_norms[2, 0], wide_norms[2, 1]
    )
    total_two = act_six + out_one.astype(jnp.float32)
    block_output = (jax.nn.silu(total_two) * mask_out[None, :]).astype(jnp.bfloat16)
    grad_two = output_grad.astype(jnp.float32) * mask_out[None, :] * slope(total_two)
    gain_six, bias_six = back_sums(grad_two, cen_six)
    grad_six = norm_back(
        grad_two, cen_six, scale_six, wide_norms[2, 0], mask_out, gain_six, bias_six, count_out
    ).astype(jnp.bfloat16)
    hid_five_grad, last_one_grad = output_back(grad_six, last_w[1], hid_five)
    act_five_grad = hid_five_grad * keep_two * mask_out[None, :] * slope(act_five)
    gain_five, bias_five = back_sums(act_five_grad, cen_five)
    grad_five = norm_back(
        act_five_grad,
        cen_five,
        scale_five,
        narrow_norms[3, 0],
        mask_out,
        gain_five,
        bias_five,
        count_out,
    ).astype(jnp.bfloat16)
    hid_four_grad, middle_one_grad = conv_backward(
        grad_five, gat_four, middle_w[1], PLAIN_TAPS, pixels, 1
    )
    act_four_grad = hid_four_grad * keep_two * mask_out[None, :] * slope(act_four)
    gain_four, bias_four = back_sums(act_four_grad, cen_four)
    grad_four = norm_back(
        act_four_grad,
        cen_four,
        scale_four,
        narrow_norms[2, 0],
        mask_out,
        gain_four,
        bias_four,
        count_out,
    ).astype(jnp.bfloat16)
    out_one_grad, second_grad, unused_side = input_back(
        out_one, grad_four, None, second_w, None, pixels
    )
    grad_one = (grad_two + out_one_grad) * mask_out[None, :] * slope(total_one)
    gains_pair, bias_pair = over_images(
        jnp.stack([jnp.sum(grad_one * cen_three, 1), jnp.sum(grad_one * cen_side, 1)]),
        jnp.sum(grad_one, 1),
    )
    grad_three = norm_back(
        grad_one,
        cen_three,
        scale_three,
        wide_norms[0, 0],
        mask_out,
        gains_pair[0],
        bias_pair,
        count_out,
    ).astype(jnp.bfloat16)
    grad_side = norm_back(
        grad_one,
        cen_side,
        scale_side,
        wide_norms[1, 0],
        mask_out,
        gains_pair[1],
        bias_pair,
        count_out,
    ).astype(jnp.bfloat16)
    hid_two_grad, last_zero_grad = output_back(grad_three, last_w[0], hid_two)
    act_two_grad = hid_two_grad * keep_one * mask_out[None, :] * slope(act_two)
    gain_two, bias_two = back_sums(act_two_grad, cen_two)
    grad_mid = norm_back(
        act_two_grad,
        cen_two,
        scale_two,
        narrow_norms[1, 0],
        mask_out,
        gain_two,
        bias_two,
        count_out,
    ).astype(jnp.bfloat16)
    hid_one_grad, middle_zero_grad = conv_backward(
        grad_mid, gat_one, middle_w[0], STRIDED_TAPS, pixels, 4
    )
    act_one_grad = hid_one_grad * keep_one * mask_in[None, :] * slope(act_one)
    gain_one, bias_one = back_sums(act_one_grad, cen_one)
    grad_first = norm_back(
        act_one_grad, cen_one, scale_one, narrow_norms[0, 0], mask_in, gain_one, bias_one, count_in
    ).astype(jnp.bfloat16)
    field_grad, first_grad, short_grad = input_back(
        field, grad_first, grad_side, first_w, short_w, pixels
    )
    input_grad = (field_grad * mask_in[None, :]).astype(jnp.bfloat16).reshape(inputs.shape)
    grads = (
        lax.psum_scatter(first_grad, "dp", scatter_dimension=0, tiled=True),
        lax.psum_scatter(short_grad, "dp", scatter_dimension=0, tiled=True),
        lax.psum_scatter(
            jnp.stack([middle_zero_grad, middle_one_grad]), "dp", scatter_dimension=2, tiled=True
        ),
        lax.psum_scatter(
            jnp.stack([last_zero_grad, last_one_grad]), "dp", scatter_dimension=2, tiled=True
        ),
        lax.psum_scatter(second_grad, "dp", scatter_dimension=0, tiled=True),
    )
    first_fix = 1.0 - BETA_ONE**STEP
    second_fix = 1.0 - BETA_TWO**STEP
    weights = (first_weight, shortcut_weight, middle_weight, last_weight, second_weight)
    means = (first_mean, shortcut_mean, middle_mean, last_mean, second_mean)
    squares_old = (first_square, shortcut_square, middle_square, last_square, second_square)
    states = []
    updates = []
    for index in range(5):
        mean_next, square_next, step = adapt(
            grads[index], means[index], squares_old[index], first_fix, second_fix
        )
        states.append((mean_next, square_next))
        updates.append(step + DECAY * weights[index])
    pairs = [
        (weights[0], updates[0]),
        (weights[1], updates[1]),
        (weights[2][0], updates[2][0]),
        (weights[2][1], updates[2][1]),
        (weights[3][0], updates[3][0]),
        (weights[3][1], updates[3][1]),
        (weights[4], updates[4]),
    ]
    partial_value = jnp.stack(
        [
            jnp.stack([jnp.sum(weight * weight), jnp.sum(update * update)])
            for weight, update in pairs
        ]
    )
    matrix_norms = jnp.sqrt(lax.psum(partial_value, ("dp", "mp")))
    ratio = matrix_norms[:, 0] / (matrix_norms[:, 1] + EPS_TRUST)
    first_next = first_weight - RATE * ratio[0] * updates[0]
    short_next = shortcut_weight - RATE * ratio[1] * updates[1]
    middle_next = middle_weight - RATE * ratio[2:4].reshape(2, 1, 1, 1) * updates[2]
    last_next = last_weight - RATE * ratio[4:6].reshape(2, 1, 1) * updates[3]
    second_next = second_weight - RATE * ratio[6] * updates[4]
    narrow_grad = jnp.stack(
        [
            jnp.stack([gain_one, bias_one]),
            jnp.stack([gain_two, bias_two]),
            jnp.stack([gain_four, bias_four]),
            jnp.stack([gain_five, bias_five]),
        ]
    )
    wide_grad = jnp.stack(
        [
            jnp.stack([gains_pair[0], bias_pair]),
            jnp.stack([gains_pair[1], bias_pair]),
            jnp.stack([gain_six, bias_six]),
        ]
    )
    narrow_mean_next, narrow_square_next, narrow_step = adapt(
        narrow_grad, narrow_mean, narrow_square, first_fix, second_fix
    )
    wide_mean_next, wide_square_next, wide_step = adapt(
        wide_grad, wide_mean, wide_square, first_fix, second_fix
    )
    return (
        block_output,
        input_grad,
        states[0][0],
        states[0][1],
        first_next,
        states[1][0],
        states[1][1],
        short_next,
        states[2][0],
        states[2][1],
        middle_next,
        states[3][0],
        states[3][1],
        last_next,
        states[4][0],
        states[4][1],
        second_next,
        narrow_mean_next,
        narrow_square_next,
        narrow_norms - RATE_NORM * narrow_step,
        wide_mean_next,
        wide_square_next,
        wide_norms - RATE_NORM * wide_step,
        matrix_norms,
        first_next.astype(jnp.bfloat16),
        short_next.astype(jnp.bfloat16),
        middle_next.astype(jnp.bfloat16),
        last_next.astype(jnp.bfloat16),
        second_next.astype(jnp.bfloat16),
    )


VMEM_BYTES = 62 * 2**20


def fits(mesh, pixel_mask):
    sizes = (mesh.shape["dp"], mesh.shape["mp"])
    powers = all(size >= 2 and size & (size - 1) == 0 for size in sizes)
    return powers and pixel_mask.shape[1] % (HO * WO * sizes[1]) == 0


def swap(values, *bits):
    sizes = {axis: lax.axis_size(axis) for axis in ("dp", "mp")}
    masks = {axis: sum(mask for at, mask in bits if at == axis) for axis in sizes}
    if not masks["dp"]:
        return lax.ppermute(values, "mp", [(at, at ^ masks["mp"]) for at in range(sizes["mp"])])
    if not masks["mp"]:
        return lax.ppermute(values, "dp", [(at, at ^ masks["dp"]) for at in range(sizes["dp"])])
    mask = masks["dp"] * sizes["mp"] + masks["mp"]
    return lax.ppermute(
        values, ("dp", "mp"), [(at, at ^ mask) for at in range(sizes["dp"] * sizes["mp"])]
    )


def subsets(bits):
    return [
        [bit for place, bit in enumerate(bits) if index >> place & 1]
        for index in range(1 << len(bits))
    ]


def bit_of(axis, mask):
    return (lax.axis_index(axis) & mask) // mask


def high_bits(axis):
    masks = []
    mask = lax.axis_size(axis) // 2
    while mask:
        masks.append(mask)
        mask //= 2
    return masks


def everywhere(values, flows=()):
    mask = 1
    while mask < lax.axis_size("mp"):
        values = values + swap(values, ("mp", mask))
        mask *= 2
    copies = jnp.broadcast_to(values[None], (lax.axis_size("dp"),) + values.shape)
    arrived = lax.all_to_all(copies, "dp", 0, 0, tiled=True)
    return wave(flows, values, arrived) if flows else arrived


def pack(block):
    lead, rows, cols = block.shape
    parts = block.reshape(lead, rows, cols // 128, 128).transpose(0, 2, 1, 3)
    return parts.reshape(-1, 128)


def column_bits():
    return [("mp", mask) for mask in high_bits("mp")[:-1]]


def row_bits():
    return [("dp", mask) for mask in high_bits("dp")]


def lanes_of(rows):
    first = rows // 32 * 16
    return ((0, first), (first, rows))


def moves_kernel(tasks, count, places, *refs):
    sources, outs, sems = refs[:count], refs[count:-1], refs[-1]
    copies = []
    for at, (source, span, out, turns, rows) in enumerate(tasks):
        dims = len(sources[source].shape) - 2
        every = [slice(None)] * dims
        start = [
            pl.ds(1 - places[dim] if turns[dim] else places[dim], 1) if dim in turns else slice(None)
            for dim in range(dims)
        ]
        copies.append(
            pltpu.make_async_copy(
                sources[source].at[(*every, pl.ds(*span), slice(None))],
                outs[out].at[(*start, pl.ds(*rows), slice(None))],
                sems.at[at],
            )
        )
        copies[-1].start()
    for copy in copies:
        copy.wait()


def moves(wanted):
    sources = []
    tasks = []
    for out, (shape, pieces) in enumerate(wanted):
        for source, span, turns, rows in pieces:
            tasks.append((len(sources), span, out, turns, rows))
            sources.append(source)
    bits = column_bits() + row_bits()
    places = jnp.stack([bit_of(*bit) for bit in bits]).astype(jnp.int32)
    return pl.pallas_call(
        functools.partial(moves_kernel, tasks, len(sources)),
        in_specs=[pl.BlockSpec(memory_space=pltpu.SMEM)]
        + [pl.BlockSpec(memory_space=pltpu.HBM)] * len(sources),
        out_specs=[pl.BlockSpec(memory_space=pltpu.VMEM)] * len(wanted),
        out_shape=[jax.ShapeDtypeStruct(shape, jnp.bfloat16) for shape, _ in wanted],
        scratch_shapes=[pltpu.SemaphoreType.DMA((len(tasks),))],
        compiler_params=pltpu.CompilerParams(vmem_limit_bytes=VMEM_BYTES),
        cost_estimate=pl.CostEstimate(
            flops=0,
            bytes_accessed=sum(2 * source.size * 2 for source in sources),
            transcendentals=0,
        ),
    )(places, *sources)


class Gather:
    def __init__(self, rows, lanes=True):
        self.dims = column_bits() + row_bits()
        near = row_bits()[-1:]
        self.rows = rows.shape[0]
        if lanes:
            self.steps = [[row_bits()[:-1]], [near, column_bits()], [column_bits(), near]]
            self.spans = lanes_of(self.rows)
        else:
            self.steps = [[row_bits()[:-1]], [near + column_bits()]]
            self.spans = ((0, self.rows),)
        self.parts = [([rows.reshape((1,) * len(self.dims) + rows.shape)], [])]
        self.step = 0

    def pending(self):
        return [values for values, bits in self.parts]

    def resume(self, values):
        self.parts = [(value, bits) for value, (_, bits) in zip(values, self.parts)]

    def wanted(self):
        if not self.parts[0][1]:
            return []
        last = self.step == len(self.steps)
        split = not last and len(self.steps[self.step]) > len(self.parts)
        lanes = [(low, high - low) for low, high in self.spans]
        result = []
        for lane, (values, bits) in enumerate(self.parts):
            shape = [
                2 if bit in bits else size
                for bit, size in zip(self.dims, values[0].shape)
            ]
            pieces = [
                (value, {self.dims.index(bit): bit in turned for bit in bits})
                for value, turned in zip(values, subsets(bits))
            ]
            height = values[0].shape[-2]
            for low, size in lanes if split else [(0, height)]:
                block = [(value, (low, size), turns, (0, size)) for value, turns in pieces]
                result.append((tuple(shape) + (size, 128), block))
        if last:
            pieces = [
                (value, span, turns, lanes[lane])
                for lane, (_, block) in enumerate(result)
                for value, span, turns, _ in block
            ]
            result = [(result[0][0][:-2] + (self.rows, 128), pieces)]
        return result

    def launch(self, values):
        if not values:
            values = [self.parts[0][0][0]]
        if self.step < len(self.steps):
            self.parts = [
                ([value] + [swap(value, *bits) for bits in subsets(group)[1:]], group)
                for value, group in zip(values, self.steps[self.step])
            ]
        else:
            self.parts = [([values[0], swap(values[0], ("mp", 1))], [])]
        self.step += 1
        return values

    def bundles(self):
        shape = (1 << len(column_bits()), lax.axis_size("dp")) + self.parts[0][0][0].shape[-2:]
        return [value.reshape(shape) for value in self.parts[0][0]]


class Scatter:
    def __init__(self, keep, send, lanes=True):
        self.dims = column_bits() + row_bits()
        shape = (2,) * len(self.dims) + keep.shape[2:]
        near = row_bits()[-1:]
        far = row_bits()[:-1]
        if lanes:
            self.steps = [None, [column_bits(), near], [near, column_bits()], [far, far]]
            self.spans = lanes_of(keep.shape[2])
        else:
            self.steps = [None, [column_bits() + near], [far]]
            self.spans = (None,)
        self.lanes = [[] for _ in self.spans]
        self.raw = [keep.reshape(shape), send.reshape(shape)]
        self.step = 0

    def pending(self):
        return self.raw

    def resume(self, values):
        self.raw = list(values)

    def fold(self, lane, group=(), turned=()):
        total = 0.0
        for index, settled, span in self.lanes[lane]:
            value = self.raw[index]
            for bit in settled + list(group):
                place = bit_of(*bit)
                place = 1 - place if bit in turned else place
                value = lax.dynamic_slice_in_dim(value, place, 1, self.dims.index(bit))
            if span is not None:
                value = value[..., span[0] : span[1], :]
            total = total + value.astype(jnp.float32)
        return total

    def settle(self, lane, group, arrived, span):
        old = [(index, settled + group, part) for index, settled, part in self.lanes[lane]]
        self.lanes[lane] = old + [(index, [], span) for index in arrived]

    def wanted(self):
        return []

    def launch(self, values):
        groups = self.steps[self.step]
        whole = self.step == len(self.steps) - 1
        sent = []
        if groups is None:
            sent.append(self.raw[1])
            self.raw[1] = swap(self.raw[1], ("mp", 1))
            for lane, span in zip(self.lanes, self.spans):
                lane += [(0, [], span), (1, [], span)]
        elif whole:
            arrived = []
            for bits in subsets(groups[0])[1:]:
                out = [
                    self.fold(lane, groups[0], bits).astype(jnp.bfloat16)
                    for lane in range(len(self.lanes))
                ]
                out = jnp.concatenate(out, -2) if len(out) > 1 else out[0]
                arrived.append(len(self.raw))
                sent.append(out)
                self.raw.append(swap(out, *bits))
            for lane, span in enumerate(self.spans):
                self.settle(lane, groups[lane], arrived, span)
        else:
            for lane, group in enumerate(groups):
                arrived = []
                for bits in subsets(group)[1:]:
                    out = self.fold(lane, group, bits).astype(jnp.bfloat16)
                    arrived.append(len(self.raw))
                    sent.append(out)
                    self.raw.append(swap(out, *bits))
                self.settle(lane, group, arrived, None)
        self.step += 1
        return sent

    def rows(self):
        total = [self.fold(lane) for lane in range(len(self.lanes))]
        total = jnp.concatenate(total, -2) if len(total) > 1 else total[0]
        return total.reshape(total.shape[-2:])


def wave(flows, after=None, before=None):
    values = [flow.pending() for flow in flows]
    if after is not None:
        values, _ = lax.optimization_barrier((values, after))
    for flow, value in zip(flows, values):
        flow.resume(value)
    wanted = [flow.wanted() for flow in flows]
    joined = [value for part in wanted for value in part]
    made = list(moves(joined)) if joined else []
    sent = []
    for flow, part in zip(flows, wanted):
        sent += flow.launch([made.pop(0) for _ in part])
    if before is not None:
        before, _ = lax.optimization_barrier((before, sent))
    return before


def chunk_kernel(units, columns, rows_ref, cols_ref, *refs):
    outs = refs[-2:]
    product = lax.dot_general(
        rows_ref[...], cols_ref[...], (((0,), (0,)), ((), ())), preferred_element_type=jnp.float32
    ).astype(jnp.bfloat16)
    groups = outs[0].shape[0]
    chunks = outs[0].shape[1]
    for half, out in enumerate(outs):
        for group in range(groups):
            for part in range(columns):
                place = ((half * groups + group) * columns + part) * 128
                block = product[:, place : place + 128].reshape(chunks, units, 128)
                out[group, :, part * units : (part + 1) * units, :] = block


def chunks_into(bundle, total, start, rows_of, cols_of, lead, units, columns):
    count = lax.axis_size("dp")
    groups = 1 << len(column_bits())
    columns = columns // 128
    pixels = cols_of.shape[0]
    height = units * columns
    if lead > 1:
        steps, wide, chunks = lead, count * units, count
        place = lambda step: (0, 0, start // height + step, 0)
    else:
        steps, wide, chunks = count, units, 1
        place = lambda step: (0, step, start // height, 0)
    shape = jax.ShapeDtypeStruct((groups, count, total, 128), jnp.bfloat16)
    block = pl.BlockSpec((groups, chunks, height, 128), place)
    earlier = () if bundle is None else tuple(bundle)
    return pl.pallas_call(
        functools.partial(chunk_kernel, units, columns),
        grid=(steps,),
        in_specs=[
            pl.BlockSpec((pixels, wide), lambda step: (0, step)),
            pl.BlockSpec(cols_of.shape, lambda step: (0, 0)),
        ]
        + [pl.BlockSpec(memory_space=pltpu.HBM)] * len(earlier),
        out_specs=[block, block],
        out_shape=[shape, shape],
        input_output_aliases={2 + place: place for place in range(len(earlier))},
        compiler_params=pltpu.CompilerParams(vmem_limit_bytes=VMEM_BYTES),
        cost_estimate=pl.CostEstimate(
            flops=2 * rows_of.size * cols_of.shape[1],
            bytes_accessed=2 * (rows_of.size + cols_of.size)
            + 2 * rows_of.shape[1] * cols_of.shape[1],
            transcendentals=0,
        ),
    )(rows_of, cols_of, *earlier)


def total_of(ref):
    return jnp.sum(ref[...], 0) if len(ref.shape) == 3 else ref[...]


def as_row(block):
    return jnp.concatenate([block[place : place + 1] for place in range(block.shape[0])], 1)


def as_rows(row):
    return jnp.concatenate(
        [row[:, place : place + 128] for place in range(0, row.shape[1], 128)], 0
    )


def hand_out(out, rows):
    missing = out.shape[-2] - sum(row.shape[0] for row in rows)
    if missing:
        rows = rows + [jnp.zeros((missing, 128), jnp.float32)]
    block = jnp.concatenate(rows, 0)
    out[...] = jnp.broadcast_to(block[None], out.shape) if len(out.shape) == 3 else block


def levels(total, first, width, count):
    rows = width // 128
    mean = total[first : first + rows] / count
    scale = lax.rsqrt(total[first + rows : first + 2 * rows] / count - mean * mean + EPS_NORM)
    return (as_row(mean), as_row(scale))


def standard(values, level):
    return (values - level[0]) * level[1]


def back_through(grad, centred, level, gain, mask, total, first, bias_first, count):
    rows = grad.shape[1] // 128
    gain_sum = as_row(total[first : first + rows] / count)
    bias_sum = as_row(total[bias_first : bias_first + rows] / count)
    return (gain * level[1]) * (grad - mask * (bias_sum + centred * gain_sum))


def column_sums(values, mask):
    weighted = values * mask
    return [
        as_rows(jnp.sum(weighted, 0, keepdims=True)),
        as_rows(jnp.sum(weighted * values, 0, keepdims=True)),
    ]


def product_sums(grad, centred):
    return as_rows(jnp.sum(grad * centred, 0, keepdims=True))


def plain_sums(grad):
    return as_rows(jnp.sum(grad, 0, keepdims=True))


def fetch(bundles, held, sems, start):
    rows = held.shape[3]
    copies = [
        pltpu.make_async_copy(ref.at[:, :, pl.ds(start, rows), :], held.at[half], sems.at[half])
        for half, ref in enumerate(bundles)
    ]
    for copy in copies:
        copy.start()
    return copies


def arrive(copies):
    for copy in copies:
        copy.wait()


def weight_part(held, chunk, chunks, start, units, columns):
    return jnp.concatenate(
        [
            held[half, group, chunk : chunk + chunks, start + part * units : start + (part + 1) * units, :]
            .reshape(chunks * units, 128)
            for half in range(2)
            for group in range(held.shape[1])
            for part in range(columns)
        ],
        1,
    )


def spots(core, groups, width):
    return [
        pl.multiple_of((2 * group + (core if half == 0 else 1 - core)) * width, 128)
        for half in range(2)
        for group in range(groups)
    ]


def in_turn(ref, core, groups):
    width = ref.shape[1] // (2 * groups)
    return jnp.concatenate([ref[:, pl.ds(at, width)] for at in spots(core, groups, width)], 1)


def in_order(ref, values, core, groups):
    width = ref.shape[1] // (2 * groups)
    for place, at in enumerate(spots(core, groups, width)):
        ref[:, pl.ds(at, width)] = values[:, place * width : (place + 1) * width]


def product(first, second):
    return lax.dot_general(
        first, second, (((1,), (0,)), ((), ())), preferred_element_type=jnp.float32
    )


def product_turned(first, second):
    return lax.dot_general(
        first, second, (((1,), (1,)), ((), ())), preferred_element_type=jnp.float32
    )


def many_in(values, held, units, columns):
    chunks = max(1, 256 // units)
    total = 0.0
    for chunk in range(0, held.shape[2], chunks):
        part = weight_part(held, chunk, chunks, 0, units, columns)
        total = total + product(
            values[:, chunk * units : (chunk + chunks) * units], part
        )
    return total


def many_out(values, held, units, columns):
    chunks = max(1, 256 // units)
    return [
        product_turned(values, weight_part(held, chunk, chunks, 0, units, columns))
        for chunk in range(0, held.shape[2], chunks)
    ]


def slid(values, offset):
    count = values.shape[0]
    return pltpu.roll(values, (-offset) % count, 0) if offset % count else values


def within(inside, drow, dcol):
    place = 3 * (drow + 1) + dcol + 1
    return inside[:, place : place + 1]


def first_layer(core, raw, mask, first, second, field, out, sums, held, sems):
    copies = fetch((first, second), held, sems, 0)
    core = core[0]
    weights = mask[...]
    width = raw.shape[2]
    for place in range(raw.shape[0]):
        part = raw[place].astype(jnp.float32) * weights
        field[:, place * width : (place + 1) * width] = part.astype(jnp.bfloat16)
    arrive(copies)
    result = many_in(field, held, held.shape[3], 1)
    in_order(out, result, core, held.shape[1])
    rows = column_sums(out[...], weights)
    pixels = weights.shape[0] // 4
    for part in (weights, weights[:pixels]):
        rows.append(jnp.broadcast_to(jnp.sum(part, 0, keepdims=True), (1, 128)))
    hand_out(sums, rows)


def side_layer(start, core, field, mask, first, second, out, sums, held, sems):
    copies = fetch((first, second), held, sems, start)
    core = core[0]
    pixels = mask.shape[0]
    arrive(copies)
    columns = out.shape[1] // (2 * held.shape[1] * 128)
    result = many_in(field[:pixels, :], held, held.shape[3] // columns, columns)
    in_order(out, result, core, held.shape[1])
    hand_out(sums, column_sums(out[...], mask[...]))


def spread_layer(start, norm, taps, core, before, sums_in, counts, tables, keep, mask_in, mask, inside,
                 first, second, cols, out, sums, held, sems):
    copies = fetch((first, second), held, sems, start)
    core = core[0]
    pixels = mask.shape[0]
    width = before.shape[1]
    counted = 0 if before.shape[0] > pixels else 1
    level = levels(total_of(sums_in), 0, width, counts[counted : counted + 1, :])
    act = standard(before[...], level) * tables[2 * norm : 2 * norm + 1, :] + tables[2 * norm + 1 : 2 * norm + 2, :]
    row = norm // 2
    hidden = jax.nn.silu(act) * mask_in[...] * keep[row : row + 1, :]
    for tap, phase, drow, dcol in taps:
        source = hidden[phase * pixels : (phase + 1) * pixels]
        moved = slid(source, drow * WO + dcol) * within(inside, drow, dcol)
        cols[:, tap * width : (tap + 1) * width] = moved.astype(jnp.bfloat16)
    arrive(copies)
    units = held.shape[3] // 9
    total = 0.0
    for tap in range(9):
        part = weight_part(held, 0, held.shape[2], tap * units, units, 1)
        total = total + product(cols[:, tap * width : (tap + 1) * width], part)
    in_order(out, total, core, held.shape[1])
    hand_out(sums, column_sums(out[...], mask[...]))


def widen_layer(start, norm, core, before, sums_in, counts, tables, keep, mask, first, second,
                hidden, out, sums, held, scratch, sems):
    copies = fetch((first, second), held, sems, start)
    core = core[0]
    level = levels(total_of(sums_in), 0, before.shape[1], counts[1:2, :])
    act = standard(before[...], level) * tables[2 * norm : 2 * norm + 1, :] + tables[2 * norm + 1 : 2 * norm + 2, :]
    row = norm // 2
    scratch[...] = jax.nn.silu(act) * mask[...] * keep[row : row + 1, :]
    hidden[...] = in_turn(scratch, core, held.shape[1]).astype(jnp.bfloat16)
    arrive(copies)
    parts = many_out(hidden[...], held, held.shape[3], 1)
    size = out.shape[1] // len(parts)
    for place, part in enumerate(parts):
        out[:, place * size : (place + 1) * size] = part
    hand_out(sums, column_sums(out[...], mask[...]))


def joined_acts(total, third, side, wide, count):
    width = third.shape[1]
    rows = width // 128
    centred_third = standard(third[...], levels(total, 0, width, count))
    centred_side = standard(side[...], levels(total, 2 * rows, width, count))
    act = (
        centred_third * wide[0:1, :]
        + wide[1:2, :]
        + (centred_side * wide[2:3, :] + wide[3:4, :])
    )
    return (centred_third, centred_side, act)


def narrow_layer(start, core, third, side, sums_in, counts, wide, mask, first, second,
                 above, out, sums, held, sems):
    copies = fetch((first, second), held, sems, start)
    core = core[0]
    centred_third, centred_side, act = joined_acts(
        total_of(sums_in), third, side, wide, counts[1:2, :]
    )
    above[...] = (jax.nn.silu(act) * mask[...]).astype(jnp.bfloat16)
    arrive(copies)
    result = many_in(above, held, held.shape[3], 1)
    in_order(out, result, core, held.shape[1])
    hand_out(sums, column_sums(out[...], mask[...]))


def last_layer(sixth, sums_in, counts, wide, above, cotangent, mask, out, grad, sums):
    level = levels(total_of(sums_in), 0, sixth.shape[1], counts[1:2, :])
    centred = standard(sixth[...], level)
    act = centred * wide[4:5, :] + wide[5:6, :] + above[...].astype(jnp.float32)
    weights = mask[...]
    result = (jax.nn.silu(act) * weights).astype(jnp.bfloat16)
    inner = weights * slope(act)
    width = out.shape[2]
    for place in range(out.shape[0]):
        span = slice(place * width, (place + 1) * width)
        out[place] = result[:, span]
        grad[:, span] = cotangent[place].astype(jnp.float32) * inner[:, span]
    result = grad[...]
    hand_out(sums, [product_sums(result, centred), plain_sums(result)])


def narrow_grad(grad, before, sums_in, counts, tables, norm, keep, mask):
    counted = 0 if norm == 0 else 1
    level = levels(total_of(sums_in), 0, before.shape[1], counts[counted : counted + 1, :])
    centred = standard(before[...], level)
    act = centred * tables[2 * norm : 2 * norm + 1, :] + tables[2 * norm + 1 : 2 * norm + 2, :]
    row = norm // 2
    result = grad * keep[row : row + 1, :] * mask * slope(act)
    return (result, [product_sums(result, centred), plain_sums(result)])


def narrow_back(norm, grad, before, sums_in, sums_back, counts, tables, mask):
    counted = 0 if norm == 0 else 1
    count = counts[counted : counted + 1, :]
    width = before.shape[1]
    level = levels(total_of(sums_in), 0, width, count)
    return back_through(
        grad[...],
        standard(before[...], level),
        level,
        tables[2 * norm : 2 * norm + 1, :],
        mask,
        total_of(sums_back),
        0,
        width // 128,
        count,
    )


def last_back(start, norm, core, grad, sixth, sums_six, back_six, counts, wide, before, sums_in, tables,
              keep, mask, first, second, grad_out, grad_in, sums, held, scratch, sems):
    copies = fetch((first, second), held, sems, start)
    core = core[0]
    width = sixth.shape[1]
    count = counts[1:2, :]
    level = levels(total_of(sums_six), 0, width, count)
    grad_out[...] = back_through(
        grad[...], standard(sixth[...], level), level, wide[4:5, :], mask[...], total_of(back_six), 0,
        width // 128, count,
    ).astype(jnp.bfloat16)
    arrive(copies)
    in_order(scratch, many_in(grad_out, held, held.shape[3], 1), core, held.shape[1])
    result, rows = narrow_grad(scratch[...], before, sums_in, counts, tables, norm, keep, mask[...])
    grad_in[...] = result
    hand_out(sums, rows)


def pair_back(start, norm, core, grad, third, side, sums_pair, back_pair, counts, wide, before, sums_in,
              tables, keep, mask, first, second, grad_third, grad_side, grad_in, sums, held, scratch,
              big, sems):
    copies = fetch((first, second), held, sems, start)
    core = core[0]
    width = third.shape[1]
    rows = width // 128
    count = counts[1:2, :]
    total = total_of(sums_pair)
    back = total_of(back_pair)
    groups = held.shape[1]
    level = levels(total, 0, width, count)
    grad_third[...] = back_through(
        grad[...], standard(third[...], level), level, wide[0:1, :], mask[...], back, 0, 2 * rows, count
    ).astype(jnp.bfloat16)
    arrive(copies)
    in_order(scratch, many_in(grad_third, held, held.shape[3], 1), core, groups)
    result, parts = narrow_grad(scratch[...], before, sums_in, counts, tables, norm, keep, mask[...])
    grad_in[...] = result
    hand_out(sums, parts)
    level = levels(total, 2 * rows, width, count)
    big[...] = back_through(
        grad[...], standard(side[...], level), level, wide[2:3, :], mask[...], back, rows, 2 * rows, count
    )
    grad_side[...] = in_turn(big, core, groups).astype(jnp.bfloat16)


def spread_back(start, norm, taps, core, grad, after, sums_after, back_after, counts, tables, before,
                sums_in, keep, mask_in, mask, inside, first, second, grad_out, grad_in, sums, held,
                scratch, sems):
    copies = fetch((first, second), held, sems, start)
    core = core[0]
    pixels = mask.shape[0]
    phases = before.shape[0] // pixels
    scratch[...] = narrow_back(norm + 1, grad, after, sums_after, back_after, counts, tables, mask[...])
    grad_out[...] = in_turn(scratch, core, held.shape[1]).astype(jnp.bfloat16)
    arrive(copies)
    units = held.shape[3] // 9
    totals = [0.0] * phases
    for tap, phase, drow, dcol in taps:
        part = weight_part(held, 0, held.shape[2], tap * units, units, 1)
        moved = product_turned(grad_out[...], part)
        totals[phase] = totals[phase] + slid(moved, -drow * WO - dcol) * within(inside, -drow, -dcol)
    hidden = jnp.concatenate(totals, 0) if phases > 1 else totals[0]
    result, rows = narrow_grad(hidden, before, sums_in, counts, tables, norm, keep, mask_in[...])
    grad_in[...] = result
    hand_out(sums, rows)


def narrow_layer_back(start, core, grad, fourth, sums_four, back_four, counts, tables, mask, grad_two,
                      third, side, sums_pair, wide, first, second, grad_out, grad_in, sums, held,
                      scratch, big, sems):
    copies = fetch((first, second), held, sems, start)
    core = core[0]
    scratch[...] = narrow_back(2, grad, fourth, sums_four, back_four, counts, tables, mask[...])
    grad_out[...] = in_turn(scratch, core, held.shape[1]).astype(jnp.bfloat16)
    arrive(copies)
    parts = many_out(grad_out[...], held, held.shape[3], 1)
    size = big.shape[1] // len(parts)
    for place, part in enumerate(parts):
        big[:, place * size : (place + 1) * size] = part
    centred_third, centred_side, act = joined_acts(
        total_of(sums_pair), third, side, wide, counts[1:2, :]
    )
    result = (grad_two[...] + big[...]) * mask[...] * slope(act)
    grad_in[...] = result
    hand_out(
        sums,
        [
            product_sums(result, centred_third),
            product_sums(result, centred_side),
            plain_sums(result),
        ],
    )


def side_back(start, grad, first, second, out, held, sems):
    copies = fetch((first, second), held, sems, start)
    arrive(copies)
    columns = grad.shape[1] // (2 * held.shape[1] * 128)
    parts = many_out(grad[...], held, held.shape[3] // columns, columns)
    size = out.shape[1] // len(parts)
    for place, part in enumerate(parts):
        out[:, place * size : (place + 1) * size] = part


def first_back(core, grad, before, sums_in, sums_back, counts, tables, mask, side, first, second,
               grad_out, out, held, scratch, sems):
    copies = fetch((first, second), held, sems, 0)
    core = core[0]
    scratch[...] = narrow_back(0, grad, before, sums_in, sums_back, counts, tables, mask[...])
    grad_out[...] = in_turn(scratch, core, held.shape[1]).astype(jnp.bfloat16)
    arrive(copies)
    parts = many_out(grad_out[...], held, held.shape[3], 1)
    size = side.shape[1] // len(parts)
    pixels = side.shape[0]
    weights = mask[...]
    width = out.shape[2]
    for place, part in enumerate(parts):
        owner = place * size // width
        span = slice(place * size % width, place * size % width + size)
        beside = side[:, place * size : (place + 1) * size]
        out[owner, :pixels, span] = ((part[:pixels] + beside) * weights[:pixels]).astype(jnp.bfloat16)
        out[owner, pixels:, span] = (part[pixels:] * weights[pixels:]).astype(jnp.bfloat16)


class Coming:
    def __init__(self, ref, copy):
        self.ref = ref
        self.copy = copy
        self.shape = ref.shape

    def settle(self):
        if self.copy is not None:
            self.copy.wait()
            self.copy = None

    def __getitem__(self, place):
        self.settle()
        return self.ref[place]


def framed(kernel, places, count, *refs):
    refs = list(refs)
    rest, held, sems = refs[: len(refs) - len(places) - 1], refs[-len(places) - 1 : -1], refs[-1]
    coming = []
    for at, place in enumerate(places):
        copy = pltpu.make_async_copy(rest[place], held[at], sems.at[at])
        copy.start()
        rest[place] = Coming(held[at], copy)
        coming.append(rest[place])
    kernel(*rest)
    for value in coming:
        value.settle()


def launch(kernel, shapes, values, bundles=(), rows=0, scratch=(), work=0):
    held = []
    sems = []
    if bundles:
        held = [pltpu.VMEM((2,) + bundles[0].shape[:2] + (rows, 128), jnp.bfloat16)]
        sems = [pltpu.SemaphoreType.DMA((2,))]
    places = [place for place, value in enumerate(values) if value.dtype != jnp.int32]
    moved = sum(value.size * value.dtype.itemsize for value in list(values) + list(shapes))
    specs = []
    for place, value in enumerate(values):
        space = pltpu.SMEM if value.dtype == jnp.int32 else pltpu.VMEM
        specs.append(pl.BlockSpec(memory_space=pltpu.HBM if place in places else space))
    late = []
    if places:
        kernel = functools.partial(framed, kernel, places, len(values))
        late = [pltpu.VMEM(values[place].shape, values[place].dtype) for place in places]
        late.append(pltpu.SemaphoreType.DMA((len(places),)))
    return pl.pallas_call(
        kernel,
        in_specs=specs + [pl.BlockSpec(memory_space=pltpu.HBM)] * len(bundles),
        out_specs=[pl.BlockSpec(memory_space=pltpu.VMEM)] * len(shapes),
        out_shape=list(shapes),
        scratch_shapes=held + [pltpu.VMEM(shape, jnp.float32) for shape in scratch] + sems + late,
        compiler_params=pltpu.CompilerParams(vmem_limit_bytes=VMEM_BYTES),
        cost_estimate=pl.CostEstimate(
            flops=2 * work, bytes_accessed=moved + rows * 16 * 512, transcendentals=0
        ),
    )(*values, *bundles)


def moved_by(grad, mean, square, weight, mean_out, square_out, update_out, at):
    first_fix = 1.0 - BETA_ONE**STEP
    second_fix = 1.0 - BETA_TWO**STEP
    old = weight[at]
    mean_next, square_next, step = adapt(grad, mean[at], square[at], first_fix, second_fix)
    update = step + DECAY * old
    mean_out[at] = mean_next
    square_out[at] = square_next
    update_out[at] = update
    result = []
    for value in (old, update):
        power = value * value
        while len(power.shape) > 2:
            power = jnp.sum(power, 0)
        row = jnp.sum(power, 0, keepdims=True)
        result.append(
            sum(row[:, place : place + 128] for place in range(0, row.shape[1], 128))
        )
    return result


def early_moves(columns, rows_a, rows_c, short_m, short_v, short_w, last_m, last_v, last_w, second_m, second_v,
                second_w, short_mo, short_vo, short_uo, last_mo, last_vo, last_uo, second_mo, second_vo,
                second_uo, powers):
    unit_in = short_w.shape[0]
    unit_out = second_w.shape[0]
    parts = short_w.shape[1] // 128
    every = (slice(None), slice(None))
    grad = jnp.concatenate(
        [rows_c[part * unit_in : (part + 1) * unit_in, :] for part in range(parts)], 1
    )
    found = moved_by(grad, short_m, short_v, short_w, short_mo, short_vo, short_uo, every)
    start = parts * unit_in
    for block, rows in enumerate((rows_c[start : start + unit_out, :], rows_a[...])):
        found += moved_by(
            jnp.transpose(rows), last_m, last_v, last_w, last_mo, last_vo, last_uo, block
        )
    start += unit_out
    found += moved_by(
        rows_c[start : start + unit_out, :], second_m, second_v, second_w, second_mo, second_vo,
        second_uo, every,
    )
    powers[...] = jnp.concatenate(found, 0)


def late_moves(rows_b, rows_d, rows_e, powers_in, first_m, first_v, first_w, mid_m, mid_v, mid_w, first_mo,
               first_vo, first_uo, mid_mo, mid_vo, mid_uo, powers):
    every = (slice(None), slice(None))
    found = moved_by(
        rows_e[...], first_m, first_v, first_w, first_mo, first_vo, first_uo, every
    )
    shape = mid_w.shape[1:]
    middle = []
    for block, rows in enumerate((rows_d, rows_b)):
        middle += moved_by(
            rows[...].reshape(shape), mid_m, mid_v, mid_w, mid_mo, mid_vo, mid_uo, block
        )
    early = powers_in[...]
    order = [found[0], found[1], early[0:2]] + middle + [early[2:8]]
    hand_out(powers, order)


def final_moves(powers, first_w, first_u, short_w, short_u, mid_w, mid_u, last_w, last_u, second_w, second_u,
                norms, first_o, short_o, mid_o, last_o, second_o, first_c, short_c, mid_c, last_c, second_c):
    total = jnp.sqrt(jnp.sum(jnp.sum(powers[...], 0), 1, keepdims=True))
    norms[...] = jnp.broadcast_to(total, norms.shape)

    def step(row, weight, update, out, copy, at):
        ratio = total[2 * row : 2 * row + 1] / (total[2 * row + 1 : 2 * row + 2] + EPS_TRUST)
        fresh = weight[at] - (RATE * ratio) * update[at]
        out[at] = fresh
        copy[at] = fresh.astype(jnp.bfloat16)

    every = (slice(None), slice(None))
    step(0, first_w, first_u, first_o, first_c, every)
    step(1, short_w, short_u, short_o, short_c, every)
    for block in range(2):
        for tap in range(mid_w.shape[1]):
            step(2 + block, mid_w, mid_u, mid_o, mid_c, (block, tap))
        step(4 + block, last_w, last_u, last_o, last_c, block)
    step(6, second_w, second_u, second_o, second_c, every)


def exchange(copies):
    return lax.all_to_all(copies, ("dp", "mp"), 0, 0, tiled=True)


def by_image(
    inputs,
    pixel_mask,
    widths,
    output_grad,
    first_weight,
    shortcut_weight,
    middle_weight,
    last_weight,
    second_weight,
    narrow_norms,
    wide_norms,
    first_mean,
    first_square,
    shortcut_mean,
    shortcut_square,
    middle_mean,
    middle_square,
    last_mean,
    last_square,
    second_mean,
    second_square,
    narrow_mean,
    narrow_square,
    wide_mean,
    wide_square,
):
    ranks = lax.axis_size("mp")
    rank = lax.axis_index("mp")
    pixels = pixel_mask.shape[1] // ranks
    narrow = first_weight.shape[1] * ranks
    wide = shortcut_weight.shape[1] * ranks
    low = jnp.bfloat16
    channels = inputs.shape[0]
    field = inputs.reshape(channels, 4, ranks, pixels).transpose(2, 1, 3, 0)
    field = field.reshape(ranks, 4 * pixels, channels)
    flow_a = Gather(pack(first_weight.astype(low)[None]), False)
    flow_b = Gather(pack(middle_weight[0].astype(low)))
    flow_c = Gather(
        jnp.concatenate(
            [
                pack(shortcut_weight.astype(low)[None]),
                pack(last_weight[0].astype(low).T[None]),
                pack(second_weight.astype(low)[None]),
            ]
        )
    )
    flow_d = Gather(
        jnp.concatenate(
            [pack(last_weight[1].astype(low).T[None]), pack(middle_weight[1].astype(low))]
        )
    )
    field = lax.all_to_all(field, "mp", 0, 0, tiled=True)
    wave([flow_a, flow_b])
    wave([flow_a, flow_b, flow_c], field)
    wave([flow_a, flow_b, flow_d])
    unit_in, column = first_weight.shape
    column_wide = shortcut_weight.shape[1]
    unit_mid = middle_weight.shape[2]
    unit_out = second_weight.shape[0]
    size_short = unit_in * column_wide // 128
    size_out = unit_out * column // 128
    size_mid = 9 * unit_mid * column // 128
    tables = jnp.concatenate([narrow_norms.reshape(-1, 128), wide_norms.reshape(-1, 128)], 0)
    tables = jnp.broadcast_to(tables[None], (ranks,) + tables.shape)
    tables = lax.all_to_all(tables, "mp", 0, 0, tiled=True)
    split = narrow_norms.size // 128
    narrow_all = (
        tables[:, :split].reshape(ranks, 4, 2, -1).transpose(1, 2, 0, 3).reshape(4, 2, narrow)
    )
    wide_all = tables[:, split:].reshape(ranks, 3, 2, -1).transpose(1, 2, 0, 3).reshape(3, 2, wide)

    narrow_all = narrow_all.reshape(8, narrow)
    wide_all = jnp.concatenate([wide_all.reshape(6, wide), jnp.zeros((2, wide), jnp.float32)], 0)

    own_mask = lax.dynamic_slice_in_dim(pixel_mask, rank * pixels, pixels, 1).astype(jnp.float32)
    mask_in = own_mask.reshape(-1, 1)
    mask = own_mask[0][:, None]
    channel = lax.iota(jnp.int32, narrow)[None]
    keep = (channel < widths[:, None]).astype(jnp.float32)
    keep = jnp.concatenate([keep, jnp.zeros((6, narrow), jnp.float32)], 0)
    place = lax.iota(jnp.int32, pixels)[:, None]
    step = lax.iota(jnp.int32, 9)[None]
    row_at = place // WO % HO + step // 3 - 1
    col_at = place % WO + step % 3 - 1
    inside = (row_at >= 0) & (row_at < HO) & (col_at >= 0) & (col_at < WO)
    inside = inside.astype(jnp.float32)
    core = bit_of("mp", 1)[None]

    above = output_grad.reshape(-1, ranks, pixels).transpose(1, 2, 0)
    above = lax.all_to_all(above, "mp", 0, 0, tiled=True)

    devices = ranks * lax.axis_size("dp")
    full = 4 * pixels

    def real(*shape):
        return jax.ShapeDtypeStruct(shape, jnp.float32)

    def short(*shape):
        return jax.ShapeDtypeStruct(shape, low)

    size = narrow // 128
    wide_rows = wide // 128
    copies = real(devices, 2 * size, 128)
    bundle_a = flow_a.bundles()
    field, pre_one, sums = launch(
        first_layer,
        [short(full, ranks * channels), real(full, narrow), real(devices, 2 * size + 8, 128)],
        [core, field, mask_in],
        bundle_a,
        unit_in,
        work=field.size * narrow,
    )
    sums_one = wave([flow_b, flow_c], sums, exchange(sums))
    counts = jnp.sum(sums_one[:, 2 * size :], 0)
    bundle_b = flow_b.bundles()
    cols_one, pre_two, sums = launch(
        functools.partial(spread_layer, 0, 0, STRIDED_TAPS),
        [short(pixels, 9 * narrow), real(pixels, narrow), copies],
        [core, pre_one, sums_one, counts, narrow_all, keep, mask_in, mask, inside],
        bundle_b,
        size_mid,
        work=9 * pixels * narrow * narrow,
    )
    sums_two = wave([flow_c], sums, exchange(sums))
    wave([flow_c, flow_d], sums_two)
    bundle_c = flow_c.bundles()
    pre_side, side_sums = launch(
        functools.partial(side_layer, 0),
        [real(pixels, wide), real(2 * wide_rows, 128)],
        [core, field, mask],
        bundle_c,
        size_short,
        work=pixels * field.shape[1] * wide,
    )
    hid_two, pre_three, sums = launch(
        functools.partial(widen_layer, size_short, 1),
        [short(pixels, narrow), real(pixels, wide), real(2 * wide_rows, 128)],
        [core, pre_two, sums_two, counts, narrow_all, keep, mask],
        bundle_c,
        size_out,
        [(pixels, narrow)],
        work=pixels * narrow * wide,
    )
    sums_pair = everywhere(jnp.concatenate([sums, side_sums], 0), [flow_d])
    out_one, pre_four, sums = launch(
        functools.partial(narrow_layer, size_short + size_out),
        [short(pixels, wide), real(pixels, narrow), copies],
        [core, pre_three, pre_side, sums_pair, counts, wide_all, mask],
        bundle_c,
        size_out,
        work=pixels * narrow * wide,
    )
    sums_four = wave([flow_d], sums, exchange(sums))
    bundle_d = flow_d.bundles()
    cols_four, pre_five, sums = launch(
        functools.partial(spread_layer, size_out, 2, PLAIN_TAPS),
        [short(pixels, 9 * narrow), real(pixels, narrow), copies],
        [core, pre_four, sums_four, counts, narrow_all, keep, mask, mask, inside],
        bundle_d,
        size_mid,
        work=9 * pixels * narrow * narrow,
    )
    sums_five = exchange(sums)
    hid_five, pre_six, sums = launch(
        functools.partial(widen_layer, 0, 3),
        [short(pixels, narrow), real(pixels, wide), real(2 * wide_rows, 128)],
        [core, pre_five, sums_five, counts, narrow_all, keep, mask],
        bundle_d,
        size_out,
        [(pixels, narrow)],
        work=pixels * narrow * wide,
    )
    sums_six = everywhere(sums)
    block_output, grad_two, sums = launch(
        last_layer,
        [short(*above.shape), real(pixels, wide), real(2 * wide_rows, 128)],
        [pre_six, sums_six, counts, wide_all, out_one, above, mask],
    )
    back_six = everywhere(sums)
    block_output = lax.all_to_all(block_output, "mp", 0, 0, tiled=True)
    block_output = block_output.transpose(2, 0, 1).reshape(-1, ranks * pixels)

    grad_six, act_five_grad, sums = launch(
        functools.partial(last_back, 0, 3),
        [short(pixels, wide), real(pixels, narrow), copies],
        [core, grad_two, pre_six, sums_six, back_six, counts, wide_all, pre_five,
         sums_five, narrow_all, keep, mask],
        bundle_d,
        size_out,
        [(pixels, narrow)],
        work=pixels * narrow * wide,
    )
    bundle = chunks_into(None, size_out, 0, grad_six, hid_five, 1, unit_out, column)
    back_a = Scatter(*bundle)
    back_five = wave([back_a], sums, exchange(sums))
    grad_five, act_four_grad, sums = launch(
        functools.partial(spread_back, size_out, 2, PLAIN_TAPS),
        [short(pixels, narrow), real(pixels, narrow), copies],
        [core, act_five_grad, pre_five, sums_five, back_five, counts, narrow_all,
         pre_four, sums_four, keep, mask, mask, inside],
        bundle_d,
        size_mid,
        [(pixels, narrow)],
        work=9 * pixels * narrow * narrow,
    )
    back_four = exchange(sums)
    bundle = chunks_into(None, size_mid, 0, cols_four, grad_five, 9, unit_mid, column)
    back_b = Scatter(*bundle)
    back_four = wave([back_a, back_b], sums, back_four)
    grad_four, grad_one, sums = launch(
        functools.partial(narrow_layer_back, size_short + size_out),
        [short(pixels, narrow), real(pixels, wide), real(3 * wide_rows, 128)],
        [core, act_four_grad, pre_four, sums_four, back_four, counts, narrow_all, mask,
         grad_two, pre_three, pre_side, sums_pair, wide_all],
        bundle_c,
        size_out,
        [(pixels, narrow), (pixels, wide)],
        work=pixels * narrow * wide,
    )
    back_pair = everywhere(sums, [back_a, back_b])
    total = size_short + 2 * size_out
    bundle = chunks_into(
        None, total, size_short + size_out, out_one, grad_four, 1, unit_out, column
    )
    back_pair, bundle = lax.optimization_barrier((back_pair, bundle))
    grad_three, grad_side, act_two_grad, sums = launch(
        functools.partial(pair_back, size_short, 1),
        [short(pixels, wide), short(pixels, wide), real(pixels, narrow), copies],
        [core, grad_one, pre_three, pre_side, sums_pair, back_pair, counts, wide_all,
         pre_two, sums_two, narrow_all, keep, mask],
        bundle_c,
        size_out,
        [(pixels, narrow), (pixels, wide)],
        work=pixels * narrow * wide,
    )
    back_two = wave([back_a, back_b], sums, exchange(sums))
    bundle = chunks_into(bundle, total, size_short, grad_three, hid_two, 1, unit_out, column)
    bundle = chunks_into(bundle, total, 0, field, grad_side, 1, unit_in, column_wide)
    back_c = Scatter(*bundle)
    back_two = wave([back_c], sums, back_two)
    grad_mid, act_one_grad, sums = launch(
        functools.partial(spread_back, 0, 0, STRIDED_TAPS),
        [short(pixels, narrow), real(full, narrow), copies],
        [core, act_two_grad, pre_two, sums_two, back_two, counts, narrow_all, pre_one,
         sums_one, keep, mask_in, mask, inside],
        bundle_b,
        size_mid,
        [(pixels, narrow)],
        work=9 * pixels * narrow * narrow,
    )
    back_one = wave([back_b, back_c], sums, exchange(sums))
    bundle = chunks_into(None, size_mid, 0, cols_one, grad_mid, 9, unit_mid, column)
    back_d = Scatter(*bundle)
    (side_grad,) = launch(
        functools.partial(side_back, 0),
        [real(pixels, field.shape[1])],
        [grad_side],
        bundle_c,
        size_short,
        work=pixels * field.shape[1] * wide,
    )
    back_one = wave([back_d], sums, back_one)
    back_one, side_grad = lax.optimization_barrier((back_one, side_grad))
    wave([back_c, back_d], back_one)
    grad_first, field_grad = launch(
        first_back,
        [short(full, narrow), short(ranks, full, channels)],
        [core, act_one_grad, pre_one, sums_one, back_one, counts, narrow_all, mask_in,
         side_grad],
        bundle_a,
        unit_in,
        [(full, narrow)],
        work=field.size * narrow,
    )
    bundle = chunks_into(None, unit_in * column // 128, 0, field, grad_first, 1, unit_in, column)
    back_e = Scatter(*bundle, False)
    wave([back_e])
    input_grad = lax.all_to_all(field_grad, "mp", 0, 0, tiled=True)
    input_grad = input_grad.reshape(ranks, 4, pixels, channels).transpose(3, 1, 0, 2)
    input_grad = input_grad.reshape(inputs.shape)
    wave([back_c, back_d, back_e])
    wave([back_d, back_e])
    rows_a, rows_b, rows_c, rows_d, rows_e = [
        flow.rows() for flow in (back_a, back_b, back_c, back_d, back_e)
    ]
    first_fix = 1.0 - BETA_ONE**STEP
    second_fix = 1.0 - BETA_TWO**STEP

    def like(*values):
        return [real(*value.shape) for value in values for _ in range(3)]

    early = launch(
        functools.partial(early_moves, column),
        like(shortcut_weight, last_weight, second_weight) + [real(8, 128)],
        [rows_a, rows_c]
        + [
            shortcut_mean, shortcut_square, shortcut_weight, last_mean, last_square, last_weight,
            second_mean, second_square, second_weight,
        ],
    )
    late = launch(
        late_moves,
        like(first_weight, middle_weight) + [real(devices, 16, 128)],
        [rows_b, rows_d, rows_e, early[-1]]
        + [first_mean, first_square, first_weight, middle_mean, middle_square, middle_weight],
    )
    powers = exchange(late[-1])
    weights = (first_weight, shortcut_weight, middle_weight, last_weight, second_weight)
    updates = (late[2], early[2], late[5], early[5], early[8])
    norms, *fresh = launch(
        final_moves,
        [real(16, 128)]
        + [real(*value.shape) for value in weights]
        + [short(*value.shape) for value in weights],
        [powers]
        + [value for pair in zip(weights, updates) for value in pair],
    )
    matrix_norms = norms[:14, 0].reshape(7, 2)
    first_next, short_next, middle_next, last_next, second_next = fresh[:5]
    states = [late[0:2], early[0:2], late[3:5], early[3:5], early[6:8]]

    def own_channels(values):
        width = values.shape[-1] // ranks
        return lax.dynamic_slice_in_dim(values, rank * width, width, values.ndim - 1)

    narrow_grads = jnp.stack([jnp.sum(rows, 0) for rows in (back_one, back_two, back_four, back_five)])
    narrow_grad = own_channels(narrow_grads.reshape(4, 2, narrow))
    gain_three, gain_side, bias_pair = jnp.sum(back_pair, 0).reshape(3, wide)
    wide_grad = own_channels(
        jnp.stack(
            [
                jnp.stack([gain_three, bias_pair]),
                jnp.stack([gain_side, bias_pair]),
                jnp.sum(back_six, 0).reshape(2, wide),
            ]
        )
    )
    narrow_mean_next, narrow_square_next, narrow_step = adapt(
        narrow_grad, narrow_mean, narrow_square, first_fix, second_fix
    )
    wide_mean_next, wide_square_next, wide_step = adapt(
        wide_grad, wide_mean, wide_square, first_fix, second_fix
    )
    return (
        block_output,
        input_grad,
        states[0][0],
        states[0][1],
        first_next,
        states[1][0],
        states[1][1],
        short_next,
        states[2][0],
        states[2][1],
        middle_next,
        states[3][0],
        states[3][1],
        last_next,
        states[4][0],
        states[4][1],
        second_next,
        narrow_mean_next,
        narrow_square_next,
        narrow_norms - RATE_NORM * narrow_step,
        wide_mean_next,
        wide_square_next,
        wide_norms - RATE_NORM * wide_step,
        matrix_norms,
        *fresh[5:],
    )


def solution(mesh):
    in_specs = (
        P("mp", None, "dp"),
        P(None, "dp"),
        P(),
        P("mp", "dp"),
        P("dp", "mp"),
        P("dp", "mp"),
        P(None, None, "dp", "mp"),
        P(None, "mp", "dp"),
        P("dp", "mp"),
        P(None, None, "mp"),
        P(None, None, "mp"),
        P("dp", "mp"),
        P("dp", "mp"),
        P("dp", "mp"),
        P("dp", "mp"),
        P(None, None, "dp", "mp"),
        P(None, None, "dp", "mp"),
        P(None, "mp", "dp"),
        P(None, "mp", "dp"),
        P("dp", "mp"),
        P("dp", "mp"),
        P(None, None, "mp"),
        P(None, None, "mp"),
        P(None, None, "mp"),
        P(None, None, "mp"),
    )
    out_specs = (
        P("mp", "dp"),
        P("mp", None, "dp"),
        P("dp", "mp"),
        P("dp", "mp"),
        P("dp", "mp"),
        P("dp", "mp"),
        P("dp", "mp"),
        P("dp", "mp"),
        P(None, None, "dp", "mp"),
        P(None, None, "dp", "mp"),
        P(None, None, "dp", "mp"),
        P(None, "mp", "dp"),
        P(None, "mp", "dp"),
        P(None, "mp", "dp"),
        P("dp", "mp"),
        P("dp", "mp"),
        P("dp", "mp"),
        P(None, None, "mp"),
        P(None, None, "mp"),
        P(None, None, "mp"),
        P(None, None, "mp"),
        P(None, None, "mp"),
        P(None, None, "mp"),
        P(),
        P("dp", "mp"),
        P("dp", "mp"),
        P(None, None, "dp", "mp"),
        P(None, "mp", "dp"),
        P("dp", "mp"),
    )
    return jax.shard_map(
        lambda *values: (by_image if fits(mesh, values[1]) else shards)(*values),
        mesh=mesh,
        in_specs=in_specs,
        out_specs=out_specs,
        check_vma=False,
    )
```

```python
import functools

import jax
import jax.numpy as jnp
from jax import lax
from jax.experimental import pallas as pl
from jax.experimental.pallas import tpu as pltpu
from jax.sharding import PartitionSpec as P

HO = 16
WO = 11
STEP = 10


EPS_NORM = 1e-05
BETA_ONE = 0.9
BETA_TWO = 0.999
EPS_ADAM = 1e-06
DECAY = 0.01
RATE = 0.3
RATE_NORM = 0.3
EPS_TRUST = 1e-06
PHASES = ((1, -1), (0, 0), (1, 0))
STRIDED_TAPS = tuple(
    (
        (
            3 * above + beside,
            2 * PHASES[above][0] + PHASES[beside][0],
            PHASES[above][1],
            PHASES[beside][1],
        )
        for above in range(3)
        for beside in range(3)
    )
)
PLAIN_TAPS = tuple(
    ((3 * above + beside, 0, above - 1, beside - 1) for above in range(3) for beside in range(3))
)


def slope(values):
    gate = jax.nn.sigmoid(values)
    return gate * (1.0 + values * (1.0 - gate))


def shifted(values, drow, dcol):
    length = values.shape[1]
    offset = drow * WO + dcol
    place = lax.iota(jnp.int32, length)
    row_at = place // WO % HO + drow
    col_at = place % WO + dcol
    inside = (row_at >= 0) & (row_at < HO) & (col_at >= 0) & (col_at < WO)
    moved = jnp.roll(values, -offset, axis=1)
    return jnp.where(inside[None, :], moved, jnp.zeros_like(moved))


def over_images(first, second):
    return lax.psum((first, second), "dp")


def moments(values, mask):
    weighted = values * mask[None, :]
    return over_images(jnp.sum(weighted, 1), jnp.sum(weighted * values, 1))


def normalize(values, totals, squares, count, gain, bias):
    mean = totals / count
    scale = lax.rsqrt(squares / count - mean * mean + EPS_NORM)
    centred = (values - mean[:, None]) * scale[:, None]
    return (centred, scale, centred * gain[:, None] + bias[:, None])


def back_sums(grad_in, centred):
    return over_images(jnp.sum(grad_in * centred, 1), jnp.sum(grad_in, 1))


def norm_back(grad_in, centred, scale, gain, mask, gain_sum, bias_sum, count):
    return (gain * scale)[:, None] * (
        grad_in - mask[None, :] * (bias_sum[:, None] + centred * gain_sum[:, None]) / count
    )


def input_mix(values, weight, side_weight, pixels):
    start_sum = (jnp.zeros((weight.shape[1], values.shape[1]), jnp.float32),)
    if side_weight is not None:
        start_sum = start_sum + (jnp.zeros((side_weight.shape[1], pixels), jnp.float32),)
    piece = lax.all_gather(values, "mp", axis=0, tiled=True)
    result = (jnp.einsum("kc,kp->cp", weight, piece, preferred_element_type=jnp.float32),)
    if side_weight is not None:
        result = result + (
            jnp.einsum(
                "kc,kp->cp", side_weight, piece[:, :pixels], preferred_element_type=jnp.float32
            ),
        )
    return result


def mid_gathered(hidden):
    return lax.all_gather(hidden, "mp", axis=0, tiled=True)


def conv_forward(gathered, kernel, taps, pixels):
    result = jnp.zeros((kernel.shape[2], pixels), jnp.float32)
    for tap, phase, drow, dcol in taps:
        source = gathered[:, phase * pixels : (phase + 1) * pixels]
        part = jnp.einsum("kc,kp->cp", kernel[tap], source, preferred_element_type=jnp.float32)
        result = result + shifted(part, drow, dcol)
    return result


def conv_backward(grad_b, gathered, kernel, taps, pixels, phases):
    moved = [shifted(grad_b, -drow, -dcol) for tap, phase, drow, dcol in taps]
    count = gathered.shape[0] // lax.axis_size("mp") * lax.axis_size("mp")
    blocks = []
    for target in range(phases):
        result = jnp.zeros((count, pixels), jnp.float32)
        for conv_index, (conv_tap, conv_phase, conv_drow, conv_dcol) in enumerate(taps):
            if conv_phase == target:
                part = kernel[conv_tap]
                result = result + jnp.dot(
                    part, moved[conv_index], preferred_element_type=jnp.float32
                )
        blocks.append(result)
    hidden_grad = lax.psum_scatter(
        jnp.concatenate(blocks, 1), "mp", scatter_dimension=0, tiled=True
    )
    kernel_grad = jnp.stack(
        [
            jnp.einsum(
                "kp,cp->kc",
                gathered[:, phase * pixels : (phase + 1) * pixels],
                moved[index],
                preferred_element_type=jnp.float32,
            )
            for index, (tap, phase, drow, dcol) in enumerate(taps)
        ]
    )
    return (hidden_grad, kernel_grad)


def output_mix(hidden, kernel):
    return lax.psum_scatter(
        jnp.einsum("kc,kp->cp", kernel, hidden, preferred_element_type=jnp.float32),
        "mp",
        scatter_dimension=0,
        tiled=True,
    )


def output_back(grad_b, kernel, hidden):
    piece = lax.all_gather(grad_b, "mp", axis=0, tiled=True)
    hidden_grad = jnp.dot(kernel, piece, preferred_element_type=jnp.float32)
    columns = jnp.einsum("cp,kp->ck", hidden, piece, preferred_element_type=jnp.float32)
    return (hidden_grad, columns)


def input_back(values, grad_b, side_b, weight, side_weight, pixels):
    width = weight.shape[1]
    result = jnp.dot(weight, grad_b, preferred_element_type=jnp.float32)
    if side_weight is not None:
        result = jnp.concatenate(
            [
                result[:, :pixels]
                + jnp.dot(side_weight, side_b, preferred_element_type=jnp.float32),
                result[:, pixels:],
            ],
            1,
        )
    values_grad = lax.psum_scatter(result, "mp", scatter_dimension=0, tiled=True)
    piece = lax.all_gather(values, "mp", axis=0, tiled=True)
    blocks = [jnp.einsum("kp,cp->kc", piece, grad_b, preferred_element_type=jnp.float32)]
    if side_weight is not None:
        blocks.append(
            jnp.einsum("kp,cp->kc", piece[:, :pixels], side_b, preferred_element_type=jnp.float32)
        )
    joined = jnp.concatenate(blocks, 1)
    return (values_grad, joined[:, :width], joined[:, width:])


def adapt(grad_in, mean, square, first_fix, second_fix):
    mean_next = BETA_ONE * mean + (1.0 - BETA_ONE) * grad_in
    square_next = BETA_TWO * square + (1.0 - BETA_TWO) * grad_in * grad_in
    step = mean_next / first_fix / (jnp.sqrt(square_next / second_fix) + EPS_ADAM)
    return (mean_next, square_next, step)


def shards(
    inputs,
    pixel_mask,
    widths,
    output_grad,
    first_weight,
    shortcut_weight,
    middle_weight,
    last_weight,
    second_weight,
    narrow_norms,
    wide_norms,
    first_mean,
    first_square,
    shortcut_mean,
    shortcut_square,
    middle_mean,
    middle_square,
    last_mean,
    last_square,
    second_mean,
    second_square,
    narrow_mean,
    narrow_square,
    wide_mean,
    wide_square,
):
    pixels = pixel_mask.shape[1]
    width = first_weight.shape[1]
    rank = lax.axis_index("mp")
    channel = rank * width + lax.iota(jnp.int32, width)
    keep_one = (channel < widths[0]).astype(jnp.float32)[:, None]
    keep_two = (channel < widths[1]).astype(jnp.float32)[:, None]
    masks = pixel_mask.astype(jnp.float32)
    mask_in = masks.reshape(-1)
    mask_out = masks[0]
    field = (inputs * pixel_mask.astype(jnp.bfloat16)[None]).reshape(inputs.shape[0], -1)
    first_w, short_w, middle_w, last_w, second_w = (
        lax.all_gather(first_weight.astype(jnp.bfloat16), "dp", axis=0, tiled=True),
        lax.all_gather(shortcut_weight.astype(jnp.bfloat16), "dp", axis=0, tiled=True),
        lax.all_gather(middle_weight.astype(jnp.bfloat16), "dp", axis=2, tiled=True),
        lax.all_gather(last_weight.astype(jnp.bfloat16), "dp", axis=2, tiled=True),
        lax.all_gather(second_weight.astype(jnp.bfloat16), "dp", axis=0, tiled=True),
    )
    count_in, count_out = over_images(jnp.sum(mask_in), jnp.sum(mask_out))
    pre_one, pre_side = input_mix(field, first_w, short_w, pixels)
    totals, squares = moments(pre_one, mask_in)
    cen_one, scale_one, act_one = normalize(
        pre_one, totals, squares, count_in, narrow_norms[0, 0], narrow_norms[0, 1]
    )
    hid_one = (jax.nn.silu(act_one) * mask_in[None, :] * keep_one).astype(jnp.bfloat16)
    gat_one = mid_gathered(hid_one)
    pre_two = conv_forward(gat_one, middle_w[0], STRIDED_TAPS, pixels)
    totals, squares = moments(pre_two, mask_out)
    cen_two, scale_two, act_two = normalize(
        pre_two, totals, squares, count_out, narrow_norms[1, 0], narrow_norms[1, 1]
    )
    hid_two = (jax.nn.silu(act_two) * mask_out[None, :] * keep_one).astype(jnp.bfloat16)
    pre_three = output_mix(hid_two, last_w[0])
    weighted_three = pre_three * mask_out[None, :]
    weighted_side = pre_side * mask_out[None, :]
    totals, squares = over_images(
        jnp.stack([jnp.sum(weighted_three, 1), jnp.sum(weighted_side, 1)]),
        jnp.stack([jnp.sum(weighted_three * pre_three, 1), jnp.sum(weighted_side * pre_side, 1)]),
    )
    cen_three, scale_three, act_three = normalize(
        pre_three, totals[0], squares[0], count_out, wide_norms[0, 0], wide_norms[0, 1]
    )
    cen_side, scale_side, act_side = normalize(
        pre_side, totals[1], squares[1], count_out, wide_norms[1, 0], wide_norms[1, 1]
    )
    total_one = act_three + act_side
    out_one = (jax.nn.silu(total_one) * mask_out[None, :]).astype(jnp.bfloat16)
    (pre_four,) = input_mix(out_one, second_w, None, pixels)
    totals, squares = moments(pre_four, mask_out)
    cen_four, scale_four, act_four = normalize(
        pre_four, totals, squares, count_out, narrow_norms[2, 0], narrow_norms[2, 1]
    )
    hid_four = (jax.nn.silu(act_four) * mask_out[None, :] * keep_two).astype(jnp.bfloat16)
    gat_four = mid_gathered(hid_four)
    pre_five = conv_forward(gat_four, middle_w[1], PLAIN_TAPS, pixels)
    totals, squares = moments(pre_five, mask_out)
    cen_five, scale_five, act_five = normalize(
        pre_five, totals, squares, count_out, narrow_norms[3, 0], narrow_norms[3, 1]
    )
    hid_five = (jax.nn.silu(act_five) * mask_out[None, :] * keep_two).astype(jnp.bfloat16)
    pre_six = output_mix(hid_five, last_w[1])
    totals, squares = moments(pre_six, mask_out)
    cen_six, scale_six, act_six = normalize(
        pre_six, totals, squares, count_out, wide_norms[2, 0], wide_norms[2, 1]
    )
    total_two = act_six + out_one.astype(jnp.float32)
    block_output = (jax.nn.silu(total_two) * mask_out[None, :]).astype(jnp.bfloat16)
    grad_two = output_grad.astype(jnp.float32) * mask_out[None, :] * slope(total_two)
    gain_six, bias_six = back_sums(grad_two, cen_six)
    grad_six = norm_back(
        grad_two, cen_six, scale_six, wide_norms[2, 0], mask_out, gain_six, bias_six, count_out
    ).astype(jnp.bfloat16)
    hid_five_grad, last_one_grad = output_back(grad_six, last_w[1], hid_five)
    act_five_grad = hid_five_grad * keep_two * mask_out[None, :] * slope(act_five)
    gain_five, bias_five = back_sums(act_five_grad, cen_five)
    grad_five = norm_back(
        act_five_grad,
        cen_five,
        scale_five,
        narrow_norms[3, 0],
        mask_out,
        gain_five,
        bias_five,
        count_out,
    ).astype(jnp.bfloat16)
    hid_four_grad, middle_one_grad = conv_backward(
        grad_five, gat_four, middle_w[1], PLAIN_TAPS, pixels, 1
    )
    act_four_grad = hid_four_grad * keep_two * mask_out[None, :] * slope(act_four)
    gain_four, bias_four = back_sums(act_four_grad, cen_four)
    grad_four = norm_back(
        act_four_grad,
        cen_four,
        scale_four,
        narrow_norms[2, 0],
        mask_out,
        gain_four,
        bias_four,
        count_out,
    ).astype(jnp.bfloat16)
    out_one_grad, second_grad, unused_side = input_back(
        out_one, grad_four, None, second_w, None, pixels
    )
    grad_one = (grad_two + out_one_grad) * mask_out[None, :] * slope(total_one)
    gains_pair, bias_pair = over_images(
        jnp.stack([jnp.sum(grad_one * cen_three, 1), jnp.sum(grad_one * cen_side, 1)]),
        jnp.sum(grad_one, 1),
    )
    grad_three = norm_back(
        grad_one,
        cen_three,
        scale_three,
        wide_norms[0, 0],
        mask_out,
        gains_pair[0],
        bias_pair,
        count_out,
    ).astype(jnp.bfloat16)
    grad_side = norm_back(
        grad_one,
        cen_side,
        scale_side,
        wide_norms[1, 0],
        mask_out,
        gains_pair[1],
        bias_pair,
        count_out,
    ).astype(jnp.bfloat16)
    hid_two_grad, last_zero_grad = output_back(grad_three, last_w[0], hid_two)
    act_two_grad = hid_two_grad * keep_one * mask_out[None, :] * slope(act_two)
    gain_two, bias_two = back_sums(act_two_grad, cen_two)
    grad_mid = norm_back(
        act_two_grad,
        cen_two,
        scale_two,
        narrow_norms[1, 0],
        mask_out,
        gain_two,
        bias_two,
        count_out,
    ).astype(jnp.bfloat16)
    hid_one_grad, middle_zero_grad = conv_backward(
        grad_mid, gat_one, middle_w[0], STRIDED_TAPS, pixels, 4
    )
    act_one_grad = hid_one_grad * keep_one * mask_in[None, :] * slope(act_one)
    gain_one, bias_one = back_sums(act_one_grad, cen_one)
    grad_first = norm_back(
        act_one_grad, cen_one, scale_one, narrow_norms[0, 0], mask_in, gain_one, bias_one, count_in
    ).astype(jnp.bfloat16)
    field_grad, first_grad, short_grad = input_back(
        field, grad_first, grad_side, first_w, short_w, pixels
    )
    input_grad = (field_grad * mask_in[None, :]).astype(jnp.bfloat16).reshape(inputs.shape)
    grads = (
        lax.psum_scatter(first_grad, "dp", scatter_dimension=0, tiled=True),
        lax.psum_scatter(short_grad, "dp", scatter_dimension=0, tiled=True),
        lax.psum_scatter(
            jnp.stack([middle_zero_grad, middle_one_grad]), "dp", scatter_dimension=2, tiled=True
        ),
        lax.psum_scatter(
            jnp.stack([last_zero_grad, last_one_grad]), "dp", scatter_dimension=2, tiled=True
        ),
        lax.psum_scatter(second_grad, "dp", scatter_dimension=0, tiled=True),
    )
    first_fix = 1.0 - BETA_ONE**STEP
    second_fix = 1.0 - BETA_TWO**STEP
    weights = (first_weight, shortcut_weight, middle_weight, last_weight, second_weight)
    means = (first_mean, shortcut_mean, middle_mean, last_mean, second_mean)
    squares_old = (first_square, shortcut_square, middle_square, last_square, second_square)
    states = []
    updates = []
    for index in range(5):
        mean_next, square_next, step = adapt(
            grads[index], means[index], squares_old[index], first_fix, second_fix
        )
        states.append((mean_next, square_next))
        updates.append(step + DECAY * weights[index])
    pairs = [
        (weights[0], updates[0]),
        (weights[1], updates[1]),
        (weights[2][0], updates[2][0]),
        (weights[2][1], updates[2][1]),
        (weights[3][0], updates[3][0]),
        (weights[3][1], updates[3][1]),
        (weights[4], updates[4]),
    ]
    partial_value = jnp.stack(
        [
            jnp.stack([jnp.sum(weight * weight), jnp.sum(update * update)])
            for weight, update in pairs
        ]
    )
    matrix_norms = jnp.sqrt(lax.psum(partial_value, ("dp", "mp")))
    ratio = matrix_norms[:, 0] / (matrix_norms[:, 1] + EPS_TRUST)
    first_next = first_weight - RATE * ratio[0] * updates[0]
    short_next = shortcut_weight - RATE * ratio[1] * updates[1]
    middle_next = middle_weight - RATE * ratio[2:4].reshape(2, 1, 1, 1) * updates[2]
    last_next = last_weight - RATE * ratio[4:6].reshape(2, 1, 1) * updates[3]
    second_next = second_weight - RATE * ratio[6] * updates[4]
    narrow_grad = jnp.stack(
        [
            jnp.stack([gain_one, bias_one]),
            jnp.stack([gain_two, bias_two]),
            jnp.stack([gain_four, bias_four]),
            jnp.stack([gain_five, bias_five]),
        ]
    )
    wide_grad = jnp.stack(
        [
            jnp.stack([gains_pair[0], bias_pair]),
            jnp.stack([gains_pair[1], bias_pair]),
            jnp.stack([gain_six, bias_six]),
        ]
    )
    narrow_mean_next, narrow_square_next, narrow_step = adapt(
        narrow_grad, narrow_mean, narrow_square, first_fix, second_fix
    )
    wide_mean_next, wide_square_next, wide_step = adapt(
        wide_grad, wide_mean, wide_square, first_fix, second_fix
    )
    return (
        block_output,
        input_grad,
        states[0][0],
        states[0][1],
        first_next,
        states[1][0],
        states[1][1],
        short_next,
        states[2][0],
        states[2][1],
        middle_next,
        states[3][0],
        states[3][1],
        last_next,
        states[4][0],
        states[4][1],
        second_next,
        narrow_mean_next,
        narrow_square_next,
        narrow_norms - RATE_NORM * narrow_step,
        wide_mean_next,
        wide_square_next,
        wide_norms - RATE_NORM * wide_step,
        matrix_norms,
        first_next.astype(jnp.bfloat16),
        short_next.astype(jnp.bfloat16),
        middle_next.astype(jnp.bfloat16),
        last_next.astype(jnp.bfloat16),
        second_next.astype(jnp.bfloat16),
    )


VMEM_BYTES = 62 * 2**20
LIGHT = pl.CostEstimate(flops=1024, bytes_accessed=1024, transcendentals=0)


def fits(mesh, pixel_mask):
    sizes = (mesh.shape["dp"], mesh.shape["mp"])
    powers = all(size >= 2 and size & (size - 1) == 0 for size in sizes)
    return powers and pixel_mask.shape[1] % (HO * WO * sizes[1]) == 0


def swap(values, *bits):
    sizes = {axis: lax.axis_size(axis) for axis in ("dp", "mp")}
    masks = {axis: sum(mask for at, mask in bits if at == axis) for axis in sizes}
    if not masks["dp"]:
        return lax.ppermute(values, "mp", [(at, at ^ masks["mp"]) for at in range(sizes["mp"])])
    if not masks["mp"]:
        return lax.ppermute(values, "dp", [(at, at ^ masks["dp"]) for at in range(sizes["dp"])])
    mask = masks["dp"] * sizes["mp"] + masks["mp"]
    return lax.ppermute(
        values, ("dp", "mp"), [(at, at ^ mask) for at in range(sizes["dp"] * sizes["mp"])]
    )


def subsets(bits):
    return [
        [bit for place, bit in enumerate(bits) if index >> place & 1]
        for index in range(1 << len(bits))
    ]


def bit_of(axis, mask):
    return (lax.axis_index(axis) & mask) // mask


def high_bits(axis):
    masks = []
    mask = lax.axis_size(axis) // 2
    while mask:
        masks.append(mask)
        mask //= 2
    return masks


def everywhere(values, flows=()):
    mask = 1
    while mask < lax.axis_size("mp"):
        values = values + swap(values, ("mp", mask))
        mask *= 2
    copies = jnp.broadcast_to(values[None], (lax.axis_size("dp"),) + values.shape)
    arrived = lax.all_to_all(copies, "dp", 0, 0, tiled=True)
    return wave(flows, values, arrived) if flows else arrived


def pack(block):
    lead, rows, cols = block.shape
    parts = block.reshape(lead, rows, cols // 128, 128).transpose(0, 2, 1, 3)
    return parts.reshape(-1, 128)


def column_bits():
    return [("mp", mask) for mask in high_bits("mp")[:-1]]


def row_bits():
    return [("dp", mask) for mask in high_bits("dp")]


def lanes_of(rows):
    first = rows // 32 * 16
    return ((0, first), (first, rows))


def moves_kernel(tasks, count, places, *refs):
    sources, outs, sems = refs[:count], refs[count:-1], refs[-1]
    copies = []
    for at, (source, span, out, turns, rows) in enumerate(tasks):
        dims = len(sources[source].shape) - 2
        every = [slice(None)] * dims
        start = [
            pl.ds(1 - places[dim] if turns[dim] else places[dim], 1) if dim in turns else slice(None)
            for dim in range(dims)
        ]
        copies.append(
            pltpu.make_async_copy(
                sources[source].at[(*every, pl.ds(*span), slice(None))],
                outs[out].at[(*start, pl.ds(*rows), slice(None))],
                sems.at[at],
            )
        )
        copies[-1].start()
    for copy in copies:
        copy.wait()


def moves(wanted):
    sources = []
    tasks = []
    for out, (shape, pieces) in enumerate(wanted):
        for source, span, turns, rows in pieces:
            tasks.append((len(sources), span, out, turns, rows))
            sources.append(source)
    bits = column_bits() + row_bits()
    places = jnp.stack([bit_of(*bit) for bit in bits]).astype(jnp.int32)
    return pl.pallas_call(
        functools.partial(moves_kernel, tasks, len(sources)),
        in_specs=[pl.BlockSpec(memory_space=pltpu.SMEM)]
        + [pl.BlockSpec(memory_space=pltpu.HBM)] * len(sources),
        out_specs=[pl.BlockSpec(memory_space=pltpu.VMEM)] * len(wanted),
        out_shape=[jax.ShapeDtypeStruct(shape, jnp.bfloat16) for shape, _ in wanted],
        scratch_shapes=[pltpu.SemaphoreType.DMA((len(tasks),))],
        compiler_params=pltpu.CompilerParams(vmem_limit_bytes=VMEM_BYTES),
        cost_estimate=LIGHT,
    )(places, *sources)


class Gather:
    def __init__(self, rows, lanes=True):
        self.dims = column_bits() + row_bits()
        near = row_bits()[-1:]
        self.rows = rows.shape[0]
        if lanes:
            self.steps = [[row_bits()[:-1]], [near, column_bits()], [column_bits(), near]]
            self.spans = lanes_of(self.rows)
        else:
            self.steps = [[row_bits()[:-1]], [near + column_bits()]]
            self.spans = ((0, self.rows),)
        self.parts = [([rows.reshape((1,) * len(self.dims) + rows.shape)], [])]
        self.step = 0

    def pending(self):
        return [values for values, bits in self.parts]

    def resume(self, values):
        self.parts = [(value, bits) for value, (_, bits) in zip(values, self.parts)]

    def wanted(self):
        if not self.parts[0][1]:
            return []
        last = self.step == len(self.steps)
        split = not last and len(self.steps[self.step]) > len(self.parts)
        lanes = [(low, high - low) for low, high in self.spans]
        result = []
        for lane, (values, bits) in enumerate(self.parts):
            shape = [
                2 if bit in bits else size
                for bit, size in zip(self.dims, values[0].shape)
            ]
            pieces = [
                (value, {self.dims.index(bit): bit in turned for bit in bits})
                for value, turned in zip(values, subsets(bits))
            ]
            height = values[0].shape[-2]
            for low, size in lanes if split else [(0, height)]:
                block = [(value, (low, size), turns, (0, size)) for value, turns in pieces]
                result.append((tuple(shape) + (size, 128), block))
        if last:
            pieces = [
                (value, span, turns, lanes[lane])
                for lane, (_, block) in enumerate(result)
                for value, span, turns, _ in block
            ]
            result = [(result[0][0][:-2] + (self.rows, 128), pieces)]
        return result

    def launch(self, values):
        if not values:
            values = [self.parts[0][0][0]]
        if self.step < len(self.steps):
            self.parts = [
                ([value] + [swap(value, *bits) for bits in subsets(group)[1:]], group)
                for value, group in zip(values, self.steps[self.step])
            ]
        else:
            self.parts = [([values[0], swap(values[0], ("mp", 1))], [])]
        self.step += 1
        return values

    def bundles(self):
        shape = (1 << len(column_bits()), lax.axis_size("dp")) + self.parts[0][0][0].shape[-2:]
        return [value.reshape(shape) for value in self.parts[0][0]]


class Scatter:
    def __init__(self, keep, send, lanes=True):
        self.dims = column_bits() + row_bits()
        shape = (2,) * len(self.dims) + keep.shape[2:]
        near = row_bits()[-1:]
        far = row_bits()[:-1]
        if lanes:
            self.steps = [None, [column_bits(), near], [near, column_bits()], [far, far]]
            self.spans = lanes_of(keep.shape[2])
        else:
            self.steps = [None, [column_bits() + near], [far]]
            self.spans = (None,)
        self.lanes = [[] for _ in self.spans]
        self.raw = [keep.reshape(shape), send.reshape(shape)]
        self.step = 0

    def pending(self):
        return self.raw

    def resume(self, values):
        self.raw = list(values)

    def fold(self, lane, group=(), turned=()):
        total = 0.0
        for index, settled, span in self.lanes[lane]:
            value = self.raw[index]
            for bit in settled + list(group):
                place = bit_of(*bit)
                place = 1 - place if bit in turned else place
                value = lax.dynamic_slice_in_dim(value, place, 1, self.dims.index(bit))
            if span is not None:
                value = value[..., span[0] : span[1], :]
            total = total + value.astype(jnp.float32)
        return total

    def settle(self, lane, group, arrived, span):
        old = [(index, settled + group, part) for index, settled, part in self.lanes[lane]]
        self.lanes[lane] = old + [(index, [], span) for index in arrived]

    def wanted(self):
        return []

    def launch(self, values):
        groups = self.steps[self.step]
        whole = self.step == len(self.steps) - 1
        sent = []
        if groups is None:
            sent.append(self.raw[1])
            self.raw[1] = swap(self.raw[1], ("mp", 1))
            for lane, span in zip(self.lanes, self.spans):
                lane += [(0, [], span), (1, [], span)]
        elif whole:
            arrived = []
            for bits in subsets(groups[0])[1:]:
                out = [
                    self.fold(lane, groups[0], bits).astype(jnp.bfloat16)
                    for lane in range(len(self.lanes))
                ]
                out = jnp.concatenate(out, -2) if len(out) > 1 else out[0]
                arrived.append(len(self.raw))
                sent.append(out)
                self.raw.append(swap(out, *bits))
            for lane, span in enumerate(self.spans):
                self.settle(lane, groups[lane], arrived, span)
        else:
            for lane, group in enumerate(groups):
                arrived = []
                for bits in subsets(group)[1:]:
                    out = self.fold(lane, group, bits).astype(jnp.bfloat16)
                    arrived.append(len(self.raw))
                    sent.append(out)
                    self.raw.append(swap(out, *bits))
                self.settle(lane, group, arrived, None)
        self.step += 1
        return sent

    def rows(self):
        total = [self.fold(lane) for lane in range(len(self.lanes))]
        total = jnp.concatenate(total, -2) if len(total) > 1 else total[0]
        return total.reshape(total.shape[-2:])


def wave(flows, after=None, before=None):
    values = [flow.pending() for flow in flows]
    if after is not None:
        values, _ = lax.optimization_barrier((values, after))
    for flow, value in zip(flows, values):
        flow.resume(value)
    wanted = [flow.wanted() for flow in flows]
    joined = [value for part in wanted for value in part]
    made = list(moves(joined)) if joined else []
    sent = []
    for flow, part in zip(flows, wanted):
        sent += flow.launch([made.pop(0) for _ in part])
    if before is not None:
        before, _ = lax.optimization_barrier((before, sent))
    return before


def chunk_kernel(units, columns, rows_ref, cols_ref, *refs):
    outs = refs[-2:]
    product = lax.dot_general(
        rows_ref[...], cols_ref[...], (((0,), (0,)), ((), ())), preferred_element_type=jnp.float32
    ).astype(jnp.bfloat16)
    groups = outs[0].shape[0]
    chunks = outs[0].shape[1]
    for half, out in enumerate(outs):
        for group in range(groups):
            for part in range(columns):
                place = ((half * groups + group) * columns + part) * 128
                block = product[:, place : place + 128].reshape(chunks, units, 128)
                out[group, :, part * units : (part + 1) * units, :] = block


def chunks_into(bundle, total, start, rows_of, cols_of, lead, units, columns):
    count = lax.axis_size("dp")
    groups = 1 << len(column_bits())
    columns = columns // 128
    pixels = cols_of.shape[0]
    height = units * columns
    if lead > 1:
        steps, wide, chunks = lead, count * units, count
        place = lambda step: (0, 0, start // height + step, 0)
    else:
        steps, wide, chunks = count, units, 1
        place = lambda step: (0, step, start // height, 0)
    shape = jax.ShapeDtypeStruct((groups, count, total, 128), jnp.bfloat16)
    block = pl.BlockSpec((groups, chunks, height, 128), place)
    earlier = () if bundle is None else tuple(bundle)
    return pl.pallas_call(
        functools.partial(chunk_kernel, units, columns),
        grid=(steps,),
        in_specs=[
            pl.BlockSpec((pixels, wide), lambda step: (0, step)),
            pl.BlockSpec(cols_of.shape, lambda step: (0, 0)),
        ]
        + [pl.BlockSpec(memory_space=pltpu.HBM)] * len(earlier),
        out_specs=[block, block],
        out_shape=[shape, shape],
        input_output_aliases={2 + place: place for place in range(len(earlier))},
        compiler_params=pltpu.CompilerParams(vmem_limit_bytes=VMEM_BYTES),
        cost_estimate=LIGHT,
    )(rows_of, cols_of, *earlier)


def total_of(ref):
    return jnp.sum(ref[...], 0) if len(ref.shape) == 3 else ref[...]


def as_row(block):
    return jnp.concatenate([block[place : place + 1] for place in range(block.shape[0])], 1)


def as_rows(row):
    return jnp.concatenate(
        [row[:, place : place + 128] for place in range(0, row.shape[1], 128)], 0
    )


def hand_out(out, rows):
    missing = out.shape[-2] - sum(row.shape[0] for row in rows)
    if missing:
        rows = rows + [jnp.zeros((missing, 128), jnp.float32)]
    block = jnp.concatenate(rows, 0)
    out[...] = jnp.broadcast_to(block[None], out.shape) if len(out.shape) == 3 else block


def levels(total, first, width, count):
    rows = width // 128
    mean = total[first : first + rows] / count
    scale = lax.rsqrt(total[first + rows : first + 2 * rows] / count - mean * mean + EPS_NORM)
    return (as_row(mean), as_row(scale))


def standard(values, level):
    return (values - level[0]) * level[1]


def back_through(grad, centred, level, gain, mask, total, first, bias_first, count):
    rows = grad.shape[1] // 128
    gain_sum = as_row(total[first : first + rows] / count)
    bias_sum = as_row(total[bias_first : bias_first + rows] / count)
    return (gain * level[1]) * (grad - mask * (bias_sum + centred * gain_sum))


def column_sums(values, mask):
    weighted = values * mask
    return [
        as_rows(jnp.sum(weighted, 0, keepdims=True)),
        as_rows(jnp.sum(weighted * values, 0, keepdims=True)),
    ]


def product_sums(grad, centred):
    return as_rows(jnp.sum(grad * centred, 0, keepdims=True))


def plain_sums(grad):
    return as_rows(jnp.sum(grad, 0, keepdims=True))


def fetch(bundles, held, sems, start):
    rows = held.shape[3]
    copies = [
        pltpu.make_async_copy(ref.at[:, :, pl.ds(start, rows), :], held.at[half], sems.at[half])
        for half, ref in enumerate(bundles)
    ]
    for copy in copies:
        copy.start()
    return copies


def arrive(copies):
    for copy in copies:
        copy.wait()


def weight_part(held, chunk, chunks, start, units, columns):
    return jnp.concatenate(
        [
            held[half, group, chunk : chunk + chunks, start + part * units : start + (part + 1) * units, :]
            .reshape(chunks * units, 128)
            for half in range(2)
            for group in range(held.shape[1])
            for part in range(columns)
        ],
        1,
    )


def spots(core, groups, width):
    return [
        pl.multiple_of((2 * group + (core if half == 0 else 1 - core)) * width, 128)
        for half in range(2)
        for group in range(groups)
    ]


def in_turn(ref, core, groups):
    width = ref.shape[1] // (2 * groups)
    return jnp.concatenate([ref[:, pl.ds(at, width)] for at in spots(core, groups, width)], 1)


def in_order(ref, values, core, groups):
    width = ref.shape[1] // (2 * groups)
    for place, at in enumerate(spots(core, groups, width)):
        ref[:, pl.ds(at, width)] = values[:, place * width : (place + 1) * width]


def product(first, second):
    return lax.dot_general(
        first, second, (((1,), (0,)), ((), ())), preferred_element_type=jnp.float32
    )


def product_turned(first, second):
    return lax.dot_general(
        first, second, (((1,), (1,)), ((), ())), preferred_element_type=jnp.float32
    )


def many_in(values, held, units, columns):
    chunks = max(1, 256 // units)
    total = 0.0
    for chunk in range(0, held.shape[2], chunks):
        part = weight_part(held, chunk, chunks, 0, units, columns)
        total = total + product(
            values[:, chunk * units : (chunk + chunks) * units], part
        )
    return total


def many_out(values, held, units, columns):
    chunks = max(1, 256 // units)
    return [
        product_turned(values, weight_part(held, chunk, chunks, 0, units, columns))
        for chunk in range(0, held.shape[2], chunks)
    ]


def slid(values, offset):
    count = values.shape[0]
    return pltpu.roll(values, (-offset) % count, 0) if offset % count else values


def within(inside, drow, dcol):
    place = 3 * (drow + 1) + dcol + 1
    return inside[:, place : place + 1]


def first_layer(core, raw, mask, first, second, field, out, sums, held, sems):
    copies = fetch((first, second), held, sems, 0)
    core = core[0]
    weights = mask[...]
    width = raw.shape[2]
    for place in range(raw.shape[0]):
        part = raw[place].astype(jnp.float32) * weights
        field[:, place * width : (place + 1) * width] = part.astype(jnp.bfloat16)
    arrive(copies)
    result = many_in(field, held, held.shape[3], 1)
    in_order(out, result, core, held.shape[1])
    rows = column_sums(out[...], weights)
    pixels = weights.shape[0] // 4
    for part in (weights, weights[:pixels]):
        rows.append(jnp.broadcast_to(jnp.sum(part, 0, keepdims=True), (1, 128)))
    hand_out(sums, rows)


def side_layer(start, core, field, mask, first, second, out, sums, held, sems):
    copies = fetch((first, second), held, sems, start)
    core = core[0]
    pixels = mask.shape[0]
    arrive(copies)
    columns = out.shape[1] // (2 * held.shape[1] * 128)
    result = many_in(field[:pixels, :], held, held.shape[3] // columns, columns)
    in_order(out, result, core, held.shape[1])
    hand_out(sums, column_sums(out[...], mask[...]))


def spread_layer(start, norm, taps, core, before, sums_in, counts, tables, keep, mask_in, mask, inside,
                 first, second, cols, out, sums, held, sems):
    copies = fetch((first, second), held, sems, start)
    core = core[0]
    pixels = mask.shape[0]
    width = before.shape[1]
    counted = 0 if before.shape[0] > pixels else 1
    level = levels(total_of(sums_in), 0, width, counts[counted : counted + 1, :])
    act = standard(before[...], level) * tables[2 * norm : 2 * norm + 1, :] + tables[2 * norm + 1 : 2 * norm + 2, :]
    row = norm // 2
    hidden = jax.nn.silu(act) * mask_in[...] * keep[row : row + 1, :]
    for tap, phase, drow, dcol in taps:
        source = hidden[phase * pixels : (phase + 1) * pixels]
        moved = slid(source, drow * WO + dcol) * within(inside, drow, dcol)
        cols[:, tap * width : (tap + 1) * width] = moved.astype(jnp.bfloat16)
    arrive(copies)
    units = held.shape[3] // 9
    total = 0.0
    for tap in range(9):
        part = weight_part(held, 0, held.shape[2], tap * units, units, 1)
        total = total + product(cols[:, tap * width : (tap + 1) * width], part)
    in_order(out, total, core, held.shape[1])
    hand_out(sums, column_sums(out[...], mask[...]))


def widen_layer(start, norm, core, before, sums_in, counts, tables, keep, mask, first, second,
                hidden, out, sums, held, scratch, sems):
    copies = fetch((first, second), held, sems, start)
    core = core[0]
    level = levels(total_of(sums_in), 0, before.shape[1], counts[1:2, :])
    act = standard(before[...], level) * tables[2 * norm : 2 * norm + 1, :] + tables[2 * norm + 1 : 2 * norm + 2, :]
    row = norm // 2
    scratch[...] = jax.nn.silu(act) * mask[...] * keep[row : row + 1, :]
    hidden[...] = in_turn(scratch, core, held.shape[1]).astype(jnp.bfloat16)
    arrive(copies)
    parts = many_out(hidden[...], held, held.shape[3], 1)
    size = out.shape[1] // len(parts)
    for place, part in enumerate(parts):
        out[:, place * size : (place + 1) * size] = part
    hand_out(sums, column_sums(out[...], mask[...]))


def joined_acts(total, third, side, wide, count):
    width = third.shape[1]
    rows = width // 128
    centred_third = standard(third[...], levels(total, 0, width, count))
    centred_side = standard(side[...], levels(total, 2 * rows, width, count))
    act = (
        centred_third * wide[0:1, :]
        + wide[1:2, :]
        + (centred_side * wide[2:3, :] + wide[3:4, :])
    )
    return (centred_third, centred_side, act)


def narrow_layer(start, core, third, side, sums_in, counts, wide, mask, first, second,
                 above, out, sums, held, sems):
    copies = fetch((first, second), held, sems, start)
    core = core[0]
    centred_third, centred_side, act = joined_acts(
        total_of(sums_in), third, side, wide, counts[1:2, :]
    )
    above[...] = (jax.nn.silu(act) * mask[...]).astype(jnp.bfloat16)
    arrive(copies)
    result = many_in(above, held, held.shape[3], 1)
    in_order(out, result, core, held.shape[1])
    hand_out(sums, column_sums(out[...], mask[...]))


def last_layer(sixth, sums_in, counts, wide, above, cotangent, mask, out, grad, sums):
    level = levels(total_of(sums_in), 0, sixth.shape[1], counts[1:2, :])
    centred = standard(sixth[...], level)
    act = centred * wide[4:5, :] + wide[5:6, :] + above[...].astype(jnp.float32)
    weights = mask[...]
    result = (jax.nn.silu(act) * weights).astype(jnp.bfloat16)
    inner = weights * slope(act)
    width = out.shape[2]
    for place in range(out.shape[0]):
        span = slice(place * width, (place + 1) * width)
        out[place] = result[:, span]
        grad[:, span] = cotangent[place].astype(jnp.float32) * inner[:, span]
    result = grad[...]
    hand_out(sums, [product_sums(result, centred), plain_sums(result)])


def narrow_grad(grad, before, sums_in, counts, tables, norm, keep, mask):
    counted = 0 if norm == 0 else 1
    level = levels(total_of(sums_in), 0, before.shape[1], counts[counted : counted + 1, :])
    centred = standard(before[...], level)
    act = centred * tables[2 * norm : 2 * norm + 1, :] + tables[2 * norm + 1 : 2 * norm + 2, :]
    row = norm // 2
    result = grad * keep[row : row + 1, :] * mask * slope(act)
    return (result, [product_sums(result, centred), plain_sums(result)])


def narrow_back(norm, grad, before, sums_in, sums_back, counts, tables, mask):
    counted = 0 if norm == 0 else 1
    count = counts[counted : counted + 1, :]
    width = before.shape[1]
    level = levels(total_of(sums_in), 0, width, count)
    return back_through(
        grad[...],
        standard(before[...], level),
        level,
        tables[2 * norm : 2 * norm + 1, :],
        mask,
        total_of(sums_back),
        0,
        width // 128,
        count,
    )


def last_back(start, norm, core, grad, sixth, sums_six, back_six, counts, wide, before, sums_in, tables,
              keep, mask, first, second, grad_out, grad_in, sums, held, scratch, sems):
    copies = fetch((first, second), held, sems, start)
    core = core[0]
    width = sixth.shape[1]
    count = counts[1:2, :]
    level = levels(total_of(sums_six), 0, width, count)
    grad_out[...] = back_through(
        grad[...], standard(sixth[...], level), level, wide[4:5, :], mask[...], total_of(back_six), 0,
        width // 128, count,
    ).astype(jnp.bfloat16)
    arrive(copies)
    in_order(scratch, many_in(grad_out, held, held.shape[3], 1), core, held.shape[1])
    result, rows = narrow_grad(scratch[...], before, sums_in, counts, tables, norm, keep, mask[...])
    grad_in[...] = result
    hand_out(sums, rows)


def pair_back(start, norm, core, grad, third, side, sums_pair, back_pair, counts, wide, before, sums_in,
              tables, keep, mask, first, second, grad_third, grad_side, grad_in, sums, held, scratch,
              big, sems):
    copies = fetch((first, second), held, sems, start)
    core = core[0]
    width = third.shape[1]
    rows = width // 128
    count = counts[1:2, :]
    total = total_of(sums_pair)
    back = total_of(back_pair)
    groups = held.shape[1]
    level = levels(total, 0, width, count)
    grad_third[...] = back_through(
        grad[...], standard(third[...], level), level, wide[0:1, :], mask[...], back, 0, 2 * rows, count
    ).astype(jnp.bfloat16)
    arrive(copies)
    in_order(scratch, many_in(grad_third, held, held.shape[3], 1), core, groups)
    result, parts = narrow_grad(scratch[...], before, sums_in, counts, tables, norm, keep, mask[...])
    grad_in[...] = result
    hand_out(sums, parts)
    level = levels(total, 2 * rows, width, count)
    big[...] = back_through(
        grad[...], standard(side[...], level), level, wide[2:3, :], mask[...], back, rows, 2 * rows, count
    )
    grad_side[...] = in_turn(big, core, groups).astype(jnp.bfloat16)


def spread_back(start, norm, taps, core, grad, after, sums_after, back_after, counts, tables, before,
                sums_in, keep, mask_in, mask, inside, first, second, grad_out, grad_in, sums, held,
                scratch, sems):
    copies = fetch((first, second), held, sems, start)
    core = core[0]
    pixels = mask.shape[0]
    phases = before.shape[0] // pixels
    scratch[...] = narrow_back(norm + 1, grad, after, sums_after, back_after, counts, tables, mask[...])
    grad_out[...] = in_turn(scratch, core, held.shape[1]).astype(jnp.bfloat16)
    arrive(copies)
    units = held.shape[3] // 9
    totals = [0.0] * phases
    for tap, phase, drow, dcol in taps:
        part = weight_part(held, 0, held.shape[2], tap * units, units, 1)
        moved = product_turned(grad_out[...], part)
        totals[phase] = totals[phase] + slid(moved, -drow * WO - dcol) * within(inside, -drow, -dcol)
    hidden = jnp.concatenate(totals, 0) if phases > 1 else totals[0]
    result, rows = narrow_grad(hidden, before, sums_in, counts, tables, norm, keep, mask_in[...])
    grad_in[...] = result
    hand_out(sums, rows)


def narrow_layer_back(start, core, grad, fourth, sums_four, back_four, counts, tables, mask, grad_two,
                      third, side, sums_pair, wide, first, second, grad_out, grad_in, sums, held,
                      scratch, big, sems):
    copies = fetch((first, second), held, sems, start)
    core = core[0]
    scratch[...] = narrow_back(2, grad, fourth, sums_four, back_four, counts, tables, mask[...])
    grad_out[...] = in_turn(scratch, core, held.shape[1]).astype(jnp.bfloat16)
    arrive(copies)
    parts = many_out(grad_out[...], held, held.shape[3], 1)
    size = big.shape[1] // len(parts)
    for place, part in enumerate(parts):
        big[:, place * size : (place + 1) * size] = part
    centred_third, centred_side, act = joined_acts(
        total_of(sums_pair), third, side, wide, counts[1:2, :]
    )
    result = (grad_two[...] + big[...]) * mask[...] * slope(act)
    grad_in[...] = result
    hand_out(
        sums,
        [
            product_sums(result, centred_third),
            product_sums(result, centred_side),
            plain_sums(result),
        ],
    )


def side_back(start, grad, first, second, out, held, sems):
    copies = fetch((first, second), held, sems, start)
    arrive(copies)
    columns = grad.shape[1] // (2 * held.shape[1] * 128)
    parts = many_out(grad[...], held, held.shape[3] // columns, columns)
    size = out.shape[1] // len(parts)
    for place, part in enumerate(parts):
        out[:, place * size : (place + 1) * size] = part


def first_back(core, grad, before, sums_in, sums_back, counts, tables, mask, side, first, second,
               grad_out, out, held, scratch, sems):
    copies = fetch((first, second), held, sems, 0)
    core = core[0]
    scratch[...] = narrow_back(0, grad, before, sums_in, sums_back, counts, tables, mask[...])
    grad_out[...] = in_turn(scratch, core, held.shape[1]).astype(jnp.bfloat16)
    arrive(copies)
    parts = many_out(grad_out[...], held, held.shape[3], 1)
    size = side.shape[1] // len(parts)
    pixels = side.shape[0]
    weights = mask[...]
    width = out.shape[2]
    for place, part in enumerate(parts):
        owner = place * size // width
        span = slice(place * size % width, place * size % width + size)
        beside = side[:, place * size : (place + 1) * size]
        out[owner, :pixels, span] = ((part[:pixels] + beside) * weights[:pixels]).astype(jnp.bfloat16)
        out[owner, pixels:, span] = (part[pixels:] * weights[pixels:]).astype(jnp.bfloat16)


class Coming:
    def __init__(self, ref, copy):
        self.ref = ref
        self.copy = copy
        self.shape = ref.shape

    def settle(self):
        if self.copy is not None:
            self.copy.wait()
            self.copy = None

    def __getitem__(self, place):
        self.settle()
        return self.ref[place]


def framed(kernel, places, count, *refs):
    refs = list(refs)
    rest, held, sems = refs[: len(refs) - len(places) - 1], refs[-len(places) - 1 : -1], refs[-1]
    coming = []
    for at, place in enumerate(places):
        copy = pltpu.make_async_copy(rest[place], held[at], sems.at[at])
        copy.start()
        rest[place] = Coming(held[at], copy)
        coming.append(rest[place])
    kernel(*rest)
    for value in coming:
        value.settle()


def launch(kernel, shapes, values, bundles=(), rows=0, scratch=()):
    held = []
    sems = []
    if bundles:
        held = [pltpu.VMEM((2,) + bundles[0].shape[:2] + (rows, 128), jnp.bfloat16)]
        sems = [pltpu.SemaphoreType.DMA((2,))]
    places = [place for place, value in enumerate(values) if value.dtype != jnp.int32]
    specs = []
    for place, value in enumerate(values):
        space = pltpu.SMEM if value.dtype == jnp.int32 else pltpu.VMEM
        specs.append(pl.BlockSpec(memory_space=pltpu.HBM if place in places else space))
    late = []
    if places:
        kernel = functools.partial(framed, kernel, places, len(values))
        late = [pltpu.VMEM(values[place].shape, values[place].dtype) for place in places]
        late.append(pltpu.SemaphoreType.DMA((len(places),)))
    return pl.pallas_call(
        kernel,
        in_specs=specs + [pl.BlockSpec(memory_space=pltpu.HBM)] * len(bundles),
        out_specs=[pl.BlockSpec(memory_space=pltpu.VMEM)] * len(shapes),
        out_shape=list(shapes),
        scratch_shapes=held + [pltpu.VMEM(shape, jnp.float32) for shape in scratch] + sems + late,
        compiler_params=pltpu.CompilerParams(vmem_limit_bytes=VMEM_BYTES),
        cost_estimate=LIGHT,
    )(*values, *bundles)


def moved_by(grad, mean, square, weight, mean_out, square_out, update_out, at):
    first_fix = 1.0 - BETA_ONE**STEP
    second_fix = 1.0 - BETA_TWO**STEP
    old = weight[at]
    mean_next, square_next, step = adapt(grad, mean[at], square[at], first_fix, second_fix)
    update = step + DECAY * old
    mean_out[at] = mean_next
    square_out[at] = square_next
    update_out[at] = update
    result = []
    for value in (old, update):
        power = value * value
        while len(power.shape) > 2:
            power = jnp.sum(power, 0)
        row = jnp.sum(power, 0, keepdims=True)
        result.append(
            sum(row[:, place : place + 128] for place in range(0, row.shape[1], 128))
        )
    return result


def early_moves(columns, rows_a, rows_c, short_m, short_v, short_w, last_m, last_v, last_w, second_m, second_v,
                second_w, short_mo, short_vo, short_uo, last_mo, last_vo, last_uo, second_mo, second_vo,
                second_uo, powers):
    unit_in = short_w.shape[0]
    unit_out = second_w.shape[0]
    parts = short_w.shape[1] // 128
    every = (slice(None), slice(None))
    grad = jnp.concatenate(
        [rows_c[part * unit_in : (part + 1) * unit_in, :] for part in range(parts)], 1
    )
    found = moved_by(grad, short_m, short_v, short_w, short_mo, short_vo, short_uo, every)
    start = parts * unit_in
    for block, rows in enumerate((rows_c[start : start + unit_out, :], rows_a[...])):
        found += moved_by(
            jnp.transpose(rows), last_m, last_v, last_w, last_mo, last_vo, last_uo, block
        )
    start += unit_out
    found += moved_by(
        rows_c[start : start + unit_out, :], second_m, second_v, second_w, second_mo, second_vo,
        second_uo, every,
    )
    powers[...] = jnp.concatenate(found, 0)


def late_moves(rows_b, rows_d, rows_e, powers_in, first_m, first_v, first_w, mid_m, mid_v, mid_w, first_mo,
               first_vo, first_uo, mid_mo, mid_vo, mid_uo, powers):
    every = (slice(None), slice(None))
    found = moved_by(
        rows_e[...], first_m, first_v, first_w, first_mo, first_vo, first_uo, every
    )
    shape = mid_w.shape[1:]
    middle = []
    for block, rows in enumerate((rows_d, rows_b)):
        middle += moved_by(
            rows[...].reshape(shape), mid_m, mid_v, mid_w, mid_mo, mid_vo, mid_uo, block
        )
    early = powers_in[...]
    order = [found[0], found[1], early[0:2]] + middle + [early[2:8]]
    hand_out(powers, order)


def final_moves(powers, first_w, first_u, short_w, short_u, mid_w, mid_u, last_w, last_u, second_w, second_u,
                norms, first_o, short_o, mid_o, last_o, second_o, first_c, short_c, mid_c, last_c, second_c):
    total = jnp.sqrt(jnp.sum(jnp.sum(powers[...], 0), 1, keepdims=True))
    norms[...] = jnp.broadcast_to(total, norms.shape)

    def step(row, weight, update, out, copy, at):
        ratio = total[2 * row : 2 * row + 1] / (total[2 * row + 1 : 2 * row + 2] + EPS_TRUST)
        fresh = weight[at] - (RATE * ratio) * update[at]
        out[at] = fresh
        copy[at] = fresh.astype(jnp.bfloat16)

    every = (slice(None), slice(None))
    step(0, first_w, first_u, first_o, first_c, every)
    step(1, short_w, short_u, short_o, short_c, every)
    for block in range(2):
        for tap in range(mid_w.shape[1]):
            step(2 + block, mid_w, mid_u, mid_o, mid_c, (block, tap))
        step(4 + block, last_w, last_u, last_o, last_c, block)
    step(6, second_w, second_u, second_o, second_c, every)


def exchange(copies):
    return lax.all_to_all(copies, ("dp", "mp"), 0, 0, tiled=True)


def by_image(
    inputs,
    pixel_mask,
    widths,
    output_grad,
    first_weight,
    shortcut_weight,
    middle_weight,
    last_weight,
    second_weight,
    narrow_norms,
    wide_norms,
    first_mean,
    first_square,
    shortcut_mean,
    shortcut_square,
    middle_mean,
    middle_square,
    last_mean,
    last_square,
    second_mean,
    second_square,
    narrow_mean,
    narrow_square,
    wide_mean,
    wide_square,
):
    ranks = lax.axis_size("mp")
    rank = lax.axis_index("mp")
    pixels = pixel_mask.shape[1] // ranks
    narrow = first_weight.shape[1] * ranks
    wide = shortcut_weight.shape[1] * ranks
    low = jnp.bfloat16
    channels = inputs.shape[0]
    field = inputs.reshape(channels, 4, ranks, pixels).transpose(2, 1, 3, 0)
    field = field.reshape(ranks, 4 * pixels, channels)
    flow_a = Gather(pack(first_weight.astype(low)[None]), False)
    flow_b = Gather(pack(middle_weight[0].astype(low)))
    flow_c = Gather(
        jnp.concatenate(
            [
                pack(shortcut_weight.astype(low)[None]),
                pack(last_weight[0].astype(low).T[None]),
                pack(second_weight.astype(low)[None]),
            ]
        )
    )
    flow_d = Gather(
        jnp.concatenate(
            [pack(last_weight[1].astype(low).T[None]), pack(middle_weight[1].astype(low))]
        )
    )
    field = lax.all_to_all(field, "mp", 0, 0, tiled=True)
    wave([flow_a, flow_b])
    wave([flow_a, flow_b, flow_c], field)
    wave([flow_a, flow_b, flow_d])
    unit_in, column = first_weight.shape
    column_wide = shortcut_weight.shape[1]
    unit_mid = middle_weight.shape[2]
    unit_out = second_weight.shape[0]
    size_short = unit_in * column_wide // 128
    size_out = unit_out * column // 128
    size_mid = 9 * unit_mid * column // 128
    tables = jnp.concatenate([narrow_norms.reshape(-1, 128), wide_norms.reshape(-1, 128)], 0)
    tables = jnp.broadcast_to(tables[None], (ranks,) + tables.shape)
    tables = lax.all_to_all(tables, "mp", 0, 0, tiled=True)
    split = narrow_norms.size // 128
    narrow_all = (
        tables[:, :split].reshape(ranks, 4, 2, -1).transpose(1, 2, 0, 3).reshape(4, 2, narrow)
    )
    wide_all = tables[:, split:].reshape(ranks, 3, 2, -1).transpose(1, 2, 0, 3).reshape(3, 2, wide)

    narrow_all = narrow_all.reshape(8, narrow)
    wide_all = jnp.concatenate([wide_all.reshape(6, wide), jnp.zeros((2, wide), jnp.float32)], 0)

    own_mask = lax.dynamic_slice_in_dim(pixel_mask, rank * pixels, pixels, 1).astype(jnp.float32)
    mask_in = own_mask.reshape(-1, 1)
    mask = own_mask[0][:, None]
    channel = lax.iota(jnp.int32, narrow)[None]
    keep = (channel < widths[:, None]).astype(jnp.float32)
    keep = jnp.concatenate([keep, jnp.zeros((6, narrow), jnp.float32)], 0)
    place = lax.iota(jnp.int32, pixels)[:, None]
    step = lax.iota(jnp.int32, 9)[None]
    row_at = place // WO % HO + step // 3 - 1
    col_at = place % WO + step % 3 - 1
    inside = (row_at >= 0) & (row_at < HO) & (col_at >= 0) & (col_at < WO)
    inside = inside.astype(jnp.float32)
    core = bit_of("mp", 1)[None]

    above = output_grad.reshape(-1, ranks, pixels).transpose(1, 2, 0)
    above = lax.all_to_all(above, "mp", 0, 0, tiled=True)

    devices = ranks * lax.axis_size("dp")
    full = 4 * pixels

    def real(*shape):
        return jax.ShapeDtypeStruct(shape, jnp.float32)

    def short(*shape):
        return jax.ShapeDtypeStruct(shape, low)

    size = narrow // 128
    wide_rows = wide // 128
    copies = real(devices, 2 * size, 128)
    bundle_a = flow_a.bundles()
    field, pre_one, sums = launch(
        first_layer,
        [short(full, ranks * channels), real(full, narrow), real(devices, 2 * size + 8, 128)],
        [core, field, mask_in],
        bundle_a,
        unit_in,
    )
    sums_one = wave([flow_b, flow_c], sums, exchange(sums))
    counts = jnp.sum(sums_one[:, 2 * size :], 0)
    bundle_b = flow_b.bundles()
    cols_one, pre_two, sums = launch(
        functools.partial(spread_layer, 0, 0, STRIDED_TAPS),
        [short(pixels, 9 * narrow), real(pixels, narrow), copies],
        [core, pre_one, sums_one, counts, narrow_all, keep, mask_in, mask, inside],
        bundle_b,
        size_mid,
    )
    sums_two = wave([flow_c], sums, exchange(sums))
    wave([flow_c, flow_d], sums_two)
    bundle_c = flow_c.bundles()
    pre_side, side_sums = launch(
        functools.partial(side_layer, 0),
        [real(pixels, wide), real(2 * wide_rows, 128)],
        [core, field, mask],
        bundle_c,
        size_short,
    )
    hid_two, pre_three, sums = launch(
        functools.partial(widen_layer, size_short, 1),
        [short(pixels, narrow), real(pixels, wide), real(2 * wide_rows, 128)],
        [core, pre_two, sums_two, counts, narrow_all, keep, mask],
        bundle_c,
        size_out,
        [(pixels, narrow)],
    )
    sums_pair = everywhere(jnp.concatenate([sums, side_sums], 0), [flow_d])
    out_one, pre_four, sums = launch(
        functools.partial(narrow_layer, size_short + size_out),
        [short(pixels, wide), real(pixels, narrow), copies],
        [core, pre_three, pre_side, sums_pair, counts, wide_all, mask],
        bundle_c,
        size_out,
    )
    sums_four = wave([flow_d], sums, exchange(sums))
    bundle_d = flow_d.bundles()
    cols_four, pre_five, sums = launch(
        functools.partial(spread_layer, size_out, 2, PLAIN_TAPS),
        [short(pixels, 9 * narrow), real(pixels, narrow), copies],
        [core, pre_four, sums_four, counts, narrow_all, keep, mask, mask, inside],
        bundle_d,
        size_mid,
    )
    sums_five = exchange(sums)
    hid_five, pre_six, sums = launch(
        functools.partial(widen_layer, 0, 3),
        [short(pixels, narrow), real(pixels, wide), real(2 * wide_rows, 128)],
        [core, pre_five, sums_five, counts, narrow_all, keep, mask],
        bundle_d,
        size_out,
        [(pixels, narrow)],
    )
    sums_six = everywhere(sums)
    block_output, grad_two, sums = launch(
        last_layer,
        [short(*above.shape), real(pixels, wide), real(2 * wide_rows, 128)],
        [pre_six, sums_six, counts, wide_all, out_one, above, mask],
    )
    back_six = everywhere(sums)
    block_output = lax.all_to_all(block_output, "mp", 0, 0, tiled=True)
    block_output = block_output.transpose(2, 0, 1).reshape(-1, ranks * pixels)

    grad_six, act_five_grad, sums = launch(
        functools.partial(last_back, 0, 3),
        [short(pixels, wide), real(pixels, narrow), copies],
        [core, grad_two, pre_six, sums_six, back_six, counts, wide_all, pre_five,
         sums_five, narrow_all, keep, mask],
        bundle_d,
        size_out,
        [(pixels, narrow)],
    )
    bundle = chunks_into(None, size_out, 0, grad_six, hid_five, 1, unit_out, column)
    back_a = Scatter(*bundle)
    back_five = wave([back_a], sums, exchange(sums))
    grad_five, act_four_grad, sums = launch(
        functools.partial(spread_back, size_out, 2, PLAIN_TAPS),
        [short(pixels, narrow), real(pixels, narrow), copies],
        [core, act_five_grad, pre_five, sums_five, back_five, counts, narrow_all,
         pre_four, sums_four, keep, mask, mask, inside],
        bundle_d,
        size_mid,
        [(pixels, narrow)],
    )
    back_four = exchange(sums)
    bundle = chunks_into(None, size_mid, 0, cols_four, grad_five, 9, unit_mid, column)
    back_b = Scatter(*bundle)
    back_four = wave([back_a, back_b], sums, back_four)
    grad_four, grad_one, sums = launch(
        functools.partial(narrow_layer_back, size_short + size_out),
        [short(pixels, narrow), real(pixels, wide), real(3 * wide_rows, 128)],
        [core, act_four_grad, pre_four, sums_four, back_four, counts, narrow_all, mask,
         grad_two, pre_three, pre_side, sums_pair, wide_all],
        bundle_c,
        size_out,
        [(pixels, narrow), (pixels, wide)],
    )
    back_pair = everywhere(sums, [back_a, back_b])
    total = size_short + 2 * size_out
    bundle = chunks_into(
        None, total, size_short + size_out, out_one, grad_four, 1, unit_out, column
    )
    back_pair, bundle = lax.optimization_barrier((back_pair, bundle))
    grad_three, grad_side, act_two_grad, sums = launch(
        functools.partial(pair_back, size_short, 1),
        [short(pixels, wide), short(pixels, wide), real(pixels, narrow), copies],
        [core, grad_one, pre_three, pre_side, sums_pair, back_pair, counts, wide_all,
         pre_two, sums_two, narrow_all, keep, mask],
        bundle_c,
        size_out,
        [(pixels, narrow), (pixels, wide)],
    )
    back_two = wave([back_a, back_b], sums, exchange(sums))
    bundle = chunks_into(bundle, total, size_short, grad_three, hid_two, 1, unit_out, column)
    bundle = chunks_into(bundle, total, 0, field, grad_side, 1, unit_in, column_wide)
    back_c = Scatter(*bundle)
    back_two = wave([back_c], sums, back_two)
    grad_mid, act_one_grad, sums = launch(
        functools.partial(spread_back, 0, 0, STRIDED_TAPS),
        [short(pixels, narrow), real(full, narrow), copies],
        [core, act_two_grad, pre_two, sums_two, back_two, counts, narrow_all, pre_one,
         sums_one, keep, mask_in, mask, inside],
        bundle_b,
        size_mid,
        [(pixels, narrow)],
    )
    sums = wave([back_c], None, sums)
    back_one = wave([back_b], sums, exchange(sums))
    bundle = chunks_into(None, size_mid, 0, cols_one, grad_mid, 9, unit_mid, column)
    back_d = Scatter(*bundle)
    (side_grad,) = launch(
        functools.partial(side_back, 0),
        [real(pixels, field.shape[1])],
        [grad_side],
        bundle_c,
        size_short,
    )
    back_one = wave([back_d], sums, back_one)
    back_one = wave([back_c], None, back_one)
    back_one, side_grad = lax.optimization_barrier((back_one, side_grad))
    grad_first, field_grad = launch(
        first_back,
        [short(full, narrow), short(ranks, full, channels)],
        [core, act_one_grad, pre_one, sums_one, back_one, counts, narrow_all, mask_in,
         side_grad],
        bundle_a,
        unit_in,
        [(full, narrow)],
    )
    grad_first = wave([back_c, back_d], back_one, grad_first)
    bundle = chunks_into(None, unit_in * column // 128, 0, field, grad_first, 1, unit_in, column)
    back_e = Scatter(*bundle, False)
    wave([back_e])
    input_grad = lax.all_to_all(field_grad, "mp", 0, 0, tiled=True)
    input_grad = input_grad.reshape(ranks, 4, pixels, channels).transpose(3, 1, 0, 2)
    input_grad = input_grad.reshape(inputs.shape)
    wave([back_d, back_e])
    wave([back_d, back_e])
    rows_a, rows_b, rows_c, rows_d, rows_e = [
        flow.rows() for flow in (back_a, back_b, back_c, back_d, back_e)
    ]
    first_fix = 1.0 - BETA_ONE**STEP
    second_fix = 1.0 - BETA_TWO**STEP

    def like(*values):
        return [real(*value.shape) for value in values for _ in range(3)]

    early = launch(
        functools.partial(early_moves, column),
        like(shortcut_weight, last_weight, second_weight) + [real(8, 128)],
        [rows_a, rows_c]
        + [
            shortcut_mean, shortcut_square, shortcut_weight, last_mean, last_square, last_weight,
            second_mean, second_square, second_weight,
        ],
    )
    late = launch(
        late_moves,
        like(first_weight, middle_weight) + [real(devices, 16, 128)],
        [rows_b, rows_d, rows_e, early[-1]]
        + [first_mean, first_square, first_weight, middle_mean, middle_square, middle_weight],
    )
    powers = exchange(late[-1])
    weights = (first_weight, shortcut_weight, middle_weight, last_weight, second_weight)
    updates = (late[2], early[2], late[5], early[5], early[8])
    norms, *fresh = launch(
        final_moves,
        [real(16, 128)]
        + [real(*value.shape) for value in weights]
        + [short(*value.shape) for value in weights],
        [powers]
        + [value for pair in zip(weights, updates) for value in pair],
    )
    matrix_norms = norms[:14, 0].reshape(7, 2)
    first_next, short_next, middle_next, last_next, second_next = fresh[:5]
    states = [late[0:2], early[0:2], late[3:5], early[3:5], early[6:8]]

    def own_channels(values):
        width = values.shape[-1] // ranks
        return lax.dynamic_slice_in_dim(values, rank * width, width, values.ndim - 1)

    narrow_grads = jnp.stack([jnp.sum(rows, 0) for rows in (back_one, back_two, back_four, back_five)])
    narrow_grad = own_channels(narrow_grads.reshape(4, 2, narrow))
    gain_three, gain_side, bias_pair = jnp.sum(back_pair, 0).reshape(3, wide)
    wide_grad = own_channels(
        jnp.stack(
            [
                jnp.stack([gain_three, bias_pair]),
                jnp.stack([gain_side, bias_pair]),
                jnp.sum(back_six, 0).reshape(2, wide),
            ]
        )
    )
    narrow_mean_next, narrow_square_next, narrow_step = adapt(
        narrow_grad, narrow_mean, narrow_square, first_fix, second_fix
    )
    wide_mean_next, wide_square_next, wide_step = adapt(
        wide_grad, wide_mean, wide_square, first_fix, second_fix
    )
    return (
        block_output,
        input_grad,
        states[0][0],
        states[0][1],
        first_next,
        states[1][0],
        states[1][1],
        short_next,
        states[2][0],
        states[2][1],
        middle_next,
        states[3][0],
        states[3][1],
        last_next,
        states[4][0],
        states[4][1],
        second_next,
        narrow_mean_next,
        narrow_square_next,
        narrow_norms - RATE_NORM * narrow_step,
        wide_mean_next,
        wide_square_next,
        wide_norms - RATE_NORM * wide_step,
        matrix_norms,
        *fresh[5:],
    )


def solution(mesh):
    in_specs = (
        P("mp", None, "dp"),
        P(None, "dp"),
        P(),
        P("mp", "dp"),
        P("dp", "mp"),
        P("dp", "mp"),
        P(None, None, "dp", "mp"),
        P(None, "mp", "dp"),
        P("dp", "mp"),
        P(None, None, "mp"),
        P(None, None, "mp"),
        P("dp", "mp"),
        P("dp", "mp"),
        P("dp", "mp"),
        P("dp", "mp"),
        P(None, None, "dp", "mp"),
        P(None, None, "dp", "mp"),
        P(None, "mp", "dp"),
        P(None, "mp", "dp"),
        P("dp", "mp"),
        P("dp", "mp"),
        P(None, None, "mp"),
        P(None, None, "mp"),
        P(None, None, "mp"),
        P(None, None, "mp"),
    )
    out_specs = (
        P("mp", "dp"),
        P("mp", None, "dp"),
        P("dp", "mp"),
        P("dp", "mp"),
        P("dp", "mp"),
        P("dp", "mp"),
        P("dp", "mp"),
        P("dp", "mp"),
        P(None, None, "dp", "mp"),
        P(None, None, "dp", "mp"),
        P(None, None, "dp", "mp"),
        P(None, "mp", "dp"),
        P(None, "mp", "dp"),
        P(None, "mp", "dp"),
        P("dp", "mp"),
        P("dp", "mp"),
        P("dp", "mp"),
        P(None, None, "mp"),
        P(None, None, "mp"),
        P(None, None, "mp"),
        P(None, None, "mp"),
        P(None, None, "mp"),
        P(None, None, "mp"),
        P(),
        P("dp", "mp"),
        P("dp", "mp"),
        P(None, None, "dp", "mp"),
        P(None, "mp", "dp"),
        P("dp", "mp"),
    )
    return jax.shard_map(
        lambda *values: (by_image if fits(mesh, values[1]) else shards)(*values),
        mesh=mesh,
        in_specs=in_specs,
        out_specs=out_specs,
        check_vma=False,
    )
```

```python
import functools

import jax
import jax.numpy as jnp
from jax import lax
from jax.experimental import pallas as pl
from jax.experimental.pallas import tpu as pltpu
from jax.sharding import PartitionSpec as P

HO = 16
WO = 11
STEP = 10


EPS_NORM = 1e-05
BETA_ONE = 0.9
BETA_TWO = 0.999
EPS_ADAM = 1e-06
DECAY = 0.01
RATE = 0.3
RATE_NORM = 0.3
EPS_TRUST = 1e-06
PHASES = ((1, -1), (0, 0), (1, 0))
STRIDED_TAPS = tuple(
    (
        (
            3 * above + beside,
            2 * PHASES[above][0] + PHASES[beside][0],
            PHASES[above][1],
            PHASES[beside][1],
        )
        for above in range(3)
        for beside in range(3)
    )
)
PLAIN_TAPS = tuple(
    ((3 * above + beside, 0, above - 1, beside - 1) for above in range(3) for beside in range(3))
)


def slope(values):
    gate = jax.nn.sigmoid(values)
    return gate * (1.0 + values * (1.0 - gate))


def shifted(values, drow, dcol):
    length = values.shape[1]
    offset = drow * WO + dcol
    place = lax.iota(jnp.int32, length)
    row_at = place // WO % HO + drow
    col_at = place % WO + dcol
    inside = (row_at >= 0) & (row_at < HO) & (col_at >= 0) & (col_at < WO)
    moved = jnp.roll(values, -offset, axis=1)
    return jnp.where(inside[None, :], moved, jnp.zeros_like(moved))


def over_images(first, second):
    return lax.psum((first, second), "dp")


def moments(values, mask):
    weighted = values * mask[None, :]
    return over_images(jnp.sum(weighted, 1), jnp.sum(weighted * values, 1))


def normalize(values, totals, squares, count, gain, bias):
    mean = totals / count
    scale = lax.rsqrt(squares / count - mean * mean + EPS_NORM)
    centred = (values - mean[:, None]) * scale[:, None]
    return (centred, scale, centred * gain[:, None] + bias[:, None])


def back_sums(grad_in, centred):
    return over_images(jnp.sum(grad_in * centred, 1), jnp.sum(grad_in, 1))


def norm_back(grad_in, centred, scale, gain, mask, gain_sum, bias_sum, count):
    return (gain * scale)[:, None] * (
        grad_in - mask[None, :] * (bias_sum[:, None] + centred * gain_sum[:, None]) / count
    )


def input_mix(values, weight, side_weight, pixels):
    start_sum = (jnp.zeros((weight.shape[1], values.shape[1]), jnp.float32),)
    if side_weight is not None:
        start_sum = start_sum + (jnp.zeros((side_weight.shape[1], pixels), jnp.float32),)
    piece = lax.all_gather(values, "mp", axis=0, tiled=True)
    result = (jnp.einsum("kc,kp->cp", weight, piece, preferred_element_type=jnp.float32),)
    if side_weight is not None:
        result = result + (
            jnp.einsum(
                "kc,kp->cp", side_weight, piece[:, :pixels], preferred_element_type=jnp.float32
            ),
        )
    return result


def mid_gathered(hidden):
    return lax.all_gather(hidden, "mp", axis=0, tiled=True)


def conv_forward(gathered, kernel, taps, pixels):
    result = jnp.zeros((kernel.shape[2], pixels), jnp.float32)
    for tap, phase, drow, dcol in taps:
        source = gathered[:, phase * pixels : (phase + 1) * pixels]
        part = jnp.einsum("kc,kp->cp", kernel[tap], source, preferred_element_type=jnp.float32)
        result = result + shifted(part, drow, dcol)
    return result


def conv_backward(grad_b, gathered, kernel, taps, pixels, phases):
    moved = [shifted(grad_b, -drow, -dcol) for tap, phase, drow, dcol in taps]
    count = gathered.shape[0] // lax.axis_size("mp") * lax.axis_size("mp")
    blocks = []
    for target in range(phases):
        result = jnp.zeros((count, pixels), jnp.float32)
        for conv_index, (conv_tap, conv_phase, conv_drow, conv_dcol) in enumerate(taps):
            if conv_phase == target:
                part = kernel[conv_tap]
                result = result + jnp.dot(
                    part, moved[conv_index], preferred_element_type=jnp.float32
                )
        blocks.append(result)
    hidden_grad = lax.psum_scatter(
        jnp.concatenate(blocks, 1), "mp", scatter_dimension=0, tiled=True
    )
    kernel_grad = jnp.stack(
        [
            jnp.einsum(
                "kp,cp->kc",
                gathered[:, phase * pixels : (phase + 1) * pixels],
                moved[index],
                preferred_element_type=jnp.float32,
            )
            for index, (tap, phase, drow, dcol) in enumerate(taps)
        ]
    )
    return (hidden_grad, kernel_grad)


def output_mix(hidden, kernel):
    return lax.psum_scatter(
        jnp.einsum("kc,kp->cp", kernel, hidden, preferred_element_type=jnp.float32),
        "mp",
        scatter_dimension=0,
        tiled=True,
    )


def output_back(grad_b, kernel, hidden):
    piece = lax.all_gather(grad_b, "mp", axis=0, tiled=True)
    hidden_grad = jnp.dot(kernel, piece, preferred_element_type=jnp.float32)
    columns = jnp.einsum("cp,kp->ck", hidden, piece, preferred_element_type=jnp.float32)
    return (hidden_grad, columns)


def input_back(values, grad_b, side_b, weight, side_weight, pixels):
    width = weight.shape[1]
    result = jnp.dot(weight, grad_b, preferred_element_type=jnp.float32)
    if side_weight is not None:
        result = jnp.concatenate(
            [
                result[:, :pixels]
                + jnp.dot(side_weight, side_b, preferred_element_type=jnp.float32),
                result[:, pixels:],
            ],
            1,
        )
    values_grad = lax.psum_scatter(result, "mp", scatter_dimension=0, tiled=True)
    piece = lax.all_gather(values, "mp", axis=0, tiled=True)
    blocks = [jnp.einsum("kp,cp->kc", piece, grad_b, preferred_element_type=jnp.float32)]
    if side_weight is not None:
        blocks.append(
            jnp.einsum("kp,cp->kc", piece[:, :pixels], side_b, preferred_element_type=jnp.float32)
        )
    joined = jnp.concatenate(blocks, 1)
    return (values_grad, joined[:, :width], joined[:, width:])


def adapt(grad_in, mean, square, first_fix, second_fix):
    mean_next = BETA_ONE * mean + (1.0 - BETA_ONE) * grad_in
    square_next = BETA_TWO * square + (1.0 - BETA_TWO) * grad_in * grad_in
    step = mean_next / first_fix / (jnp.sqrt(square_next / second_fix) + EPS_ADAM)
    return (mean_next, square_next, step)


def shards(
    inputs,
    pixel_mask,
    widths,
    output_grad,
    first_weight,
    shortcut_weight,
    middle_weight,
    last_weight,
    second_weight,
    narrow_norms,
    wide_norms,
    first_mean,
    first_square,
    shortcut_mean,
    shortcut_square,
    middle_mean,
    middle_square,
    last_mean,
    last_square,
    second_mean,
    second_square,
    narrow_mean,
    narrow_square,
    wide_mean,
    wide_square,
):
    pixels = pixel_mask.shape[1]
    width = first_weight.shape[1]
    rank = lax.axis_index("mp")
    channel = rank * width + lax.iota(jnp.int32, width)
    keep_one = (channel < widths[0]).astype(jnp.float32)[:, None]
    keep_two = (channel < widths[1]).astype(jnp.float32)[:, None]
    masks = pixel_mask.astype(jnp.float32)
    mask_in = masks.reshape(-1)
    mask_out = masks[0]
    field = (inputs * pixel_mask.astype(jnp.bfloat16)[None]).reshape(inputs.shape[0], -1)
    first_w, short_w, middle_w, last_w, second_w = (
        lax.all_gather(first_weight.astype(jnp.bfloat16), "dp", axis=0, tiled=True),
        lax.all_gather(shortcut_weight.astype(jnp.bfloat16), "dp", axis=0, tiled=True),
        lax.all_gather(middle_weight.astype(jnp.bfloat16), "dp", axis=2, tiled=True),
        lax.all_gather(last_weight.astype(jnp.bfloat16), "dp", axis=2, tiled=True),
        lax.all_gather(second_weight.astype(jnp.bfloat16), "dp", axis=0, tiled=True),
    )
    count_in, count_out = over_images(jnp.sum(mask_in), jnp.sum(mask_out))
    pre_one, pre_side = input_mix(field, first_w, short_w, pixels)
    totals, squares = moments(pre_one, mask_in)
    cen_one, scale_one, act_one = normalize(
        pre_one, totals, squares, count_in, narrow_norms[0, 0], narrow_norms[0, 1]
    )
    hid_one = (jax.nn.silu(act_one) * mask_in[None, :] * keep_one).astype(jnp.bfloat16)
    gat_one = mid_gathered(hid_one)
    pre_two = conv_forward(gat_one, middle_w[0], STRIDED_TAPS, pixels)
    totals, squares = moments(pre_two, mask_out)
    cen_two, scale_two, act_two = normalize(
        pre_two, totals, squares, count_out, narrow_norms[1, 0], narrow_norms[1, 1]
    )
    hid_two = (jax.nn.silu(act_two) * mask_out[None, :] * keep_one).astype(jnp.bfloat16)
    pre_three = output_mix(hid_two, last_w[0])
    weighted_three = pre_three * mask_out[None, :]
    weighted_side = pre_side * mask_out[None, :]
    totals, squares = over_images(
        jnp.stack([jnp.sum(weighted_three, 1), jnp.sum(weighted_side, 1)]),
        jnp.stack([jnp.sum(weighted_three * pre_three, 1), jnp.sum(weighted_side * pre_side, 1)]),
    )
    cen_three, scale_three, act_three = normalize(
        pre_three, totals[0], squares[0], count_out, wide_norms[0, 0], wide_norms[0, 1]
    )
    cen_side, scale_side, act_side = normalize(
        pre_side, totals[1], squares[1], count_out, wide_norms[1, 0], wide_norms[1, 1]
    )
    total_one = act_three + act_side
    out_one = (jax.nn.silu(total_one) * mask_out[None, :]).astype(jnp.bfloat16)
    (pre_four,) = input_mix(out_one, second_w, None, pixels)
    totals, squares = moments(pre_four, mask_out)
    cen_four, scale_four, act_four = normalize(
        pre_four, totals, squares, count_out, narrow_norms[2, 0], narrow_norms[2, 1]
    )
    hid_four = (jax.nn.silu(act_four) * mask_out[None, :] * keep_two).astype(jnp.bfloat16)
    gat_four = mid_gathered(hid_four)
    pre_five = conv_forward(gat_four, middle_w[1], PLAIN_TAPS, pixels)
    totals, squares = moments(pre_five, mask_out)
    cen_five, scale_five, act_five = normalize(
        pre_five, totals, squares, count_out, narrow_norms[3, 0], narrow_norms[3, 1]
    )
    hid_five = (jax.nn.silu(act_five) * mask_out[None, :] * keep_two).astype(jnp.bfloat16)
    pre_six = output_mix(hid_five, last_w[1])
    totals, squares = moments(pre_six, mask_out)
    cen_six, scale_six, act_six = normalize(
        pre_six, totals, squares, count_out, wide_norms[2, 0], wide_norms[2, 1]
    )
    total_two = act_six + out_one.astype(jnp.float32)
    block_output = (jax.nn.silu(total_two) * mask_out[None, :]).astype(jnp.bfloat16)
    grad_two = output_grad.astype(jnp.float32) * mask_out[None, :] * slope(total_two)
    gain_six, bias_six = back_sums(grad_two, cen_six)
    grad_six = norm_back(
        grad_two, cen_six, scale_six, wide_norms[2, 0], mask_out, gain_six, bias_six, count_out
    ).astype(jnp.bfloat16)
    hid_five_grad, last_one_grad = output_back(grad_six, last_w[1], hid_five)
    act_five_grad = hid_five_grad * keep_two * mask_out[None, :] * slope(act_five)
    gain_five, bias_five = back_sums(act_five_grad, cen_five)
    grad_five = norm_back(
        act_five_grad,
        cen_five,
        scale_five,
        narrow_norms[3, 0],
        mask_out,
        gain_five,
        bias_five,
        count_out,
    ).astype(jnp.bfloat16)
    hid_four_grad, middle_one_grad = conv_backward(
        grad_five, gat_four, middle_w[1], PLAIN_TAPS, pixels, 1
    )
    act_four_grad = hid_four_grad * keep_two * mask_out[None, :] * slope(act_four)
    gain_four, bias_four = back_sums(act_four_grad, cen_four)
    grad_four = norm_back(
        act_four_grad,
        cen_four,
        scale_four,
        narrow_norms[2, 0],
        mask_out,
        gain_four,
        bias_four,
        count_out,
    ).astype(jnp.bfloat16)
    out_one_grad, second_grad, unused_side = input_back(
        out_one, grad_four, None, second_w, None, pixels
    )
    grad_one = (grad_two + out_one_grad) * mask_out[None, :] * slope(total_one)
    gains_pair, bias_pair = over_images(
        jnp.stack([jnp.sum(grad_one * cen_three, 1), jnp.sum(grad_one * cen_side, 1)]),
        jnp.sum(grad_one, 1),
    )
    grad_three = norm_back(
        grad_one,
        cen_three,
        scale_three,
        wide_norms[0, 0],
        mask_out,
        gains_pair[0],
        bias_pair,
        count_out,
    ).astype(jnp.bfloat16)
    grad_side = norm_back(
        grad_one,
        cen_side,
        scale_side,
        wide_norms[1, 0],
        mask_out,
        gains_pair[1],
        bias_pair,
        count_out,
    ).astype(jnp.bfloat16)
    hid_two_grad, last_zero_grad = output_back(grad_three, last_w[0], hid_two)
    act_two_grad = hid_two_grad * keep_one * mask_out[None, :] * slope(act_two)
    gain_two, bias_two = back_sums(act_two_grad, cen_two)
    grad_mid = norm_back(
        act_two_grad,
        cen_two,
        scale_two,
        narrow_norms[1, 0],
        mask_out,
        gain_two,
        bias_two,
        count_out,
    ).astype(jnp.bfloat16)
    hid_one_grad, middle_zero_grad = conv_backward(
        grad_mid, gat_one, middle_w[0], STRIDED_TAPS, pixels, 4
    )
    act_one_grad = hid_one_grad * keep_one * mask_in[None, :] * slope(act_one)
    gain_one, bias_one = back_sums(act_one_grad, cen_one)
    grad_first = norm_back(
        act_one_grad, cen_one, scale_one, narrow_norms[0, 0], mask_in, gain_one, bias_one, count_in
    ).astype(jnp.bfloat16)
    field_grad, first_grad, short_grad = input_back(
        field, grad_first, grad_side, first_w, short_w, pixels
    )
    input_grad = (field_grad * mask_in[None, :]).astype(jnp.bfloat16).reshape(inputs.shape)
    grads = (
        lax.psum_scatter(first_grad, "dp", scatter_dimension=0, tiled=True),
        lax.psum_scatter(short_grad, "dp", scatter_dimension=0, tiled=True),
        lax.psum_scatter(
            jnp.stack([middle_zero_grad, middle_one_grad]), "dp", scatter_dimension=2, tiled=True
        ),
        lax.psum_scatter(
            jnp.stack([last_zero_grad, last_one_grad]), "dp", scatter_dimension=2, tiled=True
        ),
        lax.psum_scatter(second_grad, "dp", scatter_dimension=0, tiled=True),
    )
    first_fix = 1.0 - BETA_ONE**STEP
    second_fix = 1.0 - BETA_TWO**STEP
    weights = (first_weight, shortcut_weight, middle_weight, last_weight, second_weight)
    means = (first_mean, shortcut_mean, middle_mean, last_mean, second_mean)
    squares_old = (first_square, shortcut_square, middle_square, last_square, second_square)
    states = []
    updates = []
    for index in range(5):
        mean_next, square_next, step = adapt(
            grads[index], means[index], squares_old[index], first_fix, second_fix
        )
        states.append((mean_next, square_next))
        updates.append(step + DECAY * weights[index])
    pairs = [
        (weights[0], updates[0]),
        (weights[1], updates[1]),
        (weights[2][0], updates[2][0]),
        (weights[2][1], updates[2][1]),
        (weights[3][0], updates[3][0]),
        (weights[3][1], updates[3][1]),
        (weights[4], updates[4]),
    ]
    partial_value = jnp.stack(
        [
            jnp.stack([jnp.sum(weight * weight), jnp.sum(update * update)])
            for weight, update in pairs
        ]
    )
    matrix_norms = jnp.sqrt(lax.psum(partial_value, ("dp", "mp")))
    ratio = matrix_norms[:, 0] / (matrix_norms[:, 1] + EPS_TRUST)
    first_next = first_weight - RATE * ratio[0] * updates[0]
    short_next = shortcut_weight - RATE * ratio[1] * updates[1]
    middle_next = middle_weight - RATE * ratio[2:4].reshape(2, 1, 1, 1) * updates[2]
    last_next = last_weight - RATE * ratio[4:6].reshape(2, 1, 1) * updates[3]
    second_next = second_weight - RATE * ratio[6] * updates[4]
    narrow_grad = jnp.stack(
        [
            jnp.stack([gain_one, bias_one]),
            jnp.stack([gain_two, bias_two]),
            jnp.stack([gain_four, bias_four]),
            jnp.stack([gain_five, bias_five]),
        ]
    )
    wide_grad = jnp.stack(
        [
            jnp.stack([gains_pair[0], bias_pair]),
            jnp.stack([gains_pair[1], bias_pair]),
            jnp.stack([gain_six, bias_six]),
        ]
    )
    narrow_mean_next, narrow_square_next, narrow_step = adapt(
        narrow_grad, narrow_mean, narrow_square, first_fix, second_fix
    )
    wide_mean_next, wide_square_next, wide_step = adapt(
        wide_grad, wide_mean, wide_square, first_fix, second_fix
    )
    return (
        block_output,
        input_grad,
        states[0][0],
        states[0][1],
        first_next,
        states[1][0],
        states[1][1],
        short_next,
        states[2][0],
        states[2][1],
        middle_next,
        states[3][0],
        states[3][1],
        last_next,
        states[4][0],
        states[4][1],
        second_next,
        narrow_mean_next,
        narrow_square_next,
        narrow_norms - RATE_NORM * narrow_step,
        wide_mean_next,
        wide_square_next,
        wide_norms - RATE_NORM * wide_step,
        matrix_norms,
        first_next.astype(jnp.bfloat16),
        short_next.astype(jnp.bfloat16),
        middle_next.astype(jnp.bfloat16),
        last_next.astype(jnp.bfloat16),
        second_next.astype(jnp.bfloat16),
    )


VMEM_BYTES = 62 * 2**20
LIGHT = pl.CostEstimate(flops=1024, bytes_accessed=1024, transcendentals=0)


def fits(mesh, pixel_mask):
    sizes = (mesh.shape["dp"], mesh.shape["mp"])
    powers = all(size >= 2 and size & (size - 1) == 0 for size in sizes)
    return powers and pixel_mask.shape[1] % (HO * WO * sizes[1]) == 0


def swap(values, *bits):
    sizes = {axis: lax.axis_size(axis) for axis in ("dp", "mp")}
    masks = {axis: sum(mask for at, mask in bits if at == axis) for axis in sizes}
    if not masks["dp"]:
        return lax.ppermute(values, "mp", [(at, at ^ masks["mp"]) for at in range(sizes["mp"])])
    if not masks["mp"]:
        return lax.ppermute(values, "dp", [(at, at ^ masks["dp"]) for at in range(sizes["dp"])])
    mask = masks["dp"] * sizes["mp"] + masks["mp"]
    return lax.ppermute(
        values, ("dp", "mp"), [(at, at ^ mask) for at in range(sizes["dp"] * sizes["mp"])]
    )


def subsets(bits):
    return [
        [bit for place, bit in enumerate(bits) if index >> place & 1]
        for index in range(1 << len(bits))
    ]


def bit_of(axis, mask):
    return (lax.axis_index(axis) & mask) // mask


def high_bits(axis):
    masks = []
    mask = lax.axis_size(axis) // 2
    while mask:
        masks.append(mask)
        mask //= 2
    return masks


def everywhere(values, flows=()):
    mask = 1
    while mask < lax.axis_size("mp"):
        values = values + swap(values, ("mp", mask))
        mask *= 2
    copies = jnp.broadcast_to(values[None], (lax.axis_size("dp"),) + values.shape)
    arrived = lax.all_to_all(copies, "dp", 0, 0, tiled=True)
    return wave(flows, values, arrived) if flows else arrived


def pack(block):
    lead, rows, cols = block.shape
    parts = block.reshape(lead, rows, cols // 128, 128).transpose(0, 2, 1, 3)
    return parts.reshape(-1, 128)


def column_bits():
    return [("mp", mask) for mask in high_bits("mp")[:-1]]


def row_bits():
    return [("dp", mask) for mask in high_bits("dp")]


def lanes_of(rows):
    first = rows // 32 * 16
    return ((0, first), (first, rows))


def moves_kernel(tasks, count, places, *refs):
    sources, outs, sems = refs[:count], refs[count:-1], refs[-1]
    copies = []
    for at, (source, span, out, turns, rows) in enumerate(tasks):
        dims = len(sources[source].shape) - 2
        every = [slice(None)] * dims
        start = [
            pl.ds(1 - places[dim] if turns[dim] else places[dim], 1) if dim in turns else slice(None)
            for dim in range(dims)
        ]
        copies.append(
            pltpu.make_async_copy(
                sources[source].at[(*every, pl.ds(*span), slice(None))],
                outs[out].at[(*start, pl.ds(*rows), slice(None))],
                sems.at[at],
            )
        )
        copies[-1].start()
    for copy in copies:
        copy.wait()


def moves(wanted):
    sources = []
    tasks = []
    for out, (shape, pieces) in enumerate(wanted):
        for source, span, turns, rows in pieces:
            tasks.append((len(sources), span, out, turns, rows))
            sources.append(source)
    bits = column_bits() + row_bits()
    places = jnp.stack([bit_of(*bit) for bit in bits]).astype(jnp.int32)
    return pl.pallas_call(
        functools.partial(moves_kernel, tasks, len(sources)),
        in_specs=[pl.BlockSpec(memory_space=pltpu.SMEM)]
        + [pl.BlockSpec(memory_space=pltpu.HBM)] * len(sources),
        out_specs=[pl.BlockSpec(memory_space=pltpu.VMEM)] * len(wanted),
        out_shape=[jax.ShapeDtypeStruct(shape, jnp.bfloat16) for shape, _ in wanted],
        scratch_shapes=[pltpu.SemaphoreType.DMA((len(tasks),))],
        compiler_params=pltpu.CompilerParams(vmem_limit_bytes=VMEM_BYTES),
        cost_estimate=LIGHT,
    )(places, *sources)


class Gather:
    def __init__(self, rows, lanes=True):
        self.dims = column_bits() + row_bits()
        near = row_bits()[-1:]
        self.rows = rows.shape[0]
        if lanes:
            self.steps = [[row_bits()[:-1]], [near, column_bits()], [column_bits(), near]]
            self.spans = lanes_of(self.rows)
        else:
            self.steps = [[row_bits()[:-1]], [near + column_bits()]]
            self.spans = ((0, self.rows),)
        self.parts = [([rows.reshape((1,) * len(self.dims) + rows.shape)], [])]
        self.step = 0

    def pending(self):
        return [values for values, bits in self.parts]

    def resume(self, values):
        self.parts = [(value, bits) for value, (_, bits) in zip(values, self.parts)]

    def wanted(self):
        if not self.parts[0][1]:
            return []
        last = self.step == len(self.steps)
        split = not last and len(self.steps[self.step]) > len(self.parts)
        lanes = [(low, high - low) for low, high in self.spans]
        result = []
        for lane, (values, bits) in enumerate(self.parts):
            shape = [
                2 if bit in bits else size
                for bit, size in zip(self.dims, values[0].shape)
            ]
            pieces = [
                (value, {self.dims.index(bit): bit in turned for bit in bits})
                for value, turned in zip(values, subsets(bits))
            ]
            height = values[0].shape[-2]
            for low, size in lanes if split else [(0, height)]:
                block = [(value, (low, size), turns, (0, size)) for value, turns in pieces]
                result.append((tuple(shape) + (size, 128), block))
        if last:
            pieces = [
                (value, span, turns, lanes[lane])
                for lane, (_, block) in enumerate(result)
                for value, span, turns, _ in block
            ]
            result = [(result[0][0][:-2] + (self.rows, 128), pieces)]
        return result

    def launch(self, values):
        if not values:
            values = [self.parts[0][0][0]]
        if self.step < len(self.steps):
            self.parts = [
                ([value] + [swap(value, *bits) for bits in subsets(group)[1:]], group)
                for value, group in zip(values, self.steps[self.step])
            ]
        else:
            self.parts = [([values[0], swap(values[0], ("mp", 1))], [])]
        self.step += 1
        return values

    def bundles(self):
        shape = (1 << len(column_bits()), lax.axis_size("dp")) + self.parts[0][0][0].shape[-2:]
        return [value.reshape(shape) for value in self.parts[0][0]]


class Scatter:
    def __init__(self, keep, send, lanes=True):
        self.dims = column_bits() + row_bits()
        shape = (2,) * len(self.dims) + keep.shape[2:]
        near = row_bits()[-1:]
        far = row_bits()[:-1]
        if lanes:
            self.steps = [None, [column_bits(), near], [near, column_bits()], [far, far]]
            self.spans = lanes_of(keep.shape[2])
        else:
            self.steps = [None, [column_bits() + near], [far]]
            self.spans = (None,)
        self.lanes = [[] for _ in self.spans]
        self.raw = [keep.reshape(shape), send.reshape(shape)]
        self.step = 0

    def pending(self):
        return self.raw

    def resume(self, values):
        self.raw = list(values)

    def fold(self, lane, group=(), turned=()):
        total = 0.0
        for index, settled, span in self.lanes[lane]:
            value = self.raw[index]
            for bit in settled + list(group):
                place = bit_of(*bit)
                place = 1 - place if bit in turned else place
                value = lax.dynamic_slice_in_dim(value, place, 1, self.dims.index(bit))
            if span is not None:
                value = value[..., span[0] : span[1], :]
            total = total + value.astype(jnp.float32)
        return total

    def settle(self, lane, group, arrived, span):
        old = [(index, settled + group, part) for index, settled, part in self.lanes[lane]]
        self.lanes[lane] = old + [(index, [], span) for index in arrived]

    def wanted(self):
        return []

    def launch(self, values):
        groups = self.steps[self.step]
        whole = self.step == len(self.steps) - 1
        sent = []
        if groups is None:
            sent.append(self.raw[1])
            self.raw[1] = swap(self.raw[1], ("mp", 1))
            for lane, span in zip(self.lanes, self.spans):
                lane += [(0, [], span), (1, [], span)]
        elif whole:
            arrived = []
            for bits in subsets(groups[0])[1:]:
                out = [
                    self.fold(lane, groups[0], bits).astype(jnp.bfloat16)
                    for lane in range(len(self.lanes))
                ]
                out = jnp.concatenate(out, -2) if len(out) > 1 else out[0]
                arrived.append(len(self.raw))
                sent.append(out)
                self.raw.append(swap(out, *bits))
            for lane, span in enumerate(self.spans):
                self.settle(lane, groups[lane], arrived, span)
        else:
            for lane, group in enumerate(groups):
                arrived = []
                for bits in subsets(group)[1:]:
                    out = self.fold(lane, group, bits).astype(jnp.bfloat16)
                    arrived.append(len(self.raw))
                    sent.append(out)
                    self.raw.append(swap(out, *bits))
                self.settle(lane, group, arrived, None)
        self.step += 1
        return sent

    def rows(self):
        total = [self.fold(lane) for lane in range(len(self.lanes))]
        total = jnp.concatenate(total, -2) if len(total) > 1 else total[0]
        return total.reshape(total.shape[-2:])


def wave(flows, after=None, before=None):
    values = [flow.pending() for flow in flows]
    if after is not None:
        values, _ = lax.optimization_barrier((values, after))
    for flow, value in zip(flows, values):
        flow.resume(value)
    wanted = [flow.wanted() for flow in flows]
    joined = [value for part in wanted for value in part]
    made = list(moves(joined)) if joined else []
    sent = []
    for flow, part in zip(flows, wanted):
        sent += flow.launch([made.pop(0) for _ in part])
    if before is not None:
        before, _ = lax.optimization_barrier((before, sent))
    return before


def hold(flows, value):
    value, parts = lax.optimization_barrier((value, [flow.pending() for flow in flows]))
    for flow, part in zip(flows, parts):
        flow.resume(part)
    wave(flows)
    return value


def chunk_kernel(units, columns, rows_ref, cols_ref, *refs):
    outs = refs[-2:]
    product = lax.dot_general(
        rows_ref[...], cols_ref[...], (((0,), (0,)), ((), ())), preferred_element_type=jnp.float32
    ).astype(jnp.bfloat16)
    groups = outs[0].shape[0]
    chunks = outs[0].shape[1]
    for half, out in enumerate(outs):
        for group in range(groups):
            for part in range(columns):
                place = ((half * groups + group) * columns + part) * 128
                block = product[:, place : place + 128].reshape(chunks, units, 128)
                out[group, :, part * units : (part + 1) * units, :] = block


def chunks_into(bundle, total, start, rows_of, cols_of, lead, units, columns):
    count = lax.axis_size("dp")
    groups = 1 << len(column_bits())
    columns = columns // 128
    pixels = cols_of.shape[0]
    height = units * columns
    if lead > 1:
        steps, wide, chunks = lead, count * units, count
        place = lambda step: (0, 0, start // height + step, 0)
    else:
        steps, wide, chunks = count, units, 1
        place = lambda step: (0, step, start // height, 0)
    shape = jax.ShapeDtypeStruct((groups, count, total, 128), jnp.bfloat16)
    block = pl.BlockSpec((groups, chunks, height, 128), place)
    earlier = () if bundle is None else tuple(bundle)
    return pl.pallas_call(
        functools.partial(chunk_kernel, units, columns),
        grid=(steps,),
        in_specs=[
            pl.BlockSpec((pixels, wide), lambda step: (0, step)),
            pl.BlockSpec(cols_of.shape, lambda step: (0, 0)),
        ]
        + [pl.BlockSpec(memory_space=pltpu.HBM)] * len(earlier),
        out_specs=[block, block],
        out_shape=[shape, shape],
        input_output_aliases={2 + place: place for place in range(len(earlier))},
        compiler_params=pltpu.CompilerParams(vmem_limit_bytes=VMEM_BYTES),
        cost_estimate=LIGHT,
    )(rows_of, cols_of, *earlier)


def total_of(ref):
    return jnp.sum(ref[...], 0) if len(ref.shape) == 3 else ref[...]


def as_row(block):
    return jnp.concatenate([block[place : place + 1] for place in range(block.shape[0])], 1)


def as_rows(row):
    return jnp.concatenate(
        [row[:, place : place + 128] for place in range(0, row.shape[1], 128)], 0
    )


def hand_out(out, rows):
    missing = out.shape[-2] - sum(row.shape[0] for row in rows)
    if missing:
        rows = rows + [jnp.zeros((missing, 128), jnp.float32)]
    block = jnp.concatenate(rows, 0)
    out[...] = jnp.broadcast_to(block[None], out.shape) if len(out.shape) == 3 else block


def levels(total, first, width, count):
    rows = width // 128
    mean = total[first : first + rows] / count
    scale = lax.rsqrt(total[first + rows : first + 2 * rows] / count - mean * mean + EPS_NORM)
    return (as_row(mean), as_row(scale))


def standard(values, level):
    return (values - level[0]) * level[1]


def back_through(grad, centred, level, gain, mask, total, first, bias_first, count):
    rows = grad.shape[1] // 128
    gain_sum = as_row(total[first : first + rows] / count)
    bias_sum = as_row(total[bias_first : bias_first + rows] / count)
    return (gain * level[1]) * (grad - mask * (bias_sum + centred * gain_sum))


def column_sums(values, mask):
    weighted = values * mask
    return [
        as_rows(jnp.sum(weighted, 0, keepdims=True)),
        as_rows(jnp.sum(weighted * values, 0, keepdims=True)),
    ]


def product_sums(grad, centred):
    return as_rows(jnp.sum(grad * centred, 0, keepdims=True))


def plain_sums(grad):
    return as_rows(jnp.sum(grad, 0, keepdims=True))


def fetch(bundles, held, sems, start):
    rows = held.shape[3]
    copies = [
        pltpu.make_async_copy(ref.at[:, :, pl.ds(start, rows), :], held.at[half], sems.at[half])
        for half, ref in enumerate(bundles)
    ]
    for copy in copies:
        copy.start()
    return copies


def arrive(copies):
    for copy in copies:
        copy.wait()


def weight_part(held, chunk, chunks, start, units, columns):
    return jnp.concatenate(
        [
            held[half, group, chunk : chunk + chunks, start + part * units : start + (part + 1) * units, :]
            .reshape(chunks * units, 128)
            for half in range(2)
            for group in range(held.shape[1])
            for part in range(columns)
        ],
        1,
    )


def spots(core, groups, width):
    return [
        pl.multiple_of((2 * group + (core if half == 0 else 1 - core)) * width, 128)
        for half in range(2)
        for group in range(groups)
    ]


def in_turn(ref, core, groups):
    width = ref.shape[1] // (2 * groups)
    return jnp.concatenate([ref[:, pl.ds(at, width)] for at in spots(core, groups, width)], 1)


def in_order(ref, values, core, groups):
    width = ref.shape[1] // (2 * groups)
    for place, at in enumerate(spots(core, groups, width)):
        ref[:, pl.ds(at, width)] = values[:, place * width : (place + 1) * width]


def product(first, second):
    return lax.dot_general(
        first, second, (((1,), (0,)), ((), ())), preferred_element_type=jnp.float32
    )


def product_turned(first, second):
    return lax.dot_general(
        first, second, (((1,), (1,)), ((), ())), preferred_element_type=jnp.float32
    )


def many_in(values, held, units, columns):
    chunks = max(1, 256 // units)
    total = 0.0
    for chunk in range(0, held.shape[2], chunks):
        part = weight_part(held, chunk, chunks, 0, units, columns)
        total = total + product(
            values[:, chunk * units : (chunk + chunks) * units], part
        )
    return total


def many_out(values, held, units, columns):
    chunks = max(1, 256 // units)
    return [
        product_turned(values, weight_part(held, chunk, chunks, 0, units, columns))
        for chunk in range(0, held.shape[2], chunks)
    ]


def slid(values, offset):
    count = values.shape[0]
    return pltpu.roll(values, (-offset) % count, 0) if offset % count else values


def within(inside, drow, dcol):
    place = 3 * (drow + 1) + dcol + 1
    return inside[:, place : place + 1]


def first_layer(core, raw, mask, first, second, field, out, sums, held, sems):
    copies = fetch((first, second), held, sems, 0)
    core = core[0]
    weights = mask[...]
    width = raw.shape[2]
    for place in range(raw.shape[0]):
        part = raw[place].astype(jnp.float32) * weights
        field[:, place * width : (place + 1) * width] = part.astype(jnp.bfloat16)
    arrive(copies)
    result = many_in(field, held, held.shape[3], 1)
    in_order(out, result, core, held.shape[1])
    rows = column_sums(out[...], weights)
    pixels = weights.shape[0] // 4
    for part in (weights, weights[:pixels]):
        rows.append(jnp.broadcast_to(jnp.sum(part, 0, keepdims=True), (1, 128)))
    hand_out(sums, rows)


def side_layer(start, core, field, mask, first, second, out, sums, held, sems):
    copies = fetch((first, second), held, sems, start)
    core = core[0]
    pixels = mask.shape[0]
    arrive(copies)
    columns = out.shape[1] // (2 * held.shape[1] * 128)
    result = many_in(field[:pixels, :], held, held.shape[3] // columns, columns)
    in_order(out, result, core, held.shape[1])
    hand_out(sums, column_sums(out[...], mask[...]))


def spread_layer(start, norm, taps, core, before, sums_in, counts, tables, keep, mask_in, mask, inside,
                 first, second, cols, out, sums, held, sems):
    copies = fetch((first, second), held, sems, start)
    core = core[0]
    pixels = mask.shape[0]
    width = before.shape[1]
    counted = 0 if before.shape[0] > pixels else 1
    level = levels(total_of(sums_in), 0, width, counts[counted : counted + 1, :])
    act = standard(before[...], level) * tables[2 * norm : 2 * norm + 1, :] + tables[2 * norm + 1 : 2 * norm + 2, :]
    row = norm // 2
    hidden = jax.nn.silu(act) * mask_in[...] * keep[row : row + 1, :]
    for tap, phase, drow, dcol in taps:
        source = hidden[phase * pixels : (phase + 1) * pixels]
        moved = slid(source, drow * WO + dcol) * within(inside, drow, dcol)
        cols[:, tap * width : (tap + 1) * width] = moved.astype(jnp.bfloat16)
    arrive(copies)
    units = held.shape[3] // 9
    total = 0.0
    for tap in range(9):
        part = weight_part(held, 0, held.shape[2], tap * units, units, 1)
        total = total + product(cols[:, tap * width : (tap + 1) * width], part)
    in_order(out, total, core, held.shape[1])
    hand_out(sums, column_sums(out[...], mask[...]))


def widen_layer(start, norm, core, before, sums_in, counts, tables, keep, mask, first, second,
                hidden, out, sums, held, scratch, sems):
    copies = fetch((first, second), held, sems, start)
    core = core[0]
    level = levels(total_of(sums_in), 0, before.shape[1], counts[1:2, :])
    act = standard(before[...], level) * tables[2 * norm : 2 * norm + 1, :] + tables[2 * norm + 1 : 2 * norm + 2, :]
    row = norm // 2
    scratch[...] = jax.nn.silu(act) * mask[...] * keep[row : row + 1, :]
    hidden[...] = in_turn(scratch, core, held.shape[1]).astype(jnp.bfloat16)
    arrive(copies)
    parts = many_out(hidden[...], held, held.shape[3], 1)
    size = out.shape[1] // len(parts)
    for place, part in enumerate(parts):
        out[:, place * size : (place + 1) * size] = part
    hand_out(sums, column_sums(out[...], mask[...]))


def joined_acts(total, third, side, wide, count):
    width = third.shape[1]
    rows = width // 128
    centred_third = standard(third[...], levels(total, 0, width, count))
    centred_side = standard(side[...], levels(total, 2 * rows, width, count))
    act = (
        centred_third * wide[0:1, :]
        + wide[1:2, :]
        + (centred_side * wide[2:3, :] + wide[3:4, :])
    )
    return (centred_third, centred_side, act)


def narrow_layer(start, core, third, side, sums_in, counts, wide, mask, first, second,
                 above, out, sums, held, sems):
    copies = fetch((first, second), held, sems, start)
    core = core[0]
    centred_third, centred_side, act = joined_acts(
        total_of(sums_in), third, side, wide, counts[1:2, :]
    )
    above[...] = (jax.nn.silu(act) * mask[...]).astype(jnp.bfloat16)
    arrive(copies)
    result = many_in(above, held, held.shape[3], 1)
    in_order(out, result, core, held.shape[1])
    hand_out(sums, column_sums(out[...], mask[...]))


def last_layer(sixth, sums_in, counts, wide, above, cotangent, mask, out, grad, sums):
    level = levels(total_of(sums_in), 0, sixth.shape[1], counts[1:2, :])
    centred = standard(sixth[...], level)
    act = centred * wide[4:5, :] + wide[5:6, :] + above[...].astype(jnp.float32)
    weights = mask[...]
    result = (jax.nn.silu(act) * weights).astype(jnp.bfloat16)
    inner = weights * slope(act)
    width = out.shape[2]
    for place in range(out.shape[0]):
        span = slice(place * width, (place + 1) * width)
        out[place] = result[:, span]
        grad[:, span] = cotangent[place].astype(jnp.float32) * inner[:, span]
    result = grad[...]
    hand_out(sums, [product_sums(result, centred), plain_sums(result)])


def narrow_grad(grad, before, sums_in, counts, tables, norm, keep, mask):
    counted = 0 if norm == 0 else 1
    level = levels(total_of(sums_in), 0, before.shape[1], counts[counted : counted + 1, :])
    centred = standard(before[...], level)
    act = centred * tables[2 * norm : 2 * norm + 1, :] + tables[2 * norm + 1 : 2 * norm + 2, :]
    row = norm // 2
    result = grad * keep[row : row + 1, :] * mask * slope(act)
    return (result, [product_sums(result, centred), plain_sums(result)])


def narrow_back(norm, grad, before, sums_in, sums_back, counts, tables, mask):
    counted = 0 if norm == 0 else 1
    count = counts[counted : counted + 1, :]
    width = before.shape[1]
    level = levels(total_of(sums_in), 0, width, count)
    return back_through(
        grad[...],
        standard(before[...], level),
        level,
        tables[2 * norm : 2 * norm + 1, :],
        mask,
        total_of(sums_back),
        0,
        width // 128,
        count,
    )


def last_back(start, norm, core, grad, sixth, sums_six, back_six, counts, wide, before, sums_in, tables,
              keep, mask, first, second, grad_out, grad_in, sums, held, scratch, sems):
    copies = fetch((first, second), held, sems, start)
    core = core[0]
    width = sixth.shape[1]
    count = counts[1:2, :]
    level = levels(total_of(sums_six), 0, width, count)
    grad_out[...] = back_through(
        grad[...], standard(sixth[...], level), level, wide[4:5, :], mask[...], total_of(back_six), 0,
        width // 128, count,
    ).astype(jnp.bfloat16)
    arrive(copies)
    in_order(scratch, many_in(grad_out, held, held.shape[3], 1), core, held.shape[1])
    result, rows = narrow_grad(scratch[...], before, sums_in, counts, tables, norm, keep, mask[...])
    grad_in[...] = result
    hand_out(sums, rows)


def pair_back(start, norm, core, grad, third, side, sums_pair, back_pair, counts, wide, before, sums_in,
              tables, keep, mask, first, second, grad_third, grad_side, grad_in, sums, held, scratch,
              big, sems):
    copies = fetch((first, second), held, sems, start)
    core = core[0]
    width = third.shape[1]
    rows = width // 128
    count = counts[1:2, :]
    total = total_of(sums_pair)
    back = total_of(back_pair)
    groups = held.shape[1]
    level = levels(total, 0, width, count)
    grad_third[...] = back_through(
        grad[...], standard(third[...], level), level, wide[0:1, :], mask[...], back, 0, 2 * rows, count
    ).astype(jnp.bfloat16)
    arrive(copies)
    in_order(scratch, many_in(grad_third, held, held.shape[3], 1), core, groups)
    result, parts = narrow_grad(scratch[...], before, sums_in, counts, tables, norm, keep, mask[...])
    grad_in[...] = result
    hand_out(sums, parts)
    level = levels(total, 2 * rows, width, count)
    big[...] = back_through(
        grad[...], standard(side[...], level), level, wide[2:3, :], mask[...], back, rows, 2 * rows, count
    )
    grad_side[...] = in_turn(big, core, groups).astype(jnp.bfloat16)


def spread_back(start, norm, taps, core, grad, after, sums_after, back_after, counts, tables, before,
                sums_in, keep, mask_in, mask, inside, first, second, grad_out, grad_in, sums, held,
                scratch, sems):
    copies = fetch((first, second), held, sems, start)
    core = core[0]
    pixels = mask.shape[0]
    phases = before.shape[0] // pixels
    scratch[...] = narrow_back(norm + 1, grad, after, sums_after, back_after, counts, tables, mask[...])
    grad_out[...] = in_turn(scratch, core, held.shape[1]).astype(jnp.bfloat16)
    arrive(copies)
    units = held.shape[3] // 9
    totals = [0.0] * phases
    for tap, phase, drow, dcol in taps:
        part = weight_part(held, 0, held.shape[2], tap * units, units, 1)
        moved = product_turned(grad_out[...], part)
        totals[phase] = totals[phase] + slid(moved, -drow * WO - dcol) * within(inside, -drow, -dcol)
    hidden = jnp.concatenate(totals, 0) if phases > 1 else totals[0]
    result, rows = narrow_grad(hidden, before, sums_in, counts, tables, norm, keep, mask_in[...])
    grad_in[...] = result
    hand_out(sums, rows)


def narrow_layer_back(start, core, grad, fourth, sums_four, back_four, counts, tables, mask, grad_two,
                      third, side, sums_pair, wide, first, second, grad_out, grad_in, sums, held,
                      scratch, big, sems):
    copies = fetch((first, second), held, sems, start)
    core = core[0]
    scratch[...] = narrow_back(2, grad, fourth, sums_four, back_four, counts, tables, mask[...])
    grad_out[...] = in_turn(scratch, core, held.shape[1]).astype(jnp.bfloat16)
    arrive(copies)
    parts = many_out(grad_out[...], held, held.shape[3], 1)
    size = big.shape[1] // len(parts)
    for place, part in enumerate(parts):
        big[:, place * size : (place + 1) * size] = part
    centred_third, centred_side, act = joined_acts(
        total_of(sums_pair), third, side, wide, counts[1:2, :]
    )
    result = (grad_two[...] + big[...]) * mask[...] * slope(act)
    grad_in[...] = result
    hand_out(
        sums,
        [
            product_sums(result, centred_third),
            product_sums(result, centred_side),
            plain_sums(result),
        ],
    )


def side_back(start, grad, first, second, out, held, sems):
    copies = fetch((first, second), held, sems, start)
    arrive(copies)
    columns = grad.shape[1] // (2 * held.shape[1] * 128)
    parts = many_out(grad[...], held, held.shape[3] // columns, columns)
    size = out.shape[1] // len(parts)
    for place, part in enumerate(parts):
        out[:, place * size : (place + 1) * size] = part


def first_back(core, grad, before, sums_in, sums_back, counts, tables, mask, side, first, second,
               grad_out, out, held, scratch, sems):
    copies = fetch((first, second), held, sems, 0)
    core = core[0]
    scratch[...] = narrow_back(0, grad, before, sums_in, sums_back, counts, tables, mask[...])
    grad_out[...] = in_turn(scratch, core, held.shape[1]).astype(jnp.bfloat16)
    arrive(copies)
    parts = many_out(grad_out[...], held, held.shape[3], 1)
    size = side.shape[1] // len(parts)
    pixels = side.shape[0]
    weights = mask[...]
    width = out.shape[2]
    for place, part in enumerate(parts):
        owner = place * size // width
        span = slice(place * size % width, place * size % width + size)
        beside = side[:, place * size : (place + 1) * size]
        out[owner, :pixels, span] = ((part[:pixels] + beside) * weights[:pixels]).astype(jnp.bfloat16)
        out[owner, pixels:, span] = (part[pixels:] * weights[pixels:]).astype(jnp.bfloat16)


class Coming:
    def __init__(self, ref, copy):
        self.ref = ref
        self.copy = copy
        self.shape = ref.shape

    def settle(self):
        if self.copy is not None:
            self.copy.wait()
            self.copy = None

    def __getitem__(self, place):
        self.settle()
        return self.ref[place]


def framed(kernel, places, count, *refs):
    refs = list(refs)
    rest, held, sems = refs[: len(refs) - len(places) - 1], refs[-len(places) - 1 : -1], refs[-1]
    coming = []
    for at, place in enumerate(places):
        copy = pltpu.make_async_copy(rest[place], held[at], sems.at[at])
        copy.start()
        rest[place] = Coming(held[at], copy)
        coming.append(rest[place])
    kernel(*rest)
    for value in coming:
        value.settle()


def launch(kernel, shapes, values, bundles=(), rows=0, scratch=()):
    held = []
    sems = []
    if bundles:
        held = [pltpu.VMEM((2,) + bundles[0].shape[:2] + (rows, 128), jnp.bfloat16)]
        sems = [pltpu.SemaphoreType.DMA((2,))]
    places = [place for place, value in enumerate(values) if value.dtype != jnp.int32]
    specs = []
    for place, value in enumerate(values):
        space = pltpu.SMEM if value.dtype == jnp.int32 else pltpu.VMEM
        specs.append(pl.BlockSpec(memory_space=pltpu.HBM if place in places else space))
    late = []
    if places:
        kernel = functools.partial(framed, kernel, places, len(values))
        late = [pltpu.VMEM(values[place].shape, values[place].dtype) for place in places]
        late.append(pltpu.SemaphoreType.DMA((len(places),)))
    return pl.pallas_call(
        kernel,
        in_specs=specs + [pl.BlockSpec(memory_space=pltpu.HBM)] * len(bundles),
        out_specs=[pl.BlockSpec(memory_space=pltpu.VMEM)] * len(shapes),
        out_shape=list(shapes),
        scratch_shapes=held + [pltpu.VMEM(shape, jnp.float32) for shape in scratch] + sems + late,
        compiler_params=pltpu.CompilerParams(vmem_limit_bytes=VMEM_BYTES),
        cost_estimate=LIGHT,
    )(*values, *bundles)


def moved_by(grad, mean, square, weight, mean_out, square_out, update_out, at):
    first_fix = 1.0 - BETA_ONE**STEP
    second_fix = 1.0 - BETA_TWO**STEP
    old = weight[at]
    mean_next, square_next, step = adapt(grad, mean[at], square[at], first_fix, second_fix)
    update = step + DECAY * old
    mean_out[at] = mean_next
    square_out[at] = square_next
    update_out[at] = update
    result = []
    for value in (old, update):
        power = value * value
        while len(power.shape) > 2:
            power = jnp.sum(power, 0)
        row = jnp.sum(power, 0, keepdims=True)
        result.append(
            sum(row[:, place : place + 128] for place in range(0, row.shape[1], 128))
        )
    return result


def early_moves(columns, rows_a, rows_c, short_m, short_v, short_w, last_m, last_v, last_w, second_m, second_v,
                second_w, short_mo, short_vo, short_uo, last_mo, last_vo, last_uo, second_mo, second_vo,
                second_uo, powers):
    unit_in = short_w.shape[0]
    unit_out = second_w.shape[0]
    parts = short_w.shape[1] // 128
    every = (slice(None), slice(None))
    grad = jnp.concatenate(
        [rows_c[part * unit_in : (part + 1) * unit_in, :] for part in range(parts)], 1
    )
    found = moved_by(grad, short_m, short_v, short_w, short_mo, short_vo, short_uo, every)
    start = parts * unit_in
    for block, rows in enumerate((rows_c[start : start + unit_out, :], rows_a[...])):
        found += moved_by(
            jnp.transpose(rows), last_m, last_v, last_w, last_mo, last_vo, last_uo, block
        )
    start += unit_out
    found += moved_by(
        rows_c[start : start + unit_out, :], second_m, second_v, second_w, second_mo, second_vo,
        second_uo, every,
    )
    powers[...] = jnp.concatenate(found, 0)


def late_moves(rows_b, rows_d, rows_e, powers_in, first_m, first_v, first_w, mid_m, mid_v, mid_w, first_mo,
               first_vo, first_uo, mid_mo, mid_vo, mid_uo, powers):
    every = (slice(None), slice(None))
    found = moved_by(
        rows_e[...], first_m, first_v, first_w, first_mo, first_vo, first_uo, every
    )
    shape = mid_w.shape[1:]
    middle = []
    for block, rows in enumerate((rows_d, rows_b)):
        middle += moved_by(
            rows[...].reshape(shape), mid_m, mid_v, mid_w, mid_mo, mid_vo, mid_uo, block
        )
    early = powers_in[...]
    order = [found[0], found[1], early[0:2]] + middle + [early[2:8]]
    hand_out(powers, order)


def final_moves(powers, first_w, first_u, short_w, short_u, mid_w, mid_u, last_w, last_u, second_w, second_u,
                norms, first_o, short_o, mid_o, last_o, second_o, first_c, short_c, mid_c, last_c, second_c):
    total = jnp.sqrt(jnp.sum(jnp.sum(powers[...], 0), 1, keepdims=True))
    norms[...] = jnp.broadcast_to(total, norms.shape)

    def step(row, weight, update, out, copy, at):
        ratio = total[2 * row : 2 * row + 1] / (total[2 * row + 1 : 2 * row + 2] + EPS_TRUST)
        fresh = weight[at] - (RATE * ratio) * update[at]
        out[at] = fresh
        copy[at] = fresh.astype(jnp.bfloat16)

    every = (slice(None), slice(None))
    step(0, first_w, first_u, first_o, first_c, every)
    step(1, short_w, short_u, short_o, short_c, every)
    for block in range(2):
        for tap in range(mid_w.shape[1]):
            step(2 + block, mid_w, mid_u, mid_o, mid_c, (block, tap))
        step(4 + block, last_w, last_u, last_o, last_c, block)
    step(6, second_w, second_u, second_o, second_c, every)


def exchange(copies):
    return lax.all_to_all(copies, ("dp", "mp"), 0, 0, tiled=True)


def by_image(
    inputs,
    pixel_mask,
    widths,
    output_grad,
    first_weight,
    shortcut_weight,
    middle_weight,
    last_weight,
    second_weight,
    narrow_norms,
    wide_norms,
    first_mean,
    first_square,
    shortcut_mean,
    shortcut_square,
    middle_mean,
    middle_square,
    last_mean,
    last_square,
    second_mean,
    second_square,
    narrow_mean,
    narrow_square,
    wide_mean,
    wide_square,
):
    ranks = lax.axis_size("mp")
    rank = lax.axis_index("mp")
    pixels = pixel_mask.shape[1] // ranks
    narrow = first_weight.shape[1] * ranks
    wide = shortcut_weight.shape[1] * ranks
    low = jnp.bfloat16
    channels = inputs.shape[0]
    field = inputs.reshape(channels, 4, ranks, pixels).transpose(2, 1, 3, 0)
    field = field.reshape(ranks, 4 * pixels, channels)
    flow_a = Gather(pack(first_weight.astype(low)[None]), False)
    flow_b = Gather(pack(middle_weight[0].astype(low)))
    flow_c = Gather(
        jnp.concatenate(
            [
                pack(shortcut_weight.astype(low)[None]),
                pack(last_weight[0].astype(low).T[None]),
                pack(second_weight.astype(low)[None]),
            ]
        )
    )
    flow_d = Gather(
        jnp.concatenate(
            [pack(last_weight[1].astype(low).T[None]), pack(middle_weight[1].astype(low))]
        )
    )
    field = lax.all_to_all(field, "mp", 0, 0, tiled=True)
    tables = jnp.concatenate([narrow_norms.reshape(-1, 128), wide_norms.reshape(-1, 128)], 0)
    tables = jnp.broadcast_to(tables[None], (ranks,) + tables.shape)
    tables = lax.all_to_all(tables, "mp", 0, 0, tiled=True)
    wave([flow_a, flow_b])
    wave([flow_a, flow_b, flow_c], (field, tables))
    wave([flow_a, flow_b, flow_d])
    unit_in, column = first_weight.shape
    column_wide = shortcut_weight.shape[1]
    unit_mid = middle_weight.shape[2]
    unit_out = second_weight.shape[0]
    size_short = unit_in * column_wide // 128
    size_out = unit_out * column // 128
    size_mid = 9 * unit_mid * column // 128
    split = narrow_norms.size // 128
    narrow_all = (
        tables[:, :split].reshape(ranks, 4, 2, -1).transpose(1, 2, 0, 3).reshape(4, 2, narrow)
    )
    wide_all = tables[:, split:].reshape(ranks, 3, 2, -1).transpose(1, 2, 0, 3).reshape(3, 2, wide)

    narrow_all = narrow_all.reshape(8, narrow)
    wide_all = jnp.concatenate([wide_all.reshape(6, wide), jnp.zeros((2, wide), jnp.float32)], 0)

    own_mask = lax.dynamic_slice_in_dim(pixel_mask, rank * pixels, pixels, 1).astype(jnp.float32)
    mask_in = own_mask.reshape(-1, 1)
    mask = own_mask[0][:, None]
    channel = lax.iota(jnp.int32, narrow)[None]
    keep = (channel < widths[:, None]).astype(jnp.float32)
    keep = jnp.concatenate([keep, jnp.zeros((6, narrow), jnp.float32)], 0)
    place = lax.iota(jnp.int32, pixels)[:, None]
    step = lax.iota(jnp.int32, 9)[None]
    row_at = place // WO % HO + step // 3 - 1
    col_at = place % WO + step % 3 - 1
    inside = (row_at >= 0) & (row_at < HO) & (col_at >= 0) & (col_at < WO)
    inside = inside.astype(jnp.float32)
    core = bit_of("mp", 1)[None]

    above = output_grad.reshape(-1, ranks, pixels).transpose(1, 2, 0)
    above = lax.all_to_all(above, "mp", 0, 0, tiled=True)

    devices = ranks * lax.axis_size("dp")
    full = 4 * pixels

    def real(*shape):
        return jax.ShapeDtypeStruct(shape, jnp.float32)

    def short(*shape):
        return jax.ShapeDtypeStruct(shape, low)

    size = narrow // 128
    wide_rows = wide // 128
    copies = real(devices, 2 * size, 128)
    bundle_a = flow_a.bundles()
    field, pre_one, sums = launch(
        first_layer,
        [short(full, ranks * channels), real(full, narrow), real(devices, 2 * size + 8, 128)],
        [core, field, mask_in],
        bundle_a,
        unit_in,
    )
    sums_one = hold([flow_b, flow_c], exchange(sums))
    counts = jnp.sum(sums_one[:, 2 * size :], 0)
    bundle_b = flow_b.bundles()
    cols_one, pre_two, sums = launch(
        functools.partial(spread_layer, 0, 0, STRIDED_TAPS),
        [short(pixels, 9 * narrow), real(pixels, narrow), copies],
        [core, pre_one, sums_one, counts, narrow_all, keep, mask_in, mask, inside],
        bundle_b,
        size_mid,
    )
    sums_two = wave([flow_c], sums, exchange(sums))
    wave([flow_c, flow_d], sums_two)
    bundle_c = flow_c.bundles()
    pre_side, side_sums = launch(
        functools.partial(side_layer, 0),
        [real(pixels, wide), real(2 * wide_rows, 128)],
        [core, field, mask],
        bundle_c,
        size_short,
    )
    hid_two, pre_three, sums = launch(
        functools.partial(widen_layer, size_short, 1),
        [short(pixels, narrow), real(pixels, wide), real(2 * wide_rows, 128)],
        [core, pre_two, sums_two, counts, narrow_all, keep, mask],
        bundle_c,
        size_out,
        [(pixels, narrow)],
    )
    sums_pair = everywhere(jnp.concatenate([sums, side_sums], 0), [flow_d])
    out_one, pre_four, sums = launch(
        functools.partial(narrow_layer, size_short + size_out),
        [short(pixels, wide), real(pixels, narrow), copies],
        [core, pre_three, pre_side, sums_pair, counts, wide_all, mask],
        bundle_c,
        size_out,
    )
    sums_four = wave([flow_d], sums, exchange(sums))
    bundle_d = flow_d.bundles()
    cols_four, pre_five, sums = launch(
        functools.partial(spread_layer, size_out, 2, PLAIN_TAPS),
        [short(pixels, 9 * narrow), real(pixels, narrow), copies],
        [core, pre_four, sums_four, counts, narrow_all, keep, mask, mask, inside],
        bundle_d,
        size_mid,
    )
    sums_five = exchange(sums)
    hid_five, pre_six, sums = launch(
        functools.partial(widen_layer, 0, 3),
        [short(pixels, narrow), real(pixels, wide), real(2 * wide_rows, 128)],
        [core, pre_five, sums_five, counts, narrow_all, keep, mask],
        bundle_d,
        size_out,
        [(pixels, narrow)],
    )
    sums_six = everywhere(sums)
    block_output, grad_two, sums = launch(
        last_layer,
        [short(*above.shape), real(pixels, wide), real(2 * wide_rows, 128)],
        [pre_six, sums_six, counts, wide_all, out_one, above, mask],
    )
    back_six = everywhere(sums)
    back_six, block_output = lax.optimization_barrier((back_six, block_output))
    block_output = lax.all_to_all(block_output, "mp", 0, 0, tiled=True)
    shown = block_output
    block_output = block_output.transpose(2, 0, 1).reshape(-1, ranks * pixels)

    grad_six, act_five_grad, sums = launch(
        functools.partial(last_back, 0, 3),
        [short(pixels, wide), real(pixels, narrow), copies],
        [core, grad_two, pre_six, sums_six, back_six, counts, wide_all, pre_five,
         sums_five, narrow_all, keep, mask],
        bundle_d,
        size_out,
        [(pixels, narrow)],
    )
    bundle = chunks_into(None, size_out, 0, grad_six, hid_five, 1, unit_out, column)
    back_a = Scatter(*bundle)
    back_five, _ = lax.optimization_barrier((exchange(sums), shown))
    back_five = hold([back_a], back_five)
    grad_five, act_four_grad, sums = launch(
        functools.partial(spread_back, size_out, 2, PLAIN_TAPS),
        [short(pixels, narrow), real(pixels, narrow), copies],
        [core, act_five_grad, pre_five, sums_five, back_five, counts, narrow_all,
         pre_four, sums_four, keep, mask, mask, inside],
        bundle_d,
        size_mid,
        [(pixels, narrow)],
    )
    back_four = exchange(sums)
    bundle = chunks_into(None, size_mid, 0, cols_four, grad_five, 9, unit_mid, column)
    back_b = Scatter(*bundle)
    back_four = wave([back_a], sums, back_four)
    back_four = hold([back_b], back_four)
    grad_four, grad_one, sums = launch(
        functools.partial(narrow_layer_back, size_short + size_out),
        [short(pixels, narrow), real(pixels, wide), real(3 * wide_rows, 128)],
        [core, act_four_grad, pre_four, sums_four, back_four, counts, narrow_all, mask,
         grad_two, pre_three, pre_side, sums_pair, wide_all],
        bundle_c,
        size_out,
        [(pixels, narrow), (pixels, wide)],
    )
    back_pair = everywhere(sums, [back_a, back_b])
    total = size_short + 2 * size_out
    bundle = chunks_into(
        None, total, size_short + size_out, out_one, grad_four, 1, unit_out, column
    )
    back_pair, bundle = lax.optimization_barrier((back_pair, bundle))
    grad_three, grad_side, act_two_grad, sums = launch(
        functools.partial(pair_back, size_short, 1),
        [short(pixels, wide), short(pixels, wide), real(pixels, narrow), copies],
        [core, grad_one, pre_three, pre_side, sums_pair, back_pair, counts, wide_all,
         pre_two, sums_two, narrow_all, keep, mask],
        bundle_c,
        size_out,
        [(pixels, narrow), (pixels, wide)],
    )
    back_two = wave([back_a, back_b], sums, exchange(sums))
    bundle = chunks_into(bundle, total, size_short, grad_three, hid_two, 1, unit_out, column)
    bundle = chunks_into(bundle, total, 0, field, grad_side, 1, unit_in, column_wide)
    back_c = Scatter(*bundle)
    back_two = hold([back_c], back_two)
    grad_mid, act_one_grad, sums = launch(
        functools.partial(spread_back, 0, 0, STRIDED_TAPS),
        [short(pixels, narrow), real(full, narrow), copies],
        [core, act_two_grad, pre_two, sums_two, back_two, counts, narrow_all, pre_one,
         sums_one, keep, mask_in, mask, inside],
        bundle_b,
        size_mid,
        [(pixels, narrow)],
    )
    back_one = wave([back_b], sums, exchange(sums))
    back_one = wave([back_c], sums, back_one)
    bundle = chunks_into(None, size_mid, 0, cols_one, grad_mid, 9, unit_mid, column)
    back_d = Scatter(*bundle)
    (side_grad,) = launch(
        functools.partial(side_back, 0),
        [real(pixels, field.shape[1])],
        [grad_side],
        bundle_c,
        size_short,
    )
    back_one = hold([back_d], back_one)
    back_one, side_grad = lax.optimization_barrier((back_one, side_grad))
    grad_first, field_grad = launch(
        first_back,
        [short(full, narrow), short(ranks, full, channels)],
        [core, act_one_grad, pre_one, sums_one, back_one, counts, narrow_all, mask_in,
         side_grad],
        bundle_a,
        unit_in,
        [(full, narrow)],
    )
    grad_first = wave([back_c, back_d], back_one, grad_first)
    bundle = chunks_into(None, unit_in * column // 128, 0, field, grad_first, 1, unit_in, column)
    back_e = Scatter(*bundle, False)
    wave([back_e])
    input_grad = lax.all_to_all(field_grad, "mp", 0, 0, tiled=True)
    input_grad = input_grad.reshape(ranks, 4, pixels, channels).transpose(3, 1, 0, 2)
    input_grad = input_grad.reshape(inputs.shape)
    wave([back_c, back_d, back_e])
    wave([back_d, back_e])
    rows_a, rows_b, rows_c, rows_d, rows_e = [
        flow.rows() for flow in (back_a, back_b, back_c, back_d, back_e)
    ]
    first_fix = 1.0 - BETA_ONE**STEP
    second_fix = 1.0 - BETA_TWO**STEP

    def like(*values):
        return [real(*value.shape) for value in values for _ in range(3)]

    early = launch(
        functools.partial(early_moves, column),
        like(shortcut_weight, last_weight, second_weight) + [real(8, 128)],
        [rows_a, rows_c]
        + [
            shortcut_mean, shortcut_square, shortcut_weight, last_mean, last_square, last_weight,
            second_mean, second_square, second_weight,
        ],
    )
    late = launch(
        late_moves,
        like(first_weight, middle_weight) + [real(devices, 16, 128)],
        [rows_b, rows_d, rows_e, early[-1]]
        + [first_mean, first_square, first_weight, middle_mean, middle_square, middle_weight],
    )
    powers = exchange(late[-1])
    weights = (first_weight, shortcut_weight, middle_weight, last_weight, second_weight)
    updates = (late[2], early[2], late[5], early[5], early[8])
    norms, *fresh = launch(
        final_moves,
        [real(16, 128)]
        + [real(*value.shape) for value in weights]
        + [short(*value.shape) for value in weights],
        [powers]
        + [value for pair in zip(weights, updates) for value in pair],
    )
    matrix_norms = norms[:14, 0].reshape(7, 2)
    first_next, short_next, middle_next, last_next, second_next = fresh[:5]
    states = [late[0:2], early[0:2], late[3:5], early[3:5], early[6:8]]

    def own_channels(values):
        width = values.shape[-1] // ranks
        return lax.dynamic_slice_in_dim(values, rank * width, width, values.ndim - 1)

    narrow_grads = jnp.stack([jnp.sum(rows, 0) for rows in (back_one, back_two, back_four, back_five)])
    narrow_grad = own_channels(narrow_grads.reshape(4, 2, narrow))
    gain_three, gain_side, bias_pair = jnp.sum(back_pair, 0).reshape(3, wide)
    wide_grad = own_channels(
        jnp.stack(
            [
                jnp.stack([gain_three, bias_pair]),
                jnp.stack([gain_side, bias_pair]),
                jnp.sum(back_six, 0).reshape(2, wide),
            ]
        )
    )
    narrow_mean_next, narrow_square_next, narrow_step = adapt(
        narrow_grad, narrow_mean, narrow_square, first_fix, second_fix
    )
    wide_mean_next, wide_square_next, wide_step = adapt(
        wide_grad, wide_mean, wide_square, first_fix, second_fix
    )
    return (
        block_output,
        input_grad,
        states[0][0],
        states[0][1],
        first_next,
        states[1][0],
        states[1][1],
        short_next,
        states[2][0],
        states[2][1],
        middle_next,
        states[3][0],
        states[3][1],
        last_next,
        states[4][0],
        states[4][1],
        second_next,
        narrow_mean_next,
        narrow_square_next,
        narrow_norms - RATE_NORM * narrow_step,
        wide_mean_next,
        wide_square_next,
        wide_norms - RATE_NORM * wide_step,
        matrix_norms,
        *fresh[5:],
    )


def solution(mesh):
    in_specs = (
        P("mp", None, "dp"),
        P(None, "dp"),
        P(),
        P("mp", "dp"),
        P("dp", "mp"),
        P("dp", "mp"),
        P(None, None, "dp", "mp"),
        P(None, "mp", "dp"),
        P("dp", "mp"),
        P(None, None, "mp"),
        P(None, None, "mp"),
        P("dp", "mp"),
        P("dp", "mp"),
        P("dp", "mp"),
        P("dp", "mp"),
        P(None, None, "dp", "mp"),
        P(None, None, "dp", "mp"),
        P(None, "mp", "dp"),
        P(None, "mp", "dp"),
        P("dp", "mp"),
        P("dp", "mp"),
        P(None, None, "mp"),
        P(None, None, "mp"),
        P(None, None, "mp"),
        P(None, None, "mp"),
    )
    out_specs = (
        P("mp", "dp"),
        P("mp", None, "dp"),
        P("dp", "mp"),
        P("dp", "mp"),
        P("dp", "mp"),
        P("dp", "mp"),
        P("dp", "mp"),
        P("dp", "mp"),
        P(None, None, "dp", "mp"),
        P(None, None, "dp", "mp"),
        P(None, None, "dp", "mp"),
        P(None, "mp", "dp"),
        P(None, "mp", "dp"),
        P(None, "mp", "dp"),
        P("dp", "mp"),
        P("dp", "mp"),
        P("dp", "mp"),
        P(None, None, "mp"),
        P(None, None, "mp"),
        P(None, None, "mp"),
        P(None, None, "mp"),
        P(None, None, "mp"),
        P(None, None, "mp"),
        P(),
        P("dp", "mp"),
        P("dp", "mp"),
        P(None, None, "dp", "mp"),
        P(None, "mp", "dp"),
        P("dp", "mp"),
    )
    return jax.shard_map(
        lambda *values: (by_image if fits(mesh, values[1]) else shards)(*values),
        mesh=mesh,
        in_specs=in_specs,
        out_specs=out_specs,
        check_vma=False,
    )
```

```python
import functools

import jax
import jax.numpy as jnp
from jax import lax
from jax.experimental import pallas as pl
from jax.experimental.pallas import tpu as pltpu
from jax.sharding import PartitionSpec as P

HO = 16
WO = 11
STEP = 10


EPS_NORM = 1e-05
BETA_ONE = 0.9
BETA_TWO = 0.999
EPS_ADAM = 1e-06
DECAY = 0.01
RATE = 0.3
RATE_NORM = 0.3
EPS_TRUST = 1e-06
PHASES = ((1, -1), (0, 0), (1, 0))
STRIDED_TAPS = tuple(
    (
        (
            3 * above + beside,
            2 * PHASES[above][0] + PHASES[beside][0],
            PHASES[above][1],
            PHASES[beside][1],
        )
        for above in range(3)
        for beside in range(3)
    )
)
PLAIN_TAPS = tuple(
    ((3 * above + beside, 0, above - 1, beside - 1) for above in range(3) for beside in range(3))
)


def slope(values):
    gate = jax.nn.sigmoid(values)
    return gate * (1.0 + values * (1.0 - gate))


def shifted(values, drow, dcol):
    length = values.shape[1]
    offset = drow * WO + dcol
    place = lax.iota(jnp.int32, length)
    row_at = place // WO % HO + drow
    col_at = place % WO + dcol
    inside = (row_at >= 0) & (row_at < HO) & (col_at >= 0) & (col_at < WO)
    moved = jnp.roll(values, -offset, axis=1)
    return jnp.where(inside[None, :], moved, jnp.zeros_like(moved))


def over_images(first, second):
    return lax.psum((first, second), "dp")


def moments(values, mask):
    weighted = values * mask[None, :]
    return over_images(jnp.sum(weighted, 1), jnp.sum(weighted * values, 1))


def normalize(values, totals, squares, count, gain, bias):
    mean = totals / count
    scale = lax.rsqrt(squares / count - mean * mean + EPS_NORM)
    centred = (values - mean[:, None]) * scale[:, None]
    return (centred, scale, centred * gain[:, None] + bias[:, None])


def back_sums(grad_in, centred):
    return over_images(jnp.sum(grad_in * centred, 1), jnp.sum(grad_in, 1))


def norm_back(grad_in, centred, scale, gain, mask, gain_sum, bias_sum, count):
    return (gain * scale)[:, None] * (
        grad_in - mask[None, :] * (bias_sum[:, None] + centred * gain_sum[:, None]) / count
    )


def input_mix(values, weight, side_weight, pixels):
    start_sum = (jnp.zeros((weight.shape[1], values.shape[1]), jnp.float32),)
    if side_weight is not None:
        start_sum = start_sum + (jnp.zeros((side_weight.shape[1], pixels), jnp.float32),)
    piece = lax.all_gather(values, "mp", axis=0, tiled=True)
    result = (jnp.einsum("kc,kp->cp", weight, piece, preferred_element_type=jnp.float32),)
    if side_weight is not None:
        result = result + (
            jnp.einsum(
                "kc,kp->cp", side_weight, piece[:, :pixels], preferred_element_type=jnp.float32
            ),
        )
    return result


def mid_gathered(hidden):
    return lax.all_gather(hidden, "mp", axis=0, tiled=True)


def conv_forward(gathered, kernel, taps, pixels):
    result = jnp.zeros((kernel.shape[2], pixels), jnp.float32)
    for tap, phase, drow, dcol in taps:
        source = gathered[:, phase * pixels : (phase + 1) * pixels]
        part = jnp.einsum("kc,kp->cp", kernel[tap], source, preferred_element_type=jnp.float32)
        result = result + shifted(part, drow, dcol)
    return result


def conv_backward(grad_b, gathered, kernel, taps, pixels, phases):
    moved = [shifted(grad_b, -drow, -dcol) for tap, phase, drow, dcol in taps]
    count = gathered.shape[0] // lax.axis_size("mp") * lax.axis_size("mp")
    blocks = []
    for target in range(phases):
        result = jnp.zeros((count, pixels), jnp.float32)
        for conv_index, (conv_tap, conv_phase, conv_drow, conv_dcol) in enumerate(taps):
            if conv_phase == target:
                part = kernel[conv_tap]
                result = result + jnp.dot(
                    part, moved[conv_index], preferred_element_type=jnp.float32
                )
        blocks.append(result)
    hidden_grad = lax.psum_scatter(
        jnp.concatenate(blocks, 1), "mp", scatter_dimension=0, tiled=True
    )
    kernel_grad = jnp.stack(
        [
            jnp.einsum(
                "kp,cp->kc",
                gathered[:, phase * pixels : (phase + 1) * pixels],
                moved[index],
                preferred_element_type=jnp.float32,
            )
            for index, (tap, phase, drow, dcol) in enumerate(taps)
        ]
    )
    return (hidden_grad, kernel_grad)


def output_mix(hidden, kernel):
    return lax.psum_scatter(
        jnp.einsum("kc,kp->cp", kernel, hidden, preferred_element_type=jnp.float32),
        "mp",
        scatter_dimension=0,
        tiled=True,
    )


def output_back(grad_b, kernel, hidden):
    piece = lax.all_gather(grad_b, "mp", axis=0, tiled=True)
    hidden_grad = jnp.dot(kernel, piece, preferred_element_type=jnp.float32)
    columns = jnp.einsum("cp,kp->ck", hidden, piece, preferred_element_type=jnp.float32)
    return (hidden_grad, columns)


def input_back(values, grad_b, side_b, weight, side_weight, pixels):
    width = weight.shape[1]
    result = jnp.dot(weight, grad_b, preferred_element_type=jnp.float32)
    if side_weight is not None:
        result = jnp.concatenate(
            [
                result[:, :pixels]
                + jnp.dot(side_weight, side_b, preferred_element_type=jnp.float32),
                result[:, pixels:],
            ],
            1,
        )
    values_grad = lax.psum_scatter(result, "mp", scatter_dimension=0, tiled=True)
    piece = lax.all_gather(values, "mp", axis=0, tiled=True)
    blocks = [jnp.einsum("kp,cp->kc", piece, grad_b, preferred_element_type=jnp.float32)]
    if side_weight is not None:
        blocks.append(
            jnp.einsum("kp,cp->kc", piece[:, :pixels], side_b, preferred_element_type=jnp.float32)
        )
    joined = jnp.concatenate(blocks, 1)
    return (values_grad, joined[:, :width], joined[:, width:])


def adapt(grad_in, mean, square, first_fix, second_fix):
    mean_next = BETA_ONE * mean + (1.0 - BETA_ONE) * grad_in
    square_next = BETA_TWO * square + (1.0 - BETA_TWO) * grad_in * grad_in
    step = mean_next / first_fix / (jnp.sqrt(square_next / second_fix) + EPS_ADAM)
    return (mean_next, square_next, step)


def shards(
    inputs,
    pixel_mask,
    widths,
    output_grad,
    first_weight,
    shortcut_weight,
    middle_weight,
    last_weight,
    second_weight,
    narrow_norms,
    wide_norms,
    first_mean,
    first_square,
    shortcut_mean,
    shortcut_square,
    middle_mean,
    middle_square,
    last_mean,
    last_square,
    second_mean,
    second_square,
    narrow_mean,
    narrow_square,
    wide_mean,
    wide_square,
):
    pixels = pixel_mask.shape[1]
    width = first_weight.shape[1]
    rank = lax.axis_index("mp")
    channel = rank * width + lax.iota(jnp.int32, width)
    keep_one = (channel < widths[0]).astype(jnp.float32)[:, None]
    keep_two = (channel < widths[1]).astype(jnp.float32)[:, None]
    masks = pixel_mask.astype(jnp.float32)
    mask_in = masks.reshape(-1)
    mask_out = masks[0]
    field = (inputs * pixel_mask.astype(jnp.bfloat16)[None]).reshape(inputs.shape[0], -1)
    first_w, short_w, middle_w, last_w, second_w = (
        lax.all_gather(first_weight.astype(jnp.bfloat16), "dp", axis=0, tiled=True),
        lax.all_gather(shortcut_weight.astype(jnp.bfloat16), "dp", axis=0, tiled=True),
        lax.all_gather(middle_weight.astype(jnp.bfloat16), "dp", axis=2, tiled=True),
        lax.all_gather(last_weight.astype(jnp.bfloat16), "dp", axis=2, tiled=True),
        lax.all_gather(second_weight.astype(jnp.bfloat16), "dp", axis=0, tiled=True),
    )
    count_in, count_out = over_images(jnp.sum(mask_in), jnp.sum(mask_out))
    pre_one, pre_side = input_mix(field, first_w, short_w, pixels)
    totals, squares = moments(pre_one, mask_in)
    cen_one, scale_one, act_one = normalize(
        pre_one, totals, squares, count_in, narrow_norms[0, 0], narrow_norms[0, 1]
    )
    hid_one = (jax.nn.silu(act_one) * mask_in[None, :] * keep_one).astype(jnp.bfloat16)
    gat_one = mid_gathered(hid_one)
    pre_two = conv_forward(gat_one, middle_w[0], STRIDED_TAPS, pixels)
    totals, squares = moments(pre_two, mask_out)
    cen_two, scale_two, act_two = normalize(
        pre_two, totals, squares, count_out, narrow_norms[1, 0], narrow_norms[1, 1]
    )
    hid_two = (jax.nn.silu(act_two) * mask_out[None, :] * keep_one).astype(jnp.bfloat16)
    pre_three = output_mix(hid_two, last_w[0])
    weighted_three = pre_three * mask_out[None, :]
    weighted_side = pre_side * mask_out[None, :]
    totals, squares = over_images(
        jnp.stack([jnp.sum(weighted_three, 1), jnp.sum(weighted_side, 1)]),
        jnp.stack([jnp.sum(weighted_three * pre_three, 1), jnp.sum(weighted_side * pre_side, 1)]),
    )
    cen_three, scale_three, act_three = normalize(
        pre_three, totals[0], squares[0], count_out, wide_norms[0, 0], wide_norms[0, 1]
    )
    cen_side, scale_side, act_side = normalize(
        pre_side, totals[1], squares[1], count_out, wide_norms[1, 0], wide_norms[1, 1]
    )
    total_one = act_three + act_side
    out_one = (jax.nn.silu(total_one) * mask_out[None, :]).astype(jnp.bfloat16)
    (pre_four,) = input_mix(out_one, second_w, None, pixels)
    totals, squares = moments(pre_four, mask_out)
    cen_four, scale_four, act_four = normalize(
        pre_four, totals, squares, count_out, narrow_norms[2, 0], narrow_norms[2, 1]
    )
    hid_four = (jax.nn.silu(act_four) * mask_out[None, :] * keep_two).astype(jnp.bfloat16)
    gat_four = mid_gathered(hid_four)
    pre_five = conv_forward(gat_four, middle_w[1], PLAIN_TAPS, pixels)
    totals, squares = moments(pre_five, mask_out)
    cen_five, scale_five, act_five = normalize(
        pre_five, totals, squares, count_out, narrow_norms[3, 0], narrow_norms[3, 1]
    )
    hid_five = (jax.nn.silu(act_five) * mask_out[None, :] * keep_two).astype(jnp.bfloat16)
    pre_six = output_mix(hid_five, last_w[1])
    totals, squares = moments(pre_six, mask_out)
    cen_six, scale_six, act_six = normalize(
        pre_six, totals, squares, count_out, wide_norms[2, 0], wide_norms[2, 1]
    )
    total_two = act_six + out_one.astype(jnp.float32)
    block_output = (jax.nn.silu(total_two) * mask_out[None, :]).astype(jnp.bfloat16)
    grad_two = output_grad.astype(jnp.float32) * mask_out[None, :] * slope(total_two)
    gain_six, bias_six = back_sums(grad_two, cen_six)
    grad_six = norm_back(
        grad_two, cen_six, scale_six, wide_norms[2, 0], mask_out, gain_six, bias_six, count_out
    ).astype(jnp.bfloat16)
    hid_five_grad, last_one_grad = output_back(grad_six, last_w[1], hid_five)
    act_five_grad = hid_five_grad * keep_two * mask_out[None, :] * slope(act_five)
    gain_five, bias_five = back_sums(act_five_grad, cen_five)
    grad_five = norm_back(
        act_five_grad,
        cen_five,
        scale_five,
        narrow_norms[3, 0],
        mask_out,
        gain_five,
        bias_five,
        count_out,
    ).astype(jnp.bfloat16)
    hid_four_grad, middle_one_grad = conv_backward(
        grad_five, gat_four, middle_w[1], PLAIN_TAPS, pixels, 1
    )
    act_four_grad = hid_four_grad * keep_two * mask_out[None, :] * slope(act_four)
    gain_four, bias_four = back_sums(act_four_grad, cen_four)
    grad_four = norm_back(
        act_four_grad,
        cen_four,
        scale_four,
        narrow_norms[2, 0],
        mask_out,
        gain_four,
        bias_four,
        count_out,
    ).astype(jnp.bfloat16)
    out_one_grad, second_grad, unused_side = input_back(
        out_one, grad_four, None, second_w, None, pixels
    )
    grad_one = (grad_two + out_one_grad) * mask_out[None, :] * slope(total_one)
    gains_pair, bias_pair = over_images(
        jnp.stack([jnp.sum(grad_one * cen_three, 1), jnp.sum(grad_one * cen_side, 1)]),
        jnp.sum(grad_one, 1),
    )
    grad_three = norm_back(
        grad_one,
        cen_three,
        scale_three,
        wide_norms[0, 0],
        mask_out,
        gains_pair[0],
        bias_pair,
        count_out,
    ).astype(jnp.bfloat16)
    grad_side = norm_back(
        grad_one,
        cen_side,
        scale_side,
        wide_norms[1, 0],
        mask_out,
        gains_pair[1],
        bias_pair,
        count_out,
    ).astype(jnp.bfloat16)
    hid_two_grad, last_zero_grad = output_back(grad_three, last_w[0], hid_two)
    act_two_grad = hid_two_grad * keep_one * mask_out[None, :] * slope(act_two)
    gain_two, bias_two = back_sums(act_two_grad, cen_two)
    grad_mid = norm_back(
        act_two_grad,
        cen_two,
        scale_two,
        narrow_norms[1, 0],
        mask_out,
        gain_two,
        bias_two,
        count_out,
    ).astype(jnp.bfloat16)
    hid_one_grad, middle_zero_grad = conv_backward(
        grad_mid, gat_one, middle_w[0], STRIDED_TAPS, pixels, 4
    )
    act_one_grad = hid_one_grad * keep_one * mask_in[None, :] * slope(act_one)
    gain_one, bias_one = back_sums(act_one_grad, cen_one)
    grad_first = norm_back(
        act_one_grad, cen_one, scale_one, narrow_norms[0, 0], mask_in, gain_one, bias_one, count_in
    ).astype(jnp.bfloat16)
    field_grad, first_grad, short_grad = input_back(
        field, grad_first, grad_side, first_w, short_w, pixels
    )
    input_grad = (field_grad * mask_in[None, :]).astype(jnp.bfloat16).reshape(inputs.shape)
    grads = (
        lax.psum_scatter(first_grad, "dp", scatter_dimension=0, tiled=True),
        lax.psum_scatter(short_grad, "dp", scatter_dimension=0, tiled=True),
        lax.psum_scatter(
            jnp.stack([middle_zero_grad, middle_one_grad]), "dp", scatter_dimension=2, tiled=True
        ),
        lax.psum_scatter(
            jnp.stack([last_zero_grad, last_one_grad]), "dp", scatter_dimension=2, tiled=True
        ),
        lax.psum_scatter(second_grad, "dp", scatter_dimension=0, tiled=True),
    )
    first_fix = 1.0 - BETA_ONE**STEP
    second_fix = 1.0 - BETA_TWO**STEP
    weights = (first_weight, shortcut_weight, middle_weight, last_weight, second_weight)
    means = (first_mean, shortcut_mean, middle_mean, last_mean, second_mean)
    squares_old = (first_square, shortcut_square, middle_square, last_square, second_square)
    states = []
    updates = []
    for index in range(5):
        mean_next, square_next, step = adapt(
            grads[index], means[index], squares_old[index], first_fix, second_fix
        )
        states.append((mean_next, square_next))
        updates.append(step + DECAY * weights[index])
    pairs = [
        (weights[0], updates[0]),
        (weights[1], updates[1]),
        (weights[2][0], updates[2][0]),
        (weights[2][1], updates[2][1]),
        (weights[3][0], updates[3][0]),
        (weights[3][1], updates[3][1]),
        (weights[4], updates[4]),
    ]
    partial_value = jnp.stack(
        [
            jnp.stack([jnp.sum(weight * weight), jnp.sum(update * update)])
            for weight, update in pairs
        ]
    )
    matrix_norms = jnp.sqrt(lax.psum(partial_value, ("dp", "mp")))
    ratio = matrix_norms[:, 0] / (matrix_norms[:, 1] + EPS_TRUST)
    first_next = first_weight - RATE * ratio[0] * updates[0]
    short_next = shortcut_weight - RATE * ratio[1] * updates[1]
    middle_next = middle_weight - RATE * ratio[2:4].reshape(2, 1, 1, 1) * updates[2]
    last_next = last_weight - RATE * ratio[4:6].reshape(2, 1, 1) * updates[3]
    second_next = second_weight - RATE * ratio[6] * updates[4]
    narrow_grad = jnp.stack(
        [
            jnp.stack([gain_one, bias_one]),
            jnp.stack([gain_two, bias_two]),
            jnp.stack([gain_four, bias_four]),
            jnp.stack([gain_five, bias_five]),
        ]
    )
    wide_grad = jnp.stack(
        [
            jnp.stack([gains_pair[0], bias_pair]),
            jnp.stack([gains_pair[1], bias_pair]),
            jnp.stack([gain_six, bias_six]),
        ]
    )
    narrow_mean_next, narrow_square_next, narrow_step = adapt(
        narrow_grad, narrow_mean, narrow_square, first_fix, second_fix
    )
    wide_mean_next, wide_square_next, wide_step = adapt(
        wide_grad, wide_mean, wide_square, first_fix, second_fix
    )
    return (
        block_output,
        input_grad,
        states[0][0],
        states[0][1],
        first_next,
        states[1][0],
        states[1][1],
        short_next,
        states[2][0],
        states[2][1],
        middle_next,
        states[3][0],
        states[3][1],
        last_next,
        states[4][0],
        states[4][1],
        second_next,
        narrow_mean_next,
        narrow_square_next,
        narrow_norms - RATE_NORM * narrow_step,
        wide_mean_next,
        wide_square_next,
        wide_norms - RATE_NORM * wide_step,
        matrix_norms,
        first_next.astype(jnp.bfloat16),
        short_next.astype(jnp.bfloat16),
        middle_next.astype(jnp.bfloat16),
        last_next.astype(jnp.bfloat16),
        second_next.astype(jnp.bfloat16),
    )


VMEM_BYTES = 62 * 2**20
LIGHT = pl.CostEstimate(flops=1024, bytes_accessed=1024, transcendentals=0)


def fits(mesh, pixel_mask):
    sizes = (mesh.shape["dp"], mesh.shape["mp"])
    powers = all(size >= 2 and size & (size - 1) == 0 for size in sizes)
    return powers and pixel_mask.shape[1] % (HO * WO * sizes[1]) == 0


def swap(values, *bits):
    sizes = {axis: lax.axis_size(axis) for axis in ("dp", "mp")}
    masks = {axis: sum(mask for at, mask in bits if at == axis) for axis in sizes}
    if not masks["dp"]:
        return lax.ppermute(values, "mp", [(at, at ^ masks["mp"]) for at in range(sizes["mp"])])
    if not masks["mp"]:
        return lax.ppermute(values, "dp", [(at, at ^ masks["dp"]) for at in range(sizes["dp"])])
    mask = masks["dp"] * sizes["mp"] + masks["mp"]
    return lax.ppermute(
        values, ("dp", "mp"), [(at, at ^ mask) for at in range(sizes["dp"] * sizes["mp"])]
    )


def subsets(bits):
    return [
        [bit for place, bit in enumerate(bits) if index >> place & 1]
        for index in range(1 << len(bits))
    ]


def bit_of(axis, mask):
    return (lax.axis_index(axis) & mask) // mask


def high_bits(axis):
    masks = []
    mask = lax.axis_size(axis) // 2
    while mask:
        masks.append(mask)
        mask //= 2
    return masks


def everywhere(values, flows=()):
    mask = 1
    while mask < lax.axis_size("mp"):
        values = values + swap(values, ("mp", mask))
        mask *= 2
    copies = jnp.broadcast_to(values[None], (lax.axis_size("dp"),) + values.shape)
    arrived = lax.all_to_all(copies, "dp", 0, 0, tiled=True)
    return wave(flows, values, arrived) if flows else arrived


def pack(block):
    lead, rows, cols = block.shape
    parts = block.reshape(lead, rows, cols // 128, 128).transpose(0, 2, 1, 3)
    return parts.reshape(-1, 128)


def column_bits():
    return [("mp", mask) for mask in high_bits("mp")[:-1]]


def row_bits():
    return [("dp", mask) for mask in high_bits("dp")]


def lanes_of(rows):
    first = rows // 32 * 16
    return ((0, first), (first, rows))


def moves_kernel(tasks, count, places, *refs):
    sources, outs, sems = refs[:count], refs[count:-1], refs[-1]
    copies = []
    for at, (source, span, out, turns, rows) in enumerate(tasks):
        dims = len(sources[source].shape) - 2
        every = [slice(None)] * dims
        start = [
            pl.ds(1 - places[dim] if turns[dim] else places[dim], 1) if dim in turns else slice(None)
            for dim in range(dims)
        ]
        copies.append(
            pltpu.make_async_copy(
                sources[source].at[(*every, pl.ds(*span), slice(None))],
                outs[out].at[(*start, pl.ds(*rows), slice(None))],
                sems.at[at],
            )
        )
        copies[-1].start()
    for copy in copies:
        copy.wait()


def moves(wanted):
    sources = []
    tasks = []
    for out, (shape, pieces) in enumerate(wanted):
        for source, span, turns, rows in pieces:
            tasks.append((len(sources), span, out, turns, rows))
            sources.append(source)
    bits = column_bits() + row_bits()
    places = jnp.stack([bit_of(*bit) for bit in bits]).astype(jnp.int32)
    return pl.pallas_call(
        functools.partial(moves_kernel, tasks, len(sources)),
        in_specs=[pl.BlockSpec(memory_space=pltpu.SMEM)]
        + [pl.BlockSpec(memory_space=pltpu.HBM)] * len(sources),
        out_specs=[pl.BlockSpec(memory_space=pltpu.VMEM)] * len(wanted),
        out_shape=[jax.ShapeDtypeStruct(shape, jnp.bfloat16) for shape, _ in wanted],
        scratch_shapes=[pltpu.SemaphoreType.DMA((len(tasks),))],
        compiler_params=pltpu.CompilerParams(vmem_limit_bytes=VMEM_BYTES),
        cost_estimate=LIGHT,
    )(places, *sources)


class Gather:
    def __init__(self, rows, lanes=True):
        self.dims = column_bits() + row_bits()
        near = row_bits()[-1:]
        self.rows = rows.shape[0]
        if lanes:
            self.steps = [[row_bits()[:-1]], [near, column_bits()], [column_bits(), near]]
            self.spans = lanes_of(self.rows)
        else:
            self.steps = [[row_bits()[:-1]], [near + column_bits()]]
            self.spans = ((0, self.rows),)
        self.parts = [([rows.reshape((1,) * len(self.dims) + rows.shape)], [])]
        self.step = 0

    def pending(self):
        return [values for values, bits in self.parts]

    def resume(self, values):
        self.parts = [(value, bits) for value, (_, bits) in zip(values, self.parts)]

    def wanted(self):
        if not self.parts[0][1]:
            return []
        last = self.step == len(self.steps)
        split = not last and len(self.steps[self.step]) > len(self.parts)
        lanes = [(low, high - low) for low, high in self.spans]
        result = []
        for lane, (values, bits) in enumerate(self.parts):
            shape = [
                2 if bit in bits else size
                for bit, size in zip(self.dims, values[0].shape)
            ]
            pieces = [
                (value, {self.dims.index(bit): bit in turned for bit in bits})
                for value, turned in zip(values, subsets(bits))
            ]
            height = values[0].shape[-2]
            for low, size in lanes if split else [(0, height)]:
                block = [(value, (low, size), turns, (0, size)) for value, turns in pieces]
                result.append((tuple(shape) + (size, 128), block))
        if last:
            pieces = [
                (value, span, turns, lanes[lane])
                for lane, (_, block) in enumerate(result)
                for value, span, turns, _ in block
            ]
            result = [(result[0][0][:-2] + (self.rows, 128), pieces)]
        return result

    def launch(self, values):
        if not values:
            values = [self.parts[0][0][0]]
        if self.step < len(self.steps):
            self.parts = [
                ([value] + [swap(value, *bits) for bits in subsets(group)[1:]], group)
                for value, group in zip(values, self.steps[self.step])
            ]
        else:
            self.parts = [([values[0], swap(values[0], ("mp", 1))], [])]
        self.step += 1
        return values

    def bundles(self):
        shape = (1 << len(column_bits()), lax.axis_size("dp")) + self.parts[0][0][0].shape[-2:]
        return [value.reshape(shape) for value in self.parts[0][0]]


class Scatter:
    def __init__(self, keep, send, lanes=True):
        self.dims = column_bits() + row_bits()
        shape = (2,) * len(self.dims) + keep.shape[2:]
        near = row_bits()[-1:]
        far = row_bits()[:-1]
        if lanes:
            self.steps = [None, [column_bits(), near], [near, column_bits()], [far, far]]
            self.spans = lanes_of(keep.shape[2])
        else:
            self.steps = [None, [column_bits() + near], [far]]
            self.spans = (None,)
        self.lanes = [[] for _ in self.spans]
        self.raw = [keep.reshape(shape), send.reshape(shape)]
        self.step = 0

    def pending(self):
        return self.raw

    def resume(self, values):
        self.raw = list(values)

    def fold(self, lane, group=(), turned=()):
        total = 0.0
        for index, settled, span in self.lanes[lane]:
            value = self.raw[index]
            for bit in settled + list(group):
                place = bit_of(*bit)
                place = 1 - place if bit in turned else place
                value = lax.dynamic_slice_in_dim(value, place, 1, self.dims.index(bit))
            if span is not None:
                value = value[..., span[0] : span[1], :]
            total = total + value.astype(jnp.float32)
        return total

    def settle(self, lane, group, arrived, span):
        old = [(index, settled + group, part) for index, settled, part in self.lanes[lane]]
        self.lanes[lane] = old + [(index, [], span) for index in arrived]

    def wanted(self):
        return []

    def launch(self, values):
        groups = self.steps[self.step]
        whole = self.step == len(self.steps) - 1
        sent = []
        if groups is None:
            sent.append(self.raw[1])
            self.raw[1] = swap(self.raw[1], ("mp", 1))
            for lane, span in zip(self.lanes, self.spans):
                lane += [(0, [], span), (1, [], span)]
        elif whole:
            arrived = []
            for bits in subsets(groups[0])[1:]:
                out = [
                    self.fold(lane, groups[0], bits).astype(jnp.bfloat16)
                    for lane in range(len(self.lanes))
                ]
                out = jnp.concatenate(out, -2) if len(out) > 1 else out[0]
                arrived.append(len(self.raw))
                sent.append(out)
                self.raw.append(swap(out, *bits))
            for lane, span in enumerate(self.spans):
                self.settle(lane, groups[lane], arrived, span)
        else:
            for lane, group in enumerate(groups):
                arrived = []
                for bits in subsets(group)[1:]:
                    out = self.fold(lane, group, bits).astype(jnp.bfloat16)
                    arrived.append(len(self.raw))
                    sent.append(out)
                    self.raw.append(swap(out, *bits))
                self.settle(lane, group, arrived, None)
        self.step += 1
        return sent

    def rows(self):
        total = [self.fold(lane) for lane in range(len(self.lanes))]
        total = jnp.concatenate(total, -2) if len(total) > 1 else total[0]
        return total.reshape(total.shape[-2:])


def wave(flows, after=None, before=None):
    values = [flow.pending() for flow in flows]
    if after is not None:
        values, _ = lax.optimization_barrier((values, after))
    for flow, value in zip(flows, values):
        flow.resume(value)
    wanted = [flow.wanted() for flow in flows]
    joined = [value for part in wanted for value in part]
    made = list(moves(joined)) if joined else []
    sent = []
    for flow, part in zip(flows, wanted):
        sent += flow.launch([made.pop(0) for _ in part])
    if before is not None:
        before, _ = lax.optimization_barrier((before, sent))
    return before


def hold(flows, value):
    value, parts = lax.optimization_barrier((value, [flow.pending() for flow in flows]))
    for flow, part in zip(flows, parts):
        flow.resume(part)
    wave(flows)
    return value


def chunk_kernel(units, columns, rows_ref, cols_ref, *refs):
    outs = refs[-2:]
    product = lax.dot_general(
        rows_ref[...], cols_ref[...], (((0,), (0,)), ((), ())), preferred_element_type=jnp.float32
    ).astype(jnp.bfloat16)
    groups = outs[0].shape[0]
    chunks = outs[0].shape[1]
    for half, out in enumerate(outs):
        for group in range(groups):
            for part in range(columns):
                place = ((half * groups + group) * columns + part) * 128
                block = product[:, place : place + 128].reshape(chunks, units, 128)
                out[group, :, part * units : (part + 1) * units, :] = block


def chunks_into(bundle, total, start, rows_of, cols_of, lead, units, columns):
    count = lax.axis_size("dp")
    groups = 1 << len(column_bits())
    columns = columns // 128
    pixels = cols_of.shape[0]
    height = units * columns
    if lead > 1:
        steps, wide, chunks = lead, count * units, count
        place = lambda step: (0, 0, start // height + step, 0)
    else:
        steps, wide, chunks = count, units, 1
        place = lambda step: (0, step, start // height, 0)
    shape = jax.ShapeDtypeStruct((groups, count, total, 128), jnp.bfloat16)
    block = pl.BlockSpec((groups, chunks, height, 128), place)
    earlier = () if bundle is None else tuple(bundle)
    return pl.pallas_call(
        functools.partial(chunk_kernel, units, columns),
        grid=(steps,),
        in_specs=[
            pl.BlockSpec((pixels, wide), lambda step: (0, step)),
            pl.BlockSpec(cols_of.shape, lambda step: (0, 0)),
        ]
        + [pl.BlockSpec(memory_space=pltpu.HBM)] * len(earlier),
        out_specs=[block, block],
        out_shape=[shape, shape],
        input_output_aliases={2 + place: place for place in range(len(earlier))},
        compiler_params=pltpu.CompilerParams(vmem_limit_bytes=VMEM_BYTES),
        cost_estimate=LIGHT,
    )(rows_of, cols_of, *earlier)


def total_of(ref):
    return jnp.sum(ref[...], 0) if len(ref.shape) == 3 else ref[...]


def as_row(block):
    return jnp.concatenate([block[place : place + 1] for place in range(block.shape[0])], 1)


def as_rows(row):
    return jnp.concatenate(
        [row[:, place : place + 128] for place in range(0, row.shape[1], 128)], 0
    )


def hand_out(out, rows):
    missing = out.shape[-2] - sum(row.shape[0] for row in rows)
    if missing:
        rows = rows + [jnp.zeros((missing, 128), jnp.float32)]
    block = jnp.concatenate(rows, 0)
    out[...] = jnp.broadcast_to(block[None], out.shape) if len(out.shape) == 3 else block


def levels(total, first, width, count):
    rows = width // 128
    mean = total[first : first + rows] / count
    scale = lax.rsqrt(total[first + rows : first + 2 * rows] / count - mean * mean + EPS_NORM)
    return (as_row(mean), as_row(scale))


def standard(values, level):
    return (values - level[0]) * level[1]


def back_through(grad, centred, level, gain, mask, total, first, bias_first, count):
    rows = grad.shape[1] // 128
    gain_sum = as_row(total[first : first + rows] / count)
    bias_sum = as_row(total[bias_first : bias_first + rows] / count)
    return (gain * level[1]) * (grad - mask * (bias_sum + centred * gain_sum))


def column_sums(values, mask):
    weighted = values * mask
    return [
        as_rows(jnp.sum(weighted, 0, keepdims=True)),
        as_rows(jnp.sum(weighted * values, 0, keepdims=True)),
    ]


def product_sums(grad, centred):
    return as_rows(jnp.sum(grad * centred, 0, keepdims=True))


def plain_sums(grad):
    return as_rows(jnp.sum(grad, 0, keepdims=True))


def fetch(bundles, held, sems, start):
    rows = held.shape[3]
    copies = [
        pltpu.make_async_copy(ref.at[:, :, pl.ds(start, rows), :], held.at[half], sems.at[half])
        for half, ref in enumerate(bundles)
    ]
    for copy in copies:
        copy.start()
    return copies


def arrive(copies):
    for copy in copies:
        copy.wait()


def weight_part(held, chunk, chunks, start, units, columns):
    return jnp.concatenate(
        [
            held[half, group, chunk : chunk + chunks, start + part * units : start + (part + 1) * units, :]
            .reshape(chunks * units, 128)
            for half in range(2)
            for group in range(held.shape[1])
            for part in range(columns)
        ],
        1,
    )


def spots(core, groups, width):
    return [
        pl.multiple_of((2 * group + (core if half == 0 else 1 - core)) * width, 128)
        for half in range(2)
        for group in range(groups)
    ]


def in_turn(ref, core, groups):
    width = ref.shape[1] // (2 * groups)
    return jnp.concatenate([ref[:, pl.ds(at, width)] for at in spots(core, groups, width)], 1)


def in_order(ref, values, core, groups):
    width = ref.shape[1] // (2 * groups)
    for place, at in enumerate(spots(core, groups, width)):
        ref[:, pl.ds(at, width)] = values[:, place * width : (place + 1) * width]


def product(first, second):
    return lax.dot_general(
        first, second, (((1,), (0,)), ((), ())), preferred_element_type=jnp.float32
    )


def product_turned(first, second):
    return lax.dot_general(
        first, second, (((1,), (1,)), ((), ())), preferred_element_type=jnp.float32
    )


def many_in(values, held, units, columns):
    chunks = max(1, 256 // units)
    total = 0.0
    for chunk in range(0, held.shape[2], chunks):
        part = weight_part(held, chunk, chunks, 0, units, columns)
        total = total + product(
            values[:, chunk * units : (chunk + chunks) * units], part
        )
    return total


def many_out(values, held, units, columns):
    chunks = max(1, 256 // units)
    return [
        product_turned(values, weight_part(held, chunk, chunks, 0, units, columns))
        for chunk in range(0, held.shape[2], chunks)
    ]


def slid(values, offset):
    count = values.shape[0]
    return pltpu.roll(values, (-offset) % count, 0) if offset % count else values


def within(inside, drow, dcol):
    place = 3 * (drow + 1) + dcol + 1
    return inside[:, place : place + 1]


def first_layer(core, raw, mask, first, second, field, out, sums, held, sems):
    copies = fetch((first, second), held, sems, 0)
    core = core[0]
    weights = mask[...]
    width = raw.shape[2]
    for place in range(raw.shape[0]):
        part = raw[place].astype(jnp.float32) * weights
        field[:, place * width : (place + 1) * width] = part.astype(jnp.bfloat16)
    arrive(copies)
    result = many_in(field, held, held.shape[3], 1)
    in_order(out, result, core, held.shape[1])
    rows = column_sums(out[...], weights)
    pixels = weights.shape[0] // 4
    for part in (weights, weights[:pixels]):
        rows.append(jnp.broadcast_to(jnp.sum(part, 0, keepdims=True), (1, 128)))
    hand_out(sums, rows)


def side_layer(start, core, field, mask, first, second, out, sums, held, sems):
    copies = fetch((first, second), held, sems, start)
    core = core[0]
    pixels = mask.shape[0]
    arrive(copies)
    columns = out.shape[1] // (2 * held.shape[1] * 128)
    result = many_in(field[:pixels, :], held, held.shape[3] // columns, columns)
    in_order(out, result, core, held.shape[1])
    hand_out(sums, column_sums(out[...], mask[...]))


def spread_layer(start, norm, taps, core, before, sums_in, counts, tables, keep, mask_in, mask, inside,
                 first, second, cols, out, sums, held, sems):
    copies = fetch((first, second), held, sems, start)
    core = core[0]
    pixels = mask.shape[0]
    width = before.shape[1]
    counted = 0 if before.shape[0] > pixels else 1
    level = levels(total_of(sums_in), 0, width, counts[counted : counted + 1, :])
    act = standard(before[...], level) * tables[2 * norm : 2 * norm + 1, :] + tables[2 * norm + 1 : 2 * norm + 2, :]
    row = norm // 2
    hidden = jax.nn.silu(act) * mask_in[...] * keep[row : row + 1, :]
    for tap, phase, drow, dcol in taps:
        source = hidden[phase * pixels : (phase + 1) * pixels]
        moved = slid(source, drow * WO + dcol) * within(inside, drow, dcol)
        cols[:, tap * width : (tap + 1) * width] = moved.astype(jnp.bfloat16)
    arrive(copies)
    units = held.shape[3] // 9
    total = 0.0
    for tap in range(9):
        part = weight_part(held, 0, held.shape[2], tap * units, units, 1)
        total = total + product(cols[:, tap * width : (tap + 1) * width], part)
    in_order(out, total, core, held.shape[1])
    hand_out(sums, column_sums(out[...], mask[...]))


def widen_layer(start, norm, core, before, sums_in, counts, tables, keep, mask, first, second,
                hidden, out, sums, held, scratch, sems):
    copies = fetch((first, second), held, sems, start)
    core = core[0]
    level = levels(total_of(sums_in), 0, before.shape[1], counts[1:2, :])
    act = standard(before[...], level) * tables[2 * norm : 2 * norm + 1, :] + tables[2 * norm + 1 : 2 * norm + 2, :]
    row = norm // 2
    scratch[...] = jax.nn.silu(act) * mask[...] * keep[row : row + 1, :]
    hidden[...] = in_turn(scratch, core, held.shape[1]).astype(jnp.bfloat16)
    arrive(copies)
    parts = many_out(hidden[...], held, held.shape[3], 1)
    size = out.shape[1] // len(parts)
    for place, part in enumerate(parts):
        out[:, place * size : (place + 1) * size] = part
    hand_out(sums, column_sums(out[...], mask[...]))


def joined_acts(total, third, side, wide, count):
    width = third.shape[1]
    rows = width // 128
    centred_third = standard(third[...], levels(total, 0, width, count))
    centred_side = standard(side[...], levels(total, 2 * rows, width, count))
    act = (
        centred_third * wide[0:1, :]
        + wide[1:2, :]
        + (centred_side * wide[2:3, :] + wide[3:4, :])
    )
    return (centred_third, centred_side, act)


def narrow_layer(start, core, third, side, sums_in, counts, wide, mask, first, second,
                 above, out, sums, held, sems):
    copies = fetch((first, second), held, sems, start)
    core = core[0]
    centred_third, centred_side, act = joined_acts(
        total_of(sums_in), third, side, wide, counts[1:2, :]
    )
    above[...] = (jax.nn.silu(act) * mask[...]).astype(jnp.bfloat16)
    arrive(copies)
    result = many_in(above, held, held.shape[3], 1)
    in_order(out, result, core, held.shape[1])
    hand_out(sums, column_sums(out[...], mask[...]))


def last_layer(sixth, sums_in, counts, wide, above, cotangent, mask, out, grad, sums):
    level = levels(total_of(sums_in), 0, sixth.shape[1], counts[1:2, :])
    centred = standard(sixth[...], level)
    act = centred * wide[4:5, :] + wide[5:6, :] + above[...].astype(jnp.float32)
    weights = mask[...]
    result = (jax.nn.silu(act) * weights).astype(jnp.bfloat16)
    inner = weights * slope(act)
    width = out.shape[2]
    for place in range(out.shape[0]):
        span = slice(place * width, (place + 1) * width)
        out[place] = result[:, span]
        grad[:, span] = cotangent[place].astype(jnp.float32) * inner[:, span]
    result = grad[...]
    hand_out(sums, [product_sums(result, centred), plain_sums(result)])


def narrow_grad(grad, before, sums_in, counts, tables, norm, keep, mask):
    counted = 0 if norm == 0 else 1
    level = levels(total_of(sums_in), 0, before.shape[1], counts[counted : counted + 1, :])
    centred = standard(before[...], level)
    act = centred * tables[2 * norm : 2 * norm + 1, :] + tables[2 * norm + 1 : 2 * norm + 2, :]
    row = norm // 2
    result = grad * keep[row : row + 1, :] * mask * slope(act)
    return (result, [product_sums(result, centred), plain_sums(result)])


def narrow_back(norm, grad, before, sums_in, sums_back, counts, tables, mask):
    counted = 0 if norm == 0 else 1
    count = counts[counted : counted + 1, :]
    width = before.shape[1]
    level = levels(total_of(sums_in), 0, width, count)
    return back_through(
        grad[...],
        standard(before[...], level),
        level,
        tables[2 * norm : 2 * norm + 1, :],
        mask,
        total_of(sums_back),
        0,
        width // 128,
        count,
    )


def last_back(start, norm, core, grad, sixth, sums_six, back_six, counts, wide, before, sums_in, tables,
              keep, mask, first, second, grad_out, grad_in, sums, held, scratch, sems):
    copies = fetch((first, second), held, sems, start)
    core = core[0]
    width = sixth.shape[1]
    count = counts[1:2, :]
    level = levels(total_of(sums_six), 0, width, count)
    grad_out[...] = back_through(
        grad[...], standard(sixth[...], level), level, wide[4:5, :], mask[...], total_of(back_six), 0,
        width // 128, count,
    ).astype(jnp.bfloat16)
    arrive(copies)
    in_order(scratch, many_in(grad_out, held, held.shape[3], 1), core, held.shape[1])
    result, rows = narrow_grad(scratch[...], before, sums_in, counts, tables, norm, keep, mask[...])
    grad_in[...] = result
    hand_out(sums, rows)


def pair_back(start, norm, core, grad, third, side, sums_pair, back_pair, counts, wide, before, sums_in,
              tables, keep, mask, first, second, grad_third, grad_side, grad_in, sums, held, scratch,
              big, sems):
    copies = fetch((first, second), held, sems, start)
    core = core[0]
    width = third.shape[1]
    rows = width // 128
    count = counts[1:2, :]
    total = total_of(sums_pair)
    back = total_of(back_pair)
    groups = held.shape[1]
    level = levels(total, 0, width, count)
    grad_third[...] = back_through(
        grad[...], standard(third[...], level), level, wide[0:1, :], mask[...], back, 0, 2 * rows, count
    ).astype(jnp.bfloat16)
    arrive(copies)
    in_order(scratch, many_in(grad_third, held, held.shape[3], 1), core, groups)
    result, parts = narrow_grad(scratch[...], before, sums_in, counts, tables, norm, keep, mask[...])
    grad_in[...] = result
    hand_out(sums, parts)
    level = levels(total, 2 * rows, width, count)
    big[...] = back_through(
        grad[...], standard(side[...], level), level, wide[2:3, :], mask[...], back, rows, 2 * rows, count
    )
    grad_side[...] = in_turn(big, core, groups).astype(jnp.bfloat16)


def spread_back(start, norm, taps, core, grad, after, sums_after, back_after, counts, tables, before,
                sums_in, keep, mask_in, mask, inside, first, second, grad_out, grad_in, sums, held,
                scratch, sems):
    copies = fetch((first, second), held, sems, start)
    core = core[0]
    pixels = mask.shape[0]
    phases = before.shape[0] // pixels
    scratch[...] = narrow_back(norm + 1, grad, after, sums_after, back_after, counts, tables, mask[...])
    grad_out[...] = in_turn(scratch, core, held.shape[1]).astype(jnp.bfloat16)
    arrive(copies)
    units = held.shape[3] // 9
    totals = [0.0] * phases
    for tap, phase, drow, dcol in taps:
        part = weight_part(held, 0, held.shape[2], tap * units, units, 1)
        moved = product_turned(grad_out[...], part)
        totals[phase] = totals[phase] + slid(moved, -drow * WO - dcol) * within(inside, -drow, -dcol)
    hidden = jnp.concatenate(totals, 0) if phases > 1 else totals[0]
    result, rows = narrow_grad(hidden, before, sums_in, counts, tables, norm, keep, mask_in[...])
    grad_in[...] = result
    hand_out(sums, rows)


def narrow_layer_back(start, core, grad, fourth, sums_four, back_four, counts, tables, mask, grad_two,
                      third, side, sums_pair, wide, first, second, grad_out, grad_in, sums, held,
                      scratch, big, sems):
    copies = fetch((first, second), held, sems, start)
    core = core[0]
    scratch[...] = narrow_back(2, grad, fourth, sums_four, back_four, counts, tables, mask[...])
    grad_out[...] = in_turn(scratch, core, held.shape[1]).astype(jnp.bfloat16)
    arrive(copies)
    parts = many_out(grad_out[...], held, held.shape[3], 1)
    size = big.shape[1] // len(parts)
    for place, part in enumerate(parts):
        big[:, place * size : (place + 1) * size] = part
    centred_third, centred_side, act = joined_acts(
        total_of(sums_pair), third, side, wide, counts[1:2, :]
    )
    result = (grad_two[...] + big[...]) * mask[...] * slope(act)
    grad_in[...] = result
    hand_out(
        sums,
        [
            product_sums(result, centred_third),
            product_sums(result, centred_side),
            plain_sums(result),
        ],
    )


def side_back(start, grad, first, second, out, held, sems):
    copies = fetch((first, second), held, sems, start)
    arrive(copies)
    columns = grad.shape[1] // (2 * held.shape[1] * 128)
    parts = many_out(grad[...], held, held.shape[3] // columns, columns)
    size = out.shape[1] // len(parts)
    for place, part in enumerate(parts):
        out[:, place * size : (place + 1) * size] = part


def first_back(core, grad, before, sums_in, sums_back, counts, tables, mask, side, first, second,
               grad_out, out, held, scratch, sems):
    copies = fetch((first, second), held, sems, 0)
    core = core[0]
    scratch[...] = narrow_back(0, grad, before, sums_in, sums_back, counts, tables, mask[...])
    grad_out[...] = in_turn(scratch, core, held.shape[1]).astype(jnp.bfloat16)
    arrive(copies)
    parts = many_out(grad_out[...], held, held.shape[3], 1)
    size = side.shape[1] // len(parts)
    pixels = side.shape[0]
    weights = mask[...]
    width = out.shape[2]
    for place, part in enumerate(parts):
        owner = place * size // width
        span = slice(place * size % width, place * size % width + size)
        beside = side[:, place * size : (place + 1) * size]
        out[owner, :pixels, span] = ((part[:pixels] + beside) * weights[:pixels]).astype(jnp.bfloat16)
        out[owner, pixels:, span] = (part[pixels:] * weights[pixels:]).astype(jnp.bfloat16)


class Coming:
    def __init__(self, ref, copy):
        self.ref = ref
        self.copy = copy
        self.shape = ref.shape

    def settle(self):
        if self.copy is not None:
            self.copy.wait()
            self.copy = None

    def __getitem__(self, place):
        self.settle()
        return self.ref[place]


def framed(kernel, places, count, *refs):
    refs = list(refs)
    rest, held, sems = refs[: len(refs) - len(places) - 1], refs[-len(places) - 1 : -1], refs[-1]
    coming = []
    for at, place in enumerate(places):
        copy = pltpu.make_async_copy(rest[place], held[at], sems.at[at])
        copy.start()
        rest[place] = Coming(held[at], copy)
        coming.append(rest[place])
    kernel(*rest)
    for value in coming:
        value.settle()


def launch(kernel, shapes, values, bundles=(), rows=0, scratch=()):
    held = []
    sems = []
    if bundles:
        held = [pltpu.VMEM((2,) + bundles[0].shape[:2] + (rows, 128), jnp.bfloat16)]
        sems = [pltpu.SemaphoreType.DMA((2,))]
    places = [place for place, value in enumerate(values) if value.dtype != jnp.int32]
    specs = []
    for place, value in enumerate(values):
        space = pltpu.SMEM if value.dtype == jnp.int32 else pltpu.VMEM
        specs.append(pl.BlockSpec(memory_space=pltpu.HBM if place in places else space))
    late = []
    if places:
        kernel = functools.partial(framed, kernel, places, len(values))
        late = [pltpu.VMEM(values[place].shape, values[place].dtype) for place in places]
        late.append(pltpu.SemaphoreType.DMA((len(places),)))
    return pl.pallas_call(
        kernel,
        in_specs=specs + [pl.BlockSpec(memory_space=pltpu.HBM)] * len(bundles),
        out_specs=[pl.BlockSpec(memory_space=pltpu.VMEM)] * len(shapes),
        out_shape=list(shapes),
        scratch_shapes=held + [pltpu.VMEM(shape, jnp.float32) for shape in scratch] + sems + late,
        compiler_params=pltpu.CompilerParams(vmem_limit_bytes=VMEM_BYTES),
        cost_estimate=LIGHT,
    )(*values, *bundles)


def moved_by(grad, mean, square, weight, mean_out, square_out, update_out, at):
    first_fix = 1.0 - BETA_ONE**STEP
    second_fix = 1.0 - BETA_TWO**STEP
    old = weight[at]
    mean_next, square_next, step = adapt(grad, mean[at], square[at], first_fix, second_fix)
    update = step + DECAY * old
    mean_out[at] = mean_next
    square_out[at] = square_next
    update_out[at] = update
    result = []
    for value in (old, update):
        power = value * value
        while len(power.shape) > 2:
            power = jnp.sum(power, 0)
        row = jnp.sum(power, 0, keepdims=True)
        result.append(
            sum(row[:, place : place + 128] for place in range(0, row.shape[1], 128))
        )
    return result


def early_moves(columns, rows_a, rows_c, short_m, short_v, short_w, last_m, last_v, last_w, second_m, second_v,
                second_w, short_mo, short_vo, short_uo, last_mo, last_vo, last_uo, second_mo, second_vo,
                second_uo, powers):
    unit_in = short_w.shape[0]
    unit_out = second_w.shape[0]
    parts = short_w.shape[1] // 128
    every = (slice(None), slice(None))
    grad = jnp.concatenate(
        [rows_c[part * unit_in : (part + 1) * unit_in, :] for part in range(parts)], 1
    )
    found = moved_by(grad, short_m, short_v, short_w, short_mo, short_vo, short_uo, every)
    start = parts * unit_in
    for block, rows in enumerate((rows_c[start : start + unit_out, :], rows_a[...])):
        found += moved_by(
            jnp.transpose(rows), last_m, last_v, last_w, last_mo, last_vo, last_uo, block
        )
    start += unit_out
    found += moved_by(
        rows_c[start : start + unit_out, :], second_m, second_v, second_w, second_mo, second_vo,
        second_uo, every,
    )
    powers[...] = jnp.concatenate(found, 0)


def late_moves(rows_b, rows_d, rows_e, powers_in, first_m, first_v, first_w, mid_m, mid_v, mid_w, first_mo,
               first_vo, first_uo, mid_mo, mid_vo, mid_uo, powers):
    every = (slice(None), slice(None))
    found = moved_by(
        rows_e[...], first_m, first_v, first_w, first_mo, first_vo, first_uo, every
    )
    shape = mid_w.shape[1:]
    middle = []
    for block, rows in enumerate((rows_d, rows_b)):
        middle += moved_by(
            rows[...].reshape(shape), mid_m, mid_v, mid_w, mid_mo, mid_vo, mid_uo, block
        )
    early = powers_in[...]
    order = [found[0], found[1], early[0:2]] + middle + [early[2:8]]
    hand_out(powers, order)


def final_moves(powers, first_w, first_u, short_w, short_u, mid_w, mid_u, last_w, last_u, second_w, second_u,
                norms, first_o, short_o, mid_o, last_o, second_o, first_c, short_c, mid_c, last_c, second_c):
    total = jnp.sqrt(jnp.sum(jnp.sum(powers[...], 0), 1, keepdims=True))
    norms[...] = jnp.broadcast_to(total, norms.shape)

    def step(row, weight, update, out, copy, at):
        ratio = total[2 * row : 2 * row + 1] / (total[2 * row + 1 : 2 * row + 2] + EPS_TRUST)
        fresh = weight[at] - (RATE * ratio) * update[at]
        out[at] = fresh
        copy[at] = fresh.astype(jnp.bfloat16)

    every = (slice(None), slice(None))
    step(0, first_w, first_u, first_o, first_c, every)
    step(1, short_w, short_u, short_o, short_c, every)
    for block in range(2):
        for tap in range(mid_w.shape[1]):
            step(2 + block, mid_w, mid_u, mid_o, mid_c, (block, tap))
        step(4 + block, last_w, last_u, last_o, last_c, block)
    step(6, second_w, second_u, second_o, second_c, every)


def exchange(copies):
    return lax.all_to_all(copies, ("dp", "mp"), 0, 0, tiled=True)


def by_image(
    inputs,
    pixel_mask,
    widths,
    output_grad,
    first_weight,
    shortcut_weight,
    middle_weight,
    last_weight,
    second_weight,
    narrow_norms,
    wide_norms,
    first_mean,
    first_square,
    shortcut_mean,
    shortcut_square,
    middle_mean,
    middle_square,
    last_mean,
    last_square,
    second_mean,
    second_square,
    narrow_mean,
    narrow_square,
    wide_mean,
    wide_square,
):
    ranks = lax.axis_size("mp")
    rank = lax.axis_index("mp")
    pixels = pixel_mask.shape[1] // ranks
    narrow = first_weight.shape[1] * ranks
    wide = shortcut_weight.shape[1] * ranks
    low = jnp.bfloat16
    channels = inputs.shape[0]
    field = inputs.reshape(channels, 4, ranks, pixels).transpose(2, 1, 3, 0)
    field = field.reshape(ranks, 4 * pixels, channels)
    flow_a = Gather(pack(first_weight.astype(low)[None]), False)
    flow_b = Gather(pack(middle_weight[0].astype(low)))
    flow_c = Gather(
        jnp.concatenate(
            [
                pack(shortcut_weight.astype(low)[None]),
                pack(last_weight[0].astype(low).T[None]),
                pack(second_weight.astype(low)[None]),
            ]
        )
    )
    flow_d = Gather(
        jnp.concatenate(
            [pack(last_weight[1].astype(low).T[None]), pack(middle_weight[1].astype(low))]
        )
    )
    field = lax.all_to_all(field, "mp", 0, 0, tiled=True)
    tables = jnp.concatenate([narrow_norms.reshape(-1, 128), wide_norms.reshape(-1, 128)], 0)
    tables = jnp.broadcast_to(tables[None], (ranks,) + tables.shape)
    tables = lax.all_to_all(tables, "mp", 0, 0, tiled=True)
    wave([flow_a, flow_b])
    wave([flow_a, flow_b, flow_c], field)
    wave([flow_a, flow_b, flow_d], (flow_c.pending(), tables))
    unit_in, column = first_weight.shape
    column_wide = shortcut_weight.shape[1]
    unit_mid = middle_weight.shape[2]
    unit_out = second_weight.shape[0]
    size_short = unit_in * column_wide // 128
    size_out = unit_out * column // 128
    size_mid = 9 * unit_mid * column // 128
    split = narrow_norms.size // 128
    narrow_all = (
        tables[:, :split].reshape(ranks, 4, 2, -1).transpose(1, 2, 0, 3).reshape(4, 2, narrow)
    )
    wide_all = tables[:, split:].reshape(ranks, 3, 2, -1).transpose(1, 2, 0, 3).reshape(3, 2, wide)

    narrow_all = narrow_all.reshape(8, narrow)
    wide_all = jnp.concatenate([wide_all.reshape(6, wide), jnp.zeros((2, wide), jnp.float32)], 0)

    own_mask = lax.dynamic_slice_in_dim(pixel_mask, rank * pixels, pixels, 1).astype(jnp.float32)
    mask_in = own_mask.reshape(-1, 1)
    mask = own_mask[0][:, None]
    channel = lax.iota(jnp.int32, narrow)[None]
    keep = (channel < widths[:, None]).astype(jnp.float32)
    keep = jnp.concatenate([keep, jnp.zeros((6, narrow), jnp.float32)], 0)
    place = lax.iota(jnp.int32, pixels)[:, None]
    step = lax.iota(jnp.int32, 9)[None]
    row_at = place // WO % HO + step // 3 - 1
    col_at = place % WO + step % 3 - 1
    inside = (row_at >= 0) & (row_at < HO) & (col_at >= 0) & (col_at < WO)
    inside = inside.astype(jnp.float32)
    core = bit_of("mp", 1)[None]

    above = output_grad.reshape(-1, ranks, pixels).transpose(1, 2, 0)
    above = lax.all_to_all(above, "mp", 0, 0, tiled=True)

    devices = ranks * lax.axis_size("dp")
    full = 4 * pixels

    def real(*shape):
        return jax.ShapeDtypeStruct(shape, jnp.float32)

    def short(*shape):
        return jax.ShapeDtypeStruct(shape, low)

    size = narrow // 128
    wide_rows = wide // 128
    copies = real(devices, 2 * size, 128)
    bundle_a = flow_a.bundles()
    field, pre_one, sums = launch(
        first_layer,
        [short(full, ranks * channels), real(full, narrow), real(devices, 2 * size + 8, 128)],
        [core, field, mask_in],
        bundle_a,
        unit_in,
    )
    sums_one = wave([flow_c], sums, exchange(sums))
    sums_one, _ = lax.optimization_barrier((sums_one, flow_d.pending()))
    sums_one = hold([flow_b, flow_c], sums_one)
    counts = jnp.sum(sums_one[:, 2 * size :], 0)
    bundle_b = flow_b.bundles()
    cols_one, pre_two, sums = launch(
        functools.partial(spread_layer, 0, 0, STRIDED_TAPS),
        [short(pixels, 9 * narrow), real(pixels, narrow), copies],
        [core, pre_one, sums_one, counts, narrow_all, keep, mask_in, mask, inside],
        bundle_b,
        size_mid,
    )
    sums_two = hold([flow_c, flow_d], exchange(sums))
    bundle_c = flow_c.bundles()
    pre_side, side_sums = launch(
        functools.partial(side_layer, 0),
        [real(pixels, wide), real(2 * wide_rows, 128)],
        [core, field, mask],
        bundle_c,
        size_short,
    )
    hid_two, pre_three, sums = launch(
        functools.partial(widen_layer, size_short, 1),
        [short(pixels, narrow), real(pixels, wide), real(2 * wide_rows, 128)],
        [core, pre_two, sums_two, counts, narrow_all, keep, mask],
        bundle_c,
        size_out,
        [(pixels, narrow)],
    )
    sums_pair = everywhere(jnp.concatenate([sums, side_sums], 0), [flow_d])
    out_one, pre_four, sums = launch(
        functools.partial(narrow_layer, size_short + size_out),
        [short(pixels, wide), real(pixels, narrow), copies],
        [core, pre_three, pre_side, sums_pair, counts, wide_all, mask],
        bundle_c,
        size_out,
    )
    sums_four = wave([flow_d], sums, exchange(sums))
    bundle_d = flow_d.bundles()
    cols_four, pre_five, sums = launch(
        functools.partial(spread_layer, size_out, 2, PLAIN_TAPS),
        [short(pixels, 9 * narrow), real(pixels, narrow), copies],
        [core, pre_four, sums_four, counts, narrow_all, keep, mask, mask, inside],
        bundle_d,
        size_mid,
    )
    sums_five = exchange(sums)
    hid_five, pre_six, sums = launch(
        functools.partial(widen_layer, 0, 3),
        [short(pixels, narrow), real(pixels, wide), real(2 * wide_rows, 128)],
        [core, pre_five, sums_five, counts, narrow_all, keep, mask],
        bundle_d,
        size_out,
        [(pixels, narrow)],
    )
    sums_six = everywhere(sums)
    block_output, grad_two, sums = launch(
        last_layer,
        [short(*above.shape), real(pixels, wide), real(2 * wide_rows, 128)],
        [pre_six, sums_six, counts, wide_all, out_one, above, mask],
    )
    back_six = everywhere(sums)
    back_six, block_output = lax.optimization_barrier((back_six, block_output))
    block_output = lax.all_to_all(block_output, "mp", 0, 0, tiled=True)
    shown = block_output
    block_output = block_output.transpose(2, 0, 1).reshape(-1, ranks * pixels)

    grad_six, act_five_grad, sums = launch(
        functools.partial(last_back, 0, 3),
        [short(pixels, wide), real(pixels, narrow), copies],
        [core, grad_two, pre_six, sums_six, back_six, counts, wide_all, pre_five,
         sums_five, narrow_all, keep, mask],
        bundle_d,
        size_out,
        [(pixels, narrow)],
    )
    bundle = chunks_into(None, size_out, 0, grad_six, hid_five, 1, unit_out, column)
    back_a = Scatter(*bundle)
    back_five, _ = lax.optimization_barrier((exchange(sums), shown))
    back_five = hold([back_a], back_five)
    grad_five, act_four_grad, sums = launch(
        functools.partial(spread_back, size_out, 2, PLAIN_TAPS),
        [short(pixels, narrow), real(pixels, narrow), copies],
        [core, act_five_grad, pre_five, sums_five, back_five, counts, narrow_all,
         pre_four, sums_four, keep, mask, mask, inside],
        bundle_d,
        size_mid,
        [(pixels, narrow)],
    )
    back_four = exchange(sums)
    bundle = chunks_into(None, size_mid, 0, cols_four, grad_five, 9, unit_mid, column)
    back_b = Scatter(*bundle)
    back_four = wave([back_a], sums, back_four)
    back_four = hold([back_b], back_four)
    grad_four, grad_one, sums = launch(
        functools.partial(narrow_layer_back, size_short + size_out),
        [short(pixels, narrow), real(pixels, wide), real(3 * wide_rows, 128)],
        [core, act_four_grad, pre_four, sums_four, back_four, counts, narrow_all, mask,
         grad_two, pre_three, pre_side, sums_pair, wide_all],
        bundle_c,
        size_out,
        [(pixels, narrow), (pixels, wide)],
    )
    back_pair = everywhere(sums, [back_a, back_b])
    total = size_short + 2 * size_out
    bundle = chunks_into(
        None, total, size_short + size_out, out_one, grad_four, 1, unit_out, column
    )
    back_pair, bundle = lax.optimization_barrier((back_pair, bundle))
    grad_three, grad_side, act_two_grad, sums = launch(
        functools.partial(pair_back, size_short, 1),
        [short(pixels, wide), short(pixels, wide), real(pixels, narrow), copies],
        [core, grad_one, pre_three, pre_side, sums_pair, back_pair, counts, wide_all,
         pre_two, sums_two, narrow_all, keep, mask],
        bundle_c,
        size_out,
        [(pixels, narrow), (pixels, wide)],
    )
    back_two = wave([back_a, back_b], sums, exchange(sums))
    bundle = chunks_into(bundle, total, size_short, grad_three, hid_two, 1, unit_out, column)
    bundle = chunks_into(bundle, total, 0, field, grad_side, 1, unit_in, column_wide)
    back_c = Scatter(*bundle)
    wave([back_c])
    back_two = wave([back_c], None, back_two)
    grad_mid, act_one_grad, sums = launch(
        functools.partial(spread_back, 0, 0, STRIDED_TAPS),
        [short(pixels, narrow), real(full, narrow), copies],
        [core, act_two_grad, pre_two, sums_two, back_two, counts, narrow_all, pre_one,
         sums_one, keep, mask_in, mask, inside],
        bundle_b,
        size_mid,
        [(pixels, narrow)],
    )
    back_one = wave([back_b, back_c], sums, exchange(sums))
    bundle = chunks_into(None, size_mid, 0, cols_one, grad_mid, 9, unit_mid, column)
    back_d = Scatter(*bundle)
    (side_grad,) = launch(
        functools.partial(side_back, 0),
        [real(pixels, field.shape[1])],
        [grad_side],
        bundle_c,
        size_short,
    )
    back_one = hold([back_d], back_one)
    back_one, side_grad = lax.optimization_barrier((back_one, side_grad))
    grad_first, field_grad = launch(
        first_back,
        [short(full, narrow), short(ranks, full, channels)],
        [core, act_one_grad, pre_one, sums_one, back_one, counts, narrow_all, mask_in,
         side_grad],
        bundle_a,
        unit_in,
        [(full, narrow)],
    )
    grad_first = wave([back_c, back_d], back_one, grad_first)
    bundle = chunks_into(None, unit_in * column // 128, 0, field, grad_first, 1, unit_in, column)
    back_e = Scatter(*bundle, False)
    wave([back_e])
    input_grad = lax.all_to_all(field_grad, "mp", 0, 0, tiled=True)
    input_grad = input_grad.reshape(ranks, 4, pixels, channels).transpose(3, 1, 0, 2)
    input_grad = input_grad.reshape(inputs.shape)
    wave([back_d, back_e])
    wave([back_d, back_e])
    rows_a, rows_b, rows_c, rows_d, rows_e = [
        flow.rows() for flow in (back_a, back_b, back_c, back_d, back_e)
    ]
    first_fix = 1.0 - BETA_ONE**STEP
    second_fix = 1.0 - BETA_TWO**STEP

    def like(*values):
        return [real(*value.shape) for value in values for _ in range(3)]

    early = launch(
        functools.partial(early_moves, column),
        like(shortcut_weight, last_weight, second_weight) + [real(8, 128)],
        [rows_a, rows_c]
        + [
            shortcut_mean, shortcut_square, shortcut_weight, last_mean, last_square, last_weight,
            second_mean, second_square, second_weight,
        ],
    )
    late = launch(
        late_moves,
        like(first_weight, middle_weight) + [real(devices, 16, 128)],
        [rows_b, rows_d, rows_e, early[-1]]
        + [first_mean, first_square, first_weight, middle_mean, middle_square, middle_weight],
    )
    powers = exchange(late[-1])
    weights = (first_weight, shortcut_weight, middle_weight, last_weight, second_weight)
    updates = (late[2], early[2], late[5], early[5], early[8])
    norms, *fresh = launch(
        final_moves,
        [real(16, 128)]
        + [real(*value.shape) for value in weights]
        + [short(*value.shape) for value in weights],
        [powers]
        + [value for pair in zip(weights, updates) for value in pair],
    )
    matrix_norms = norms[:14, 0].reshape(7, 2)
    first_next, short_next, middle_next, last_next, second_next = fresh[:5]
    states = [late[0:2], early[0:2], late[3:5], early[3:5], early[6:8]]

    def own_channels(values):
        width = values.shape[-1] // ranks
        return lax.dynamic_slice_in_dim(values, rank * width, width, values.ndim - 1)

    narrow_grads = jnp.stack([jnp.sum(rows, 0) for rows in (back_one, back_two, back_four, back_five)])
    narrow_grad = own_channels(narrow_grads.reshape(4, 2, narrow))
    gain_three, gain_side, bias_pair = jnp.sum(back_pair, 0).reshape(3, wide)
    wide_grad = own_channels(
        jnp.stack(
            [
                jnp.stack([gain_three, bias_pair]),
                jnp.stack([gain_side, bias_pair]),
                jnp.sum(back_six, 0).reshape(2, wide),
            ]
        )
    )
    narrow_mean_next, narrow_square_next, narrow_step = adapt(
        narrow_grad, narrow_mean, narrow_square, first_fix, second_fix
    )
    wide_mean_next, wide_square_next, wide_step = adapt(
        wide_grad, wide_mean, wide_square, first_fix, second_fix
    )
    return (
        block_output,
        input_grad,
        states[0][0],
        states[0][1],
        first_next,
        states[1][0],
        states[1][1],
        short_next,
        states[2][0],
        states[2][1],
        middle_next,
        states[3][0],
        states[3][1],
        last_next,
        states[4][0],
        states[4][1],
        second_next,
        narrow_mean_next,
        narrow_square_next,
        narrow_norms - RATE_NORM * narrow_step,
        wide_mean_next,
        wide_square_next,
        wide_norms - RATE_NORM * wide_step,
        matrix_norms,
        *fresh[5:],
    )


def solution(mesh):
    in_specs = (
        P("mp", None, "dp"),
        P(None, "dp"),
        P(),
        P("mp", "dp"),
        P("dp", "mp"),
        P("dp", "mp"),
        P(None, None, "dp", "mp"),
        P(None, "mp", "dp"),
        P("dp", "mp"),
        P(None, None, "mp"),
        P(None, None, "mp"),
        P("dp", "mp"),
        P("dp", "mp"),
        P("dp", "mp"),
        P("dp", "mp"),
        P(None, None, "dp", "mp"),
        P(None, None, "dp", "mp"),
        P(None, "mp", "dp"),
        P(None, "mp", "dp"),
        P("dp", "mp"),
        P("dp", "mp"),
        P(None, None, "mp"),
        P(None, None, "mp"),
        P(None, None, "mp"),
        P(None, None, "mp"),
    )
    out_specs = (
        P("mp", "dp"),
        P("mp", None, "dp"),
        P("dp", "mp"),
        P("dp", "mp"),
        P("dp", "mp"),
        P("dp", "mp"),
        P("dp", "mp"),
        P("dp", "mp"),
        P(None, None, "dp", "mp"),
        P(None, None, "dp", "mp"),
        P(None, None, "dp", "mp"),
        P(None, "mp", "dp"),
        P(None, "mp", "dp"),
        P(None, "mp", "dp"),
        P("dp", "mp"),
        P("dp", "mp"),
        P("dp", "mp"),
        P(None, None, "mp"),
        P(None, None, "mp"),
        P(None, None, "mp"),
        P(None, None, "mp"),
        P(None, None, "mp"),
        P(None, None, "mp"),
        P(),
        P("dp", "mp"),
        P("dp", "mp"),
        P(None, None, "dp", "mp"),
        P(None, "mp", "dp"),
        P("dp", "mp"),
    )
    return jax.shard_map(
        lambda *values: (by_image if fits(mesh, values[1]) else shards)(*values),
        mesh=mesh,
        in_specs=in_specs,
        out_specs=out_specs,
        check_vma=False,
    )
```

```python
import functools

import jax
import jax.numpy as jnp
from jax import lax
from jax.experimental import pallas as pl
from jax.experimental.pallas import tpu as pltpu
from jax.sharding import PartitionSpec as P

HO = 16
WO = 11
STEP = 10


EPS_NORM = 1e-05
BETA_ONE = 0.9
BETA_TWO = 0.999
EPS_ADAM = 1e-06
DECAY = 0.01
RATE = 0.3
RATE_NORM = 0.3
EPS_TRUST = 1e-06
PHASES = ((1, -1), (0, 0), (1, 0))
STRIDED_TAPS = tuple(
    (
        (
            3 * above + beside,
            2 * PHASES[above][0] + PHASES[beside][0],
            PHASES[above][1],
            PHASES[beside][1],
        )
        for above in range(3)
        for beside in range(3)
    )
)
PLAIN_TAPS = tuple(
    ((3 * above + beside, 0, above - 1, beside - 1) for above in range(3) for beside in range(3))
)


def slope(values):
    gate = jax.nn.sigmoid(values)
    return gate * (1.0 + values * (1.0 - gate))


def shifted(values, drow, dcol):
    length = values.shape[1]
    offset = drow * WO + dcol
    place = lax.iota(jnp.int32, length)
    row_at = place // WO % HO + drow
    col_at = place % WO + dcol
    inside = (row_at >= 0) & (row_at < HO) & (col_at >= 0) & (col_at < WO)
    moved = jnp.roll(values, -offset, axis=1)
    return jnp.where(inside[None, :], moved, jnp.zeros_like(moved))


def over_images(first, second):
    return lax.psum((first, second), "dp")


def moments(values, mask):
    weighted = values * mask[None, :]
    return over_images(jnp.sum(weighted, 1), jnp.sum(weighted * values, 1))


def normalize(values, totals, squares, count, gain, bias):
    mean = totals / count
    scale = lax.rsqrt(squares / count - mean * mean + EPS_NORM)
    centred = (values - mean[:, None]) * scale[:, None]
    return (centred, scale, centred * gain[:, None] + bias[:, None])


def back_sums(grad_in, centred):
    return over_images(jnp.sum(grad_in * centred, 1), jnp.sum(grad_in, 1))


def norm_back(grad_in, centred, scale, gain, mask, gain_sum, bias_sum, count):
    return (gain * scale)[:, None] * (
        grad_in - mask[None, :] * (bias_sum[:, None] + centred * gain_sum[:, None]) / count
    )


def input_mix(values, weight, side_weight, pixels):
    start_sum = (jnp.zeros((weight.shape[1], values.shape[1]), jnp.float32),)
    if side_weight is not None:
        start_sum = start_sum + (jnp.zeros((side_weight.shape[1], pixels), jnp.float32),)
    piece = lax.all_gather(values, "mp", axis=0, tiled=True)
    result = (jnp.einsum("kc,kp->cp", weight, piece, preferred_element_type=jnp.float32),)
    if side_weight is not None:
        result = result + (
            jnp.einsum(
                "kc,kp->cp", side_weight, piece[:, :pixels], preferred_element_type=jnp.float32
            ),
        )
    return result


def mid_gathered(hidden):
    return lax.all_gather(hidden, "mp", axis=0, tiled=True)


def conv_forward(gathered, kernel, taps, pixels):
    result = jnp.zeros((kernel.shape[2], pixels), jnp.float32)
    for tap, phase, drow, dcol in taps:
        source = gathered[:, phase * pixels : (phase + 1) * pixels]
        part = jnp.einsum("kc,kp->cp", kernel[tap], source, preferred_element_type=jnp.float32)
        result = result + shifted(part, drow, dcol)
    return result


def conv_backward(grad_b, gathered, kernel, taps, pixels, phases):
    moved = [shifted(grad_b, -drow, -dcol) for tap, phase, drow, dcol in taps]
    count = gathered.shape[0] // lax.axis_size("mp") * lax.axis_size("mp")
    blocks = []
    for target in range(phases):
        result = jnp.zeros((count, pixels), jnp.float32)
        for conv_index, (conv_tap, conv_phase, conv_drow, conv_dcol) in enumerate(taps):
            if conv_phase == target:
                part = kernel[conv_tap]
                result = result + jnp.dot(
                    part, moved[conv_index], preferred_element_type=jnp.float32
                )
        blocks.append(result)
    hidden_grad = lax.psum_scatter(
        jnp.concatenate(blocks, 1), "mp", scatter_dimension=0, tiled=True
    )
    kernel_grad = jnp.stack(
        [
            jnp.einsum(
                "kp,cp->kc",
                gathered[:, phase * pixels : (phase + 1) * pixels],
                moved[index],
                preferred_element_type=jnp.float32,
            )
            for index, (tap, phase, drow, dcol) in enumerate(taps)
        ]
    )
    return (hidden_grad, kernel_grad)


def output_mix(hidden, kernel):
    return lax.psum_scatter(
        jnp.einsum("kc,kp->cp", kernel, hidden, preferred_element_type=jnp.float32),
        "mp",
        scatter_dimension=0,
        tiled=True,
    )


def output_back(grad_b, kernel, hidden):
    piece = lax.all_gather(grad_b, "mp", axis=0, tiled=True)
    hidden_grad = jnp.dot(kernel, piece, preferred_element_type=jnp.float32)
    columns = jnp.einsum("cp,kp->ck", hidden, piece, preferred_element_type=jnp.float32)
    return (hidden_grad, columns)


def input_back(values, grad_b, side_b, weight, side_weight, pixels):
    width = weight.shape[1]
    result = jnp.dot(weight, grad_b, preferred_element_type=jnp.float32)
    if side_weight is not None:
        result = jnp.concatenate(
            [
                result[:, :pixels]
                + jnp.dot(side_weight, side_b, preferred_element_type=jnp.float32),
                result[:, pixels:],
            ],
            1,
        )
    values_grad = lax.psum_scatter(result, "mp", scatter_dimension=0, tiled=True)
    piece = lax.all_gather(values, "mp", axis=0, tiled=True)
    blocks = [jnp.einsum("kp,cp->kc", piece, grad_b, preferred_element_type=jnp.float32)]
    if side_weight is not None:
        blocks.append(
            jnp.einsum("kp,cp->kc", piece[:, :pixels], side_b, preferred_element_type=jnp.float32)
        )
    joined = jnp.concatenate(blocks, 1)
    return (values_grad, joined[:, :width], joined[:, width:])


def adapt(grad_in, mean, square, first_fix, second_fix):
    mean_next = BETA_ONE * mean + (1.0 - BETA_ONE) * grad_in
    square_next = BETA_TWO * square + (1.0 - BETA_TWO) * grad_in * grad_in
    step = mean_next / first_fix / (jnp.sqrt(square_next / second_fix) + EPS_ADAM)
    return (mean_next, square_next, step)


def shards(
    inputs,
    pixel_mask,
    widths,
    output_grad,
    first_weight,
    shortcut_weight,
    middle_weight,
    last_weight,
    second_weight,
    narrow_norms,
    wide_norms,
    first_mean,
    first_square,
    shortcut_mean,
    shortcut_square,
    middle_mean,
    middle_square,
    last_mean,
    last_square,
    second_mean,
    second_square,
    narrow_mean,
    narrow_square,
    wide_mean,
    wide_square,
):
    pixels = pixel_mask.shape[1]
    width = first_weight.shape[1]
    rank = lax.axis_index("mp")
    channel = rank * width + lax.iota(jnp.int32, width)
    keep_one = (channel < widths[0]).astype(jnp.float32)[:, None]
    keep_two = (channel < widths[1]).astype(jnp.float32)[:, None]
    masks = pixel_mask.astype(jnp.float32)
    mask_in = masks.reshape(-1)
    mask_out = masks[0]
    field = (inputs * pixel_mask.astype(jnp.bfloat16)[None]).reshape(inputs.shape[0], -1)
    first_w, short_w, middle_w, last_w, second_w = (
        lax.all_gather(first_weight.astype(jnp.bfloat16), "dp", axis=0, tiled=True),
        lax.all_gather(shortcut_weight.astype(jnp.bfloat16), "dp", axis=0, tiled=True),
        lax.all_gather(middle_weight.astype(jnp.bfloat16), "dp", axis=2, tiled=True),
        lax.all_gather(last_weight.astype(jnp.bfloat16), "dp", axis=2, tiled=True),
        lax.all_gather(second_weight.astype(jnp.bfloat16), "dp", axis=0, tiled=True),
    )
    count_in, count_out = over_images(jnp.sum(mask_in), jnp.sum(mask_out))
    pre_one, pre_side = input_mix(field, first_w, short_w, pixels)
    totals, squares = moments(pre_one, mask_in)
    cen_one, scale_one, act_one = normalize(
        pre_one, totals, squares, count_in, narrow_norms[0, 0], narrow_norms[0, 1]
    )
    hid_one = (jax.nn.silu(act_one) * mask_in[None, :] * keep_one).astype(jnp.bfloat16)
    gat_one = mid_gathered(hid_one)
    pre_two = conv_forward(gat_one, middle_w[0], STRIDED_TAPS, pixels)
    totals, squares = moments(pre_two, mask_out)
    cen_two, scale_two, act_two = normalize(
        pre_two, totals, squares, count_out, narrow_norms[1, 0], narrow_norms[1, 1]
    )
    hid_two = (jax.nn.silu(act_two) * mask_out[None, :] * keep_one).astype(jnp.bfloat16)
    pre_three = output_mix(hid_two, last_w[0])
    weighted_three = pre_three * mask_out[None, :]
    weighted_side = pre_side * mask_out[None, :]
    totals, squares = over_images(
        jnp.stack([jnp.sum(weighted_three, 1), jnp.sum(weighted_side, 1)]),
        jnp.stack([jnp.sum(weighted_three * pre_three, 1), jnp.sum(weighted_side * pre_side, 1)]),
    )
    cen_three, scale_three, act_three = normalize(
        pre_three, totals[0], squares[0], count_out, wide_norms[0, 0], wide_norms[0, 1]
    )
    cen_side, scale_side, act_side = normalize(
        pre_side, totals[1], squares[1], count_out, wide_norms[1, 0], wide_norms[1, 1]
    )
    total_one = act_three + act_side
    out_one = (jax.nn.silu(total_one) * mask_out[None, :]).astype(jnp.bfloat16)
    (pre_four,) = input_mix(out_one, second_w, None, pixels)
    totals, squares = moments(pre_four, mask_out)
    cen_four, scale_four, act_four = normalize(
        pre_four, totals, squares, count_out, narrow_norms[2, 0], narrow_norms[2, 1]
    )
    hid_four = (jax.nn.silu(act_four) * mask_out[None, :] * keep_two).astype(jnp.bfloat16)
    gat_four = mid_gathered(hid_four)
    pre_five = conv_forward(gat_four, middle_w[1], PLAIN_TAPS, pixels)
    totals, squares = moments(pre_five, mask_out)
    cen_five, scale_five, act_five = normalize(
        pre_five, totals, squares, count_out, narrow_norms[3, 0], narrow_norms[3, 1]
    )
    hid_five = (jax.nn.silu(act_five) * mask_out[None, :] * keep_two).astype(jnp.bfloat16)
    pre_six = output_mix(hid_five, last_w[1])
    totals, squares = moments(pre_six, mask_out)
    cen_six, scale_six, act_six = normalize(
        pre_six, totals, squares, count_out, wide_norms[2, 0], wide_norms[2, 1]
    )
    total_two = act_six + out_one.astype(jnp.float32)
    block_output = (jax.nn.silu(total_two) * mask_out[None, :]).astype(jnp.bfloat16)
    grad_two = output_grad.astype(jnp.float32) * mask_out[None, :] * slope(total_two)
    gain_six, bias_six = back_sums(grad_two, cen_six)
    grad_six = norm_back(
        grad_two, cen_six, scale_six, wide_norms[2, 0], mask_out, gain_six, bias_six, count_out
    ).astype(jnp.bfloat16)
    hid_five_grad, last_one_grad = output_back(grad_six, last_w[1], hid_five)
    act_five_grad = hid_five_grad * keep_two * mask_out[None, :] * slope(act_five)
    gain_five, bias_five = back_sums(act_five_grad, cen_five)
    grad_five = norm_back(
        act_five_grad,
        cen_five,
        scale_five,
        narrow_norms[3, 0],
        mask_out,
        gain_five,
        bias_five,
        count_out,
    ).astype(jnp.bfloat16)
    hid_four_grad, middle_one_grad = conv_backward(
        grad_five, gat_four, middle_w[1], PLAIN_TAPS, pixels, 1
    )
    act_four_grad = hid_four_grad * keep_two * mask_out[None, :] * slope(act_four)
    gain_four, bias_four = back_sums(act_four_grad, cen_four)
    grad_four = norm_back(
        act_four_grad,
        cen_four,
        scale_four,
        narrow_norms[2, 0],
        mask_out,
        gain_four,
        bias_four,
        count_out,
    ).astype(jnp.bfloat16)
    out_one_grad, second_grad, unused_side = input_back(
        out_one, grad_four, None, second_w, None, pixels
    )
    grad_one = (grad_two + out_one_grad) * mask_out[None, :] * slope(total_one)
    gains_pair, bias_pair = over_images(
        jnp.stack([jnp.sum(grad_one * cen_three, 1), jnp.sum(grad_one * cen_side, 1)]),
        jnp.sum(grad_one, 1),
    )
    grad_three = norm_back(
        grad_one,
        cen_three,
        scale_three,
        wide_norms[0, 0],
        mask_out,
        gains_pair[0],
        bias_pair,
        count_out,
    ).astype(jnp.bfloat16)
    grad_side = norm_back(
        grad_one,
        cen_side,
        scale_side,
        wide_norms[1, 0],
        mask_out,
        gains_pair[1],
        bias_pair,
        count_out,
    ).astype(jnp.bfloat16)
    hid_two_grad, last_zero_grad = output_back(grad_three, last_w[0], hid_two)
    act_two_grad = hid_two_grad * keep_one * mask_out[None, :] * slope(act_two)
    gain_two, bias_two = back_sums(act_two_grad, cen_two)
    grad_mid = norm_back(
        act_two_grad,
        cen_two,
        scale_two,
        narrow_norms[1, 0],
        mask_out,
        gain_two,
        bias_two,
        count_out,
    ).astype(jnp.bfloat16)
    hid_one_grad, middle_zero_grad = conv_backward(
        grad_mid, gat_one, middle_w[0], STRIDED_TAPS, pixels, 4
    )
    act_one_grad = hid_one_grad * keep_one * mask_in[None, :] * slope(act_one)
    gain_one, bias_one = back_sums(act_one_grad, cen_one)
    grad_first = norm_back(
        act_one_grad, cen_one, scale_one, narrow_norms[0, 0], mask_in, gain_one, bias_one, count_in
    ).astype(jnp.bfloat16)
    field_grad, first_grad, short_grad = input_back(
        field, grad_first, grad_side, first_w, short_w, pixels
    )
    input_grad = (field_grad * mask_in[None, :]).astype(jnp.bfloat16).reshape(inputs.shape)
    grads = (
        lax.psum_scatter(first_grad, "dp", scatter_dimension=0, tiled=True),
        lax.psum_scatter(short_grad, "dp", scatter_dimension=0, tiled=True),
        lax.psum_scatter(
            jnp.stack([middle_zero_grad, middle_one_grad]), "dp", scatter_dimension=2, tiled=True
        ),
        lax.psum_scatter(
            jnp.stack([last_zero_grad, last_one_grad]), "dp", scatter_dimension=2, tiled=True
        ),
        lax.psum_scatter(second_grad, "dp", scatter_dimension=0, tiled=True),
    )
    first_fix = 1.0 - BETA_ONE**STEP
    second_fix = 1.0 - BETA_TWO**STEP
    weights = (first_weight, shortcut_weight, middle_weight, last_weight, second_weight)
    means = (first_mean, shortcut_mean, middle_mean, last_mean, second_mean)
    squares_old = (first_square, shortcut_square, middle_square, last_square, second_square)
    states = []
    updates = []
    for index in range(5):
        mean_next, square_next, step = adapt(
            grads[index], means[index], squares_old[index], first_fix, second_fix
        )
        states.append((mean_next, square_next))
        updates.append(step + DECAY * weights[index])
    pairs = [
        (weights[0], updates[0]),
        (weights[1], updates[1]),
        (weights[2][0], updates[2][0]),
        (weights[2][1], updates[2][1]),
        (weights[3][0], updates[3][0]),
        (weights[3][1], updates[3][1]),
        (weights[4], updates[4]),
    ]
    partial_value = jnp.stack(
        [
            jnp.stack([jnp.sum(weight * weight), jnp.sum(update * update)])
            for weight, update in pairs
        ]
    )
    matrix_norms = jnp.sqrt(lax.psum(partial_value, ("dp", "mp")))
    ratio = matrix_norms[:, 0] / (matrix_norms[:, 1] + EPS_TRUST)
    first_next = first_weight - RATE * ratio[0] * updates[0]
    short_next = shortcut_weight - RATE * ratio[1] * updates[1]
    middle_next = middle_weight - RATE * ratio[2:4].reshape(2, 1, 1, 1) * updates[2]
    last_next = last_weight - RATE * ratio[4:6].reshape(2, 1, 1) * updates[3]
    second_next = second_weight - RATE * ratio[6] * updates[4]
    narrow_grad = jnp.stack(
        [
            jnp.stack([gain_one, bias_one]),
            jnp.stack([gain_two, bias_two]),
            jnp.stack([gain_four, bias_four]),
            jnp.stack([gain_five, bias_five]),
        ]
    )
    wide_grad = jnp.stack(
        [
            jnp.stack([gains_pair[0], bias_pair]),
            jnp.stack([gains_pair[1], bias_pair]),
            jnp.stack([gain_six, bias_six]),
        ]
    )
    narrow_mean_next, narrow_square_next, narrow_step = adapt(
        narrow_grad, narrow_mean, narrow_square, first_fix, second_fix
    )
    wide_mean_next, wide_square_next, wide_step = adapt(
        wide_grad, wide_mean, wide_square, first_fix, second_fix
    )
    return (
        block_output,
        input_grad,
        states[0][0],
        states[0][1],
        first_next,
        states[1][0],
        states[1][1],
        short_next,
        states[2][0],
        states[2][1],
        middle_next,
        states[3][0],
        states[3][1],
        last_next,
        states[4][0],
        states[4][1],
        second_next,
        narrow_mean_next,
        narrow_square_next,
        narrow_norms - RATE_NORM * narrow_step,
        wide_mean_next,
        wide_square_next,
        wide_norms - RATE_NORM * wide_step,
        matrix_norms,
        first_next.astype(jnp.bfloat16),
        short_next.astype(jnp.bfloat16),
        middle_next.astype(jnp.bfloat16),
        last_next.astype(jnp.bfloat16),
        second_next.astype(jnp.bfloat16),
    )


VMEM_BYTES = 62 * 2**20
LIGHT = pl.CostEstimate(flops=1024, bytes_accessed=1024, transcendentals=0)


def fits(mesh, pixel_mask):
    sizes = (mesh.shape["dp"], mesh.shape["mp"])
    powers = all(size >= 2 and size & (size - 1) == 0 for size in sizes)
    return powers and pixel_mask.shape[1] % (HO * WO * sizes[1]) == 0


def swap(values, *bits):
    sizes = {axis: lax.axis_size(axis) for axis in ("dp", "mp")}
    masks = {axis: sum(mask for at, mask in bits if at == axis) for axis in sizes}
    if not masks["dp"]:
        return lax.ppermute(values, "mp", [(at, at ^ masks["mp"]) for at in range(sizes["mp"])])
    if not masks["mp"]:
        return lax.ppermute(values, "dp", [(at, at ^ masks["dp"]) for at in range(sizes["dp"])])
    mask = masks["dp"] * sizes["mp"] + masks["mp"]
    return lax.ppermute(
        values, ("dp", "mp"), [(at, at ^ mask) for at in range(sizes["dp"] * sizes["mp"])]
    )


def subsets(bits):
    return [
        [bit for place, bit in enumerate(bits) if index >> place & 1]
        for index in range(1 << len(bits))
    ]


def bit_of(axis, mask):
    return (lax.axis_index(axis) & mask) // mask


def high_bits(axis):
    masks = []
    mask = lax.axis_size(axis) // 2
    while mask:
        masks.append(mask)
        mask //= 2
    return masks


def everywhere(values, flows=()):
    mask = 1
    while mask < lax.axis_size("mp"):
        values = values + swap(values, ("mp", mask))
        mask *= 2
    copies = jnp.broadcast_to(values[None], (lax.axis_size("dp"),) + values.shape)
    arrived = lax.all_to_all(copies, "dp", 0, 0, tiled=True)
    return wave(flows, values, arrived) if flows else arrived


def pack(block):
    lead, rows, cols = block.shape
    parts = block.reshape(lead, rows, cols // 128, 128).transpose(0, 2, 1, 3)
    return parts.reshape(-1, 128)


def column_bits():
    return [("mp", mask) for mask in high_bits("mp")[:-1]]


def row_bits():
    return [("dp", mask) for mask in high_bits("dp")]


def lanes_of(rows):
    first = rows // 32 * 16
    return ((0, first), (first, rows))


def moves_kernel(tasks, count, places, *refs):
    sources, outs, sems = refs[:count], refs[count:-1], refs[-1]
    copies = []
    for at, (source, span, out, turns, rows) in enumerate(tasks):
        dims = len(sources[source].shape) - 2
        every = [slice(None)] * dims
        start = [
            pl.ds(1 - places[dim] if turns[dim] else places[dim], 1) if dim in turns else slice(None)
            for dim in range(dims)
        ]
        copies.append(
            pltpu.make_async_copy(
                sources[source].at[(*every, pl.ds(*span), slice(None))],
                outs[out].at[(*start, pl.ds(*rows), slice(None))],
                sems.at[at],
            )
        )
        copies[-1].start()
    for copy in copies:
        copy.wait()


def moves(wanted):
    sources = []
    tasks = []
    for out, (shape, pieces) in enumerate(wanted):
        for source, span, turns, rows in pieces:
            tasks.append((len(sources), span, out, turns, rows))
            sources.append(source)
    bits = column_bits() + row_bits()
    places = jnp.stack([bit_of(*bit) for bit in bits]).astype(jnp.int32)
    return pl.pallas_call(
        functools.partial(moves_kernel, tasks, len(sources)),
        in_specs=[pl.BlockSpec(memory_space=pltpu.SMEM)]
        + [pl.BlockSpec(memory_space=pltpu.HBM)] * len(sources),
        out_specs=[pl.BlockSpec(memory_space=pltpu.VMEM)] * len(wanted),
        out_shape=[jax.ShapeDtypeStruct(shape, jnp.bfloat16) for shape, _ in wanted],
        scratch_shapes=[pltpu.SemaphoreType.DMA((len(tasks),))],
        compiler_params=pltpu.CompilerParams(vmem_limit_bytes=VMEM_BYTES),
        cost_estimate=LIGHT,
    )(places, *sources)


class Gather:
    def __init__(self, rows, lanes=True):
        self.dims = column_bits() + row_bits()
        near = row_bits()[-1:]
        self.rows = rows.shape[0]
        if lanes:
            self.steps = [[row_bits()[:-1]], [near, column_bits()], [column_bits(), near]]
            self.spans = lanes_of(self.rows)
        else:
            self.steps = [[row_bits()[:-1]], [near + column_bits()]]
            self.spans = ((0, self.rows),)
        self.parts = [([rows.reshape((1,) * len(self.dims) + rows.shape)], [])]
        self.step = 0

    def pending(self):
        return [values for values, bits in self.parts]

    def resume(self, values):
        self.parts = [(value, bits) for value, (_, bits) in zip(values, self.parts)]

    def wanted(self):
        if not self.parts[0][1]:
            return []
        last = self.step == len(self.steps)
        split = not last and len(self.steps[self.step]) > len(self.parts)
        lanes = [(low, high - low) for low, high in self.spans]
        result = []
        for lane, (values, bits) in enumerate(self.parts):
            shape = [
                2 if bit in bits else size
                for bit, size in zip(self.dims, values[0].shape)
            ]
            pieces = [
                (value, {self.dims.index(bit): bit in turned for bit in bits})
                for value, turned in zip(values, subsets(bits))
            ]
            height = values[0].shape[-2]
            for low, size in lanes if split else [(0, height)]:
                block = [(value, (low, size), turns, (0, size)) for value, turns in pieces]
                result.append((tuple(shape) + (size, 128), block))
        if last:
            pieces = [
                (value, span, turns, lanes[lane])
                for lane, (_, block) in enumerate(result)
                for value, span, turns, _ in block
            ]
            result = [(result[0][0][:-2] + (self.rows, 128), pieces)]
        return result

    def launch(self, values):
        if not values:
            values = [self.parts[0][0][0]]
        if self.step < len(self.steps):
            self.parts = [
                ([value] + [swap(value, *bits) for bits in subsets(group)[1:]], group)
                for value, group in zip(values, self.steps[self.step])
            ]
        else:
            self.parts = [([values[0], swap(values[0], ("mp", 1))], [])]
        self.step += 1
        return values

    def bundles(self):
        shape = (1 << len(column_bits()), lax.axis_size("dp")) + self.parts[0][0][0].shape[-2:]
        return [value.reshape(shape) for value in self.parts[0][0]]


class Scatter:
    def __init__(self, keep, send, lanes=True):
        self.dims = column_bits() + row_bits()
        shape = (2,) * len(self.dims) + keep.shape[2:]
        near = row_bits()[-1:]
        far = row_bits()[:-1]
        if lanes:
            self.steps = [None, [column_bits(), near], [near, column_bits()], [far, far]]
            self.spans = lanes_of(keep.shape[2])
        else:
            self.steps = [None, [column_bits() + near], [far]]
            self.spans = (None,)
        self.lanes = [[] for _ in self.spans]
        self.raw = [keep.reshape(shape), send.reshape(shape)]
        self.step = 0

    def pending(self):
        return self.raw

    def resume(self, values):
        self.raw = list(values)

    def fold(self, lane, group=(), turned=()):
        total = 0.0
        for index, settled, span in self.lanes[lane]:
            value = self.raw[index]
            for bit in settled + list(group):
                place = bit_of(*bit)
                place = 1 - place if bit in turned else place
                value = lax.dynamic_slice_in_dim(value, place, 1, self.dims.index(bit))
            if span is not None:
                value = value[..., span[0] : span[1], :]
            total = total + value.astype(jnp.float32)
        return total

    def settle(self, lane, group, arrived, span):
        old = [(index, settled + group, part) for index, settled, part in self.lanes[lane]]
        self.lanes[lane] = old + [(index, [], span) for index in arrived]

    def wanted(self):
        return []

    def launch(self, values):
        groups = self.steps[self.step]
        whole = self.step == len(self.steps) - 1
        sent = []
        if groups is None:
            sent.append(self.raw[1])
            self.raw[1] = swap(self.raw[1], ("mp", 1))
            for lane, span in zip(self.lanes, self.spans):
                lane += [(0, [], span), (1, [], span)]
        elif whole:
            arrived = []
            for bits in subsets(groups[0])[1:]:
                out = [
                    self.fold(lane, groups[0], bits).astype(jnp.bfloat16)
                    for lane in range(len(self.lanes))
                ]
                out = jnp.concatenate(out, -2) if len(out) > 1 else out[0]
                arrived.append(len(self.raw))
                sent.append(out)
                self.raw.append(swap(out, *bits))
            for lane, span in enumerate(self.spans):
                self.settle(lane, groups[lane], arrived, span)
        else:
            for lane, group in enumerate(groups):
                arrived = []
                for bits in subsets(group)[1:]:
                    out = self.fold(lane, group, bits).astype(jnp.bfloat16)
                    arrived.append(len(self.raw))
                    sent.append(out)
                    self.raw.append(swap(out, *bits))
                self.settle(lane, group, arrived, None)
        self.step += 1
        return sent

    def rows(self):
        total = [self.fold(lane) for lane in range(len(self.lanes))]
        total = jnp.concatenate(total, -2) if len(total) > 1 else total[0]
        return total.reshape(total.shape[-2:])


def wave(flows, after=None, before=None):
    values = [flow.pending() for flow in flows]
    if after is not None:
        values, _ = lax.optimization_barrier((values, after))
    for flow, value in zip(flows, values):
        flow.resume(value)
    wanted = [flow.wanted() for flow in flows]
    joined = [value for part in wanted for value in part]
    made = list(moves(joined)) if joined else []
    sent = []
    for flow, part in zip(flows, wanted):
        sent += flow.launch([made.pop(0) for _ in part])
    if before is not None:
        before, _ = lax.optimization_barrier((before, sent))
    return before


def hold(flows, value):
    value, parts = lax.optimization_barrier((value, [flow.pending() for flow in flows]))
    for flow, part in zip(flows, parts):
        flow.resume(part)
    wave(flows)
    return value


def chunk_kernel(units, columns, rows_ref, cols_ref, *refs):
    outs = refs[-2:]
    product = lax.dot_general(
        rows_ref[...], cols_ref[...], (((0,), (0,)), ((), ())), preferred_element_type=jnp.float32
    ).astype(jnp.bfloat16)
    groups = outs[0].shape[0]
    chunks = outs[0].shape[1]
    for half, out in enumerate(outs):
        for group in range(groups):
            for part in range(columns):
                place = ((half * groups + group) * columns + part) * 128
                block = product[:, place : place + 128].reshape(chunks, units, 128)
                out[group, :, part * units : (part + 1) * units, :] = block


def chunks_into(bundle, total, start, rows_of, cols_of, lead, units, columns):
    count = lax.axis_size("dp")
    groups = 1 << len(column_bits())
    columns = columns // 128
    pixels = cols_of.shape[0]
    height = units * columns
    if lead > 1:
        steps, wide, chunks = lead, count * units, count
        place = lambda step: (0, 0, start // height + step, 0)
    else:
        steps, wide, chunks = count, units, 1
        place = lambda step: (0, step, start // height, 0)
    shape = jax.ShapeDtypeStruct((groups, count, total, 128), jnp.bfloat16)
    block = pl.BlockSpec((groups, chunks, height, 128), place)
    earlier = () if bundle is None else tuple(bundle)
    return pl.pallas_call(
        functools.partial(chunk_kernel, units, columns),
        grid=(steps,),
        in_specs=[
            pl.BlockSpec((pixels, wide), lambda step: (0, step)),
            pl.BlockSpec(cols_of.shape, lambda step: (0, 0)),
        ]
        + [pl.BlockSpec(memory_space=pltpu.HBM)] * len(earlier),
        out_specs=[block, block],
        out_shape=[shape, shape],
        input_output_aliases={2 + place: place for place in range(len(earlier))},
        compiler_params=pltpu.CompilerParams(vmem_limit_bytes=VMEM_BYTES),
        cost_estimate=LIGHT,
    )(rows_of, cols_of, *earlier)


def total_of(ref):
    return jnp.sum(ref[...], 0) if len(ref.shape) == 3 else ref[...]


def as_row(block):
    return jnp.concatenate([block[place : place + 1] for place in range(block.shape[0])], 1)


def as_rows(row):
    return jnp.concatenate(
        [row[:, place : place + 128] for place in range(0, row.shape[1], 128)], 0
    )


def hand_out(out, rows):
    missing = out.shape[-2] - sum(row.shape[0] for row in rows)
    if missing:
        rows = rows + [jnp.zeros((missing, 128), jnp.float32)]
    block = jnp.concatenate(rows, 0)
    out[...] = jnp.broadcast_to(block[None], out.shape) if len(out.shape) == 3 else block


def levels(total, first, width, count):
    rows = width // 128
    mean = total[first : first + rows] / count
    scale = lax.rsqrt(total[first + rows : first + 2 * rows] / count - mean * mean + EPS_NORM)
    return (as_row(mean), as_row(scale))


def standard(values, level):
    return (values - level[0]) * level[1]


def back_through(grad, centred, level, gain, mask, total, first, bias_first, count):
    rows = grad.shape[1] // 128
    gain_sum = as_row(total[first : first + rows] / count)
    bias_sum = as_row(total[bias_first : bias_first + rows] / count)
    return (gain * level[1]) * (grad - mask * (bias_sum + centred * gain_sum))


def column_sums(values, mask):
    weighted = values * mask
    return [
        as_rows(jnp.sum(weighted, 0, keepdims=True)),
        as_rows(jnp.sum(weighted * values, 0, keepdims=True)),
    ]


def product_sums(grad, centred):
    return as_rows(jnp.sum(grad * centred, 0, keepdims=True))


def plain_sums(grad):
    return as_rows(jnp.sum(grad, 0, keepdims=True))


def fetch(bundles, held, sems, start):
    rows = held.shape[3]
    copies = [
        pltpu.make_async_copy(ref.at[:, :, pl.ds(start, rows), :], held.at[half], sems.at[half])
        for half, ref in enumerate(bundles)
    ]
    for copy in copies:
        copy.start()
    return copies


def arrive(copies):
    for copy in copies:
        copy.wait()


def weight_part(held, chunk, chunks, start, units, columns):
    return jnp.concatenate(
        [
            held[half, group, chunk : chunk + chunks, start + part * units : start + (part + 1) * units, :]
            .reshape(chunks * units, 128)
            for half in range(2)
            for group in range(held.shape[1])
            for part in range(columns)
        ],
        1,
    )


def spots(core, groups, width):
    return [
        pl.multiple_of((2 * group + (core if half == 0 else 1 - core)) * width, 128)
        for half in range(2)
        for group in range(groups)
    ]


def in_turn(ref, core, groups):
    width = ref.shape[1] // (2 * groups)
    return jnp.concatenate([ref[:, pl.ds(at, width)] for at in spots(core, groups, width)], 1)


def in_order(ref, values, core, groups):
    width = ref.shape[1] // (2 * groups)
    for place, at in enumerate(spots(core, groups, width)):
        ref[:, pl.ds(at, width)] = values[:, place * width : (place + 1) * width]


def product(first, second):
    return lax.dot_general(
        first, second, (((1,), (0,)), ((), ())), preferred_element_type=jnp.float32
    )


def product_turned(first, second):
    return lax.dot_general(
        first, second, (((1,), (1,)), ((), ())), preferred_element_type=jnp.float32
    )


def many_in(values, held, units, columns):
    chunks = max(1, 256 // units)
    total = 0.0
    for chunk in range(0, held.shape[2], chunks):
        part = weight_part(held, chunk, chunks, 0, units, columns)
        total = total + product(
            values[:, chunk * units : (chunk + chunks) * units], part
        )
    return total


def many_out(values, held, units, columns):
    chunks = max(1, 256 // units)
    return [
        product_turned(values, weight_part(held, chunk, chunks, 0, units, columns))
        for chunk in range(0, held.shape[2], chunks)
    ]


def slid(values, offset):
    count = values.shape[0]
    return pltpu.roll(values, (-offset) % count, 0) if offset % count else values


def within(inside, drow, dcol):
    place = 3 * (drow + 1) + dcol + 1
    return inside[:, place : place + 1]


def first_layer(core, raw, mask, first, second, field, out, sums, held, sems):
    copies = fetch((first, second), held, sems, 0)
    core = core[0]
    weights = mask[...]
    width = raw.shape[2]
    for place in range(raw.shape[0]):
        part = raw[place].astype(jnp.float32) * weights
        field[:, place * width : (place + 1) * width] = part.astype(jnp.bfloat16)
    arrive(copies)
    result = many_in(field, held, held.shape[3], 1)
    in_order(out, result, core, held.shape[1])
    rows = column_sums(out[...], weights)
    pixels = weights.shape[0] // 4
    for part in (weights, weights[:pixels]):
        rows.append(jnp.broadcast_to(jnp.sum(part, 0, keepdims=True), (1, 128)))
    hand_out(sums, rows)


def side_layer(start, core, field, mask, first, second, out, sums, held, sems):
    copies = fetch((first, second), held, sems, start)
    core = core[0]
    pixels = mask.shape[0]
    arrive(copies)
    columns = out.shape[1] // (2 * held.shape[1] * 128)
    result = many_in(field[:pixels, :], held, held.shape[3] // columns, columns)
    in_order(out, result, core, held.shape[1])
    hand_out(sums, column_sums(out[...], mask[...]))


def spread_layer(start, norm, taps, core, before, sums_in, counts, tables, keep, mask_in, mask, inside,
                 first, second, cols, out, sums, held, sems):
    copies = fetch((first, second), held, sems, start)
    core = core[0]
    pixels = mask.shape[0]
    width = before.shape[1]
    counted = 0 if before.shape[0] > pixels else 1
    level = levels(total_of(sums_in), 0, width, counts[counted : counted + 1, :])
    act = standard(before[...], level) * tables[2 * norm : 2 * norm + 1, :] + tables[2 * norm + 1 : 2 * norm + 2, :]
    row = norm // 2
    hidden = jax.nn.silu(act) * mask_in[...] * keep[row : row + 1, :]
    for tap, phase, drow, dcol in taps:
        source = hidden[phase * pixels : (phase + 1) * pixels]
        moved = slid(source, drow * WO + dcol) * within(inside, drow, dcol)
        cols[:, tap * width : (tap + 1) * width] = moved.astype(jnp.bfloat16)
    arrive(copies)
    units = held.shape[3] // 9
    total = 0.0
    for tap in range(9):
        part = weight_part(held, 0, held.shape[2], tap * units, units, 1)
        total = total + product(cols[:, tap * width : (tap + 1) * width], part)
    in_order(out, total, core, held.shape[1])
    hand_out(sums, column_sums(out[...], mask[...]))


def widen_layer(start, norm, core, before, sums_in, counts, tables, keep, mask, first, second,
                hidden, out, sums, held, scratch, sems):
    copies = fetch((first, second), held, sems, start)
    core = core[0]
    level = levels(total_of(sums_in), 0, before.shape[1], counts[1:2, :])
    act = standard(before[...], level) * tables[2 * norm : 2 * norm + 1, :] + tables[2 * norm + 1 : 2 * norm + 2, :]
    row = norm // 2
    scratch[...] = jax.nn.silu(act) * mask[...] * keep[row : row + 1, :]
    hidden[...] = in_turn(scratch, core, held.shape[1]).astype(jnp.bfloat16)
    arrive(copies)
    parts = many_out(hidden[...], held, held.shape[3], 1)
    size = out.shape[1] // len(parts)
    for place, part in enumerate(parts):
        out[:, place * size : (place + 1) * size] = part
    hand_out(sums, column_sums(out[...], mask[...]))


def joined_acts(total, third, side, wide, count):
    width = third.shape[1]
    rows = width // 128
    centred_third = standard(third[...], levels(total, 0, width, count))
    centred_side = standard(side[...], levels(total, 2 * rows, width, count))
    act = (
        centred_third * wide[0:1, :]
        + wide[1:2, :]
        + (centred_side * wide[2:3, :] + wide[3:4, :])
    )
    return (centred_third, centred_side, act)


def narrow_layer(start, core, third, side, sums_in, counts, wide, mask, first, second,
                 above, out, sums, held, sems):
    copies = fetch((first, second), held, sems, start)
    core = core[0]
    centred_third, centred_side, act = joined_acts(
        total_of(sums_in), third, side, wide, counts[1:2, :]
    )
    above[...] = (jax.nn.silu(act) * mask[...]).astype(jnp.bfloat16)
    arrive(copies)
    result = many_in(above, held, held.shape[3], 1)
    in_order(out, result, core, held.shape[1])
    hand_out(sums, column_sums(out[...], mask[...]))


def last_layer(sixth, sums_in, counts, wide, above, cotangent, mask, out, grad, sums):
    level = levels(total_of(sums_in), 0, sixth.shape[1], counts[1:2, :])
    centred = standard(sixth[...], level)
    act = centred * wide[4:5, :] + wide[5:6, :] + above[...].astype(jnp.float32)
    weights = mask[...]
    result = (jax.nn.silu(act) * weights).astype(jnp.bfloat16)
    inner = weights * slope(act)
    width = out.shape[2]
    for place in range(out.shape[0]):
        span = slice(place * width, (place + 1) * width)
        out[place] = result[:, span]
        grad[:, span] = cotangent[place].astype(jnp.float32) * inner[:, span]
    result = grad[...]
    hand_out(sums, [product_sums(result, centred), plain_sums(result)])


def narrow_grad(grad, before, sums_in, counts, tables, norm, keep, mask):
    counted = 0 if norm == 0 else 1
    level = levels(total_of(sums_in), 0, before.shape[1], counts[counted : counted + 1, :])
    centred = standard(before[...], level)
    act = centred * tables[2 * norm : 2 * norm + 1, :] + tables[2 * norm + 1 : 2 * norm + 2, :]
    row = norm // 2
    result = grad * keep[row : row + 1, :] * mask * slope(act)
    return (result, [product_sums(result, centred), plain_sums(result)])


def narrow_back(norm, grad, before, sums_in, sums_back, counts, tables, mask):
    counted = 0 if norm == 0 else 1
    count = counts[counted : counted + 1, :]
    width = before.shape[1]
    level = levels(total_of(sums_in), 0, width, count)
    return back_through(
        grad[...],
        standard(before[...], level),
        level,
        tables[2 * norm : 2 * norm + 1, :],
        mask,
        total_of(sums_back),
        0,
        width // 128,
        count,
    )


def last_back(start, norm, core, grad, sixth, sums_six, back_six, counts, wide, before, sums_in, tables,
              keep, mask, first, second, grad_out, grad_in, sums, held, scratch, sems):
    copies = fetch((first, second), held, sems, start)
    core = core[0]
    width = sixth.shape[1]
    count = counts[1:2, :]
    level = levels(total_of(sums_six), 0, width, count)
    grad_out[...] = back_through(
        grad[...], standard(sixth[...], level), level, wide[4:5, :], mask[...], total_of(back_six), 0,
        width // 128, count,
    ).astype(jnp.bfloat16)
    arrive(copies)
    in_order(scratch, many_in(grad_out, held, held.shape[3], 1), core, held.shape[1])
    result, rows = narrow_grad(scratch[...], before, sums_in, counts, tables, norm, keep, mask[...])
    grad_in[...] = result
    hand_out(sums, rows)


def pair_back(start, norm, core, grad, third, side, sums_pair, back_pair, counts, wide, before, sums_in,
              tables, keep, mask, first, second, grad_third, grad_side, grad_in, sums, held, scratch,
              big, sems):
    copies = fetch((first, second), held, sems, start)
    core = core[0]
    width = third.shape[1]
    rows = width // 128
    count = counts[1:2, :]
    total = total_of(sums_pair)
    back = total_of(back_pair)
    groups = held.shape[1]
    level = levels(total, 0, width, count)
    grad_third[...] = back_through(
        grad[...], standard(third[...], level), level, wide[0:1, :], mask[...], back, 0, 2 * rows, count
    ).astype(jnp.bfloat16)
    arrive(copies)
    in_order(scratch, many_in(grad_third, held, held.shape[3], 1), core, groups)
    result, parts = narrow_grad(scratch[...], before, sums_in, counts, tables, norm, keep, mask[...])
    grad_in[...] = result
    hand_out(sums, parts)
    level = levels(total, 2 * rows, width, count)
    big[...] = back_through(
        grad[...], standard(side[...], level), level, wide[2:3, :], mask[...], back, rows, 2 * rows, count
    )
    grad_side[...] = in_turn(big, core, groups).astype(jnp.bfloat16)


def spread_back(start, norm, taps, core, grad, after, sums_after, back_after, counts, tables, before,
                sums_in, keep, mask_in, mask, inside, first, second, grad_out, grad_in, sums, held,
                scratch, sems):
    copies = fetch((first, second), held, sems, start)
    core = core[0]
    pixels = mask.shape[0]
    phases = before.shape[0] // pixels
    scratch[...] = narrow_back(norm + 1, grad, after, sums_after, back_after, counts, tables, mask[...])
    grad_out[...] = in_turn(scratch, core, held.shape[1]).astype(jnp.bfloat16)
    arrive(copies)
    units = held.shape[3] // 9
    totals = [0.0] * phases
    for tap, phase, drow, dcol in taps:
        part = weight_part(held, 0, held.shape[2], tap * units, units, 1)
        moved = product_turned(grad_out[...], part)
        totals[phase] = totals[phase] + slid(moved, -drow * WO - dcol) * within(inside, -drow, -dcol)
    hidden = jnp.concatenate(totals, 0) if phases > 1 else totals[0]
    result, rows = narrow_grad(hidden, before, sums_in, counts, tables, norm, keep, mask_in[...])
    grad_in[...] = result
    hand_out(sums, rows)


def narrow_layer_back(start, core, grad, fourth, sums_four, back_four, counts, tables, mask, grad_two,
                      third, side, sums_pair, wide, first, second, grad_out, grad_in, sums, held,
                      scratch, big, sems):
    copies = fetch((first, second), held, sems, start)
    core = core[0]
    scratch[...] = narrow_back(2, grad, fourth, sums_four, back_four, counts, tables, mask[...])
    grad_out[...] = in_turn(scratch, core, held.shape[1]).astype(jnp.bfloat16)
    arrive(copies)
    parts = many_out(grad_out[...], held, held.shape[3], 1)
    size = big.shape[1] // len(parts)
    for place, part in enumerate(parts):
        big[:, place * size : (place + 1) * size] = part
    centred_third, centred_side, act = joined_acts(
        total_of(sums_pair), third, side, wide, counts[1:2, :]
    )
    result = (grad_two[...] + big[...]) * mask[...] * slope(act)
    grad_in[...] = result
    hand_out(
        sums,
        [
            product_sums(result, centred_third),
            product_sums(result, centred_side),
            plain_sums(result),
        ],
    )


def side_back(start, grad, first, second, out, held, sems):
    copies = fetch((first, second), held, sems, start)
    arrive(copies)
    columns = grad.shape[1] // (2 * held.shape[1] * 128)
    parts = many_out(grad[...], held, held.shape[3] // columns, columns)
    size = out.shape[1] // len(parts)
    for place, part in enumerate(parts):
        out[:, place * size : (place + 1) * size] = part


def first_back(core, grad, before, sums_in, sums_back, counts, tables, mask, side, first, second,
               grad_out, out, held, scratch, sems):
    copies = fetch((first, second), held, sems, 0)
    core = core[0]
    scratch[...] = narrow_back(0, grad, before, sums_in, sums_back, counts, tables, mask[...])
    grad_out[...] = in_turn(scratch, core, held.shape[1]).astype(jnp.bfloat16)
    arrive(copies)
    parts = many_out(grad_out[...], held, held.shape[3], 1)
    size = side.shape[1] // len(parts)
    pixels = side.shape[0]
    weights = mask[...]
    width = out.shape[2]
    for place, part in enumerate(parts):
        owner = place * size // width
        span = slice(place * size % width, place * size % width + size)
        beside = side[:, place * size : (place + 1) * size]
        out[owner, :pixels, span] = ((part[:pixels] + beside) * weights[:pixels]).astype(jnp.bfloat16)
        out[owner, pixels:, span] = (part[pixels:] * weights[pixels:]).astype(jnp.bfloat16)


class Coming:
    def __init__(self, ref, copy):
        self.ref = ref
        self.copy = copy
        self.shape = ref.shape

    def settle(self):
        if self.copy is not None:
            self.copy.wait()
            self.copy = None

    def __getitem__(self, place):
        self.settle()
        return self.ref[place]


def framed(kernel, places, count, *refs):
    refs = list(refs)
    rest, held, sems = refs[: len(refs) - len(places) - 1], refs[-len(places) - 1 : -1], refs[-1]
    coming = []
    for at, place in enumerate(places):
        copy = pltpu.make_async_copy(rest[place], held[at], sems.at[at])
        copy.start()
        rest[place] = Coming(held[at], copy)
        coming.append(rest[place])
    kernel(*rest)
    for value in coming:
        value.settle()


def launch(kernel, shapes, values, bundles=(), rows=0, scratch=()):
    held = []
    sems = []
    if bundles:
        held = [pltpu.VMEM((2,) + bundles[0].shape[:2] + (rows, 128), jnp.bfloat16)]
        sems = [pltpu.SemaphoreType.DMA((2,))]
    places = [place for place, value in enumerate(values) if value.dtype != jnp.int32]
    specs = []
    for place, value in enumerate(values):
        space = pltpu.SMEM if value.dtype == jnp.int32 else pltpu.VMEM
        specs.append(pl.BlockSpec(memory_space=pltpu.HBM if place in places else space))
    late = []
    if places:
        kernel = functools.partial(framed, kernel, places, len(values))
        late = [pltpu.VMEM(values[place].shape, values[place].dtype) for place in places]
        late.append(pltpu.SemaphoreType.DMA((len(places),)))
    return pl.pallas_call(
        kernel,
        in_specs=specs + [pl.BlockSpec(memory_space=pltpu.HBM)] * len(bundles),
        out_specs=[pl.BlockSpec(memory_space=pltpu.VMEM)] * len(shapes),
        out_shape=list(shapes),
        scratch_shapes=held + [pltpu.VMEM(shape, jnp.float32) for shape in scratch] + sems + late,
        compiler_params=pltpu.CompilerParams(vmem_limit_bytes=VMEM_BYTES),
        cost_estimate=LIGHT,
    )(*values, *bundles)


def moved_by(grad, mean, square, weight, mean_out, square_out, update_out, at):
    first_fix = 1.0 - BETA_ONE**STEP
    second_fix = 1.0 - BETA_TWO**STEP
    old = weight[at]
    mean_next, square_next, step = adapt(grad, mean[at], square[at], first_fix, second_fix)
    update = step + DECAY * old
    mean_out[at] = mean_next
    square_out[at] = square_next
    update_out[at] = update
    result = []
    for value in (old, update):
        power = value * value
        while len(power.shape) > 2:
            power = jnp.sum(power, 0)
        row = jnp.sum(power, 0, keepdims=True)
        result.append(
            sum(row[:, place : place + 128] for place in range(0, row.shape[1], 128))
        )
    return result


def early_moves(columns, rows_a, rows_c, short_m, short_v, short_w, last_m, last_v, last_w, second_m, second_v,
                second_w, short_mo, short_vo, short_uo, last_mo, last_vo, last_uo, second_mo, second_vo,
                second_uo, powers):
    unit_in = short_w.shape[0]
    unit_out = second_w.shape[0]
    parts = short_w.shape[1] // 128
    every = (slice(None), slice(None))
    grad = jnp.concatenate(
        [rows_c[part * unit_in : (part + 1) * unit_in, :] for part in range(parts)], 1
    )
    found = moved_by(grad, short_m, short_v, short_w, short_mo, short_vo, short_uo, every)
    start = parts * unit_in
    for block, rows in enumerate((rows_c[start : start + unit_out, :], rows_a[...])):
        found += moved_by(
            jnp.transpose(rows), last_m, last_v, last_w, last_mo, last_vo, last_uo, block
        )
    start += unit_out
    found += moved_by(
        rows_c[start : start + unit_out, :], second_m, second_v, second_w, second_mo, second_vo,
        second_uo, every,
    )
    powers[...] = jnp.concatenate(found, 0)


def late_moves(rows_b, rows_d, rows_e, powers_in, first_m, first_v, first_w, mid_m, mid_v, mid_w, first_mo,
               first_vo, first_uo, mid_mo, mid_vo, mid_uo, powers):
    every = (slice(None), slice(None))
    found = moved_by(
        rows_e[...], first_m, first_v, first_w, first_mo, first_vo, first_uo, every
    )
    shape = mid_w.shape[1:]
    middle = []
    for block, rows in enumerate((rows_d, rows_b)):
        middle += moved_by(
            rows[...].reshape(shape), mid_m, mid_v, mid_w, mid_mo, mid_vo, mid_uo, block
        )
    early = powers_in[...]
    order = [found[0], found[1], early[0:2]] + middle + [early[2:8]]
    hand_out(powers, order)


def final_moves(powers, first_w, first_u, short_w, short_u, mid_w, mid_u, last_w, last_u, second_w, second_u,
                norms, first_o, short_o, mid_o, last_o, second_o, first_c, short_c, mid_c, last_c, second_c):
    total = jnp.sqrt(jnp.sum(jnp.sum(powers[...], 0), 1, keepdims=True))
    norms[...] = jnp.broadcast_to(total, norms.shape)

    def step(row, weight, update, out, copy, at):
        ratio = total[2 * row : 2 * row + 1] / (total[2 * row + 1 : 2 * row + 2] + EPS_TRUST)
        fresh = weight[at] - (RATE * ratio) * update[at]
        out[at] = fresh
        copy[at] = fresh.astype(jnp.bfloat16)

    every = (slice(None), slice(None))
    step(0, first_w, first_u, first_o, first_c, every)
    step(1, short_w, short_u, short_o, short_c, every)
    for block in range(2):
        for tap in range(mid_w.shape[1]):
            step(2 + block, mid_w, mid_u, mid_o, mid_c, (block, tap))
        step(4 + block, last_w, last_u, last_o, last_c, block)
    step(6, second_w, second_u, second_o, second_c, every)


def exchange(copies):
    return lax.all_to_all(copies, ("dp", "mp"), 0, 0, tiled=True)


def by_image(
    inputs,
    pixel_mask,
    widths,
    output_grad,
    first_weight,
    shortcut_weight,
    middle_weight,
    last_weight,
    second_weight,
    narrow_norms,
    wide_norms,
    first_mean,
    first_square,
    shortcut_mean,
    shortcut_square,
    middle_mean,
    middle_square,
    last_mean,
    last_square,
    second_mean,
    second_square,
    narrow_mean,
    narrow_square,
    wide_mean,
    wide_square,
):
    ranks = lax.axis_size("mp")
    rank = lax.axis_index("mp")
    pixels = pixel_mask.shape[1] // ranks
    narrow = first_weight.shape[1] * ranks
    wide = shortcut_weight.shape[1] * ranks
    low = jnp.bfloat16
    channels = inputs.shape[0]
    field = inputs.reshape(channels, 4, ranks, pixels).transpose(2, 1, 3, 0)
    field = field.reshape(ranks, 4 * pixels, channels)
    flow_a = Gather(pack(first_weight.astype(low)[None]), False)
    flow_b = Gather(pack(middle_weight[0].astype(low)))
    flow_c = Gather(
        jnp.concatenate(
            [
                pack(shortcut_weight.astype(low)[None]),
                pack(last_weight[0].astype(low).T[None]),
                pack(second_weight.astype(low)[None]),
            ]
        )
    )
    flow_d = Gather(
        jnp.concatenate(
            [pack(last_weight[1].astype(low).T[None]), pack(middle_weight[1].astype(low))]
        )
    )
    field = lax.all_to_all(field, "mp", 0, 0, tiled=True)
    tables = jnp.concatenate([narrow_norms.reshape(-1, 128), wide_norms.reshape(-1, 128)], 0)
    tables = jnp.broadcast_to(tables[None], (ranks,) + tables.shape)
    tables = lax.all_to_all(tables, "mp", 0, 0, tiled=True)
    wave([flow_a, flow_b])
    wave([flow_a, flow_b, flow_c], field)
    wave([flow_a, flow_b, flow_d], (flow_c.pending(), tables))
    unit_in, column = first_weight.shape
    column_wide = shortcut_weight.shape[1]
    unit_mid = middle_weight.shape[2]
    unit_out = second_weight.shape[0]
    size_short = unit_in * column_wide // 128
    size_out = unit_out * column // 128
    size_mid = 9 * unit_mid * column // 128
    split = narrow_norms.size // 128
    narrow_all = (
        tables[:, :split].reshape(ranks, 4, 2, -1).transpose(1, 2, 0, 3).reshape(4, 2, narrow)
    )
    wide_all = tables[:, split:].reshape(ranks, 3, 2, -1).transpose(1, 2, 0, 3).reshape(3, 2, wide)

    narrow_all = narrow_all.reshape(8, narrow)
    wide_all = jnp.concatenate([wide_all.reshape(6, wide), jnp.zeros((2, wide), jnp.float32)], 0)

    own_mask = lax.dynamic_slice_in_dim(pixel_mask, rank * pixels, pixels, 1).astype(jnp.float32)
    mask_in = own_mask.reshape(-1, 1)
    mask = own_mask[0][:, None]
    channel = lax.iota(jnp.int32, narrow)[None]
    keep = (channel < widths[:, None]).astype(jnp.float32)
    keep = jnp.concatenate([keep, jnp.zeros((6, narrow), jnp.float32)], 0)
    place = lax.iota(jnp.int32, pixels)[:, None]
    step = lax.iota(jnp.int32, 9)[None]
    row_at = place // WO % HO + step // 3 - 1
    col_at = place % WO + step % 3 - 1
    inside = (row_at >= 0) & (row_at < HO) & (col_at >= 0) & (col_at < WO)
    inside = inside.astype(jnp.float32)
    core = bit_of("mp", 1)[None]

    above = output_grad.reshape(-1, ranks, pixels).transpose(1, 2, 0)
    above = lax.all_to_all(above, "mp", 0, 0, tiled=True)

    devices = ranks * lax.axis_size("dp")
    full = 4 * pixels

    def real(*shape):
        return jax.ShapeDtypeStruct(shape, jnp.float32)

    def short(*shape):
        return jax.ShapeDtypeStruct(shape, low)

    size = narrow // 128
    wide_rows = wide // 128
    copies = real(devices, 2 * size, 128)
    bundle_a = flow_a.bundles()
    field, pre_one, sums = launch(
        first_layer,
        [short(full, ranks * channels), real(full, narrow), real(devices, 2 * size + 8, 128)],
        [core, field, mask_in],
        bundle_a,
        unit_in,
    )
    sums_one = wave([flow_c], sums, exchange(sums))
    sums_one = hold([flow_b, flow_c], sums_one)
    counts = jnp.sum(sums_one[:, 2 * size :], 0)
    bundle_b = flow_b.bundles()
    cols_one, pre_two, sums = launch(
        functools.partial(spread_layer, 0, 0, STRIDED_TAPS),
        [short(pixels, 9 * narrow), real(pixels, narrow), copies],
        [core, pre_one, sums_one, counts, narrow_all, keep, mask_in, mask, inside],
        bundle_b,
        size_mid,
    )
    sums_two = hold([flow_c, flow_d], exchange(sums))
    bundle_c = flow_c.bundles()
    pre_side, side_sums = launch(
        functools.partial(side_layer, 0),
        [real(pixels, wide), real(2 * wide_rows, 128)],
        [core, field, mask],
        bundle_c,
        size_short,
    )
    hid_two, pre_three, sums = launch(
        functools.partial(widen_layer, size_short, 1),
        [short(pixels, narrow), real(pixels, wide), real(2 * wide_rows, 128)],
        [core, pre_two, sums_two, counts, narrow_all, keep, mask],
        bundle_c,
        size_out,
        [(pixels, narrow)],
    )
    sums_pair = everywhere(jnp.concatenate([sums, side_sums], 0), [flow_d])
    out_one, pre_four, sums = launch(
        functools.partial(narrow_layer, size_short + size_out),
        [short(pixels, wide), real(pixels, narrow), copies],
        [core, pre_three, pre_side, sums_pair, counts, wide_all, mask],
        bundle_c,
        size_out,
    )
    sums_four = wave([flow_d], sums, exchange(sums))
    bundle_d = flow_d.bundles()
    cols_four, pre_five, sums = launch(
        functools.partial(spread_layer, size_out, 2, PLAIN_TAPS),
        [short(pixels, 9 * narrow), real(pixels, narrow), copies],
        [core, pre_four, sums_four, counts, narrow_all, keep, mask, mask, inside],
        bundle_d,
        size_mid,
    )
    sums_five = exchange(sums)
    hid_five, pre_six, sums = launch(
        functools.partial(widen_layer, 0, 3),
        [short(pixels, narrow), real(pixels, wide), real(2 * wide_rows, 128)],
        [core, pre_five, sums_five, counts, narrow_all, keep, mask],
        bundle_d,
        size_out,
        [(pixels, narrow)],
    )
    sums_six = everywhere(sums)
    block_output, grad_two, sums = launch(
        last_layer,
        [short(*above.shape), real(pixels, wide), real(2 * wide_rows, 128)],
        [pre_six, sums_six, counts, wide_all, out_one, above, mask],
    )
    back_six = everywhere(sums)

    grad_six, act_five_grad, sums = launch(
        functools.partial(last_back, 0, 3),
        [short(pixels, wide), real(pixels, narrow), copies],
        [core, grad_two, pre_six, sums_six, back_six, counts, wide_all, pre_five,
         sums_five, narrow_all, keep, mask],
        bundle_d,
        size_out,
        [(pixels, narrow)],
    )
    bundle = chunks_into(None, size_out, 0, grad_six, hid_five, 1, unit_out, column)
    back_a = Scatter(*bundle, False)
    back_five = hold([back_a], exchange(sums))
    grad_five, act_four_grad, sums = launch(
        functools.partial(spread_back, size_out, 2, PLAIN_TAPS),
        [short(pixels, narrow), real(pixels, narrow), copies],
        [core, act_five_grad, pre_five, sums_five, back_five, counts, narrow_all,
         pre_four, sums_four, keep, mask, mask, inside],
        bundle_d,
        size_mid,
        [(pixels, narrow)],
    )
    back_four = exchange(sums)
    bundle = chunks_into(None, size_mid, 0, cols_four, grad_five, 9, unit_mid, column)
    back_b = Scatter(*bundle)
    back_four = wave([back_a], sums, back_four)
    back_four = hold([back_b], back_four)
    grad_four, grad_one, sums = launch(
        functools.partial(narrow_layer_back, size_short + size_out),
        [short(pixels, narrow), real(pixels, wide), real(3 * wide_rows, 128)],
        [core, act_four_grad, pre_four, sums_four, back_four, counts, narrow_all, mask,
         grad_two, pre_three, pre_side, sums_pair, wide_all],
        bundle_c,
        size_out,
        [(pixels, narrow), (pixels, wide)],
    )
    back_pair = everywhere(sums, [back_a, back_b])
    total = size_short + 2 * size_out
    bundle = chunks_into(
        None, total, size_short + size_out, out_one, grad_four, 1, unit_out, column
    )
    back_pair, bundle = lax.optimization_barrier((back_pair, bundle))
    grad_three, grad_side, act_two_grad, sums = launch(
        functools.partial(pair_back, size_short, 1),
        [short(pixels, wide), short(pixels, wide), real(pixels, narrow), copies],
        [core, grad_one, pre_three, pre_side, sums_pair, back_pair, counts, wide_all,
         pre_two, sums_two, narrow_all, keep, mask],
        bundle_c,
        size_out,
        [(pixels, narrow), (pixels, wide)],
    )
    back_two = wave([back_b], sums, exchange(sums))
    bundle = chunks_into(bundle, total, size_short, grad_three, hid_two, 1, unit_out, column)
    bundle = chunks_into(bundle, total, 0, field, grad_side, 1, unit_in, column_wide)
    back_c = Scatter(*bundle)
    back_two = hold([back_c], back_two)
    back_two = wave([back_c], None, back_two)
    grad_mid, act_one_grad, sums = launch(
        functools.partial(spread_back, 0, 0, STRIDED_TAPS),
        [short(pixels, narrow), real(full, narrow), copies],
        [core, act_two_grad, pre_two, sums_two, back_two, counts, narrow_all, pre_one,
         sums_one, keep, mask_in, mask, inside],
        bundle_b,
        size_mid,
        [(pixels, narrow)],
    )
    back_one = wave([back_b, back_c], sums, exchange(sums))
    bundle = chunks_into(None, size_mid, 0, cols_one, grad_mid, 9, unit_mid, column)
    back_d = Scatter(*bundle)
    (side_grad,) = launch(
        functools.partial(side_back, 0),
        [real(pixels, field.shape[1])],
        [grad_side],
        bundle_c,
        size_short,
    )
    back_one = hold([back_d], back_one)
    back_one, side_grad = lax.optimization_barrier((back_one, side_grad))
    grad_first, field_grad = launch(
        first_back,
        [short(full, narrow), short(ranks, full, channels)],
        [core, act_one_grad, pre_one, sums_one, back_one, counts, narrow_all, mask_in,
         side_grad],
        bundle_a,
        unit_in,
        [(full, narrow)],
    )
    grad_first = wave([back_c, back_d], back_one, grad_first)
    bundle = chunks_into(None, unit_in * column // 128, 0, field, grad_first, 1, unit_in, column)
    back_e = Scatter(*bundle, False)
    wave([back_e])
    input_grad = lax.all_to_all(field_grad, "mp", 0, 0, tiled=True)
    input_grad = input_grad.reshape(ranks, 4, pixels, channels).transpose(3, 1, 0, 2)
    input_grad = input_grad.reshape(inputs.shape)
    wave([back_d, back_e])
    wave([back_d, back_e])
    rows_a, rows_b, rows_c, rows_d, rows_e = [
        flow.rows() for flow in (back_a, back_b, back_c, back_d, back_e)
    ]
    first_fix = 1.0 - BETA_ONE**STEP
    second_fix = 1.0 - BETA_TWO**STEP

    def like(*values):
        return [real(*value.shape) for value in values for _ in range(3)]

    early = launch(
        functools.partial(early_moves, column),
        like(shortcut_weight, last_weight, second_weight) + [real(8, 128)],
        [rows_a, rows_c]
        + [
            shortcut_mean, shortcut_square, shortcut_weight, last_mean, last_square, last_weight,
            second_mean, second_square, second_weight,
        ],
    )
    block_output, _ = lax.optimization_barrier((block_output, early[-1]))
    block_output = lax.all_to_all(block_output, "mp", 0, 0, tiled=True)
    block_output = block_output.transpose(2, 0, 1).reshape(-1, ranks * pixels)
    late = launch(
        late_moves,
        like(first_weight, middle_weight) + [real(devices, 16, 128)],
        [rows_b, rows_d, rows_e, early[-1]]
        + [first_mean, first_square, first_weight, middle_mean, middle_square, middle_weight],
    )
    powers = exchange(late[-1])
    weights = (first_weight, shortcut_weight, middle_weight, last_weight, second_weight)
    updates = (late[2], early[2], late[5], early[5], early[8])
    norms, *fresh = launch(
        final_moves,
        [real(16, 128)]
        + [real(*value.shape) for value in weights]
        + [short(*value.shape) for value in weights],
        [powers]
        + [value for pair in zip(weights, updates) for value in pair],
    )
    matrix_norms = norms[:14, 0].reshape(7, 2)
    first_next, short_next, middle_next, last_next, second_next = fresh[:5]
    states = [late[0:2], early[0:2], late[3:5], early[3:5], early[6:8]]

    def own_channels(values):
        width = values.shape[-1] // ranks
        return lax.dynamic_slice_in_dim(values, rank * width, width, values.ndim - 1)

    narrow_grads = jnp.stack([jnp.sum(rows, 0) for rows in (back_one, back_two, back_four, back_five)])
    narrow_grad = own_channels(narrow_grads.reshape(4, 2, narrow))
    gain_three, gain_side, bias_pair = jnp.sum(back_pair, 0).reshape(3, wide)
    wide_grad = own_channels(
        jnp.stack(
            [
                jnp.stack([gain_three, bias_pair]),
                jnp.stack([gain_side, bias_pair]),
                jnp.sum(back_six, 0).reshape(2, wide),
            ]
        )
    )
    narrow_mean_next, narrow_square_next, narrow_step = adapt(
        narrow_grad, narrow_mean, narrow_square, first_fix, second_fix
    )
    wide_mean_next, wide_square_next, wide_step = adapt(
        wide_grad, wide_mean, wide_square, first_fix, second_fix
    )
    return (
        block_output,
        input_grad,
        states[0][0],
        states[0][1],
        first_next,
        states[1][0],
        states[1][1],
        short_next,
        states[2][0],
        states[2][1],
        middle_next,
        states[3][0],
        states[3][1],
        last_next,
        states[4][0],
        states[4][1],
        second_next,
        narrow_mean_next,
        narrow_square_next,
        narrow_norms - RATE_NORM * narrow_step,
        wide_mean_next,
        wide_square_next,
        wide_norms - RATE_NORM * wide_step,
        matrix_norms,
        *fresh[5:],
    )


def solution(mesh):
    in_specs = (
        P("mp", None, "dp"),
        P(None, "dp"),
        P(),
        P("mp", "dp"),
        P("dp", "mp"),
        P("dp", "mp"),
        P(None, None, "dp", "mp"),
        P(None, "mp", "dp"),
        P("dp", "mp"),
        P(None, None, "mp"),
        P(None, None, "mp"),
        P("dp", "mp"),
        P("dp", "mp"),
        P("dp", "mp"),
        P("dp", "mp"),
        P(None, None, "dp", "mp"),
        P(None, None, "dp", "mp"),
        P(None, "mp", "dp"),
        P(None, "mp", "dp"),
        P("dp", "mp"),
        P("dp", "mp"),
        P(None, None, "mp"),
        P(None, None, "mp"),
        P(None, None, "mp"),
        P(None, None, "mp"),
    )
    out_specs = (
        P("mp", "dp"),
        P("mp", None, "dp"),
        P("dp", "mp"),
        P("dp", "mp"),
        P("dp", "mp"),
        P("dp", "mp"),
        P("dp", "mp"),
        P("dp", "mp"),
        P(None, None, "dp", "mp"),
        P(None, None, "dp", "mp"),
        P(None, None, "dp", "mp"),
        P(None, "mp", "dp"),
        P(None, "mp", "dp"),
        P(None, "mp", "dp"),
        P("dp", "mp"),
        P("dp", "mp"),
        P("dp", "mp"),
        P(None, None, "mp"),
        P(None, None, "mp"),
        P(None, None, "mp"),
        P(None, None, "mp"),
        P(None, None, "mp"),
        P(None, None, "mp"),
        P(),
        P("dp", "mp"),
        P("dp", "mp"),
        P(None, None, "dp", "mp"),
        P(None, "mp", "dp"),
        P("dp", "mp"),
    )
    return jax.shard_map(
        lambda *values: (by_image if fits(mesh, values[1]) else shards)(*values),
        mesh=mesh,
        in_specs=in_specs,
        out_specs=out_specs,
        check_vma=False,
    )
```

```python
import functools

import jax
import jax.numpy as jnp
from jax import lax
from jax.experimental import pallas as pl
from jax.experimental.pallas import tpu as pltpu
from jax.sharding import PartitionSpec as P

HO = 16
WO = 11
STEP = 10


EPS_NORM = 1e-05
BETA_ONE = 0.9
BETA_TWO = 0.999
EPS_ADAM = 1e-06
DECAY = 0.01
RATE = 0.3
RATE_NORM = 0.3
EPS_TRUST = 1e-06
PHASES = ((1, -1), (0, 0), (1, 0))
STRIDED_TAPS = tuple(
    (
        (
            3 * above + beside,
            2 * PHASES[above][0] + PHASES[beside][0],
            PHASES[above][1],
            PHASES[beside][1],
        )
        for above in range(3)
        for beside in range(3)
    )
)
PLAIN_TAPS = tuple(
    ((3 * above + beside, 0, above - 1, beside - 1) for above in range(3) for beside in range(3))
)


def slope(values):
    gate = jax.nn.sigmoid(values)
    return gate * (1.0 + values * (1.0 - gate))


def shifted(values, drow, dcol):
    length = values.shape[1]
    offset = drow * WO + dcol
    place = lax.iota(jnp.int32, length)
    row_at = place // WO % HO + drow
    col_at = place % WO + dcol
    inside = (row_at >= 0) & (row_at < HO) & (col_at >= 0) & (col_at < WO)
    moved = jnp.roll(values, -offset, axis=1)
    return jnp.where(inside[None, :], moved, jnp.zeros_like(moved))


def over_images(first, second):
    return lax.psum((first, second), "dp")


def moments(values, mask):
    weighted = values * mask[None, :]
    return over_images(jnp.sum(weighted, 1), jnp.sum(weighted * values, 1))


def normalize(values, totals, squares, count, gain, bias):
    mean = totals / count
    scale = lax.rsqrt(squares / count - mean * mean + EPS_NORM)
    centred = (values - mean[:, None]) * scale[:, None]
    return (centred, scale, centred * gain[:, None] + bias[:, None])


def back_sums(grad_in, centred):
    return over_images(jnp.sum(grad_in * centred, 1), jnp.sum(grad_in, 1))


def norm_back(grad_in, centred, scale, gain, mask, gain_sum, bias_sum, count):
    return (gain * scale)[:, None] * (
        grad_in - mask[None, :] * (bias_sum[:, None] + centred * gain_sum[:, None]) / count
    )


def input_mix(values, weight, side_weight, pixels):
    start_sum = (jnp.zeros((weight.shape[1], values.shape[1]), jnp.float32),)
    if side_weight is not None:
        start_sum = start_sum + (jnp.zeros((side_weight.shape[1], pixels), jnp.float32),)
    piece = lax.all_gather(values, "mp", axis=0, tiled=True)
    result = (jnp.einsum("kc,kp->cp", weight, piece, preferred_element_type=jnp.float32),)
    if side_weight is not None:
        result = result + (
            jnp.einsum(
                "kc,kp->cp", side_weight, piece[:, :pixels], preferred_element_type=jnp.float32
            ),
        )
    return result


def mid_gathered(hidden):
    return lax.all_gather(hidden, "mp", axis=0, tiled=True)


def conv_forward(gathered, kernel, taps, pixels):
    result = jnp.zeros((kernel.shape[2], pixels), jnp.float32)
    for tap, phase, drow, dcol in taps:
        source = gathered[:, phase * pixels : (phase + 1) * pixels]
        part = jnp.einsum("kc,kp->cp", kernel[tap], source, preferred_element_type=jnp.float32)
        result = result + shifted(part, drow, dcol)
    return result


def conv_backward(grad_b, gathered, kernel, taps, pixels, phases):
    moved = [shifted(grad_b, -drow, -dcol) for tap, phase, drow, dcol in taps]
    count = gathered.shape[0] // lax.axis_size("mp") * lax.axis_size("mp")
    blocks = []
    for target in range(phases):
        result = jnp.zeros((count, pixels), jnp.float32)
        for conv_index, (conv_tap, conv_phase, conv_drow, conv_dcol) in enumerate(taps):
            if conv_phase == target:
                part = kernel[conv_tap]
                result = result + jnp.dot(
                    part, moved[conv_index], preferred_element_type=jnp.float32
                )
        blocks.append(result)
    hidden_grad = lax.psum_scatter(
        jnp.concatenate(blocks, 1), "mp", scatter_dimension=0, tiled=True
    )
    kernel_grad = jnp.stack(
        [
            jnp.einsum(
                "kp,cp->kc",
                gathered[:, phase * pixels : (phase + 1) * pixels],
                moved[index],
                preferred_element_type=jnp.float32,
            )
            for index, (tap, phase, drow, dcol) in enumerate(taps)
        ]
    )
    return (hidden_grad, kernel_grad)


def output_mix(hidden, kernel):
    return lax.psum_scatter(
        jnp.einsum("kc,kp->cp", kernel, hidden, preferred_element_type=jnp.float32),
        "mp",
        scatter_dimension=0,
        tiled=True,
    )


def output_back(grad_b, kernel, hidden):
    piece = lax.all_gather(grad_b, "mp", axis=0, tiled=True)
    hidden_grad = jnp.dot(kernel, piece, preferred_element_type=jnp.float32)
    columns = jnp.einsum("cp,kp->ck", hidden, piece, preferred_element_type=jnp.float32)
    return (hidden_grad, columns)


def input_back(values, grad_b, side_b, weight, side_weight, pixels):
    width = weight.shape[1]
    result = jnp.dot(weight, grad_b, preferred_element_type=jnp.float32)
    if side_weight is not None:
        result = jnp.concatenate(
            [
                result[:, :pixels]
                + jnp.dot(side_weight, side_b, preferred_element_type=jnp.float32),
                result[:, pixels:],
            ],
            1,
        )
    values_grad = lax.psum_scatter(result, "mp", scatter_dimension=0, tiled=True)
    piece = lax.all_gather(values, "mp", axis=0, tiled=True)
    blocks = [jnp.einsum("kp,cp->kc", piece, grad_b, preferred_element_type=jnp.float32)]
    if side_weight is not None:
        blocks.append(
            jnp.einsum("kp,cp->kc", piece[:, :pixels], side_b, preferred_element_type=jnp.float32)
        )
    joined = jnp.concatenate(blocks, 1)
    return (values_grad, joined[:, :width], joined[:, width:])


def adapt(grad_in, mean, square, first_fix, second_fix):
    mean_next = BETA_ONE * mean + (1.0 - BETA_ONE) * grad_in
    square_next = BETA_TWO * square + (1.0 - BETA_TWO) * grad_in * grad_in
    step = mean_next / first_fix / (jnp.sqrt(square_next / second_fix) + EPS_ADAM)
    return (mean_next, square_next, step)


def shards(
    inputs,
    pixel_mask,
    widths,
    output_grad,
    first_weight,
    shortcut_weight,
    middle_weight,
    last_weight,
    second_weight,
    narrow_norms,
    wide_norms,
    first_mean,
    first_square,
    shortcut_mean,
    shortcut_square,
    middle_mean,
    middle_square,
    last_mean,
    last_square,
    second_mean,
    second_square,
    narrow_mean,
    narrow_square,
    wide_mean,
    wide_square,
):
    pixels = pixel_mask.shape[1]
    width = first_weight.shape[1]
    rank = lax.axis_index("mp")
    channel = rank * width + lax.iota(jnp.int32, width)
    keep_one = (channel < widths[0]).astype(jnp.float32)[:, None]
    keep_two = (channel < widths[1]).astype(jnp.float32)[:, None]
    masks = pixel_mask.astype(jnp.float32)
    mask_in = masks.reshape(-1)
    mask_out = masks[0]
    field = (inputs * pixel_mask.astype(jnp.bfloat16)[None]).reshape(inputs.shape[0], -1)
    first_w, short_w, middle_w, last_w, second_w = (
        lax.all_gather(first_weight.astype(jnp.bfloat16), "dp", axis=0, tiled=True),
        lax.all_gather(shortcut_weight.astype(jnp.bfloat16), "dp", axis=0, tiled=True),
        lax.all_gather(middle_weight.astype(jnp.bfloat16), "dp", axis=2, tiled=True),
        lax.all_gather(last_weight.astype(jnp.bfloat16), "dp", axis=2, tiled=True),
        lax.all_gather(second_weight.astype(jnp.bfloat16), "dp", axis=0, tiled=True),
    )
    count_in, count_out = over_images(jnp.sum(mask_in), jnp.sum(mask_out))
    pre_one, pre_side = input_mix(field, first_w, short_w, pixels)
    totals, squares = moments(pre_one, mask_in)
    cen_one, scale_one, act_one = normalize(
        pre_one, totals, squares, count_in, narrow_norms[0, 0], narrow_norms[0, 1]
    )
    hid_one = (jax.nn.silu(act_one) * mask_in[None, :] * keep_one).astype(jnp.bfloat16)
    gat_one = mid_gathered(hid_one)
    pre_two = conv_forward(gat_one, middle_w[0], STRIDED_TAPS, pixels)
    totals, squares = moments(pre_two, mask_out)
    cen_two, scale_two, act_two = normalize(
        pre_two, totals, squares, count_out, narrow_norms[1, 0], narrow_norms[1, 1]
    )
    hid_two = (jax.nn.silu(act_two) * mask_out[None, :] * keep_one).astype(jnp.bfloat16)
    pre_three = output_mix(hid_two, last_w[0])
    weighted_three = pre_three * mask_out[None, :]
    weighted_side = pre_side * mask_out[None, :]
    totals, squares = over_images(
        jnp.stack([jnp.sum(weighted_three, 1), jnp.sum(weighted_side, 1)]),
        jnp.stack([jnp.sum(weighted_three * pre_three, 1), jnp.sum(weighted_side * pre_side, 1)]),
    )
    cen_three, scale_three, act_three = normalize(
        pre_three, totals[0], squares[0], count_out, wide_norms[0, 0], wide_norms[0, 1]
    )
    cen_side, scale_side, act_side = normalize(
        pre_side, totals[1], squares[1], count_out, wide_norms[1, 0], wide_norms[1, 1]
    )
    total_one = act_three + act_side
    out_one = (jax.nn.silu(total_one) * mask_out[None, :]).astype(jnp.bfloat16)
    (pre_four,) = input_mix(out_one, second_w, None, pixels)
    totals, squares = moments(pre_four, mask_out)
    cen_four, scale_four, act_four = normalize(
        pre_four, totals, squares, count_out, narrow_norms[2, 0], narrow_norms[2, 1]
    )
    hid_four = (jax.nn.silu(act_four) * mask_out[None, :] * keep_two).astype(jnp.bfloat16)
    gat_four = mid_gathered(hid_four)
    pre_five = conv_forward(gat_four, middle_w[1], PLAIN_TAPS, pixels)
    totals, squares = moments(pre_five, mask_out)
    cen_five, scale_five, act_five = normalize(
        pre_five, totals, squares, count_out, narrow_norms[3, 0], narrow_norms[3, 1]
    )
    hid_five = (jax.nn.silu(act_five) * mask_out[None, :] * keep_two).astype(jnp.bfloat16)
    pre_six = output_mix(hid_five, last_w[1])
    totals, squares = moments(pre_six, mask_out)
    cen_six, scale_six, act_six = normalize(
        pre_six, totals, squares, count_out, wide_norms[2, 0], wide_norms[2, 1]
    )
    total_two = act_six + out_one.astype(jnp.float32)
    block_output = (jax.nn.silu(total_two) * mask_out[None, :]).astype(jnp.bfloat16)
    grad_two = output_grad.astype(jnp.float32) * mask_out[None, :] * slope(total_two)
    gain_six, bias_six = back_sums(grad_two, cen_six)
    grad_six = norm_back(
        grad_two, cen_six, scale_six, wide_norms[2, 0], mask_out, gain_six, bias_six, count_out
    ).astype(jnp.bfloat16)
    hid_five_grad, last_one_grad = output_back(grad_six, last_w[1], hid_five)
    act_five_grad = hid_five_grad * keep_two * mask_out[None, :] * slope(act_five)
    gain_five, bias_five = back_sums(act_five_grad, cen_five)
    grad_five = norm_back(
        act_five_grad,
        cen_five,
        scale_five,
        narrow_norms[3, 0],
        mask_out,
        gain_five,
        bias_five,
        count_out,
    ).astype(jnp.bfloat16)
    hid_four_grad, middle_one_grad = conv_backward(
        grad_five, gat_four, middle_w[1], PLAIN_TAPS, pixels, 1
    )
    act_four_grad = hid_four_grad * keep_two * mask_out[None, :] * slope(act_four)
    gain_four, bias_four = back_sums(act_four_grad, cen_four)
    grad_four = norm_back(
        act_four_grad,
        cen_four,
        scale_four,
        narrow_norms[2, 0],
        mask_out,
        gain_four,
        bias_four,
        count_out,
    ).astype(jnp.bfloat16)
    out_one_grad, second_grad, unused_side = input_back(
        out_one, grad_four, None, second_w, None, pixels
    )
    grad_one = (grad_two + out_one_grad) * mask_out[None, :] * slope(total_one)
    gains_pair, bias_pair = over_images(
        jnp.stack([jnp.sum(grad_one * cen_three, 1), jnp.sum(grad_one * cen_side, 1)]),
        jnp.sum(grad_one, 1),
    )
    grad_three = norm_back(
        grad_one,
        cen_three,
        scale_three,
        wide_norms[0, 0],
        mask_out,
        gains_pair[0],
        bias_pair,
        count_out,
    ).astype(jnp.bfloat16)
    grad_side = norm_back(
        grad_one,
        cen_side,
        scale_side,
        wide_norms[1, 0],
        mask_out,
        gains_pair[1],
        bias_pair,
        count_out,
    ).astype(jnp.bfloat16)
    hid_two_grad, last_zero_grad = output_back(grad_three, last_w[0], hid_two)
    act_two_grad = hid_two_grad * keep_one * mask_out[None, :] * slope(act_two)
    gain_two, bias_two = back_sums(act_two_grad, cen_two)
    grad_mid = norm_back(
        act_two_grad,
        cen_two,
        scale_two,
        narrow_norms[1, 0],
        mask_out,
        gain_two,
        bias_two,
        count_out,
    ).astype(jnp.bfloat16)
    hid_one_grad, middle_zero_grad = conv_backward(
        grad_mid, gat_one, middle_w[0], STRIDED_TAPS, pixels, 4
    )
    act_one_grad = hid_one_grad * keep_one * mask_in[None, :] * slope(act_one)
    gain_one, bias_one = back_sums(act_one_grad, cen_one)
    grad_first = norm_back(
        act_one_grad, cen_one, scale_one, narrow_norms[0, 0], mask_in, gain_one, bias_one, count_in
    ).astype(jnp.bfloat16)
    field_grad, first_grad, short_grad = input_back(
        field, grad_first, grad_side, first_w, short_w, pixels
    )
    input_grad = (field_grad * mask_in[None, :]).astype(jnp.bfloat16).reshape(inputs.shape)
    grads = (
        lax.psum_scatter(first_grad, "dp", scatter_dimension=0, tiled=True),
        lax.psum_scatter(short_grad, "dp", scatter_dimension=0, tiled=True),
        lax.psum_scatter(
            jnp.stack([middle_zero_grad, middle_one_grad]), "dp", scatter_dimension=2, tiled=True
        ),
        lax.psum_scatter(
            jnp.stack([last_zero_grad, last_one_grad]), "dp", scatter_dimension=2, tiled=True
        ),
        lax.psum_scatter(second_grad, "dp", scatter_dimension=0, tiled=True),
    )
    first_fix = 1.0 - BETA_ONE**STEP
    second_fix = 1.0 - BETA_TWO**STEP
    weights = (first_weight, shortcut_weight, middle_weight, last_weight, second_weight)
    means = (first_mean, shortcut_mean, middle_mean, last_mean, second_mean)
    squares_old = (first_square, shortcut_square, middle_square, last_square, second_square)
    states = []
    updates = []
    for index in range(5):
        mean_next, square_next, step = adapt(
            grads[index], means[index], squares_old[index], first_fix, second_fix
        )
        states.append((mean_next, square_next))
        updates.append(step + DECAY * weights[index])
    pairs = [
        (weights[0], updates[0]),
        (weights[1], updates[1]),
        (weights[2][0], updates[2][0]),
        (weights[2][1], updates[2][1]),
        (weights[3][0], updates[3][0]),
        (weights[3][1], updates[3][1]),
        (weights[4], updates[4]),
    ]
    partial_value = jnp.stack(
        [
            jnp.stack([jnp.sum(weight * weight), jnp.sum(update * update)])
            for weight, update in pairs
        ]
    )
    matrix_norms = jnp.sqrt(lax.psum(partial_value, ("dp", "mp")))
    ratio = matrix_norms[:, 0] / (matrix_norms[:, 1] + EPS_TRUST)
    first_next = first_weight - RATE * ratio[0] * updates[0]
    short_next = shortcut_weight - RATE * ratio[1] * updates[1]
    middle_next = middle_weight - RATE * ratio[2:4].reshape(2, 1, 1, 1) * updates[2]
    last_next = last_weight - RATE * ratio[4:6].reshape(2, 1, 1) * updates[3]
    second_next = second_weight - RATE * ratio[6] * updates[4]
    narrow_grad = jnp.stack(
        [
            jnp.stack([gain_one, bias_one]),
            jnp.stack([gain_two, bias_two]),
            jnp.stack([gain_four, bias_four]),
            jnp.stack([gain_five, bias_five]),
        ]
    )
    wide_grad = jnp.stack(
        [
            jnp.stack([gains_pair[0], bias_pair]),
            jnp.stack([gains_pair[1], bias_pair]),
            jnp.stack([gain_six, bias_six]),
        ]
    )
    narrow_mean_next, narrow_square_next, narrow_step = adapt(
        narrow_grad, narrow_mean, narrow_square, first_fix, second_fix
    )
    wide_mean_next, wide_square_next, wide_step = adapt(
        wide_grad, wide_mean, wide_square, first_fix, second_fix
    )
    return (
        block_output,
        input_grad,
        states[0][0],
        states[0][1],
        first_next,
        states[1][0],
        states[1][1],
        short_next,
        states[2][0],
        states[2][1],
        middle_next,
        states[3][0],
        states[3][1],
        last_next,
        states[4][0],
        states[4][1],
        second_next,
        narrow_mean_next,
        narrow_square_next,
        narrow_norms - RATE_NORM * narrow_step,
        wide_mean_next,
        wide_square_next,
        wide_norms - RATE_NORM * wide_step,
        matrix_norms,
        first_next.astype(jnp.bfloat16),
        short_next.astype(jnp.bfloat16),
        middle_next.astype(jnp.bfloat16),
        last_next.astype(jnp.bfloat16),
        second_next.astype(jnp.bfloat16),
    )


VMEM_BYTES = 62 * 2**20
LIGHT = pl.CostEstimate(flops=1024, bytes_accessed=1024, transcendentals=0)


def fits(mesh, pixel_mask):
    sizes = (mesh.shape["dp"], mesh.shape["mp"])
    powers = all(size >= 2 and size & (size - 1) == 0 for size in sizes)
    return powers and pixel_mask.shape[1] % (HO * WO * sizes[1]) == 0


def swap(values, *bits):
    sizes = {axis: lax.axis_size(axis) for axis in ("dp", "mp")}
    masks = {axis: sum(mask for at, mask in bits if at == axis) for axis in sizes}
    if not masks["dp"]:
        return lax.ppermute(values, "mp", [(at, at ^ masks["mp"]) for at in range(sizes["mp"])])
    if not masks["mp"]:
        return lax.ppermute(values, "dp", [(at, at ^ masks["dp"]) for at in range(sizes["dp"])])
    mask = masks["dp"] * sizes["mp"] + masks["mp"]
    return lax.ppermute(
        values, ("dp", "mp"), [(at, at ^ mask) for at in range(sizes["dp"] * sizes["mp"])]
    )


def subsets(bits):
    return [
        [bit for place, bit in enumerate(bits) if index >> place & 1]
        for index in range(1 << len(bits))
    ]


def bit_of(axis, mask):
    return (lax.axis_index(axis) & mask) // mask


def high_bits(axis):
    masks = []
    mask = lax.axis_size(axis) // 2
    while mask:
        masks.append(mask)
        mask //= 2
    return masks


def everywhere(values, flows=()):
    mask = 1
    while mask < lax.axis_size("mp"):
        values = values + swap(values, ("mp", mask))
        mask *= 2
    copies = jnp.broadcast_to(values[None], (lax.axis_size("dp"),) + values.shape)
    arrived = lax.all_to_all(copies, "dp", 0, 0, tiled=True)
    return wave(flows, values, arrived) if flows else arrived


def pack(block):
    lead, rows, cols = block.shape
    parts = block.reshape(lead, rows, cols // 128, 128).transpose(0, 2, 1, 3)
    return parts.reshape(-1, 128)


def column_bits():
    return [("mp", mask) for mask in high_bits("mp")[:-1]]


def row_bits():
    return [("dp", mask) for mask in high_bits("dp")]


def lanes_of(rows):
    first = rows // 32 * 16
    return ((0, first), (first, rows))


def moves_kernel(tasks, count, places, *refs):
    sources, outs, sems = refs[:count], refs[count:-1], refs[-1]
    copies = []
    for at, (source, span, out, turns, rows) in enumerate(tasks):
        dims = len(sources[source].shape) - 2
        every = [slice(None)] * dims
        start = [
            pl.ds(1 - places[dim] if turns[dim] else places[dim], 1) if dim in turns else slice(None)
            for dim in range(dims)
        ]
        copies.append(
            pltpu.make_async_copy(
                sources[source].at[(*every, pl.ds(*span), slice(None))],
                outs[out].at[(*start, pl.ds(*rows), slice(None))],
                sems.at[at],
            )
        )
        copies[-1].start()
    for copy in copies:
        copy.wait()


def moves(wanted):
    sources = []
    tasks = []
    for out, (shape, pieces) in enumerate(wanted):
        for source, span, turns, rows in pieces:
            tasks.append((len(sources), span, out, turns, rows))
            sources.append(source)
    bits = column_bits() + row_bits()
    places = jnp.stack([bit_of(*bit) for bit in bits]).astype(jnp.int32)
    return pl.pallas_call(
        functools.partial(moves_kernel, tasks, len(sources)),
        in_specs=[pl.BlockSpec(memory_space=pltpu.SMEM)]
        + [pl.BlockSpec(memory_space=pltpu.HBM)] * len(sources),
        out_specs=[pl.BlockSpec(memory_space=pltpu.VMEM)] * len(wanted),
        out_shape=[jax.ShapeDtypeStruct(shape, jnp.bfloat16) for shape, _ in wanted],
        scratch_shapes=[pltpu.SemaphoreType.DMA((len(tasks),))],
        compiler_params=pltpu.CompilerParams(vmem_limit_bytes=VMEM_BYTES),
        cost_estimate=LIGHT,
    )(places, *sources)


class Gather:
    def __init__(self, rows, lanes=True, single=False):
        self.dims = column_bits() + row_bits()
        near = row_bits()[-1:]
        self.rows = rows.shape[0]
        if lanes:
            far = [[[bit]] for bit in row_bits()[:-1]] if single else [[row_bits()[:-1]]]
            self.steps = far + [[near, column_bits()], [column_bits(), near]]
            self.spans = lanes_of(self.rows)
        else:
            self.steps = [[row_bits()[:-1]], [near + column_bits()]]
            self.spans = ((0, self.rows),)
        self.parts = [([rows.reshape((1,) * len(self.dims) + rows.shape)], [])]
        self.step = 0

    def pending(self):
        return [values for values, bits in self.parts]

    def resume(self, values):
        self.parts = [(value, bits) for value, (_, bits) in zip(values, self.parts)]

    def wanted(self):
        if not self.parts[0][1]:
            return []
        last = self.step == len(self.steps)
        split = not last and len(self.steps[self.step]) > len(self.parts)
        lanes = [(low, high - low) for low, high in self.spans]
        result = []
        for lane, (values, bits) in enumerate(self.parts):
            shape = [
                2 if bit in bits else size
                for bit, size in zip(self.dims, values[0].shape)
            ]
            pieces = [
                (value, {self.dims.index(bit): bit in turned for bit in bits})
                for value, turned in zip(values, subsets(bits))
            ]
            height = values[0].shape[-2]
            for low, size in lanes if split else [(0, height)]:
                block = [(value, (low, size), turns, (0, size)) for value, turns in pieces]
                result.append((tuple(shape) + (size, 128), block))
        if last:
            pieces = [
                (value, span, turns, lanes[lane])
                for lane, (_, block) in enumerate(result)
                for value, span, turns, _ in block
            ]
            result = [(result[0][0][:-2] + (self.rows, 128), pieces)]
        return result

    def launch(self, values):
        if not values:
            values = [self.parts[0][0][0]]
        if self.step < len(self.steps):
            self.parts = [
                ([value] + [swap(value, *bits) for bits in subsets(group)[1:]], group)
                for value, group in zip(values, self.steps[self.step])
            ]
        else:
            self.parts = [([values[0], swap(values[0], ("mp", 1))], [])]
        self.step += 1
        return values

    def bundles(self):
        shape = (1 << len(column_bits()), lax.axis_size("dp")) + self.parts[0][0][0].shape[-2:]
        return [value.reshape(shape) for value in self.parts[0][0]]


class Scatter:
    def __init__(self, keep, send, lanes=True):
        self.dims = column_bits() + row_bits()
        shape = (2,) * len(self.dims) + keep.shape[2:]
        near = row_bits()[-1:]
        far = row_bits()[:-1]
        if lanes:
            self.steps = [None, [column_bits(), near], [near, column_bits()], [far, far]]
            self.spans = lanes_of(keep.shape[2])
        else:
            self.steps = [None, [column_bits() + near], [far]]
            self.spans = (None,)
        self.lanes = [[] for _ in self.spans]
        self.raw = [keep.reshape(shape), send.reshape(shape)]
        self.step = 0

    def pending(self):
        return self.raw

    def resume(self, values):
        self.raw = list(values)

    def fold(self, lane, group=(), turned=()):
        total = 0.0
        for index, settled, span in self.lanes[lane]:
            value = self.raw[index]
            for bit in settled + list(group):
                place = bit_of(*bit)
                place = 1 - place if bit in turned else place
                value = lax.dynamic_slice_in_dim(value, place, 1, self.dims.index(bit))
            if span is not None:
                value = value[..., span[0] : span[1], :]
            total = total + value.astype(jnp.float32)
        return total

    def settle(self, lane, group, arrived, span):
        old = [(index, settled + group, part) for index, settled, part in self.lanes[lane]]
        self.lanes[lane] = old + [(index, [], span) for index in arrived]

    def wanted(self):
        return []

    def launch(self, values):
        groups = self.steps[self.step]
        whole = self.step == len(self.steps) - 1
        sent = []
        if groups is None:
            sent.append(self.raw[1])
            self.raw[1] = swap(self.raw[1], ("mp", 1))
            for lane, span in zip(self.lanes, self.spans):
                lane += [(0, [], span), (1, [], span)]
        elif whole:
            arrived = []
            for bits in subsets(groups[0])[1:]:
                out = [
                    self.fold(lane, groups[0], bits).astype(jnp.bfloat16)
                    for lane in range(len(self.lanes))
                ]
                out = jnp.concatenate(out, -2) if len(out) > 1 else out[0]
                arrived.append(len(self.raw))
                sent.append(out)
                self.raw.append(swap(out, *bits))
            for lane, span in enumerate(self.spans):
                self.settle(lane, groups[lane], arrived, span)
        else:
            for lane, group in enumerate(groups):
                arrived = []
                for bits in subsets(group)[1:]:
                    out = self.fold(lane, group, bits).astype(jnp.bfloat16)
                    arrived.append(len(self.raw))
                    sent.append(out)
                    self.raw.append(swap(out, *bits))
                self.settle(lane, group, arrived, None)
        self.step += 1
        return sent

    def rows(self):
        total = [self.fold(lane) for lane in range(len(self.lanes))]
        total = jnp.concatenate(total, -2) if len(total) > 1 else total[0]
        return total.reshape(total.shape[-2:])


def wave(flows, after=None, before=None):
    values = [flow.pending() for flow in flows]
    if after is not None:
        values, _ = lax.optimization_barrier((values, after))
    for flow, value in zip(flows, values):
        flow.resume(value)
    wanted = [flow.wanted() for flow in flows]
    joined = [value for part in wanted for value in part]
    made = list(moves(joined)) if joined else []
    sent = []
    for flow, part in zip(flows, wanted):
        sent += flow.launch([made.pop(0) for _ in part])
    if before is not None:
        before, _ = lax.optimization_barrier((before, sent))
    return before


def hold(flows, value):
    value, parts = lax.optimization_barrier((value, [flow.pending() for flow in flows]))
    for flow, part in zip(flows, parts):
        flow.resume(part)
    wave(flows)
    return value


def chunk_kernel(units, columns, rows_ref, cols_ref, *refs):
    outs = refs[-2:]
    product = lax.dot_general(
        rows_ref[...], cols_ref[...], (((0,), (0,)), ((), ())), preferred_element_type=jnp.float32
    ).astype(jnp.bfloat16)
    groups = outs[0].shape[0]
    chunks = outs[0].shape[1]
    for half, out in enumerate(outs):
        for group in range(groups):
            for part in range(columns):
                place = ((half * groups + group) * columns + part) * 128
                block = product[:, place : place + 128].reshape(chunks, units, 128)
                out[group, :, part * units : (part + 1) * units, :] = block


def chunks_into(bundle, total, start, rows_of, cols_of, lead, units, columns):
    count = lax.axis_size("dp")
    groups = 1 << len(column_bits())
    columns = columns // 128
    pixels = cols_of.shape[0]
    height = units * columns
    if lead > 1:
        steps, wide, chunks = lead, count * units, count
        place = lambda step: (0, 0, start // height + step, 0)
    else:
        steps, wide, chunks = count, units, 1
        place = lambda step: (0, step, start // height, 0)
    shape = jax.ShapeDtypeStruct((groups, count, total, 128), jnp.bfloat16)
    block = pl.BlockSpec((groups, chunks, height, 128), place)
    earlier = () if bundle is None else tuple(bundle)
    return pl.pallas_call(
        functools.partial(chunk_kernel, units, columns),
        grid=(steps,),
        in_specs=[
            pl.BlockSpec((pixels, wide), lambda step: (0, step)),
            pl.BlockSpec(cols_of.shape, lambda step: (0, 0)),
        ]
        + [pl.BlockSpec(memory_space=pltpu.HBM)] * len(earlier),
        out_specs=[block, block],
        out_shape=[shape, shape],
        input_output_aliases={2 + place: place for place in range(len(earlier))},
        compiler_params=pltpu.CompilerParams(vmem_limit_bytes=VMEM_BYTES),
        cost_estimate=LIGHT,
    )(rows_of, cols_of, *earlier)


def total_of(ref):
    return jnp.sum(ref[...], 0) if len(ref.shape) == 3 else ref[...]


def as_row(block):
    return jnp.concatenate([block[place : place + 1] for place in range(block.shape[0])], 1)


def as_rows(row):
    return jnp.concatenate(
        [row[:, place : place + 128] for place in range(0, row.shape[1], 128)], 0
    )


def hand_out(out, rows):
    missing = out.shape[-2] - sum(row.shape[0] for row in rows)
    if missing:
        rows = rows + [jnp.zeros((missing, 128), jnp.float32)]
    block = jnp.concatenate(rows, 0)
    out[...] = jnp.broadcast_to(block[None], out.shape) if len(out.shape) == 3 else block


def levels(total, first, width, count):
    rows = width // 128
    mean = total[first : first + rows] / count
    scale = lax.rsqrt(total[first + rows : first + 2 * rows] / count - mean * mean + EPS_NORM)
    return (as_row(mean), as_row(scale))


def standard(values, level):
    return (values - level[0]) * level[1]


def back_through(grad, centred, level, gain, mask, total, first, bias_first, count):
    rows = grad.shape[1] // 128
    gain_sum = as_row(total[first : first + rows] / count)
    bias_sum = as_row(total[bias_first : bias_first + rows] / count)
    return (gain * level[1]) * (grad - mask * (bias_sum + centred * gain_sum))


def column_sums(values, mask):
    weighted = values * mask
    return [
        as_rows(jnp.sum(weighted, 0, keepdims=True)),
        as_rows(jnp.sum(weighted * values, 0, keepdims=True)),
    ]


def product_sums(grad, centred):
    return as_rows(jnp.sum(grad * centred, 0, keepdims=True))


def plain_sums(grad):
    return as_rows(jnp.sum(grad, 0, keepdims=True))


def fetch(bundles, held, sems, start):
    rows = held.shape[3]
    copies = [
        pltpu.make_async_copy(ref.at[:, :, pl.ds(start, rows), :], held.at[half], sems.at[half])
        for half, ref in enumerate(bundles)
    ]
    for copy in copies:
        copy.start()
    return copies


def arrive(copies):
    for copy in copies:
        copy.wait()


def weight_part(held, chunk, chunks, start, units, columns):
    return jnp.concatenate(
        [
            held[half, group, chunk : chunk + chunks, start + part * units : start + (part + 1) * units, :]
            .reshape(chunks * units, 128)
            for half in range(2)
            for group in range(held.shape[1])
            for part in range(columns)
        ],
        1,
    )


def spots(core, groups, width):
    return [
        pl.multiple_of((2 * group + (core if half == 0 else 1 - core)) * width, 128)
        for half in range(2)
        for group in range(groups)
    ]


def in_turn(ref, core, groups):
    width = ref.shape[1] // (2 * groups)
    return jnp.concatenate([ref[:, pl.ds(at, width)] for at in spots(core, groups, width)], 1)


def in_order(ref, values, core, groups):
    width = ref.shape[1] // (2 * groups)
    for place, at in enumerate(spots(core, groups, width)):
        ref[:, pl.ds(at, width)] = values[:, place * width : (place + 1) * width]


def product(first, second):
    return lax.dot_general(
        first, second, (((1,), (0,)), ((), ())), preferred_element_type=jnp.float32
    )


def product_turned(first, second):
    return lax.dot_general(
        first, second, (((1,), (1,)), ((), ())), preferred_element_type=jnp.float32
    )


def many_in(values, held, units, columns):
    chunks = max(1, 256 // units)
    total = 0.0
    for chunk in range(0, held.shape[2], chunks):
        part = weight_part(held, chunk, chunks, 0, units, columns)
        total = total + product(
            values[:, chunk * units : (chunk + chunks) * units], part
        )
    return total


def many_out(values, held, units, columns):
    chunks = max(1, 256 // units)
    return [
        product_turned(values, weight_part(held, chunk, chunks, 0, units, columns))
        for chunk in range(0, held.shape[2], chunks)
    ]


def slid(values, offset):
    count = values.shape[0]
    return pltpu.roll(values, (-offset) % count, 0) if offset % count else values


def within(inside, drow, dcol):
    place = 3 * (drow + 1) + dcol + 1
    return inside[:, place : place + 1]


def first_layer(core, raw, mask, first, second, field, out, sums, held, sems):
    copies = fetch((first, second), held, sems, 0)
    core = core[0]
    weights = mask[...]
    width = raw.shape[2]
    for place in range(raw.shape[0]):
        part = raw[place].astype(jnp.float32) * weights
        field[:, place * width : (place + 1) * width] = part.astype(jnp.bfloat16)
    arrive(copies)
    result = many_in(field, held, held.shape[3], 1)
    in_order(out, result, core, held.shape[1])
    rows = column_sums(out[...], weights)
    pixels = weights.shape[0] // 4
    for part in (weights, weights[:pixels]):
        rows.append(jnp.broadcast_to(jnp.sum(part, 0, keepdims=True), (1, 128)))
    hand_out(sums, rows)


def side_layer(start, core, field, mask, first, second, out, sums, held, sems):
    copies = fetch((first, second), held, sems, start)
    core = core[0]
    pixels = mask.shape[0]
    arrive(copies)
    columns = out.shape[1] // (2 * held.shape[1] * 128)
    result = many_in(field[:pixels, :], held, held.shape[3] // columns, columns)
    in_order(out, result, core, held.shape[1])
    hand_out(sums, column_sums(out[...], mask[...]))


def spread_layer(start, norm, taps, core, before, sums_in, counts, tables, keep, mask_in, mask, inside,
                 first, second, cols, out, sums, held, sems):
    copies = fetch((first, second), held, sems, start)
    core = core[0]
    pixels = mask.shape[0]
    width = before.shape[1]
    counted = 0 if before.shape[0] > pixels else 1
    level = levels(total_of(sums_in), 0, width, counts[counted : counted + 1, :])
    act = standard(before[...], level) * tables[2 * norm : 2 * norm + 1, :] + tables[2 * norm + 1 : 2 * norm + 2, :]
    row = norm // 2
    hidden = jax.nn.silu(act) * mask_in[...] * keep[row : row + 1, :]
    for tap, phase, drow, dcol in taps:
        source = hidden[phase * pixels : (phase + 1) * pixels]
        moved = slid(source, drow * WO + dcol) * within(inside, drow, dcol)
        cols[:, tap * width : (tap + 1) * width] = moved.astype(jnp.bfloat16)
    arrive(copies)
    units = held.shape[3] // 9
    total = 0.0
    for tap in range(9):
        part = weight_part(held, 0, held.shape[2], tap * units, units, 1)
        total = total + product(cols[:, tap * width : (tap + 1) * width], part)
    in_order(out, total, core, held.shape[1])
    hand_out(sums, column_sums(out[...], mask[...]))


def widen_layer(start, norm, core, before, sums_in, counts, tables, keep, mask, first, second,
                hidden, out, sums, held, scratch, sems):
    copies = fetch((first, second), held, sems, start)
    core = core[0]
    level = levels(total_of(sums_in), 0, before.shape[1], counts[1:2, :])
    act = standard(before[...], level) * tables[2 * norm : 2 * norm + 1, :] + tables[2 * norm + 1 : 2 * norm + 2, :]
    row = norm // 2
    scratch[...] = jax.nn.silu(act) * mask[...] * keep[row : row + 1, :]
    hidden[...] = in_turn(scratch, core, held.shape[1]).astype(jnp.bfloat16)
    arrive(copies)
    parts = many_out(hidden[...], held, held.shape[3], 1)
    size = out.shape[1] // len(parts)
    for place, part in enumerate(parts):
        out[:, place * size : (place + 1) * size] = part
    hand_out(sums, column_sums(out[...], mask[...]))


def joined_acts(total, third, side, wide, count):
    width = third.shape[1]
    rows = width // 128
    centred_third = standard(third[...], levels(total, 0, width, count))
    centred_side = standard(side[...], levels(total, 2 * rows, width, count))
    act = (
        centred_third * wide[0:1, :]
        + wide[1:2, :]
        + (centred_side * wide[2:3, :] + wide[3:4, :])
    )
    return (centred_third, centred_side, act)


def narrow_layer(start, core, third, side, sums_in, counts, wide, mask, first, second,
                 above, out, sums, held, sems):
    copies = fetch((first, second), held, sems, start)
    core = core[0]
    centred_third, centred_side, act = joined_acts(
        total_of(sums_in), third, side, wide, counts[1:2, :]
    )
    above[...] = (jax.nn.silu(act) * mask[...]).astype(jnp.bfloat16)
    arrive(copies)
    result = many_in(above, held, held.shape[3], 1)
    in_order(out, result, core, held.shape[1])
    hand_out(sums, column_sums(out[...], mask[...]))


def last_layer(sixth, sums_in, counts, wide, above, cotangent, mask, out, grad, sums):
    level = levels(total_of(sums_in), 0, sixth.shape[1], counts[1:2, :])
    centred = standard(sixth[...], level)
    act = centred * wide[4:5, :] + wide[5:6, :] + above[...].astype(jnp.float32)
    weights = mask[...]
    result = (jax.nn.silu(act) * weights).astype(jnp.bfloat16)
    inner = weights * slope(act)
    width = out.shape[2]
    for place in range(out.shape[0]):
        span = slice(place * width, (place + 1) * width)
        out[place] = result[:, span]
        grad[:, span] = cotangent[place].astype(jnp.float32) * inner[:, span]
    result = grad[...]
    hand_out(sums, [product_sums(result, centred), plain_sums(result)])


def narrow_grad(grad, before, sums_in, counts, tables, norm, keep, mask):
    counted = 0 if norm == 0 else 1
    level = levels(total_of(sums_in), 0, before.shape[1], counts[counted : counted + 1, :])
    centred = standard(before[...], level)
    act = centred * tables[2 * norm : 2 * norm + 1, :] + tables[2 * norm + 1 : 2 * norm + 2, :]
    row = norm // 2
    result = grad * keep[row : row + 1, :] * mask * slope(act)
    return (result, [product_sums(result, centred), plain_sums(result)])


def narrow_back(norm, grad, before, sums_in, sums_back, counts, tables, mask):
    counted = 0 if norm == 0 else 1
    count = counts[counted : counted + 1, :]
    width = before.shape[1]
    level = levels(total_of(sums_in), 0, width, count)
    return back_through(
        grad[...],
        standard(before[...], level),
        level,
        tables[2 * norm : 2 * norm + 1, :],
        mask,
        total_of(sums_back),
        0,
        width // 128,
        count,
    )


def last_back(start, norm, core, grad, sixth, sums_six, back_six, counts, wide, before, sums_in, tables,
              keep, mask, first, second, grad_out, grad_in, sums, held, scratch, sems):
    copies = fetch((first, second), held, sems, start)
    core = core[0]
    width = sixth.shape[1]
    count = counts[1:2, :]
    level = levels(total_of(sums_six), 0, width, count)
    grad_out[...] = back_through(
        grad[...], standard(sixth[...], level), level, wide[4:5, :], mask[...], total_of(back_six), 0,
        width // 128, count,
    ).astype(jnp.bfloat16)
    arrive(copies)
    in_order(scratch, many_in(grad_out, held, held.shape[3], 1), core, held.shape[1])
    result, rows = narrow_grad(scratch[...], before, sums_in, counts, tables, norm, keep, mask[...])
    grad_in[...] = result
    hand_out(sums, rows)


def pair_back(start, norm, core, grad, third, side, sums_pair, back_pair, counts, wide, before, sums_in,
              tables, keep, mask, first, second, grad_third, grad_side, grad_in, sums, held, scratch,
              big, sems):
    copies = fetch((first, second), held, sems, start)
    core = core[0]
    width = third.shape[1]
    rows = width // 128
    count = counts[1:2, :]
    total = total_of(sums_pair)
    back = total_of(back_pair)
    groups = held.shape[1]
    level = levels(total, 0, width, count)
    grad_third[...] = back_through(
        grad[...], standard(third[...], level), level, wide[0:1, :], mask[...], back, 0, 2 * rows, count
    ).astype(jnp.bfloat16)
    arrive(copies)
    in_order(scratch, many_in(grad_third, held, held.shape[3], 1), core, groups)
    result, parts = narrow_grad(scratch[...], before, sums_in, counts, tables, norm, keep, mask[...])
    grad_in[...] = result
    hand_out(sums, parts)
    level = levels(total, 2 * rows, width, count)
    big[...] = back_through(
        grad[...], standard(side[...], level), level, wide[2:3, :], mask[...], back, rows, 2 * rows, count
    )
    grad_side[...] = in_turn(big, core, groups).astype(jnp.bfloat16)


def spread_back(start, norm, taps, core, grad, after, sums_after, back_after, counts, tables, before,
                sums_in, keep, mask_in, mask, inside, first, second, grad_out, grad_in, sums, held,
                scratch, sems):
    copies = fetch((first, second), held, sems, start)
    core = core[0]
    pixels = mask.shape[0]
    phases = before.shape[0] // pixels
    scratch[...] = narrow_back(norm + 1, grad, after, sums_after, back_after, counts, tables, mask[...])
    grad_out[...] = in_turn(scratch, core, held.shape[1]).astype(jnp.bfloat16)
    arrive(copies)
    units = held.shape[3] // 9
    totals = [0.0] * phases
    for tap, phase, drow, dcol in taps:
        part = weight_part(held, 0, held.shape[2], tap * units, units, 1)
        moved = product_turned(grad_out[...], part)
        totals[phase] = totals[phase] + slid(moved, -drow * WO - dcol) * within(inside, -drow, -dcol)
    hidden = jnp.concatenate(totals, 0) if phases > 1 else totals[0]
    result, rows = narrow_grad(hidden, before, sums_in, counts, tables, norm, keep, mask_in[...])
    grad_in[...] = result
    hand_out(sums, rows)


def narrow_layer_back(start, core, grad, fourth, sums_four, back_four, counts, tables, mask, grad_two,
                      third, side, sums_pair, wide, first, second, grad_out, grad_in, sums, held,
                      scratch, big, sems):
    copies = fetch((first, second), held, sems, start)
    core = core[0]
    scratch[...] = narrow_back(2, grad, fourth, sums_four, back_four, counts, tables, mask[...])
    grad_out[...] = in_turn(scratch, core, held.shape[1]).astype(jnp.bfloat16)
    arrive(copies)
    parts = many_out(grad_out[...], held, held.shape[3], 1)
    size = big.shape[1] // len(parts)
    for place, part in enumerate(parts):
        big[:, place * size : (place + 1) * size] = part
    centred_third, centred_side, act = joined_acts(
        total_of(sums_pair), third, side, wide, counts[1:2, :]
    )
    result = (grad_two[...] + big[...]) * mask[...] * slope(act)
    grad_in[...] = result
    hand_out(
        sums,
        [
            product_sums(result, centred_third),
            product_sums(result, centred_side),
            plain_sums(result),
        ],
    )


def side_back(start, grad, first, second, out, held, sems):
    copies = fetch((first, second), held, sems, start)
    arrive(copies)
    columns = grad.shape[1] // (2 * held.shape[1] * 128)
    parts = many_out(grad[...], held, held.shape[3] // columns, columns)
    size = out.shape[1] // len(parts)
    for place, part in enumerate(parts):
        out[:, place * size : (place + 1) * size] = part


def first_back(core, grad, before, sums_in, sums_back, counts, tables, mask, side, first, second,
               grad_out, out, held, scratch, sems):
    copies = fetch((first, second), held, sems, 0)
    core = core[0]
    scratch[...] = narrow_back(0, grad, before, sums_in, sums_back, counts, tables, mask[...])
    grad_out[...] = in_turn(scratch, core, held.shape[1]).astype(jnp.bfloat16)
    arrive(copies)
    parts = many_out(grad_out[...], held, held.shape[3], 1)
    size = side.shape[1] // len(parts)
    pixels = side.shape[0]
    weights = mask[...]
    width = out.shape[2]
    for place, part in enumerate(parts):
        owner = place * size // width
        span = slice(place * size % width, place * size % width + size)
        beside = side[:, place * size : (place + 1) * size]
        out[owner, :pixels, span] = ((part[:pixels] + beside) * weights[:pixels]).astype(jnp.bfloat16)
        out[owner, pixels:, span] = (part[pixels:] * weights[pixels:]).astype(jnp.bfloat16)


class Coming:
    def __init__(self, ref, copy):
        self.ref = ref
        self.copy = copy
        self.shape = ref.shape

    def settle(self):
        if self.copy is not None:
            self.copy.wait()
            self.copy = None

    def __getitem__(self, place):
        self.settle()
        return self.ref[place]


def framed(kernel, places, count, *refs):
    refs = list(refs)
    rest, held, sems = refs[: len(refs) - len(places) - 1], refs[-len(places) - 1 : -1], refs[-1]
    coming = []
    for at, place in enumerate(places):
        copy = pltpu.make_async_copy(rest[place], held[at], sems.at[at])
        copy.start()
        rest[place] = Coming(held[at], copy)
        coming.append(rest[place])
    kernel(*rest)
    for value in coming:
        value.settle()


def launch(kernel, shapes, values, bundles=(), rows=0, scratch=()):
    held = []
    sems = []
    if bundles:
        held = [pltpu.VMEM((2,) + bundles[0].shape[:2] + (rows, 128), jnp.bfloat16)]
        sems = [pltpu.SemaphoreType.DMA((2,))]
    places = [place for place, value in enumerate(values) if value.dtype != jnp.int32]
    specs = []
    for place, value in enumerate(values):
        space = pltpu.SMEM if value.dtype == jnp.int32 else pltpu.VMEM
        specs.append(pl.BlockSpec(memory_space=pltpu.HBM if place in places else space))
    late = []
    if places:
        kernel = functools.partial(framed, kernel, places, len(values))
        late = [pltpu.VMEM(values[place].shape, values[place].dtype) for place in places]
        late.append(pltpu.SemaphoreType.DMA((len(places),)))
    return pl.pallas_call(
        kernel,
        in_specs=specs + [pl.BlockSpec(memory_space=pltpu.HBM)] * len(bundles),
        out_specs=[pl.BlockSpec(memory_space=pltpu.VMEM)] * len(shapes),
        out_shape=list(shapes),
        scratch_shapes=held + [pltpu.VMEM(shape, jnp.float32) for shape in scratch] + sems + late,
        compiler_params=pltpu.CompilerParams(vmem_limit_bytes=VMEM_BYTES),
        cost_estimate=LIGHT,
    )(*values, *bundles)


def moved_by(grad, mean, square, weight, mean_out, square_out, update_out, at):
    first_fix = 1.0 - BETA_ONE**STEP
    second_fix = 1.0 - BETA_TWO**STEP
    old = weight[at]
    mean_next, square_next, step = adapt(grad, mean[at], square[at], first_fix, second_fix)
    update = step + DECAY * old
    mean_out[at] = mean_next
    square_out[at] = square_next
    update_out[at] = update
    result = []
    for value in (old, update):
        power = value * value
        while len(power.shape) > 2:
            power = jnp.sum(power, 0)
        row = jnp.sum(power, 0, keepdims=True)
        result.append(
            sum(row[:, place : place + 128] for place in range(0, row.shape[1], 128))
        )
    return result


def early_moves(columns, rows_a, rows_c, short_m, short_v, short_w, last_m, last_v, last_w, second_m, second_v,
                second_w, short_mo, short_vo, short_uo, last_mo, last_vo, last_uo, second_mo, second_vo,
                second_uo, powers):
    unit_in = short_w.shape[0]
    unit_out = second_w.shape[0]
    parts = short_w.shape[1] // 128
    every = (slice(None), slice(None))
    grad = jnp.concatenate(
        [rows_c[part * unit_in : (part + 1) * unit_in, :] for part in range(parts)], 1
    )
    found = moved_by(grad, short_m, short_v, short_w, short_mo, short_vo, short_uo, every)
    start = parts * unit_in
    for block, rows in enumerate((rows_c[start : start + unit_out, :], rows_a[...])):
        found += moved_by(
            jnp.transpose(rows), last_m, last_v, last_w, last_mo, last_vo, last_uo, block
        )
    start += unit_out
    found += moved_by(
        rows_c[start : start + unit_out, :], second_m, second_v, second_w, second_mo, second_vo,
        second_uo, every,
    )
    powers[...] = jnp.concatenate(found, 0)


def late_moves(rows_b, rows_d, rows_e, powers_in, first_m, first_v, first_w, mid_m, mid_v, mid_w, first_mo,
               first_vo, first_uo, mid_mo, mid_vo, mid_uo, powers):
    every = (slice(None), slice(None))
    found = moved_by(
        rows_e[...], first_m, first_v, first_w, first_mo, first_vo, first_uo, every
    )
    shape = mid_w.shape[1:]
    middle = []
    for block, rows in enumerate((rows_d, rows_b)):
        middle += moved_by(
            rows[...].reshape(shape), mid_m, mid_v, mid_w, mid_mo, mid_vo, mid_uo, block
        )
    early = powers_in[...]
    order = [found[0], found[1], early[0:2]] + middle + [early[2:8]]
    hand_out(powers, order)


def final_moves(powers, first_w, first_u, short_w, short_u, mid_w, mid_u, last_w, last_u, second_w, second_u,
                norms, first_o, short_o, mid_o, last_o, second_o, first_c, short_c, mid_c, last_c, second_c):
    total = jnp.sqrt(jnp.sum(jnp.sum(powers[...], 0), 1, keepdims=True))
    norms[...] = jnp.broadcast_to(total, norms.shape)

    def step(row, weight, update, out, copy, at):
        ratio = total[2 * row : 2 * row + 1] / (total[2 * row + 1 : 2 * row + 2] + EPS_TRUST)
        fresh = weight[at] - (RATE * ratio) * update[at]
        out[at] = fresh
        copy[at] = fresh.astype(jnp.bfloat16)

    every = (slice(None), slice(None))
    step(0, first_w, first_u, first_o, first_c, every)
    step(1, short_w, short_u, short_o, short_c, every)
    for block in range(2):
        for tap in range(mid_w.shape[1]):
            step(2 + block, mid_w, mid_u, mid_o, mid_c, (block, tap))
        step(4 + block, last_w, last_u, last_o, last_c, block)
    step(6, second_w, second_u, second_o, second_c, every)


def exchange(copies):
    return lax.all_to_all(copies, ("dp", "mp"), 0, 0, tiled=True)


def by_image(
    inputs,
    pixel_mask,
    widths,
    output_grad,
    first_weight,
    shortcut_weight,
    middle_weight,
    last_weight,
    second_weight,
    narrow_norms,
    wide_norms,
    first_mean,
    first_square,
    shortcut_mean,
    shortcut_square,
    middle_mean,
    middle_square,
    last_mean,
    last_square,
    second_mean,
    second_square,
    narrow_mean,
    narrow_square,
    wide_mean,
    wide_square,
):
    ranks = lax.axis_size("mp")
    rank = lax.axis_index("mp")
    pixels = pixel_mask.shape[1] // ranks
    narrow = first_weight.shape[1] * ranks
    wide = shortcut_weight.shape[1] * ranks
    low = jnp.bfloat16
    channels = inputs.shape[0]
    field = inputs.reshape(channels, 4, ranks, pixels).transpose(2, 1, 3, 0)
    field = field.reshape(ranks, 4 * pixels, channels)
    flow_a = Gather(pack(first_weight.astype(low)[None]), False)
    flow_b = Gather(pack(middle_weight[0].astype(low)))
    flow_c = Gather(
        jnp.concatenate(
            [
                pack(shortcut_weight.astype(low)[None]),
                pack(last_weight[0].astype(low).T[None]),
                pack(second_weight.astype(low)[None]),
            ]
        )
    )
    flow_d = Gather(
        jnp.concatenate(
            [pack(last_weight[1].astype(low).T[None]), pack(middle_weight[1].astype(low))]
        ),
        single=True,
    )
    field = lax.all_to_all(field, "mp", 0, 0, tiled=True)
    tables = jnp.concatenate([narrow_norms.reshape(-1, 128), wide_norms.reshape(-1, 128)], 0)
    tables = jnp.broadcast_to(tables[None], (ranks,) + tables.shape)
    tables = lax.all_to_all(tables, "mp", 0, 0, tiled=True)
    wave([flow_a, flow_b])
    wave([flow_a, flow_b, flow_c], field)
    wave([flow_a, flow_b, flow_d], (flow_c.pending(), tables))
    unit_in, column = first_weight.shape
    column_wide = shortcut_weight.shape[1]
    unit_mid = middle_weight.shape[2]
    unit_out = second_weight.shape[0]
    size_short = unit_in * column_wide // 128
    size_out = unit_out * column // 128
    size_mid = 9 * unit_mid * column // 128
    split = narrow_norms.size // 128
    narrow_all = (
        tables[:, :split].reshape(ranks, 4, 2, -1).transpose(1, 2, 0, 3).reshape(4, 2, narrow)
    )
    wide_all = tables[:, split:].reshape(ranks, 3, 2, -1).transpose(1, 2, 0, 3).reshape(3, 2, wide)

    narrow_all = narrow_all.reshape(8, narrow)
    wide_all = jnp.concatenate([wide_all.reshape(6, wide), jnp.zeros((2, wide), jnp.float32)], 0)

    own_mask = lax.dynamic_slice_in_dim(pixel_mask, rank * pixels, pixels, 1).astype(jnp.float32)
    mask_in = own_mask.reshape(-1, 1)
    mask = own_mask[0][:, None]
    channel = lax.iota(jnp.int32, narrow)[None]
    keep = (channel < widths[:, None]).astype(jnp.float32)
    keep = jnp.concatenate([keep, jnp.zeros((6, narrow), jnp.float32)], 0)
    place = lax.iota(jnp.int32, pixels)[:, None]
    step = lax.iota(jnp.int32, 9)[None]
    row_at = place // WO % HO + step // 3 - 1
    col_at = place % WO + step % 3 - 1
    inside = (row_at >= 0) & (row_at < HO) & (col_at >= 0) & (col_at < WO)
    inside = inside.astype(jnp.float32)
    core = bit_of("mp", 1)[None]

    above = output_grad.reshape(-1, ranks, pixels).transpose(1, 2, 0)
    above = lax.all_to_all(above, "mp", 0, 0, tiled=True)

    devices = ranks * lax.axis_size("dp")
    full = 4 * pixels

    def real(*shape):
        return jax.ShapeDtypeStruct(shape, jnp.float32)

    def short(*shape):
        return jax.ShapeDtypeStruct(shape, low)

    size = narrow // 128
    wide_rows = wide // 128
    copies = real(devices, 2 * size, 128)
    bundle_a = flow_a.bundles()
    field, pre_one, sums = launch(
        first_layer,
        [short(full, ranks * channels), real(full, narrow), real(devices, 2 * size + 8, 128)],
        [core, field, mask_in],
        bundle_a,
        unit_in,
    )
    sums_one = wave([flow_c], sums, exchange(sums))
    sums_one = hold([flow_b, flow_c, flow_d], sums_one)
    for _ in range(len(row_bits()) - 3):
        wave([flow_d])
    counts = jnp.sum(sums_one[:, 2 * size :], 0)
    bundle_b = flow_b.bundles()
    cols_one, pre_two, sums = launch(
        functools.partial(spread_layer, 0, 0, STRIDED_TAPS),
        [short(pixels, 9 * narrow), real(pixels, narrow), copies],
        [core, pre_one, sums_one, counts, narrow_all, keep, mask_in, mask, inside],
        bundle_b,
        size_mid,
    )
    sums_two = hold([flow_c, flow_d], exchange(sums))
    bundle_c = flow_c.bundles()
    pre_side, side_sums = launch(
        functools.partial(side_layer, 0),
        [real(pixels, wide), real(2 * wide_rows, 128)],
        [core, field, mask],
        bundle_c,
        size_short,
    )
    hid_two, pre_three, sums = launch(
        functools.partial(widen_layer, size_short, 1),
        [short(pixels, narrow), real(pixels, wide), real(2 * wide_rows, 128)],
        [core, pre_two, sums_two, counts, narrow_all, keep, mask],
        bundle_c,
        size_out,
        [(pixels, narrow)],
    )
    sums_pair = everywhere(jnp.concatenate([sums, side_sums], 0), [flow_d])
    out_one, pre_four, sums = launch(
        functools.partial(narrow_layer, size_short + size_out),
        [short(pixels, wide), real(pixels, narrow), copies],
        [core, pre_three, pre_side, sums_pair, counts, wide_all, mask],
        bundle_c,
        size_out,
    )
    sums_four = wave([flow_d], sums, exchange(sums))
    bundle_d = flow_d.bundles()
    cols_four, pre_five, sums = launch(
        functools.partial(spread_layer, size_out, 2, PLAIN_TAPS),
        [short(pixels, 9 * narrow), real(pixels, narrow), copies],
        [core, pre_four, sums_four, counts, narrow_all, keep, mask, mask, inside],
        bundle_d,
        size_mid,
    )
    sums_five = exchange(sums)
    hid_five, pre_six, sums = launch(
        functools.partial(widen_layer, 0, 3),
        [short(pixels, narrow), real(pixels, wide), real(2 * wide_rows, 128)],
        [core, pre_five, sums_five, counts, narrow_all, keep, mask],
        bundle_d,
        size_out,
        [(pixels, narrow)],
    )
    sums_six = everywhere(sums)
    block_output, grad_two, sums = launch(
        last_layer,
        [short(*above.shape), real(pixels, wide), real(2 * wide_rows, 128)],
        [pre_six, sums_six, counts, wide_all, out_one, above, mask],
    )
    back_six = everywhere(sums)

    grad_six, act_five_grad, sums = launch(
        functools.partial(last_back, 0, 3),
        [short(pixels, wide), real(pixels, narrow), copies],
        [core, grad_two, pre_six, sums_six, back_six, counts, wide_all, pre_five,
         sums_five, narrow_all, keep, mask],
        bundle_d,
        size_out,
        [(pixels, narrow)],
    )
    bundle = chunks_into(None, size_out, 0, grad_six, hid_five, 1, unit_out, column)
    back_a = Scatter(*bundle, False)
    back_five = hold([back_a], exchange(sums))
    grad_five, act_four_grad, sums = launch(
        functools.partial(spread_back, size_out, 2, PLAIN_TAPS),
        [short(pixels, narrow), real(pixels, narrow), copies],
        [core, act_five_grad, pre_five, sums_five, back_five, counts, narrow_all,
         pre_four, sums_four, keep, mask, mask, inside],
        bundle_d,
        size_mid,
        [(pixels, narrow)],
    )
    back_four = exchange(sums)
    bundle = chunks_into(None, size_mid, 0, cols_four, grad_five, 9, unit_mid, column)
    back_b = Scatter(*bundle)
    back_four = wave([back_a], sums, back_four)
    back_four = hold([back_b], back_four)
    grad_four, grad_one, sums = launch(
        functools.partial(narrow_layer_back, size_short + size_out),
        [short(pixels, narrow), real(pixels, wide), real(3 * wide_rows, 128)],
        [core, act_four_grad, pre_four, sums_four, back_four, counts, narrow_all, mask,
         grad_two, pre_three, pre_side, sums_pair, wide_all],
        bundle_c,
        size_out,
        [(pixels, narrow), (pixels, wide)],
    )
    back_pair = everywhere(sums, [back_a, back_b])
    total = size_short + 2 * size_out
    bundle = chunks_into(
        None, total, size_short + size_out, out_one, grad_four, 1, unit_out, column
    )
    back_pair, bundle = lax.optimization_barrier((back_pair, bundle))
    grad_three, grad_side, act_two_grad, sums = launch(
        functools.partial(pair_back, size_short, 1),
        [short(pixels, wide), short(pixels, wide), real(pixels, narrow), copies],
        [core, grad_one, pre_three, pre_side, sums_pair, back_pair, counts, wide_all,
         pre_two, sums_two, narrow_all, keep, mask],
        bundle_c,
        size_out,
        [(pixels, narrow), (pixels, wide)],
    )
    back_two = wave([back_b], sums, exchange(sums))
    bundle = chunks_into(bundle, total, size_short, grad_three, hid_two, 1, unit_out, column)
    bundle = chunks_into(bundle, total, 0, field, grad_side, 1, unit_in, column_wide)
    back_c = Scatter(*bundle)
    back_two = hold([back_c], back_two)
    back_two = wave([back_c], None, back_two)
    grad_mid, act_one_grad, sums = launch(
        functools.partial(spread_back, 0, 0, STRIDED_TAPS),
        [short(pixels, narrow), real(full, narrow), copies],
        [core, act_two_grad, pre_two, sums_two, back_two, counts, narrow_all, pre_one,
         sums_one, keep, mask_in, mask, inside],
        bundle_b,
        size_mid,
        [(pixels, narrow)],
    )
    back_one = wave([back_c], sums, exchange(sums))
    bundle = chunks_into(None, size_mid, 0, cols_one, grad_mid, 9, unit_mid, column)
    back_d = Scatter(*bundle)
    (side_grad,) = launch(
        functools.partial(side_back, 0),
        [real(pixels, field.shape[1])],
        [grad_side],
        bundle_c,
        size_short,
    )
    back_one = hold([back_d], back_one)
    back_one, side_grad = lax.optimization_barrier((back_one, side_grad))
    grad_first, field_grad = launch(
        first_back,
        [short(full, narrow), short(ranks, full, channels)],
        [core, act_one_grad, pre_one, sums_one, back_one, counts, narrow_all, mask_in,
         side_grad],
        bundle_a,
        unit_in,
        [(full, narrow)],
    )
    grad_first = wave([back_b, back_c, back_d], back_one, grad_first)
    bundle = chunks_into(None, unit_in * column // 128, 0, field, grad_first, 1, unit_in, column)
    back_e = Scatter(*bundle, False)
    wave([back_e])
    input_grad = lax.all_to_all(field_grad, "mp", 0, 0, tiled=True)
    input_grad = input_grad.reshape(ranks, 4, pixels, channels).transpose(3, 1, 0, 2)
    input_grad = input_grad.reshape(inputs.shape)
    wave([back_d, back_e])
    wave([back_d, back_e])
    rows_a, rows_b, rows_c, rows_d, rows_e = [
        flow.rows() for flow in (back_a, back_b, back_c, back_d, back_e)
    ]
    first_fix = 1.0 - BETA_ONE**STEP
    second_fix = 1.0 - BETA_TWO**STEP

    def like(*values):
        return [real(*value.shape) for value in values for _ in range(3)]

    early = launch(
        functools.partial(early_moves, column),
        like(shortcut_weight, last_weight, second_weight) + [real(8, 128)],
        [rows_a, rows_c]
        + [
            shortcut_mean, shortcut_square, shortcut_weight, last_mean, last_square, last_weight,
            second_mean, second_square, second_weight,
        ],
    )
    block_output, _ = lax.optimization_barrier((block_output, early[-1]))
    block_output = lax.all_to_all(block_output, "mp", 0, 0, tiled=True)
    block_output = block_output.transpose(2, 0, 1).reshape(-1, ranks * pixels)
    late = launch(
        late_moves,
        like(first_weight, middle_weight) + [real(devices, 16, 128)],
        [rows_b, rows_d, rows_e, early[-1]]
        + [first_mean, first_square, first_weight, middle_mean, middle_square, middle_weight],
    )
    powers = exchange(late[-1])
    weights = (first_weight, shortcut_weight, middle_weight, last_weight, second_weight)
    updates = (late[2], early[2], late[5], early[5], early[8])
    norms, *fresh = launch(
        final_moves,
        [real(16, 128)]
        + [real(*value.shape) for value in weights]
        + [short(*value.shape) for value in weights],
        [powers]
        + [value for pair in zip(weights, updates) for value in pair],
    )
    matrix_norms = norms[:14, 0].reshape(7, 2)
    first_next, short_next, middle_next, last_next, second_next = fresh[:5]
    states = [late[0:2], early[0:2], late[3:5], early[3:5], early[6:8]]

    def own_channels(values):
        width = values.shape[-1] // ranks
        return lax.dynamic_slice_in_dim(values, rank * width, width, values.ndim - 1)

    narrow_grads = jnp.stack([jnp.sum(rows, 0) for rows in (back_one, back_two, back_four, back_five)])
    narrow_grad = own_channels(narrow_grads.reshape(4, 2, narrow))
    gain_three, gain_side, bias_pair = jnp.sum(back_pair, 0).reshape(3, wide)
    wide_grad = own_channels(
        jnp.stack(
            [
                jnp.stack([gain_three, bias_pair]),
                jnp.stack([gain_side, bias_pair]),
                jnp.sum(back_six, 0).reshape(2, wide),
            ]
        )
    )
    narrow_mean_next, narrow_square_next, narrow_step = adapt(
        narrow_grad, narrow_mean, narrow_square, first_fix, second_fix
    )
    wide_mean_next, wide_square_next, wide_step = adapt(
        wide_grad, wide_mean, wide_square, first_fix, second_fix
    )
    return (
        block_output,
        input_grad,
        states[0][0],
        states[0][1],
        first_next,
        states[1][0],
        states[1][1],
        short_next,
        states[2][0],
        states[2][1],
        middle_next,
        states[3][0],
        states[3][1],
        last_next,
        states[4][0],
        states[4][1],
        second_next,
        narrow_mean_next,
        narrow_square_next,
        narrow_norms - RATE_NORM * narrow_step,
        wide_mean_next,
        wide_square_next,
        wide_norms - RATE_NORM * wide_step,
        matrix_norms,
        *fresh[5:],
    )


def solution(mesh):
    in_specs = (
        P("mp", None, "dp"),
        P(None, "dp"),
        P(),
        P("mp", "dp"),
        P("dp", "mp"),
        P("dp", "mp"),
        P(None, None, "dp", "mp"),
        P(None, "mp", "dp"),
        P("dp", "mp"),
        P(None, None, "mp"),
        P(None, None, "mp"),
        P("dp", "mp"),
        P("dp", "mp"),
        P("dp", "mp"),
        P("dp", "mp"),
        P(None, None, "dp", "mp"),
        P(None, None, "dp", "mp"),
        P(None, "mp", "dp"),
        P(None, "mp", "dp"),
        P("dp", "mp"),
        P("dp", "mp"),
        P(None, None, "mp"),
        P(None, None, "mp"),
        P(None, None, "mp"),
        P(None, None, "mp"),
    )
    out_specs = (
        P("mp", "dp"),
        P("mp", None, "dp"),
        P("dp", "mp"),
        P("dp", "mp"),
        P("dp", "mp"),
        P("dp", "mp"),
        P("dp", "mp"),
        P("dp", "mp"),
        P(None, None, "dp", "mp"),
        P(None, None, "dp", "mp"),
        P(None, None, "dp", "mp"),
        P(None, "mp", "dp"),
        P(None, "mp", "dp"),
        P(None, "mp", "dp"),
        P("dp", "mp"),
        P("dp", "mp"),
        P("dp", "mp"),
        P(None, None, "mp"),
        P(None, None, "mp"),
        P(None, None, "mp"),
        P(None, None, "mp"),
        P(None, None, "mp"),
        P(None, None, "mp"),
        P(),
        P("dp", "mp"),
        P("dp", "mp"),
        P(None, None, "dp", "mp"),
        P(None, "mp", "dp"),
        P("dp", "mp"),
    )
    return jax.shard_map(
        lambda *values: (by_image if fits(mesh, values[1]) else shards)(*values),
        mesh=mesh,
        in_specs=in_specs,
        out_specs=out_specs,
        check_vma=False,
    )
```
